32 devices in a mesh: fsdp: 16 (over z, y, core), seq: 2 (over x).
Axes of the slice: x: 2, y: 2, z: 4, core: 2. Of those that a mesh axis runs over, the one named last changes fastest.
Arguments:
- tokens: bfloat16 [16, 1376, 1024], P('fsdp', 'seq'), may hold values from -6 to 6
- lengths: int32 [16], P('fsdp'), may hold values from 1032 to 1376
- norm1_gain: bfloat16 [1024], P('fsdp'), may hold values from 0.5 to 1.5
- norm1_bias: bfloat16 [1024], P('fsdp'), may hold values from -1.5 to 1.5
- packed_weight: bfloat16 [1024, 3072], P('fsdp'), may hold values from -0.1875 to 0.1875
- query_bias: bfloat16 [1024], P('fsdp'), may hold values from -1.5 to 1.5
- value_bias: bfloat16 [1024], P('fsdp'), may hold values from -1.5 to 1.5
- output_weight: bfloat16 [1024, 1024], P('fsdp'), may hold values from -2.5 to 2.5
- output_bias: bfloat16 [1024], P('fsdp'), may hold values from -1.5 to 1.5
- layer_scale1: bfloat16 [1024], P('fsdp'), may hold values from 0.5 to 1.5
- norm2_gain: bfloat16 [1024], P('fsdp'), may hold values from 0.5 to 1.5
- norm2_bias: bfloat16 [1024], P('fsdp'), may hold values from -1.5 to 1.5
- up_weight: bfloat16 [1024, 4096], P('fsdp'), may hold values from -0.1875 to 0.1875
- up_bias: bfloat16 [4096], P('fsdp'), may hold values from -1.5 to 1.5
- down_weight: bfloat16 [4096, 1024], P('fsdp'), may hold values from -0.125 to 0.125
- down_bias: bfloat16 [1024], P('fsdp'), may hold values from -1.5 to 1.5
- layer_scale2: bfloat16 [1024], P('fsdp'), may hold values from 0.5 to 1.5
- cotangent: bfloat16 [16, 1376, 1024], P('fsdp', 'seq'), may hold values from -6 to 6
Outputs:
- output: bfloat16 [16, 1376, 1024], P('fsdp', 'seq')
- grad_tokens: float32 [16, 1376, 1024], P('fsdp', 'seq')
- grad_norm1_gain: float32 [1024], P('fsdp')
- grad_norm1_bias: float32 [1024], P('fsdp')
- grad_packed_weight: float32 [1024, 3072], P('fsdp')
- grad_query_bias: float32 [1024], P('fsdp')
- grad_value_bias: float32 [1024], P('fsdp')
- grad_output_weight: float32 [1024, 1024], P('fsdp')
- grad_output_bias: float32 [1024], P('fsdp')
- grad_layer_scale1: float32 [1024], P('fsdp')
- grad_norm2_gain: float32 [1024], P('fsdp')
- grad_norm2_bias: float32 [1024], P('fsdp')
- grad_up_weight: float32 [1024, 4096], P('fsdp')
- grad_up_bias: float32 [4096], P('fsdp')
- grad_down_weight: float32 [4096, 1024], P('fsdp')
- grad_down_bias: float32 [1024], P('fsdp')
- grad_layer_scale2: float32 [1024], P('fsdp')
The draws below stay inside these ranges and needn't reach their ends.
Inputs may be any that keep to these rules, and one draw needn't show every extreme that they name: Positions from lengths[b] on of image b are padding.
All inputs are finite; a program needn't handle non-finite values.
Results may differ from the reference program's by a relative error of at most 0.02.
Values may be sent and summed in bfloat16 or wider, within the bound.
No kernel may reach another device: no remote copies, remote signals or barrier semaphores. Data moves between devices by JAX's collectives and lax.ppermute only.
A program may use at most 384 MiB of HBM per device.

```python
import jax
import jax.numpy as jnp
from jax import lax

D = 1024
H = 16
HD = 64
FF = 4096
SEQ_LEN = 1376
IMAGES = 16
N_SEQ = 2


def set_ends(entries, own_key, least, high):
    index_at = [jax.random.randint(jax.random.fold_in(own_key, axis), (), 0, length) for axis, length in enumerate(entries.shape)]
    main_axis = entries.shape.index(max(entries.shape))
    next_to = index_at[:main_axis] + [(index_at[main_axis] + 1) % entries.shape[main_axis]] + index_at[main_axis + 1:]
    return entries.at[tuple(index_at)].set(least).at[tuple(next_to)].set(high)


def level_of(rng, extent, shards, least, high):
    factor_of = 1.0
    for position, parts in shards:
        steps = jax.random.uniform(jax.random.fold_in(jax.random.fold_in(rng, 6), position), (parts,), jnp.float32, least / len(shards), high / len(shards))
        factor_of = factor_of * jnp.repeat(jnp.exp(steps), extent[position] // parts).reshape((-1,) + (1,) * (len(extent) - 1 - position))
    return factor_of


def noise(stream_key, dims, deviation, most, split=(), held_as=jnp.bfloat16):
    drawn = deviation * jax.random.normal(stream_key, dims, jnp.float32)
    if split:
        drawn = drawn * level_of(stream_key, dims, split, -0.22, 0.18)
    return jnp.clip(drawn, -most, most).astype(held_as)


def setup_inputs(seed: int = 0) -> dict:
    key_list = jax.random.split(jax.random.key(seed), 19)
    return {
        "tokens": noise(key_list[0], (IMAGES, SEQ_LEN, D), 1.0, 6.0, ((0, 16), (1, 2))),
        "lengths": set_ends(jax.random.randint(key_list[1], (IMAGES,), SEQ_LEN - SEQ_LEN // (2 * N_SEQ), SEQ_LEN + 1), jax.random.fold_in(key_list[1], 1), SEQ_LEN - SEQ_LEN // (2 * N_SEQ), SEQ_LEN).astype(jnp.int32),
        "norm1_gain": jnp.clip(1.0 + 0.1 * jax.random.normal(key_list[2], (D,), jnp.float32), 0.5, 1.5).astype(jnp.bfloat16),
        "norm1_bias": noise(key_list[3], (D,), 0.3, 1.5, ((0, 16),)),
        "packed_weight": noise(key_list[4], (D, 3 * D), D ** -0.5, 0.1875, ((0, 16),)),
        "query_bias": noise(key_list[5], (D,), 0.3, 1.5, ((0, 16),)),
        "value_bias": noise(key_list[6], (D,), 0.3, 1.5, ((0, 16),)),
        "output_weight": noise(key_list[7], (D, D), (max(1, D * 8 // SEQ_LEN)) ** -0.5, 2.5, ((0, 16),)),
        "output_bias": noise(key_list[8], (D,), 0.3, 1.5, ((0, 16),)),
        "layer_scale1": jnp.clip(0.5 + 1.0 * jax.random.uniform(key_list[9], (D,), jnp.float32) ** level_of(key_list[9], (D,), ((0, 16),), -0.2, 0.2), 0.5, 1.5).astype(jnp.bfloat16),
        "norm2_gain": jnp.clip(1.0 + 0.1 * jax.random.normal(key_list[10], (D,), jnp.float32), 0.5, 1.5).astype(jnp.bfloat16),
        "norm2_bias": noise(key_list[11], (D,), 0.3, 1.5, ((0, 16),)),
        "up_weight": noise(key_list[12], (D, FF), D ** -0.5, 0.1875, ((0, 16),)),
        "up_bias": noise(key_list[13], (FF,), 0.3, 1.5, ((0, 16),)),
        "down_weight": noise(key_list[14], (FF, D), (FF // 2) ** -0.5, 0.125, ((0, 16),)),
        "down_bias": noise(key_list[15], (D,), 0.3, 1.5, ((0, 16),)),
        "layer_scale2": jnp.clip(0.5 + 1.0 * jax.random.uniform(key_list[16], (D,), jnp.float32) ** level_of(key_list[16], (D,), ((0, 16),), -0.2, 0.2), 0.5, 1.5).astype(jnp.bfloat16),
        "cotangent": noise(key_list[17], (IMAGES, SEQ_LEN, D), 1.0, 6.0, ((0, 16), (1, 2))),
    }


@jax.custom_vjp
def low(v):
    return lax.optimization_barrier(v.astype(jnp.bfloat16)).astype(jnp.float32)

@jax.custom_vjp
def low_back(v):
    return v

def low_keep(v):
    return (low(v), None)

def low_pass(kept, grad):
    return (grad,)

def back_keep(v):
    return (v, None)

def back_low(kept, grad):
    return (low(grad),)
low.defvjp(low_keep, low_pass)
low_back.defvjp(back_keep, back_low)
norm_eps = 1e-06
highest = lax.Precision.HIGHEST

def layer_norm(values, norm_gain, norm_shift):
    center = values - lax.optimization_barrier(jnp.mean(values, axis=-1, keepdims=True))
    spread = lax.optimization_barrier(jnp.mean(center * center, axis=-1, keepdims=True))
    return center * lax.rsqrt(spread + norm_eps) * norm_gain + norm_shift

def product(left, right):
    return jnp.dot(left, right, precision=highest)

def forward(patches, valid_count, params):
    gain_one, shift_one, packed_matrix, query_shift, value_shift, output_matrix, output_shift, scale_one, gain_two, shift_two, up_matrix, up_shift, down_matrix, down_shift, scale_two = params
    score_scale = HD ** (-0.5)
    normed = low(layer_norm(patches, gain_one, shift_one))
    packed_shift = jnp.concatenate([query_shift, jnp.zeros_like(query_shift), value_shift])
    packed = low(low_back(product(normed, packed_matrix) + packed_shift)).reshape(SEQ_LEN, 3, H, HD)
    scores = low_back(score_scale * jnp.einsum('qhd,khd->hqk', packed[:, 0], packed[:, 1], precision=highest))
    key_valid = jnp.arange(SEQ_LEN) < valid_count
    scores = jnp.where(key_valid[None, None, :], scores, -jnp.inf)
    largest = lax.optimization_barrier(jnp.max(scores, axis=-1, keepdims=True))
    exponent = jnp.exp(scores - largest)
    attention = exponent / lax.optimization_barrier(jnp.sum(exponent, axis=-1, keepdims=True))
    mixture = jnp.einsum('hqk,khd->qhd', low(attention), packed[:, 2], precision=highest)
    mixture = low(low_back(mixture)).reshape(SEQ_LEN, H * HD)
    branch_one = low_back(product(mixture, output_matrix) + output_shift)
    middle = patches + scale_one * branch_one
    normed_two = low(layer_norm(middle, gain_two, shift_two))
    hidden = low_back(product(normed_two, up_matrix) + up_shift)
    active = low(jax.nn.gelu(hidden, approximate=False))
    branch_two = low_back(product(active, down_matrix) + down_shift)
    return middle + scale_two * branch_two

def reference(tokens, lengths, norm1_gain, norm1_bias, packed_weight, query_bias, value_bias, output_weight, output_bias, layer_scale1, norm2_gain, norm2_bias, up_weight, up_bias, down_weight, down_bias, layer_scale2, cotangent):
    params = tuple((entry.astype(jnp.float32) for entry in (norm1_gain, norm1_bias, packed_weight, query_bias, value_bias, output_weight, output_bias, layer_scale1, norm2_gain, norm2_bias, up_weight, up_bias, down_weight, down_bias, layer_scale2)))

    def one_image(totals, per_image):
        patches, valid_count, upstream = per_image
        result, pullback = jax.vjp(lambda inputs, weights: forward(inputs, valid_count, weights), patches.astype(jnp.float32), params)
        grad_inputs, grad_params = pullback(upstream.astype(jnp.float32))
        totals = jax.tree.map(lambda first, second: first + second, totals, grad_params)
        return (totals, (result.astype(jnp.bfloat16), grad_inputs))
    zeros_start = tuple((jnp.zeros_like(entry) for entry in params))
    totals, (output, grad_tokens) = lax.scan(one_image, zeros_start, (tokens, lengths.astype(jnp.int32), cotangent))
    return (output, grad_tokens, totals[0], totals[1], totals[2], totals[3], totals[4], totals[5], totals[6], totals[7], totals[8], totals[9], totals[10], totals[11], totals[12], totals[13], totals[14])
```

```python
import functools

import jax
import jax.numpy as jnp
from jax import lax
from jax.experimental import pallas as pl
from jax.experimental.pallas import tpu as pltpu
from jax.sharding import PartitionSpec as P

H = 16
HD = 64


norm_eps = 1e-06


def layer_norm(values, norm_gain, norm_shift):
    center = values - jnp.mean(values, axis=-1, keepdims=True)
    spread = jnp.mean(center * center, axis=-1, keepdims=True)
    return center * lax.rsqrt(spread + norm_eps) * norm_gain + norm_shift


def gelu_exact(values):
    return jax.nn.gelu(values, approximate=False)


def matmul(left, right):
    return jnp.dot(left, right, preferred_element_type=jnp.float32)


def left_outer(left, right):
    return jnp.einsum("ti,tj->ij", left, right, preferred_element_type=jnp.float32)


def right_back(left, right):
    return jnp.einsum("tj,ij->ti", left, right, preferred_element_type=jnp.float32)


def column_sum(values):
    return jnp.sum(values.astype(jnp.float32), axis=0)


def attention_probs(queries, key_rows, valid_count, score_scale):
    scores = score_scale * jnp.einsum(
        "qhd,khd->hqk", queries, key_rows, preferred_element_type=jnp.float32
    )
    key_valid = jnp.arange(key_rows.shape[0]) < valid_count
    scores = jnp.where(key_valid[None, None, :], scores, -jnp.inf)
    return scores


def attend(queries, key_rows, values, valid_count, score_scale):
    scores = attention_probs(queries, key_rows, valid_count, score_scale)
    largest = jnp.max(scores, axis=-1, keepdims=True)
    log_total = largest[..., 0] + jnp.log(jnp.sum(jnp.exp(scores - largest), axis=-1))
    attention = jnp.exp(scores - log_total[..., None]).astype(jnp.bfloat16)
    mixture = jnp.einsum("hqk,khd->qhd", attention, values, preferred_element_type=jnp.float32)
    return (mixture.astype(jnp.bfloat16), log_total)


def attend_back(queries, key_rows, values, valid_count, score_scale, log_total, grad_mixture):
    scores = attention_probs(queries, key_rows, valid_count, score_scale)
    probs = jnp.exp(scores - log_total[..., None])
    grad_values = jnp.einsum(
        "hqk,qhd->khd", probs.astype(jnp.bfloat16), grad_mixture, preferred_element_type=jnp.float32
    )
    grad_probs = jnp.einsum(
        "qhd,khd->hqk", grad_mixture, values, preferred_element_type=jnp.float32
    )
    inner_sum = jnp.sum(probs * grad_probs, axis=-1, keepdims=True)
    grad_scores = (probs * (grad_probs - inner_sum)).astype(jnp.bfloat16)
    grad_queries = score_scale * jnp.einsum(
        "hqk,khd->qhd", grad_scores, key_rows, preferred_element_type=jnp.float32
    )
    grad_keys = score_scale * jnp.einsum(
        "hqk,qhd->khd", grad_scores, queries, preferred_element_type=jnp.float32
    )
    return (grad_queries, grad_keys, grad_values)


def general_body(
    tokens,
    lengths,
    norm1_gain,
    norm1_bias,
    packed_weight,
    query_bias,
    value_bias,
    output_weight,
    output_bias,
    layer_scale1,
    norm2_gain,
    norm2_bias,
    up_weight,
    up_bias,
    down_weight,
    down_bias,
    layer_scale2,
    cotangent,
):
    gathered = (
        lax.all_gather(norm1_gain, "fsdp", axis=0, tiled=True),
        lax.all_gather(norm1_bias, "fsdp", axis=0, tiled=True),
        lax.all_gather(packed_weight, "fsdp", axis=0, tiled=True),
        lax.all_gather(query_bias, "fsdp", axis=0, tiled=True),
        lax.all_gather(value_bias, "fsdp", axis=0, tiled=True),
        lax.all_gather(output_weight, "fsdp", axis=0, tiled=True),
        lax.all_gather(output_bias, "fsdp", axis=0, tiled=True),
        lax.all_gather(layer_scale1, "fsdp", axis=0, tiled=True),
        lax.all_gather(norm2_gain, "fsdp", axis=0, tiled=True),
        lax.all_gather(norm2_bias, "fsdp", axis=0, tiled=True),
        lax.all_gather(up_weight, "fsdp", axis=0, tiled=True),
        lax.all_gather(up_bias, "fsdp", axis=0, tiled=True),
        lax.all_gather(down_weight, "fsdp", axis=0, tiled=True),
        lax.all_gather(down_bias, "fsdp", axis=0, tiled=True),
        lax.all_gather(layer_scale2, "fsdp", axis=0, tiled=True),
    )
    (
        gain_one,
        shift_one,
        packed_full,
        query_shift,
        value_shift,
        output_full,
        output_shift,
        scale_one,
        gain_two,
        shift_two,
        up_full,
        up_shift,
        down_full,
        down_shift,
        scale_two,
    ) = gathered
    gain_one = gain_one.astype(jnp.float32)
    shift_one = shift_one.astype(jnp.float32)
    query_shift = query_shift.astype(jnp.float32)
    value_shift = value_shift.astype(jnp.float32)
    output_shift = output_shift.astype(jnp.float32)
    scale_one = scale_one.astype(jnp.float32)
    gain_two = gain_two.astype(jnp.float32)
    shift_two = shift_two.astype(jnp.float32)
    up_shift = up_shift.astype(jnp.float32)
    down_shift = down_shift.astype(jnp.float32)
    scale_two = scale_two.astype(jnp.float32)
    groups = lax.axis_size("seq")
    images, local_len, model_width = tokens.shape
    seq_len = local_len * groups
    per_group = H // groups
    score_scale = HD ** (-0.5)
    token_rows = tokens.astype(jnp.float32).reshape(images * local_len, model_width)
    normed = layer_norm(token_rows, gain_one, shift_one).astype(jnp.bfloat16)
    packed_shift = jnp.concatenate([query_shift, jnp.zeros_like(query_shift), value_shift])
    packed = (matmul(normed, packed_full) + packed_shift).astype(jnp.bfloat16)
    packed = packed.reshape(images, local_len, 3, groups, per_group * HD)
    spread = lax.all_to_all(packed, "seq", split_axis=3, concat_axis=1, tiled=True)
    spread = spread.reshape(images, seq_len, 3, per_group, HD)

    def forward_image(per_image):
        image_block, valid_count = per_image
        return attend(
            image_block[:, 0], image_block[:, 1], image_block[:, 2], valid_count, score_scale
        )

    mixture, log_total = lax.map(forward_image, (spread, lengths))
    mixture = mixture.reshape(images, seq_len, 1, per_group * HD)
    mixture_rows = lax.all_to_all(mixture, "seq", split_axis=1, concat_axis=2, tiled=True).reshape(
        images * local_len, model_width
    )
    branch_one = matmul(mixture_rows, output_full) + output_shift
    middle = token_rows + scale_one * branch_one
    normed_two = layer_norm(middle, gain_two, shift_two).astype(jnp.bfloat16)
    hidden = matmul(normed_two, up_full) + up_shift
    active = gelu_exact(hidden).astype(jnp.bfloat16)
    branch_two = matmul(active, down_full) + down_shift
    output = (middle + scale_two * branch_two).astype(jnp.bfloat16).reshape(tokens.shape)
    upstream = cotangent.astype(jnp.float32).reshape(images * local_len, model_width)
    grad_scale_two = jnp.sum(upstream * branch_two, axis=0)
    delta_two = (scale_two * upstream).astype(jnp.bfloat16)
    grad_down_shift = column_sum(delta_two)
    grad_down = left_outer(active, delta_two)
    grad_active = right_back(delta_two, down_full)
    _, gelu_pull = jax.vjp(gelu_exact, hidden)
    delta_hidden = gelu_pull(grad_active)[0].astype(jnp.bfloat16)
    grad_up_shift = column_sum(delta_hidden)
    grad_up = left_outer(normed_two, delta_hidden)
    delta_normed_two = right_back(delta_hidden, up_full)
    _, norm_pull_two = jax.vjp(layer_norm, middle, gain_two, shift_two)
    grad_middle_norm, grad_gain_two, grad_shift_two = norm_pull_two(delta_normed_two)
    delta_middle = upstream + grad_middle_norm
    grad_scale_one = jnp.sum(delta_middle * branch_one, axis=0)
    delta_one = (scale_one * delta_middle).astype(jnp.bfloat16)
    grad_output_shift = column_sum(delta_one)
    grad_output = left_outer(mixture_rows, delta_one)
    delta_mixture = right_back(delta_one, output_full).astype(jnp.bfloat16)
    delta_mixture = delta_mixture.reshape(images, local_len, groups, per_group * HD)
    grad_spread = lax.all_to_all(delta_mixture, "seq", split_axis=2, concat_axis=1, tiled=True)
    grad_spread = grad_spread.reshape(images, seq_len, per_group, HD)

    def backward_image(per_image):
        image_block, valid_count, image_total, image_grad = per_image
        grad_queries, grad_keys, grad_values = attend_back(
            image_block[:, 0],
            image_block[:, 1],
            image_block[:, 2],
            valid_count,
            score_scale,
            image_total,
            image_grad,
        )
        return jnp.stack([grad_queries, grad_keys, grad_values], axis=1).astype(jnp.bfloat16)

    delta_packed = lax.map(backward_image, (spread, lengths, log_total, grad_spread))
    delta_packed = delta_packed.reshape(images, seq_len, 3, 1, per_group * HD)
    delta_back = lax.all_to_all(delta_packed, "seq", split_axis=1, concat_axis=3, tiled=True)
    delta_back = delta_back.reshape(images * local_len, 3 * model_width)
    grad_query_shift = column_sum(delta_back[:, :model_width])
    grad_value_shift = column_sum(delta_back[:, 2 * model_width :])
    grad_packed = left_outer(normed, delta_back)
    delta_normed = right_back(delta_back, packed_full)
    _, norm_pull_one = jax.vjp(layer_norm, token_rows, gain_one, shift_one)
    grad_rows_norm, grad_gain_one, grad_shift_one = norm_pull_one(delta_normed)
    grad_tokens = (delta_middle + grad_rows_norm).reshape(tokens.shape)
    local_grads = (
        grad_gain_one,
        grad_shift_one,
        grad_packed,
        grad_query_shift,
        grad_value_shift,
        grad_output,
        grad_output_shift,
        grad_scale_one,
        grad_gain_two,
        grad_shift_two,
        grad_up,
        grad_up_shift,
        grad_down,
        grad_down_shift,
        grad_scale_two,
    )
    owned_grads = (
        lax.psum_scatter(
            local_grads[0].astype(jnp.bfloat16), "fsdp", scatter_dimension=0, tiled=True
        ).astype(jnp.float32),
        lax.psum_scatter(
            local_grads[1].astype(jnp.bfloat16), "fsdp", scatter_dimension=0, tiled=True
        ).astype(jnp.float32),
        lax.psum_scatter(
            local_grads[2].astype(jnp.bfloat16), "fsdp", scatter_dimension=0, tiled=True
        ).astype(jnp.float32),
        lax.psum_scatter(
            local_grads[3].astype(jnp.bfloat16), "fsdp", scatter_dimension=0, tiled=True
        ).astype(jnp.float32),
        lax.psum_scatter(
            local_grads[4].astype(jnp.bfloat16), "fsdp", scatter_dimension=0, tiled=True
        ).astype(jnp.float32),
        lax.psum_scatter(
            local_grads[5].astype(jnp.bfloat16), "fsdp", scatter_dimension=0, tiled=True
        ).astype(jnp.float32),
        lax.psum_scatter(
            local_grads[6].astype(jnp.bfloat16), "fsdp", scatter_dimension=0, tiled=True
        ).astype(jnp.float32),
        lax.psum_scatter(
            local_grads[7].astype(jnp.bfloat16), "fsdp", scatter_dimension=0, tiled=True
        ).astype(jnp.float32),
        lax.psum_scatter(
            local_grads[8].astype(jnp.bfloat16), "fsdp", scatter_dimension=0, tiled=True
        ).astype(jnp.float32),
        lax.psum_scatter(
            local_grads[9].astype(jnp.bfloat16), "fsdp", scatter_dimension=0, tiled=True
        ).astype(jnp.float32),
        lax.psum_scatter(
            local_grads[10].astype(jnp.bfloat16), "fsdp", scatter_dimension=0, tiled=True
        ).astype(jnp.float32),
        lax.psum_scatter(
            local_grads[11].astype(jnp.bfloat16), "fsdp", scatter_dimension=0, tiled=True
        ).astype(jnp.float32),
        lax.psum_scatter(
            local_grads[12].astype(jnp.bfloat16), "fsdp", scatter_dimension=0, tiled=True
        ).astype(jnp.float32),
        lax.psum_scatter(
            local_grads[13].astype(jnp.bfloat16), "fsdp", scatter_dimension=0, tiled=True
        ).astype(jnp.float32),
        lax.psum_scatter(
            local_grads[14].astype(jnp.bfloat16), "fsdp", scatter_dimension=0, tiled=True
        ).astype(jnp.float32),
    )
    owned_grads = (
        lax.psum(owned_grads[0].astype(jnp.bfloat16), "seq").astype(jnp.float32),
        lax.psum(owned_grads[1].astype(jnp.bfloat16), "seq").astype(jnp.float32),
        lax.psum(owned_grads[2].astype(jnp.bfloat16), "seq").astype(jnp.float32),
        lax.psum(owned_grads[3].astype(jnp.bfloat16), "seq").astype(jnp.float32),
        lax.psum(owned_grads[4].astype(jnp.bfloat16), "seq").astype(jnp.float32),
        lax.psum(owned_grads[5].astype(jnp.bfloat16), "seq").astype(jnp.float32),
        lax.psum(owned_grads[6].astype(jnp.bfloat16), "seq").astype(jnp.float32),
        lax.psum(owned_grads[7].astype(jnp.bfloat16), "seq").astype(jnp.float32),
        lax.psum(owned_grads[8].astype(jnp.bfloat16), "seq").astype(jnp.float32),
        lax.psum(owned_grads[9].astype(jnp.bfloat16), "seq").astype(jnp.float32),
        lax.psum(owned_grads[10].astype(jnp.bfloat16), "seq").astype(jnp.float32),
        lax.psum(owned_grads[11].astype(jnp.bfloat16), "seq").astype(jnp.float32),
        lax.psum(owned_grads[12].astype(jnp.bfloat16), "seq").astype(jnp.float32),
        lax.psum(owned_grads[13].astype(jnp.bfloat16), "seq").astype(jnp.float32),
        lax.psum(owned_grads[14].astype(jnp.bfloat16), "seq").astype(jnp.float32),
    )
    return (output, grad_tokens) + tuple(owned_grads)


BF16 = jnp.bfloat16
F32 = jnp.float32
NT = (((1,), (1,)), ((), ()))
NN = (((1,), (0,)), ((), ()))
MASKED = -1e30
LANES = 128
VMEM_LIMIT = 60 * 2**20

GAIN1, SHIFT1, QUERY, VALUE, OUT_SHIFT, SCALE1, GAIN2, SHIFT2, DOWN_SHIFT, SCALE2 = range(10)


def dot(left, right, dims=NN):
    return lax.dot_general(left, right, dims, preferred_element_type=F32)


def turned(values):
    return values.astype(F32).T.astype(BF16)


def lane_ids(rows):
    return lax.broadcasted_iota(jnp.int32, (rows, LANES), 1)


def split3(values):
    high = values.astype(BF16).astype(F32)
    rest = values - high
    mid = rest.astype(BF16).astype(F32)
    return high, mid, rest - mid


def params_for(flops, nbytes, transcendentals=0):
    return dict(
        compiler_params=pltpu.CompilerParams(vmem_limit_bytes=VMEM_LIMIT),
        cost_estimate=pl.CostEstimate(
            flops=flops, bytes_accessed=nbytes, transcendentals=transcendentals
        ),
    )


def whole(shape):
    return pl.BlockSpec(shape, lambda *_: (0,) * len(shape))


def normalize(values, gain, shift):
    center = values - jnp.mean(values, axis=-1, keepdims=True)
    spread = jnp.mean(center * center, axis=-1, keepdims=True)
    return center * lax.rsqrt(spread + norm_eps) * gain + shift


def normalize_back(values, gain, delta):
    center = values - jnp.mean(values, axis=-1, keepdims=True)
    inverse = lax.rsqrt(jnp.mean(center * center, axis=-1, keepdims=True) + norm_eps)
    unit = center * inverse
    scaled = delta * gain
    mean_scaled = jnp.mean(scaled, axis=-1, keepdims=True)
    mean_unit = jnp.mean(scaled * unit, axis=-1, keepdims=True)
    return inverse * (scaled - mean_scaled - unit * mean_unit), delta * unit


def total_rows(values):
    return jnp.sum(values, axis=0, keepdims=True)


def project_kernel(order, x_ref, all_ref, half_ref, weight_ref, other_ref, own_ref, normed_ref):
    step = pl.program_id(0)

    @pl.when(step == 0)
    def _():
        normed_ref[...] = normalize(
            x_ref[...].astype(F32), all_ref[GAIN1 : GAIN1 + 1, :], all_ref[SHIFT1 : SHIFT1 + 1, :]
        ).astype(BF16)

    kind = lax.rem(step, 3)
    shift = jnp.where(
        kind == 0,
        half_ref[QUERY : QUERY + 1, :],
        jnp.where(kind == 2, half_ref[VALUE : VALUE + 1, :], 0.0),
    )
    block = (dot(normed_ref[...], weight_ref[...]) + shift).astype(BF16)

    @pl.when(step < 3)
    def _():
        other_ref[0] = block

    @pl.when(step >= 3)
    def _():
        own_ref[0] = block


def project(order, x, table, weight):
    tokens, width = x.shape
    half = width // 2
    return pl.pallas_call(
        project_kernel,
        grid_spec=pltpu.PrefetchScalarGridSpec(
            num_scalar_prefetch=1,
            grid=(6,),
            in_specs=[
                whole((tokens, width)),
                whole(table.shape),
                pl.BlockSpec((table.shape[0], half), lambda j, order: (0, lax.rem(order[j], 2))),
                pl.BlockSpec((width, half), lambda j, order: (0, order[j])),
            ],
            out_specs=[
                pl.BlockSpec((1, tokens, half), lambda j, order: (jnp.minimum(j, 2), 0, 0)),
                pl.BlockSpec((1, tokens, half), lambda j, order: (jnp.maximum(j - 3, 0), 0, 0)),
                whole((tokens, width)),
            ],
        ),
        out_shape=[
            jax.ShapeDtypeStruct((3, tokens, half), BF16),
            jax.ShapeDtypeStruct((3, tokens, half), BF16),
            jax.ShapeDtypeStruct((tokens, width), BF16),
        ],
        name="project",
        **params_for(6 * tokens * width * width, 12 * tokens * width + 6 * width * width),
    )(order, x, table, table, weight)


def padded_len(count, block):
    return -(-count // block) * block


def attend_kernel(valid, *refs, pieces, block, scale):
    in_refs, out_refs = refs[:pieces], refs[pieces : 2 * pieces]
    total_refs = refs[2 * pieces : 3 * pieces]
    keys, values, queries, mixed, totals = refs[3 * pieces :]
    pair = pl.program_id(0)
    size = in_refs[0].shape[1]
    count, padded = pieces * size, keys.shape[0]
    lane = lane_ids(size)
    row = lax.broadcasted_iota(jnp.int32, (size, LANES), 0)
    for i in range(pieces):
        at = pl.ds(i * size, size)
        keys[at, :LANES] = in_refs[i][1]
        keys[at, LANES:] = jnp.where((lane == 0) & (row >= valid[i]), MASKED, 0.0).astype(BF16)
        values[at, :LANES] = in_refs[i][2]
        values[at, LANES:] = jnp.where(lane == 0, 1.0, 0.0).astype(BF16)
        for j in range(2):
            mine = lane // HD == j
            queries[j, at, :LANES] = jnp.where(mine, in_refs[i][0].astype(F32) * scale, 0.0).astype(BF16)
            queries[j, at, LANES:] = jnp.where(lane == 0, 1.0, 0.0).astype(BF16)
    if padded > count:
        rest = pl.ds(count, padded - count)
        rest_lane = lane_ids(padded - count)
        keys[rest, :LANES] = jnp.zeros((padded - count, LANES), BF16)
        keys[rest, LANES:] = jnp.where(rest_lane == 0, MASKED, 0.0).astype(BF16)
        values[rest, :] = jnp.zeros((padded - count, 2 * LANES), BF16)
        for j in range(2):
            queries[j, rest, :] = jnp.zeros((padded - count, 2 * LANES), BF16)

    @pl.when(pair == 0)
    def _():
        for i in range(pieces):
            total_refs[i][...] = jnp.zeros_like(total_refs[i])

    block_lane = lane_ids(block)
    for b in range(padded // block):
        at = pl.ds(b * block, block)
        results, logs = [], 0.0
        for j in range(2):
            scores = dot(queries[j, at, :], keys[...], NT)
            largest = jnp.max(scores, axis=1, keepdims=True)
            weights = jnp.exp(scores - largest).astype(BF16)
            result = dot(weights, values[...])
            total = result[:, LANES : LANES + 1]
            results.append(result[:, :LANES] * (1.0 / total))
            logs += jnp.where(block_lane == 2 * pair + j, largest + jnp.log(total), 0.0)
        mixed[at, :] = jnp.where(block_lane < HD, results[0], results[1])
        totals[at, :] = logs
    for i in range(pieces):
        at = pl.ds(i * size, size)
        out_refs[i][...] = mixed[at, :].astype(BF16)
        total_refs[i][...] += totals[at, :]


def attention(valid, parts, block):
    pieces = len(parts)
    _, size, width = parts[0].shape
    pairs = width // LANES
    padded = padded_len(pieces * size, block)
    outs = pl.pallas_call(
        functools.partial(attend_kernel, pieces=pieces, block=block, scale=HD**-0.5),
        grid_spec=pltpu.PrefetchScalarGridSpec(
            num_scalar_prefetch=1,
            grid=(pairs,),
            in_specs=[pl.BlockSpec((3, size, LANES), lambda h, _: (0, 0, h))] * pieces,
            out_specs=[pl.BlockSpec((size, LANES), lambda h, _: (0, h))] * pieces
            + [whole((size, LANES))] * pieces,
            scratch_shapes=[
                pltpu.VMEM((padded, 2 * LANES), BF16),
                pltpu.VMEM((padded, 2 * LANES), BF16),
                pltpu.VMEM((2, padded, 2 * LANES), BF16),
                pltpu.VMEM((padded, LANES), F32),
                pltpu.VMEM((padded, LANES), F32),
            ],
        ),
        out_shape=[jax.ShapeDtypeStruct((size, width), BF16)] * pieces
        + [jax.ShapeDtypeStruct((size, LANES), F32)] * pieces,
        name="attend",
        **params_for(16 * pairs * LANES * padded * padded, 8 * size * width * pieces, pairs * 2 * padded * padded),
    )(valid, *parts)
    return outs[:pieces], outs[pieces:]


def attend_back_kernel(valid, *refs, pieces, block, scale):
    in_refs, mix_refs = refs[:pieces], refs[pieces : 2 * pieces]
    grad_refs, total_refs = refs[2 * pieces : 3 * pieces], refs[3 * pieces : 4 * pieces]
    out_refs = refs[4 * pieces : 5 * pieces]
    keys, values, queries, grads, queries_t, grads_t, dq, dk_t, dv_t = refs[5 * pieces :]
    pair = pl.program_id(0)
    size = in_refs[0].shape[1]
    count, padded = pieces * size, keys.shape[0]
    blocks = padded // block
    lane = lane_ids(size)
    row = lax.broadcasted_iota(jnp.int32, (size, LANES), 0)
    for i in range(pieces):
        at = pl.ds(i * size, size)
        keys[at, :LANES] = in_refs[i][1]
        keys[at, LANES:] = jnp.where(
            lane == 0, jnp.where(row >= valid[i], MASKED, 0.0), jnp.where(lane < 4, 1.0, 0.0)
        ).astype(BF16)
        values[at, :LANES] = in_refs[i][2]
        values[at, LANES:] = jnp.where((lane > 0) & (lane < 4), 1.0, 0.0).astype(BF16)
        queries[0, at, :LANES] = in_refs[i][0]
        grads[0, at, :LANES] = grad_refs[i][...]
    if padded > count:
        left = padded - count
        rest = pl.ds(count, left)
        keys[rest, :LANES] = jnp.zeros((left, LANES), BF16)
        keys[rest, LANES:] = jnp.where(lane_ids(left) == 0, MASKED, 0.0).astype(BF16)
        values[rest, :] = jnp.zeros((left, 2 * LANES), BF16)
        for j in range(2):
            queries[j, rest, :] = jnp.zeros((left, 2 * LANES), BF16)
            grads[j, rest, :] = jnp.zeros((left, 2 * LANES), BF16)
    for b in range(blocks):
        at = pl.ds(b * block, block)
        queries_t[b] = (queries[0, at, :LANES].astype(F32) * scale).T.astype(BF16)
        grads_t[b] = turned(grads[0, at, :LANES])
    for j in range(2):
        mine = lane // HD == j
        for i in range(pieces):
            at = pl.ds(i * size, size)
            grad = jnp.where(mine, grad_refs[i][...].astype(F32), 0.0)
            queries[j, at, :LANES] = jnp.where(mine, in_refs[i][0].astype(F32) * scale, 0.0).astype(BF16)
            grads[j, at, :LANES] = grad.astype(BF16)
            log_total = jnp.sum(
                jnp.where(lane == 2 * pair + j, total_refs[i][...], 0.0), axis=1, keepdims=True
            )
            high, mid, low = split3(-log_total)
            queries[j, at, LANES:] = jnp.where(
                lane == 0,
                1.0,
                jnp.where(lane == 1, high, jnp.where(lane == 2, mid, jnp.where(lane == 3, low, 0.0))),
            ).astype(BF16)
            inner = jnp.sum(grad * mix_refs[i][...].astype(F32), axis=1, keepdims=True)
            high, mid, low = split3(-inner)
            grads[j, at, LANES:] = jnp.where(
                lane == 1, high, jnp.where(lane == 2, mid, jnp.where(lane == 3, low, 0.0))
            ).astype(BF16)
    dk_t[...] = jnp.zeros_like(dk_t)
    dv_t[...] = jnp.zeros_like(dv_t)
    block_lane = lane_ids(block)
    for b in range(blocks):
        at = pl.ds(b * block, block)
        results = []
        for j in range(2):
            mine = pl.ds(j * HD, HD)
            probs = jnp.exp(dot(queries[j, at, :], keys[...], NT))
            grad_scores = (probs * dot(grads[j, at, :], values[...], NT)).astype(BF16)
            results.append(dot(grad_scores, keys[:, :LANES]) * scale)
            dv_t[mine, :] += dot(grads_t[b, mine, :], probs.astype(BF16))
            dk_t[mine, :] += dot(queries_t[b, mine, :], grad_scores)
        dq[at, :] = jnp.where(block_lane < HD, results[0], results[1])
    dk, dv = dk_t[...].T, dv_t[...].T
    for i in range(pieces):
        at = slice(i * size, (i + 1) * size)
        out_refs[i][0] = dq[at, :].astype(BF16)
        out_refs[i][1] = dk[at, :].astype(BF16)
        out_refs[i][2] = dv[at, :].astype(BF16)


def attention_back(valid, parts, mixtures, grads, totals, block):
    pieces = len(parts)
    _, size, width = parts[0].shape
    pairs = width // LANES
    padded = padded_len(pieces * size, block)
    triple = pl.BlockSpec((3, size, LANES), lambda h, _: (0, 0, h))
    single = pl.BlockSpec((size, LANES), lambda h, _: (0, h))
    return pl.pallas_call(
        functools.partial(attend_back_kernel, pieces=pieces, block=block, scale=HD**-0.5),
        grid_spec=pltpu.PrefetchScalarGridSpec(
            num_scalar_prefetch=1,
            grid=(pairs,),
            in_specs=[triple] * pieces + [single] * 2 * pieces + [whole((size, LANES))] * pieces,
            out_specs=[triple] * pieces,
            scratch_shapes=[
                pltpu.VMEM((padded, 2 * LANES), BF16),
                pltpu.VMEM((padded, 2 * LANES), BF16),
                pltpu.VMEM((2, padded, 2 * LANES), BF16),
                pltpu.VMEM((2, padded, 2 * LANES), BF16),
                pltpu.VMEM((padded // block, LANES, block), BF16),
                pltpu.VMEM((padded // block, LANES, block), BF16),
                pltpu.VMEM((padded, LANES), F32),
                pltpu.VMEM((LANES, padded), F32),
                pltpu.VMEM((LANES, padded), F32),
            ],
        ),
        out_shape=[jax.ShapeDtypeStruct((3, size, width), BF16)] * pieces,
        name="attend_back",
        **params_for(30 * pairs * LANES * padded * padded, 16 * size * width * pieces, pairs * 2 * padded * padded),
    )(valid, *parts, *mixtures, *grads, *totals)


def merge_kernel(order, x_ref, own_ref, far_ref, table, own_w, far_w, middle_ref, branch_ref, normed_ref):
    branch = dot(own_ref[...], own_w[...]) + dot(far_ref[...], far_w[...])
    branch += table[OUT_SHIFT : OUT_SHIFT + 1, :]
    middle = x_ref[...].astype(F32) + table[SCALE1 : SCALE1 + 1, :] * branch
    middle_ref[...] = middle
    branch_ref[...] = branch
    normed_ref[...] = normalize(
        middle, table[GAIN2 : GAIN2 + 1, :], table[SHIFT2 : SHIFT2 + 1, :]
    ).astype(BF16)


ROWS = 352


def row_steps(tokens):
    return -(-tokens // ROWS)


def merge(order, x, own, far, table, weight):
    tokens, width = x.shape
    half = width // 2
    wide = pl.BlockSpec((ROWS, width), lambda i, _: (i, 0))
    narrow = pl.BlockSpec((ROWS, half), lambda i, _: (i, 0))
    return pl.pallas_call(
        merge_kernel,
        grid_spec=pltpu.PrefetchScalarGridSpec(
            num_scalar_prefetch=1,
            grid=(row_steps(tokens),),
            in_specs=[
                wide,
                narrow,
                narrow,
                whole(table.shape),
                pl.BlockSpec((half, width), lambda i, order: (order[3], 0)),
                pl.BlockSpec((half, width), lambda i, order: (order[0], 0)),
            ],
            out_specs=[wide, wide, wide],
        ),
        out_shape=[
            jax.ShapeDtypeStruct((tokens, width), F32),
            jax.ShapeDtypeStruct((tokens, width), F32),
            jax.ShapeDtypeStruct((tokens, width), BF16),
        ],
        name="merge",
        **params_for(2 * tokens * width * width, 14 * tokens * width + 2 * width * width),
    )(order, x, own, far, table, weight, weight)


def gelu_and_slope(values):
    size = jnp.abs(values) * 0.7071067811865476
    t = 1.0 / (1.0 + 0.3275911 * size)
    bell = jnp.exp(-0.5 * (values * values))
    poly = t * (0.254829592 + t * (-0.284496736 + t * (1.421413741 + t * (-1.453152027 + t * 1.061405429))))
    tail = 0.5 * poly * bell
    phi = jnp.where(values < 0, tail, 1.0 - tail)
    return values * phi, phi + values * bell * 0.3989422804014327


def mlp_kernel(
    normed_ref, cotangent_ref, table, up_ref, shift_ref, down_ref,
    branch_ref, delta_ref, grad_up_ref, grad_down_ref, grad_shift_ref,
    upstream, upstream_t, normed_t,
):
    @pl.when(pl.program_id(0) == 0)
    def _():
        scaled = (cotangent_ref[...].astype(F32) * table[SCALE2 : SCALE2 + 1, :]).astype(BF16)
        upstream[...] = scaled
        upstream_t[...] = turned(scaled)
        normed_t[...] = turned(normed_ref[...])
        branch_ref[...] = jnp.zeros_like(branch_ref)
        delta_ref[...] = jnp.zeros_like(delta_ref)

    up, down = up_ref[...], down_ref[...]
    hidden = dot(normed_ref[...], up) + shift_ref[...]
    grad_active = dot(upstream[...], down, NT)
    active, slope = gelu_and_slope(hidden)
    active = active.astype(BF16)
    delta_hidden = (grad_active * slope).astype(BF16)
    branch_ref[...] += dot(active, down)
    delta_ref[...] += dot(delta_hidden, up, NT)
    grad_up_ref[...] = dot(normed_t[...], delta_hidden).astype(BF16)
    grad_down = dot(upstream_t[...], active).astype(BF16)
    each = grad_down_ref.shape[2]
    for i in range(grad_down_ref.shape[0]):
        grad_down_ref[i] = grad_down[:, i * each : (i + 1) * each]
    grad_shift_ref[...] = total_rows(delta_hidden.astype(F32))


def mlp(normed, cotangent, table, up, up_shift, down, owners, block=512):
    tokens, width = normed.shape
    hidden = up.shape[1]
    each = hidden // owners
    held = block // each
    return pl.pallas_call(
        mlp_kernel,
        grid=(hidden // block,),
        in_specs=[
            whole((tokens, width)),
            whole((tokens, width)),
            whole(table.shape),
            pl.BlockSpec((width, block), lambda j: (0, j)),
            pl.BlockSpec((1, block), lambda j: (0, j)),
            pl.BlockSpec((block, width), lambda j: (j, 0)),
        ],
        out_specs=[
            whole((tokens, width)),
            whole((tokens, width)),
            pl.BlockSpec((width, block), lambda j: (0, j)),
            pl.BlockSpec((held, width, each), lambda j: (j, 0, 0)),
            pl.BlockSpec((1, block), lambda j: (0, j)),
        ],
        out_shape=[
            jax.ShapeDtypeStruct((tokens, width), F32),
            jax.ShapeDtypeStruct((tokens, width), F32),
            jax.ShapeDtypeStruct((width, hidden), BF16),
            jax.ShapeDtypeStruct((owners, width, each), BF16),
            jax.ShapeDtypeStruct((1, hidden), F32),
        ],
        scratch_shapes=[
            pltpu.VMEM((tokens, width), BF16),
            pltpu.VMEM((width, tokens), BF16),
            pltpu.VMEM((width, tokens), BF16),
        ],
        name="mlp",
        **params_for(12 * tokens * width * hidden, 12 * tokens * width + 8 * width * hidden, 2 * tokens * hidden),
    )(normed, cotangent, table, up, up_shift, down)


SUM_ROWS = 8


def unmerge_kernel(
    order, middle_ref, branch1_ref, branch2_ref, delta_ref, cotangent_ref, own_ref, far_ref, table, own_w, far_w,
    output_ref, delta_middle_ref, own_grad_ref, far_grad_ref, weight_ref, sums_ref,
    delta1_all,
    *, tokens,
):
    step = pl.program_id(0)

    @pl.when(step == 0)
    def _():
        sums_ref[...] = jnp.zeros_like(sums_ref)

    rows, width = middle_ref.shape
    inside = lax.broadcasted_iota(jnp.int32, (rows, width), 0) + step * rows < tokens

    def kept(values):
        return jnp.where(inside, values, 0.0)

    upstream = cotangent_ref[...].astype(F32)
    scale2 = table[SCALE2 : SCALE2 + 1, :]
    middle = middle_ref[...]
    branch2 = branch2_ref[...] + table[DOWN_SHIFT : DOWN_SHIFT + 1, :]
    output_ref[...] = (middle + scale2 * branch2).astype(BF16)
    delta2 = (scale2 * upstream).astype(BF16).astype(F32)
    delta = delta_ref[...]
    inner, gain_terms = normalize_back(middle, table[GAIN2 : GAIN2 + 1, :], delta)
    delta_middle = upstream + inner
    delta_middle_ref[...] = delta_middle
    delta1 = kept(table[SCALE1 : SCALE1 + 1, :] * delta_middle).astype(BF16)
    delta1_all[pl.ds(pl.multiple_of(step * rows, 16), rows), :] = delta1
    own_grad_ref[...] = dot(delta1, own_w[...], NT).astype(BF16)
    far_grad_ref[...] = dot(delta1, far_w[...], NT).astype(BF16)
    terms = (
        upstream * branch2,
        delta2,
        gain_terms,
        delta,
        delta_middle * branch1_ref[...],
        delta1.astype(F32),
    )
    for i, term in enumerate(terms):
        sums_ref[i : i + 1, :] += total_rows(kept(term))

    @pl.when(step == pl.num_programs(0) - 1)
    def _():
        delta1_kept = delta1_all[:tokens, :]
        half = own_ref.shape[1]
        own_at = pl.multiple_of(order[3] * half, half)
        far_at = pl.multiple_of(order[0] * half, half)
        weight_ref[pl.ds(own_at, half), :] = dot(turned(own_ref[...]), delta1_kept).astype(BF16)
        weight_ref[pl.ds(far_at, half), :] = dot(turned(far_ref[...]), delta1_kept).astype(BF16)


def unmerge(order, middle, branch1, branch2, delta, cotangent, own, far, table, weight):
    tokens, width = middle.shape
    half = width // 2
    steps = row_steps(tokens)
    wide = pl.BlockSpec((ROWS, width), lambda i, _: (i, 0))
    narrow = pl.BlockSpec((ROWS, half), lambda i, _: (i, 0))
    return pl.pallas_call(
        functools.partial(unmerge_kernel, tokens=tokens),
        grid_spec=pltpu.PrefetchScalarGridSpec(
            num_scalar_prefetch=1,
            grid=(steps,),
            in_specs=[wide] * 5
            + [whole((tokens, half))] * 2
            + [
                whole(table.shape),
                pl.BlockSpec((half, width), lambda i, order: (order[3], 0)),
                pl.BlockSpec((half, width), lambda i, order: (order[0], 0)),
            ],
            out_specs=[wide, wide, narrow, narrow, whole((width, width)), whole((SUM_ROWS, width))],
            scratch_shapes=[pltpu.VMEM((steps * ROWS, width), BF16)],
        ),
        out_shape=[
            jax.ShapeDtypeStruct((tokens, width), BF16),
            jax.ShapeDtypeStruct((tokens, width), F32),
            jax.ShapeDtypeStruct((tokens, half), BF16),
            jax.ShapeDtypeStruct((tokens, half), BF16),
            jax.ShapeDtypeStruct((width, width), BF16),
            jax.ShapeDtypeStruct((SUM_ROWS, width), F32),
        ],
        name="unmerge",
        **params_for(4 * tokens * width * width, 30 * tokens * width + 4 * width * width),
    )(order, middle, branch1, branch2, delta, cotangent, own, far, table, weight, weight)


def packed_grad_kernel(order, normed_ref, far_ref, own_ref, grad_ref, sums_ref, normed_t):
    step = pl.program_id(0)

    @pl.when(step == 0)
    def _():
        normed_t[...] = turned(normed_ref[...])

    block = jnp.where(step < 3, far_ref[0], own_ref[0])
    grad_ref[...] = dot(normed_t[...], block).astype(BF16)
    sums_ref[...] = jnp.broadcast_to(total_rows(block.astype(F32)), sums_ref.shape)


def far_block(j, _):
    return (jnp.minimum(j, 2), 0, 0)


def own_block(j, _):
    return (jnp.maximum(j - 3, 0), 0, 0)


def packed_grad(order, normed, far, own):
    tokens, width = normed.shape
    half = width // 2
    return pl.pallas_call(
        packed_grad_kernel,
        grid_spec=pltpu.PrefetchScalarGridSpec(
            num_scalar_prefetch=1,
            grid=(6,),
            in_specs=[
                whole((tokens, width)),
                pl.BlockSpec((1, tokens, half), far_block),
                pl.BlockSpec((1, tokens, half), own_block),
            ],
            out_specs=[
                pl.BlockSpec((width, half), lambda j, order: (0, order[j])),
                pl.BlockSpec((8, half), lambda j, order: (0, order[j])),
            ],
            scratch_shapes=[pltpu.VMEM((width, tokens), BF16)],
        ),
        out_shape=[
            jax.ShapeDtypeStruct((width, 3 * width), BF16),
            jax.ShapeDtypeStruct((8, 3 * width), F32),
        ],
        name="packed_grad",
        **params_for(6 * tokens * width * width, 8 * tokens * width + 6 * width * width),
    )(order, normed, far, own)


def unproject_kernel(
    order, x_ref, delta_middle_ref, table, far_ref, own_ref, weight_ref, out_ref, sums_ref, delta
):
    step = pl.program_id(0)

    @pl.when(step == 0)
    def _():
        delta[...] = jnp.zeros_like(delta)

    block = jnp.where(step < 3, far_ref[0], own_ref[0])
    delta[...] += dot(block, weight_ref[...], NT)

    @pl.when(step == pl.num_programs(0) - 1)
    def _():
        delta_normed = delta[...]
        inner, gain_terms = normalize_back(
            x_ref[...].astype(F32), table[GAIN1 : GAIN1 + 1, :], delta_normed
        )
        out_ref[...] = (delta_middle_ref[...] + inner).astype(BF16)
        sums_ref[...] = jnp.zeros_like(sums_ref)
        sums_ref[0:1, :] = total_rows(gain_terms)
        sums_ref[1:2, :] = total_rows(delta_normed)


def unproject(order, x, delta_middle, table, far, own, weight):
    tokens, width = x.shape
    half = width // 2
    return pl.pallas_call(
        unproject_kernel,
        grid_spec=pltpu.PrefetchScalarGridSpec(
            num_scalar_prefetch=1,
            grid=(6,),
            in_specs=[
                whole((tokens, width)),
                whole((tokens, width)),
                whole(table.shape),
                pl.BlockSpec((1, tokens, half), far_block),
                pl.BlockSpec((1, tokens, half), own_block),
                pl.BlockSpec((width, half), lambda j, order: (0, order[j])),
            ],
            out_specs=[whole((tokens, width)), whole((SUM_ROWS, width))],
            scratch_shapes=[pltpu.VMEM((tokens, width), F32)],
        ),
        out_shape=[
            jax.ShapeDtypeStruct((tokens, width), BF16),
            jax.ShapeDtypeStruct((SUM_ROWS, width), F32),
        ],
        name="unproject",
        **params_for(6 * tokens * width * width, 12 * tokens * width + 6 * width * width),
    )(order, x, delta_middle, table, far, own, weight)


def paired_body(
    tokens, lengths, norm1_gain, norm1_bias, packed_weight, query_bias, value_bias, output_weight, output_bias,
    layer_scale1, norm2_gain, norm2_bias, up_weight, up_bias, down_weight, down_bias, layer_scale2, cotangent,
):
    owners = lax.axis_size("fsdp")
    images, local_len, width = tokens.shape
    core = lax.rem(lax.axis_index("fsdp"), 2)
    regroup = [(f * 2 + s, (f - f % 2 + s) * 2 + f % 2) for f in range(owners) for s in range(2)]
    twin = [(f, f ^ 1) for f in range(owners)]

    def regrouped(values):
        return lax.ppermute(values, ("fsdp", "seq"), regroup)

    def to_twin(values):
        return lax.ppermute(values, "fsdp", twin)

    x = regrouped(tokens.reshape(local_len, width))
    valid_count = regrouped(lengths)
    vectors = (
        norm1_gain, norm1_bias, query_bias, value_bias, output_bias, layer_scale1, norm2_gain, norm2_bias,
        down_bias, layer_scale2,
    )
    rows = norm1_gain.shape[0]
    small = jnp.concatenate(vectors + (up_bias,))
    first_rows = packed_weight.shape[0]
    small_block = jnp.zeros((first_rows * LANES,), BF16).at[: small.shape[0]].set(small)
    first = jnp.concatenate([packed_weight, small_block.reshape(first_rows, LANES)], axis=1)
    first_full = lax.all_gather(first, "fsdp", axis=0, tiled=True)
    small_full = first_full[:, 3 * width :].reshape(owners, first_rows * LANES)
    table = small_full[:, : 10 * rows].reshape(owners, 10, rows).transpose(1, 0, 2).reshape(10, width)
    table = jnp.pad(table, ((0, 6), (0, 0))).astype(F32)
    up_shift = small_full[:, 10 * rows : small.shape[0]].reshape(1, -1).astype(F32)
    output_full = lax.all_gather(output_weight, "fsdp", axis=0, tiled=True)
    up_full = lax.all_gather(up_weight, "fsdp", axis=0, tiled=True)
    down_full = lax.all_gather(down_weight, "fsdp", axis=0, tiled=True)

    order = jnp.stack([1 - core, 3 - core, 5 - core, core, 2 + core, 4 + core]).astype(jnp.int32)
    starts = jnp.stack([core, 1 - core]) * local_len
    valid = jnp.clip(valid_count - starts, 0, local_len).astype(jnp.int32)

    far_out, own_part, normed = project(order, x, table, first_full)
    far_part = to_twin(far_out)
    parts = [own_part, far_part]
    (own_mix, far_mix_out), totals = attention(valid, parts, 352)
    far_mix = to_twin(far_mix_out)
    middle, branch1, normed2 = merge(order, x, own_mix, far_mix, table, output_full)
    upstream = regrouped(cotangent.reshape(local_len, width))
    branch2, delta_normed2, grad_up, grad_down, grad_up_shift = mlp(
        normed2, upstream, table, up_full, up_shift, down_full, owners
    )
    output, delta_middle, own_grad, far_grad_out, grad_output, sums2 = unmerge(
        order, middle, branch1, branch2, delta_normed2, upstream, own_mix, far_mix, table, output_full
    )
    output = regrouped(output).reshape(tokens.shape)
    far_grad = to_twin(far_grad_out)
    own_delta, far_delta_out = attention_back(
        valid, parts, [own_mix, far_mix_out], [own_grad, far_grad], totals, 352
    )
    far_delta = to_twin(far_delta_out)
    grad_packed, packed_sums = packed_grad(order, normed, far_delta, own_delta)
    grad_x, sums1 = unproject(order, x, delta_middle, table, far_delta, own_delta, first_full)
    grad_tokens = regrouped(grad_x).astype(F32).reshape(tokens.shape)

    def owned(grad):
        part = lax.psum_scatter(grad, "fsdp", scatter_dimension=0, tiled=True)
        return part.astype(F32) + lax.ppermute(part, "seq", [(0, 1), (1, 0)]).astype(F32)

    grad_up = owned(grad_up)
    grad_down = owned(grad_down)[0].T
    grad_output = owned(grad_output)
    grad_packed = owned(grad_packed)
    sums = jnp.concatenate(
        [
            sums1[0], sums1[1], packed_sums[0, :width], packed_sums[0, 2 * width :], sums2[5], sums2[4], sums2[2],
            sums2[3], sums2[1], sums2[0], grad_up_shift[0],
        ]
    )
    all_sums = lax.psum(sums, ("fsdp", "seq"))
    me = lax.axis_index("fsdp")
    mine = [lax.dynamic_slice(all_sums, (i * width + me * rows,), (rows,)) for i in range(10)]
    each = up_bias.shape[0]
    mine_up = lax.dynamic_slice(all_sums, (10 * width + me * each,), (each,))
    return (
        output, grad_tokens, mine[0], mine[1], grad_packed, mine[2], mine[3], grad_output, mine[4], mine[5],
        mine[6], mine[7], grad_up, mine_up, grad_down, mine[8], mine[9],
    )


def solution(mesh):
    in_specs = (
        P("fsdp", "seq", None),
        P("fsdp"),
        P("fsdp"),
        P("fsdp"),
        P("fsdp", None),
        P("fsdp"),
        P("fsdp"),
        P("fsdp", None),
        P("fsdp"),
        P("fsdp"),
        P("fsdp"),
        P("fsdp"),
        P("fsdp", None),
        P("fsdp"),
        P("fsdp", None),
        P("fsdp"),
        P("fsdp"),
        P("fsdp", "seq", None),
    )
    out_specs = (
        P("fsdp", "seq", None),
        P("fsdp", "seq", None),
        P("fsdp"),
        P("fsdp"),
        P("fsdp", None),
        P("fsdp"),
        P("fsdp"),
        P("fsdp", None),
        P("fsdp"),
        P("fsdp"),
        P("fsdp"),
        P("fsdp"),
        P("fsdp", None),
        P("fsdp"),
        P("fsdp", None),
        P("fsdp"),
        P("fsdp"),
    )
    paired = mesh.shape["seq"] == 2 and mesh.shape["fsdp"] % 2 == 0
    chosen = paired_body if paired else general_body
    return jax.shard_map(chosen, mesh=mesh, in_specs=in_specs, out_specs=out_specs, check_vma=False)
```

```python
import functools

import jax
import jax.numpy as jnp
import numpy as np
from jax import lax
from jax.experimental import pallas as pl
from jax.experimental.pallas import tpu as pltpu
from jax.sharding import PartitionSpec as P

H = 16
HD = 64


norm_eps = 1e-06


def layer_norm(values, norm_gain, norm_shift):
    center = values - jnp.mean(values, axis=-1, keepdims=True)
    spread = jnp.mean(center * center, axis=-1, keepdims=True)
    return center * lax.rsqrt(spread + norm_eps) * norm_gain + norm_shift


def gelu_exact(values):
    return jax.nn.gelu(values, approximate=False)


def matmul(left, right):
    return jnp.dot(left, right, preferred_element_type=jnp.float32)


def left_outer(left, right):
    return jnp.einsum("ti,tj->ij", left, right, preferred_element_type=jnp.float32)


def right_back(left, right):
    return jnp.einsum("tj,ij->ti", left, right, preferred_element_type=jnp.float32)


def column_sum(values):
    return jnp.sum(values.astype(jnp.float32), axis=0)


def attention_probs(queries, key_rows, valid_count, score_scale):
    scores = score_scale * jnp.einsum(
        "qhd,khd->hqk", queries, key_rows, preferred_element_type=jnp.float32
    )
    key_valid = jnp.arange(key_rows.shape[0]) < valid_count
    scores = jnp.where(key_valid[None, None, :], scores, -jnp.inf)
    return scores


def attend(queries, key_rows, values, valid_count, score_scale):
    scores = attention_probs(queries, key_rows, valid_count, score_scale)
    largest = jnp.max(scores, axis=-1, keepdims=True)
    log_total = largest[..., 0] + jnp.log(jnp.sum(jnp.exp(scores - largest), axis=-1))
    attention = jnp.exp(scores - log_total[..., None]).astype(jnp.bfloat16)
    mixture = jnp.einsum("hqk,khd->qhd", attention, values, preferred_element_type=jnp.float32)
    return (mixture.astype(jnp.bfloat16), log_total)


def attend_back(queries, key_rows, values, valid_count, score_scale, log_total, grad_mixture):
    scores = attention_probs(queries, key_rows, valid_count, score_scale)
    probs = jnp.exp(scores - log_total[..., None])
    grad_values = jnp.einsum(
        "hqk,qhd->khd", probs.astype(jnp.bfloat16), grad_mixture, preferred_element_type=jnp.float32
    )
    grad_probs = jnp.einsum(
        "qhd,khd->hqk", grad_mixture, values, preferred_element_type=jnp.float32
    )
    inner_sum = jnp.sum(probs * grad_probs, axis=-1, keepdims=True)
    grad_scores = (probs * (grad_probs - inner_sum)).astype(jnp.bfloat16)
    grad_queries = score_scale * jnp.einsum(
        "hqk,khd->qhd", grad_scores, key_rows, preferred_element_type=jnp.float32
    )
    grad_keys = score_scale * jnp.einsum(
        "hqk,qhd->khd", grad_scores, queries, preferred_element_type=jnp.float32
    )
    return (grad_queries, grad_keys, grad_values)


def general_body(
    tokens,
    lengths,
    norm1_gain,
    norm1_bias,
    packed_weight,
    query_bias,
    value_bias,
    output_weight,
    output_bias,
    layer_scale1,
    norm2_gain,
    norm2_bias,
    up_weight,
    up_bias,
    down_weight,
    down_bias,
    layer_scale2,
    cotangent,
):
    gathered = (
        lax.all_gather(norm1_gain, "fsdp", axis=0, tiled=True),
        lax.all_gather(norm1_bias, "fsdp", axis=0, tiled=True),
        lax.all_gather(packed_weight, "fsdp", axis=0, tiled=True),
        lax.all_gather(query_bias, "fsdp", axis=0, tiled=True),
        lax.all_gather(value_bias, "fsdp", axis=0, tiled=True),
        lax.all_gather(output_weight, "fsdp", axis=0, tiled=True),
        lax.all_gather(output_bias, "fsdp", axis=0, tiled=True),
        lax.all_gather(layer_scale1, "fsdp", axis=0, tiled=True),
        lax.all_gather(norm2_gain, "fsdp", axis=0, tiled=True),
        lax.all_gather(norm2_bias, "fsdp", axis=0, tiled=True),
        lax.all_gather(up_weight, "fsdp", axis=0, tiled=True),
        lax.all_gather(up_bias, "fsdp", axis=0, tiled=True),
        lax.all_gather(down_weight, "fsdp", axis=0, tiled=True),
        lax.all_gather(down_bias, "fsdp", axis=0, tiled=True),
        lax.all_gather(layer_scale2, "fsdp", axis=0, tiled=True),
    )
    (
        gain_one,
        shift_one,
        packed_full,
        query_shift,
        value_shift,
        output_full,
        output_shift,
        scale_one,
        gain_two,
        shift_two,
        up_full,
        up_shift,
        down_full,
        down_shift,
        scale_two,
    ) = gathered
    gain_one = gain_one.astype(jnp.float32)
    shift_one = shift_one.astype(jnp.float32)
    query_shift = query_shift.astype(jnp.float32)
    value_shift = value_shift.astype(jnp.float32)
    output_shift = output_shift.astype(jnp.float32)
    scale_one = scale_one.astype(jnp.float32)
    gain_two = gain_two.astype(jnp.float32)
    shift_two = shift_two.astype(jnp.float32)
    up_shift = up_shift.astype(jnp.float32)
    down_shift = down_shift.astype(jnp.float32)
    scale_two = scale_two.astype(jnp.float32)
    groups = lax.axis_size("seq")
    images, local_len, model_width = tokens.shape
    seq_len = local_len * groups
    per_group = H // groups
    score_scale = HD ** (-0.5)
    token_rows = tokens.astype(jnp.float32).reshape(images * local_len, model_width)
    normed = layer_norm(token_rows, gain_one, shift_one).astype(jnp.bfloat16)
    packed_shift = jnp.concatenate([query_shift, jnp.zeros_like(query_shift), value_shift])
    packed = (matmul(normed, packed_full) + packed_shift).astype(jnp.bfloat16)
    packed = packed.reshape(images, local_len, 3, groups, per_group * HD)
    spread = lax.all_to_all(packed, "seq", split_axis=3, concat_axis=1, tiled=True)
    spread = spread.reshape(images, seq_len, 3, per_group, HD)

    def forward_image(per_image):
        image_block, valid_count = per_image
        return attend(
            image_block[:, 0], image_block[:, 1], image_block[:, 2], valid_count, score_scale
        )

    mixture, log_total = lax.map(forward_image, (spread, lengths))
    mixture = mixture.reshape(images, seq_len, 1, per_group * HD)
    mixture_rows = lax.all_to_all(mixture, "seq", split_axis=1, concat_axis=2, tiled=True).reshape(
        images * local_len, model_width
    )
    branch_one = matmul(mixture_rows, output_full) + output_shift
    middle = token_rows + scale_one * branch_one
    normed_two = layer_norm(middle, gain_two, shift_two).astype(jnp.bfloat16)
    hidden = matmul(normed_two, up_full) + up_shift
    active = gelu_exact(hidden).astype(jnp.bfloat16)
    branch_two = matmul(active, down_full) + down_shift
    output = (middle + scale_two * branch_two).astype(jnp.bfloat16).reshape(tokens.shape)
    upstream = cotangent.astype(jnp.float32).reshape(images * local_len, model_width)
    grad_scale_two = jnp.sum(upstream * branch_two, axis=0)
    delta_two = (scale_two * upstream).astype(jnp.bfloat16)
    grad_down_shift = column_sum(delta_two)
    grad_down = left_outer(active, delta_two)
    grad_active = right_back(delta_two, down_full)
    _, gelu_pull = jax.vjp(gelu_exact, hidden)
    delta_hidden = gelu_pull(grad_active)[0].astype(jnp.bfloat16)
    grad_up_shift = column_sum(delta_hidden)
    grad_up = left_outer(normed_two, delta_hidden)
    delta_normed_two = right_back(delta_hidden, up_full)
    _, norm_pull_two = jax.vjp(layer_norm, middle, gain_two, shift_two)
    grad_middle_norm, grad_gain_two, grad_shift_two = norm_pull_two(delta_normed_two)
    delta_middle = upstream + grad_middle_norm
    grad_scale_one = jnp.sum(delta_middle * branch_one, axis=0)
    delta_one = (scale_one * delta_middle).astype(jnp.bfloat16)
    grad_output_shift = column_sum(delta_one)
    grad_output = left_outer(mixture_rows, delta_one)
    delta_mixture = right_back(delta_one, output_full).astype(jnp.bfloat16)
    delta_mixture = delta_mixture.reshape(images, local_len, groups, per_group * HD)
    grad_spread = lax.all_to_all(delta_mixture, "seq", split_axis=2, concat_axis=1, tiled=True)
    grad_spread = grad_spread.reshape(images, seq_len, per_group, HD)

    def backward_image(per_image):
        image_block, valid_count, image_total, image_grad = per_image
        grad_queries, grad_keys, grad_values = attend_back(
            image_block[:, 0],
            image_block[:, 1],
            image_block[:, 2],
            valid_count,
            score_scale,
            image_total,
            image_grad,
        )
        return jnp.stack([grad_queries, grad_keys, grad_values], axis=1).astype(jnp.bfloat16)

    delta_packed = lax.map(backward_image, (spread, lengths, log_total, grad_spread))
    delta_packed = delta_packed.reshape(images, seq_len, 3, 1, per_group * HD)
    delta_back = lax.all_to_all(delta_packed, "seq", split_axis=1, concat_axis=3, tiled=True)
    delta_back = delta_back.reshape(images * local_len, 3 * model_width)
    grad_query_shift = column_sum(delta_back[:, :model_width])
    grad_value_shift = column_sum(delta_back[:, 2 * model_width :])
    grad_packed = left_outer(normed, delta_back)
    delta_normed = right_back(delta_back, packed_full)
    _, norm_pull_one = jax.vjp(layer_norm, token_rows, gain_one, shift_one)
    grad_rows_norm, grad_gain_one, grad_shift_one = norm_pull_one(delta_normed)
    grad_tokens = (delta_middle + grad_rows_norm).reshape(tokens.shape)
    local_grads = (
        grad_gain_one,
        grad_shift_one,
        grad_packed,
        grad_query_shift,
        grad_value_shift,
        grad_output,
        grad_output_shift,
        grad_scale_one,
        grad_gain_two,
        grad_shift_two,
        grad_up,
        grad_up_shift,
        grad_down,
        grad_down_shift,
        grad_scale_two,
    )
    owned_grads = (
        lax.psum_scatter(
            local_grads[0].astype(jnp.bfloat16), "fsdp", scatter_dimension=0, tiled=True
        ).astype(jnp.float32),
        lax.psum_scatter(
            local_grads[1].astype(jnp.bfloat16), "fsdp", scatter_dimension=0, tiled=True
        ).astype(jnp.float32),
        lax.psum_scatter(
            local_grads[2].astype(jnp.bfloat16), "fsdp", scatter_dimension=0, tiled=True
        ).astype(jnp.float32),
        lax.psum_scatter(
            local_grads[3].astype(jnp.bfloat16), "fsdp", scatter_dimension=0, tiled=True
        ).astype(jnp.float32),
        lax.psum_scatter(
            local_grads[4].astype(jnp.bfloat16), "fsdp", scatter_dimension=0, tiled=True
        ).astype(jnp.float32),
        lax.psum_scatter(
            local_grads[5].astype(jnp.bfloat16), "fsdp", scatter_dimension=0, tiled=True
        ).astype(jnp.float32),
        lax.psum_scatter(
            local_grads[6].astype(jnp.bfloat16), "fsdp", scatter_dimension=0, tiled=True
        ).astype(jnp.float32),
        lax.psum_scatter(
            local_grads[7].astype(jnp.bfloat16), "fsdp", scatter_dimension=0, tiled=True
        ).astype(jnp.float32),
        lax.psum_scatter(
            local_grads[8].astype(jnp.bfloat16), "fsdp", scatter_dimension=0, tiled=True
        ).astype(jnp.float32),
        lax.psum_scatter(
            local_grads[9].astype(jnp.bfloat16), "fsdp", scatter_dimension=0, tiled=True
        ).astype(jnp.float32),
        lax.psum_scatter(
            local_grads[10].astype(jnp.bfloat16), "fsdp", scatter_dimension=0, tiled=True
        ).astype(jnp.float32),
        lax.psum_scatter(
            local_grads[11].astype(jnp.bfloat16), "fsdp", scatter_dimension=0, tiled=True
        ).astype(jnp.float32),
        lax.psum_scatter(
            local_grads[12].astype(jnp.bfloat16), "fsdp", scatter_dimension=0, tiled=True
        ).astype(jnp.float32),
        lax.psum_scatter(
            local_grads[13].astype(jnp.bfloat16), "fsdp", scatter_dimension=0, tiled=True
        ).astype(jnp.float32),
        lax.psum_scatter(
            local_grads[14].astype(jnp.bfloat16), "fsdp", scatter_dimension=0, tiled=True
        ).astype(jnp.float32),
    )
    owned_grads = (
        lax.psum(owned_grads[0].astype(jnp.bfloat16), "seq").astype(jnp.float32),
        lax.psum(owned_grads[1].astype(jnp.bfloat16), "seq").astype(jnp.float32),
        lax.psum(owned_grads[2].astype(jnp.bfloat16), "seq").astype(jnp.float32),
        lax.psum(owned_grads[3].astype(jnp.bfloat16), "seq").astype(jnp.float32),
        lax.psum(owned_grads[4].astype(jnp.bfloat16), "seq").astype(jnp.float32),
        lax.psum(owned_grads[5].astype(jnp.bfloat16), "seq").astype(jnp.float32),
        lax.psum(owned_grads[6].astype(jnp.bfloat16), "seq").astype(jnp.float32),
        lax.psum(owned_grads[7].astype(jnp.bfloat16), "seq").astype(jnp.float32),
        lax.psum(owned_grads[8].astype(jnp.bfloat16), "seq").astype(jnp.float32),
        lax.psum(owned_grads[9].astype(jnp.bfloat16), "seq").astype(jnp.float32),
        lax.psum(owned_grads[10].astype(jnp.bfloat16), "seq").astype(jnp.float32),
        lax.psum(owned_grads[11].astype(jnp.bfloat16), "seq").astype(jnp.float32),
        lax.psum(owned_grads[12].astype(jnp.bfloat16), "seq").astype(jnp.float32),
        lax.psum(owned_grads[13].astype(jnp.bfloat16), "seq").astype(jnp.float32),
        lax.psum(owned_grads[14].astype(jnp.bfloat16), "seq").astype(jnp.float32),
    )
    return (output, grad_tokens) + tuple(owned_grads)


BF16 = jnp.bfloat16
F32 = jnp.float32
NT = (((1,), (1,)), ((), ()))
NN = (((1,), (0,)), ((), ()))
MASKED = -1e30
LANES = 128
VMEM_LIMIT = 60 * 2**20

GAIN1, SHIFT1, QUERY, VALUE, OUT_SHIFT, SCALE1, GAIN2, SHIFT2, DOWN_SHIFT, SCALE2 = range(10)


def dot(left, right, dims=NN):
    return lax.dot_general(left, right, dims, preferred_element_type=F32)


def turned(values):
    return values.T


def lane_ids(rows):
    return lax.broadcasted_iota(jnp.int32, (rows, LANES), 1)


def split3(values):
    high = values.astype(BF16).astype(F32)
    rest = values - high
    mid = rest.astype(BF16).astype(F32)
    return high, mid, rest - mid


LONG, SHORT = 16.0, 1 / 64


def params_for(flops, nbytes, transcendentals=0, weight=1.0):
    flops, nbytes, transcendentals = (int(weight * count) for count in (flops, nbytes, transcendentals))
    return dict(
        compiler_params=pltpu.CompilerParams(vmem_limit_bytes=VMEM_LIMIT),
        cost_estimate=pl.CostEstimate(
            flops=flops, bytes_accessed=nbytes, transcendentals=transcendentals
        ),
    )


def whole(shape):
    return pl.BlockSpec(shape, lambda *_: (0,) * len(shape))


def normalize(values, gain, shift):
    center = values - jnp.mean(values, axis=-1, keepdims=True)
    spread = jnp.mean(center * center, axis=-1, keepdims=True)
    return center * lax.rsqrt(spread + norm_eps) * gain + shift


def normalize_back(values, gain, delta):
    center = values - jnp.mean(values, axis=-1, keepdims=True)
    inverse = lax.rsqrt(jnp.mean(center * center, axis=-1, keepdims=True) + norm_eps)
    unit = center * inverse
    scaled = delta * gain
    mean_scaled = jnp.mean(scaled, axis=-1, keepdims=True)
    mean_unit = jnp.mean(scaled * unit, axis=-1, keepdims=True)
    return inverse * (scaled - mean_scaled - unit * mean_unit), delta * unit


def total_rows(values):
    return jnp.sum(values, axis=0, keepdims=True)


VECTORS = 10


def pack_kernel(place, weight_ref, up_ref, down_ref, output_ref, *refs):
    vector_refs, shift_ref = refs[:VECTORS], refs[VECTORS]
    first_ref, rest_ref = refs[VECTORS + 1 :]
    rows, width = weight_ref.shape
    first_ref[:, :width] = weight_ref[...]
    first_ref[:, width:] = jnp.zeros((rows, LANES), BF16)
    for i, ref in enumerate(vector_refs):
        values = ref[...].astype(F32).reshape(1, -1)
        empty = jnp.zeros_like(values)
        first, second = jnp.concatenate([values, empty], 1), jnp.concatenate([empty, values], 1)
        first_ref[i : i + 1, width:] = jnp.where(place[CORE] == 0, first, second).astype(BF16)
    shift = shift_ref[...].astype(F32).reshape(-1, LANES)
    first_ref[VECTORS : VECTORS + shift.shape[0], width:] = shift.astype(BF16)
    at = 0
    for ref in (up_ref, down_ref, output_ref):
        for g in range(ref.shape[0] // rows):
            rest_ref[:, at : at + ref.shape[1]] = ref[g * rows : (g + 1) * rows, :]
            at += ref.shape[1]


def pack(place, weight, up, down, output, vectors, up_shift):
    in_vmem = pl.BlockSpec(memory_space=pltpu.VMEM)
    rows, width = weight.shape
    others = (up.size + down.size + output.size) // rows
    return pl.pallas_call(
        pack_kernel,
        in_specs=[pl.BlockSpec(memory_space=pltpu.SMEM)] + [in_vmem] * (VECTORS + 5),
        out_specs=[in_vmem, in_vmem],
        out_shape=[
            jax.ShapeDtypeStruct((rows, width + LANES), BF16),
            jax.ShapeDtypeStruct((rows, others), BF16),
        ],
        name="pack",
        **params_for(0, 4 * rows * (width + others)),
    )(place, weight, up, down, output, *vectors, up_shift)


CORE, CHIPS = 6, 7


def project_kernel(place, x_ref, *refs, chips):
    own_refs, far_refs = refs[:chips], refs[chips : 2 * chips]
    far_out_ref, own_ref, normed_ref, weight_ref, table_ref, up_ref = refs[2 * chips :]
    step = pl.program_id(0)
    rows, block = own_refs[0].shape[0], weight_ref.shape[1]
    packed = own_refs[0].shape[1] - LANES
    core = place[CORE]

    @pl.when(step == 0)
    def _():
        vector = lax.broadcasted_iota(jnp.int32, (table_ref.shape[0], LANES), 0) < VECTORS
        each = up_ref.shape[1] // (2 * chips)
        for k in range(chips):
            chip = place[CHIPS + k]
            own = own_refs[k][: table_ref.shape[0], packed:].astype(F32)
            far = far_refs[k][: table_ref.shape[0], packed:].astype(F32)
            at = pl.ds(pl.multiple_of(chip * LANES, LANES), LANES)
            table_ref[:, at] = jnp.where(vector, own + far, 0.0)
            for part, side in ((own, core), (far, 1 - core)):
                for r in range(each // LANES):
                    at = pl.multiple_of((2 * chip + side) * each + r * LANES, LANES)
                    up_ref[:, pl.ds(at, LANES)] = part[VECTORS + r : VECTORS + r + 1, :]
        normed_ref[...] = normalize(
            x_ref[...].astype(F32), table_ref[GAIN1 : GAIN1 + 1, :], table_ref[SHIFT1 : SHIFT1 + 1, :]
        ).astype(BF16)

    columns = pl.ds(pl.multiple_of(place[step] * block, block), block)
    for k in range(chips):
        start = 2 * place[CHIPS + k]
        weight_ref[pl.ds(pl.multiple_of((start + core) * rows, rows), rows), :] = own_refs[k][:, columns]
        weight_ref[pl.ds(pl.multiple_of((start + 1 - core) * rows, rows), rows), :] = far_refs[k][:, columns]
    kind = lax.rem(step, 3)
    side = pl.ds(pl.multiple_of(lax.rem(place[step], 2) * block, block), block)
    shift = jnp.where(
        kind == 0,
        table_ref[QUERY : QUERY + 1, side],
        jnp.where(kind == 2, table_ref[VALUE : VALUE + 1, side], 0.0),
    )
    result = (dot(normed_ref[...], weight_ref[...]) + shift).astype(BF16)

    @pl.when(step < 3)
    def _():
        far_out_ref[0] = result

    @pl.when(step >= 3)
    def _():
        own_ref[0] = result


def project(place, x, own_pieces, far_pieces, hidden):
    chips = len(own_pieces)
    tokens, width = x.shape
    half = width // 2
    piece = own_pieces[0].shape
    return pl.pallas_call(
        functools.partial(project_kernel, chips=chips),
        grid_spec=pltpu.PrefetchScalarGridSpec(
            num_scalar_prefetch=1,
            grid=(6,),
            in_specs=[whole((tokens, width))] + [whole(piece)] * 2 * chips,
            out_specs=[
                pl.BlockSpec((1, tokens, half), lambda j, _: (jnp.minimum(j, 2), 0, 0)),
                pl.BlockSpec((1, tokens, half), lambda j, _: (jnp.maximum(j - 3, 0), 0, 0)),
                whole((tokens, width)),
                pl.BlockSpec((width, half), lambda j, place: (0, place[j])),
                whole((16, width)),
                whole((1, hidden)),
            ],
        ),
        out_shape=[
            jax.ShapeDtypeStruct((3, tokens, half), BF16),
            jax.ShapeDtypeStruct((3, tokens, half), BF16),
            jax.ShapeDtypeStruct((tokens, width), BF16),
            jax.ShapeDtypeStruct((width, 3 * width), BF16),
            jax.ShapeDtypeStruct((16, width), F32),
            jax.ShapeDtypeStruct((1, hidden), F32),
        ],
        name="project",
        **params_for(6 * tokens * width * width, 12 * tokens * width + 12 * width * width),
    )(place, x, *own_pieces, *far_pieces)


def padded_len(count, block):
    return -(-count // block) * block


def attend_kernel(valid, *refs, pieces, block, scale):
    in_refs, out_refs = refs[:pieces], refs[pieces : 2 * pieces]
    total_refs = refs[2 * pieces : 3 * pieces]
    keys, values, queries, mixed, totals = refs[3 * pieces :]
    pair = pl.program_id(0)
    size = in_refs[0].shape[1]
    count, padded = pieces * size, keys.shape[0]
    lane = lane_ids(size)
    row = lax.broadcasted_iota(jnp.int32, (size, LANES), 0)
    for i in range(pieces):
        at = pl.ds(i * size, size)
        keys[at, :LANES] = in_refs[i][1]
        keys[at, LANES:] = jnp.where((lane == 0) & (row >= valid[i]), MASKED, 0.0).astype(BF16)
        values[at, :LANES] = in_refs[i][2]
        values[at, LANES:] = jnp.where(lane == 0, 1.0, 0.0).astype(BF16)
        for j in range(2):
            mine = lane // HD == j
            queries[j, at, :LANES] = jnp.where(mine, in_refs[i][0].astype(F32) * scale, 0.0).astype(BF16)
            queries[j, at, LANES:] = jnp.where(lane == 0, 1.0, 0.0).astype(BF16)
    if padded > count:
        rest = pl.ds(count, padded - count)
        rest_lane = lane_ids(padded - count)
        keys[rest, :LANES] = jnp.zeros((padded - count, LANES), BF16)
        keys[rest, LANES:] = jnp.where(rest_lane == 0, MASKED, 0.0).astype(BF16)
        values[rest, :] = jnp.zeros((padded - count, 2 * LANES), BF16)
        for j in range(2):
            queries[j, rest, :] = jnp.zeros((padded - count, 2 * LANES), BF16)

    @pl.when(pair == 0)
    def _():
        for i in range(pieces):
            total_refs[i][...] = jnp.zeros_like(total_refs[i])

    block_lane = lane_ids(block)
    for b in range(padded // block):
        at = pl.ds(b * block, block)
        results, logs = [], 0.0
        for j in range(2):
            scores = dot(queries[j, at, :], keys[...], NT)
            largest = jnp.max(scores, axis=1, keepdims=True)
            weights = jnp.exp(scores - largest).astype(BF16)
            result = dot(weights, values[...])
            total = result[:, LANES : LANES + 1]
            results.append(result[:, :LANES] * (1.0 / total))
            logs += jnp.where(block_lane == 2 * pair + j, largest + jnp.log(total), 0.0)
        mixed[at, :] = jnp.where(block_lane < HD, results[0], results[1])
        totals[at, :] = logs
    for i in range(pieces):
        at = pl.ds(i * size, size)
        out_refs[i][...] = mixed[at, :].astype(BF16)
        total_refs[i][...] += totals[at, :]


def attention(valid, parts, block):
    pieces = len(parts)
    _, size, width = parts[0].shape
    pairs = width // LANES
    padded = padded_len(pieces * size, block)
    outs = pl.pallas_call(
        functools.partial(attend_kernel, pieces=pieces, block=block, scale=HD**-0.5),
        grid_spec=pltpu.PrefetchScalarGridSpec(
            num_scalar_prefetch=1,
            grid=(pairs,),
            in_specs=[pl.BlockSpec((3, size, LANES), lambda h, _: (0, 0, h))] * pieces,
            out_specs=[pl.BlockSpec((size, LANES), lambda h, _: (0, h))] * pieces
            + [whole((size, LANES))] * pieces,
            scratch_shapes=[
                pltpu.VMEM((padded, 2 * LANES), BF16),
                pltpu.VMEM((padded, 2 * LANES), BF16),
                pltpu.VMEM((2, padded, 2 * LANES), BF16),
                pltpu.VMEM((padded, LANES), F32),
                pltpu.VMEM((padded, LANES), F32),
            ],
        ),
        out_shape=[jax.ShapeDtypeStruct((size, width), BF16)] * pieces
        + [jax.ShapeDtypeStruct((size, LANES), F32)] * pieces,
        name="attend",
        **params_for(16 * pairs * LANES * padded * padded, 8 * size * width * pieces, pairs * 2 * padded * padded),
    )(valid, *parts)
    return outs[:pieces], outs[pieces:]


def attend_back_kernel(valid, *refs, pieces, block, scale, first):
    in_refs, mix_refs = refs[:pieces], refs[pieces : 2 * pieces]
    grad_refs, total_refs = refs[2 * pieces : 3 * pieces], refs[3 * pieces : 4 * pieces]
    out_refs = refs[-9 - pieces : -9]
    keys, values, queries, grads, queries_t, grads_t, dq, dk_t, dv_t = refs[-9:]
    pair = first + pl.program_id(0)
    size = in_refs[0].shape[1]
    count, padded = pieces * size, keys.shape[0]
    blocks = padded // block
    lane = lane_ids(size)
    row = lax.broadcasted_iota(jnp.int32, (size, LANES), 0)
    for i in range(pieces):
        at = pl.ds(i * size, size)
        keys[at, :LANES] = in_refs[i][1]
        keys[at, LANES:] = jnp.where(
            lane == 0, jnp.where(row >= valid[i], MASKED, 0.0), jnp.where(lane < 4, 1.0, 0.0)
        ).astype(BF16)
        values[at, :LANES] = in_refs[i][2]
        values[at, LANES:] = jnp.where((lane > 0) & (lane < 4), 1.0, 0.0).astype(BF16)
        queries[0, at, :LANES] = in_refs[i][0]
        grads[0, at, :LANES] = grad_refs[i][...]
    if padded > count:
        left = padded - count
        rest = pl.ds(count, left)
        keys[rest, :LANES] = jnp.zeros((left, LANES), BF16)
        keys[rest, LANES:] = jnp.where(lane_ids(left) == 0, MASKED, 0.0).astype(BF16)
        values[rest, :] = jnp.zeros((left, 2 * LANES), BF16)
        for j in range(2):
            queries[j, rest, :] = jnp.zeros((left, 2 * LANES), BF16)
            grads[j, rest, :] = jnp.zeros((left, 2 * LANES), BF16)
    for b in range(blocks):
        at = pl.ds(b * block, block)
        queries_t[b] = (queries[0, at, :LANES].astype(F32) * scale).T.astype(BF16)
        grads_t[b] = turned(grads[0, at, :LANES])
    for j in range(2):
        mine = lane // HD == j
        for i in range(pieces):
            at = pl.ds(i * size, size)
            grad = jnp.where(mine, grad_refs[i][...].astype(F32), 0.0)
            queries[j, at, :LANES] = jnp.where(mine, in_refs[i][0].astype(F32) * scale, 0.0).astype(BF16)
            grads[j, at, :LANES] = grad.astype(BF16)
            log_total = jnp.sum(
                jnp.where(lane == 2 * pair + j, total_refs[i][...], 0.0), axis=1, keepdims=True
            )
            high, mid, low = split3(-log_total)
            queries[j, at, LANES:] = jnp.where(
                lane == 0,
                1.0,
                jnp.where(lane == 1, high, jnp.where(lane == 2, mid, jnp.where(lane == 3, low, 0.0))),
            ).astype(BF16)
            inner = jnp.sum(grad * mix_refs[i][...].astype(F32), axis=1, keepdims=True)
            high, mid, low = split3(-inner)
            grads[j, at, LANES:] = jnp.where(
                lane == 1, high, jnp.where(lane == 2, mid, jnp.where(lane == 3, low, 0.0))
            ).astype(BF16)
    dk_t[...] = jnp.zeros_like(dk_t)
    dv_t[...] = jnp.zeros_like(dv_t)
    block_lane = lane_ids(block)
    for b in range(blocks):
        at = pl.ds(b * block, block)
        results = []
        for j in range(2):
            mine = pl.ds(j * HD, HD)
            probs = jnp.exp(dot(queries[j, at, :], keys[...], NT))
            grad_scores = (probs * dot(grads[j, at, :], values[...], NT)).astype(BF16)
            results.append(dot(grad_scores, keys[:, :LANES]) * scale)
            dv_t[mine, :] += dot(grads_t[b, mine, :], probs.astype(BF16))
            dk_t[mine, :] += dot(queries_t[b, mine, :], grad_scores)
        dq[at, :] = jnp.where(block_lane < HD, results[0], results[1])
    dk, dv = dk_t[...].T, dv_t[...].T
    for i in range(pieces):
        at = slice(i * size, (i + 1) * size)
        out_refs[i][0] = dq[at, :].astype(BF16)
        out_refs[i][1] = dk[at, :].astype(BF16)
        out_refs[i][2] = dv[at, :].astype(BF16)


def attention_back(valid, parts, mixtures, grads, totals, block, first, pairs, into, after):
    pieces = len(parts)
    _, size, width = parts[0].shape
    padded = padded_len(pieces * size, block)
    triple = pl.BlockSpec((3, size, LANES), lambda h, _: (0, 0, first + h))
    single = pl.BlockSpec((size, LANES), lambda h, _: (0, first + h))
    in_specs = [triple] * pieces + [single] * 2 * pieces + [whole((size, LANES))] * pieces
    aliases = {1 + len(in_specs) + i: i for i in range(len(into))}
    return pl.pallas_call(
        functools.partial(attend_back_kernel, pieces=pieces, block=block, scale=HD**-0.5, first=first),
        grid_spec=pltpu.PrefetchScalarGridSpec(
            num_scalar_prefetch=1,
            grid=(pairs,),
            in_specs=in_specs + [pl.BlockSpec(memory_space=pl.ANY)] * (len(into) + len(after)),
            out_specs=[triple] * pieces,
            scratch_shapes=[
                pltpu.VMEM((padded, 2 * LANES), BF16),
                pltpu.VMEM((padded, 2 * LANES), BF16),
                pltpu.VMEM((2, padded, 2 * LANES), BF16),
                pltpu.VMEM((2, padded, 2 * LANES), BF16),
                pltpu.VMEM((padded // block, LANES, block), BF16),
                pltpu.VMEM((padded // block, LANES, block), BF16),
                pltpu.VMEM((padded, LANES), F32),
                pltpu.VMEM((LANES, padded), F32),
                pltpu.VMEM((LANES, padded), F32),
            ],
        ),
        out_shape=[jax.ShapeDtypeStruct((3, size, width), BF16)] * pieces,
        input_output_aliases=aliases,
        name="attend_back",
        **params_for(30 * pairs * LANES * padded * padded, 16 * size * LANES * pairs * pieces, pairs * 2 * padded * padded, weight=LONG),
    )(valid, *parts, *mixtures, *grads, *totals, *into, *after)


def merge_kernel(place, x_ref, own_ref, far_ref, table, own_w, far_w, middle_ref, branch_ref, normed_ref):
    branch = dot(own_ref[...], own_w[...]) + dot(far_ref[...], far_w[...])
    branch += table[OUT_SHIFT : OUT_SHIFT + 1, :]
    middle = x_ref[...].astype(F32) + table[SCALE1 : SCALE1 + 1, :] * branch
    middle_ref[...] = middle
    branch_ref[...] = branch
    normed_ref[...] = normalize(
        middle, table[GAIN2 : GAIN2 + 1, :], table[SHIFT2 : SHIFT2 + 1, :]
    ).astype(BF16)


ROWS = 352


def row_steps(tokens):
    return -(-tokens // ROWS)


def merge(place, x, own, far, table, rest):
    tokens, width = x.shape
    half = width // 2
    wide = pl.BlockSpec((ROWS, width), lambda i, _: (i, 0))
    narrow = pl.BlockSpec((ROWS, half), lambda i, _: (i, 0))
    return pl.pallas_call(
        merge_kernel,
        grid_spec=pltpu.PrefetchScalarGridSpec(
            num_scalar_prefetch=1,
            grid=(row_steps(tokens),),
            in_specs=[
                wide,
                narrow,
                narrow,
                whole(table.shape),
                pl.BlockSpec((half, width), lambda i, place: (place[CORE], rest.shape[1] // width - 1)),
                pl.BlockSpec((half, width), lambda i, place: (1 - place[CORE], rest.shape[1] // width - 1)),
            ],
            out_specs=[wide, wide, wide],
        ),
        out_shape=[
            jax.ShapeDtypeStruct((tokens, width), F32),
            jax.ShapeDtypeStruct((tokens, width), F32),
            jax.ShapeDtypeStruct((tokens, width), BF16),
        ],
        name="merge",
        **params_for(2 * tokens * width * width, 14 * tokens * width + 2 * width * width),
    )(place, x, own, far, table, rest, rest)


def gelu_and_slope(values):
    size = jnp.abs(values) * 0.7071067811865476
    t = 1.0 / (1.0 + 0.3275911 * size)
    bell = jnp.exp(-0.5 * (values * values))
    poly = t * (0.254829592 + t * (-0.284496736 + t * (1.421413741 + t * (-1.453152027 + t * 1.061405429))))
    tail = 0.5 * poly * bell
    phi = jnp.where(values < 0, tail, 1.0 - tail)
    return values * phi, phi + values * bell * 0.3989422804014327


def ungroup(grouped_ref, down):
    width = down.shape[1]
    groups = grouped_ref.shape[1] // width
    each = grouped_ref.shape[0] // 2
    for device in range(2):
        for g in range(groups):
            at = (device * groups + g) * each
            down[at : at + each, :] = grouped_ref[device * each : (device + 1) * each, g * width : (g + 1) * width]


def scaled_upstream(cotangent_ref, table):
    return (cotangent_ref[...].astype(F32) * table[SCALE2 : SCALE2 + 1, :]).astype(BF16)


def place_turned(place, block, target, k, chips):
    half = block.shape[1] // 2
    turned_block = block.T
    first, second = turned_block[:half], turned_block[half:]
    target[k * half : (k + 1) * half, :] = jnp.where(place[CORE] == 0, first, second)
    target[(chips + k) * half : (chips + k + 1) * half, :] = jnp.where(place[CORE] == 0, second, first)


def fill_turned(place, source_ref, target, chips):
    wide = source_ref.shape[1] // chips
    for k in range(chips):
        at = pl.ds(pl.multiple_of(place[CHIPS + k] * wide, wide), wide)
        place_turned(place, source_ref[:, at], target, k, chips)


def split_rows(grad, mine_ref, other_ref):
    chips, rows, _ = mine_ref.shape
    for k in range(chips):
        mine_ref[k] = grad[k * rows : (k + 1) * rows, :]
        other_ref[k] = grad[(chips + k) * rows : (chips + k + 1) * rows, :]


def group(grad, out_ref):
    rows, columns = out_ref.shape[1], grad.shape[1]
    for g in range(grad.shape[0] // rows):
        out_ref[0, :, g * columns : (g + 1) * columns] = grad[g * rows : (g + 1) * rows, :]


def mlp_kernel(
    place, normed_ref, cotangent_ref, table, up_ref, shift_ref, grouped_ref,
    branch_ref, delta_ref, up_mine_ref, up_other_ref, down_mine_ref, down_other_ref, grad_shift_ref,
    upstream, upstream_t, normed_t, down,
    *, chips,
):
    @pl.when(pl.program_id(0) == 0)
    def _():
        scaled = (cotangent_ref[...].astype(F32) * table[SCALE2 : SCALE2 + 1, :]).astype(BF16)
        upstream[...] = scaled
        upstream_t[...] = turned(scaled)
        fill_turned(place, normed_ref, normed_t, chips)
        branch_ref[...] = jnp.zeros_like(branch_ref)
        delta_ref[...] = jnp.zeros_like(delta_ref)

    ungroup(grouped_ref, down)
    hidden = dot(normed_ref[...], up_ref[...]) + shift_ref[...]
    grad_active = dot(upstream[...], down[...], NT)
    active, slope = gelu_and_slope(hidden)
    active = active.astype(BF16)
    delta_hidden = (grad_active * slope).astype(BF16)
    branch_ref[...] += dot(active, down[...])
    delta_ref[...] += dot(delta_hidden, up_ref[...], NT)
    split_rows(dot(normed_t[...], delta_hidden).astype(BF16), up_mine_ref, up_other_ref)
    grad_down = dot(upstream_t[...], active)
    each = grad_down.shape[1] // 2
    first, second = grad_down[:, :each], grad_down[:, each:]
    group(jnp.where(place[CORE] == 0, first, second).astype(BF16), down_mine_ref)
    group(jnp.where(place[CORE] == 0, second, first).astype(BF16), down_other_ref)
    grad_shift_ref[...] = total_rows(delta_hidden.astype(F32))


def mlp(place, normed, cotangent, table, rest, up_shift, owners):
    tokens, width = normed.shape
    hidden = up_shift.shape[1]
    rows = rest.shape[0] // owners
    chips = owners // 2
    block = hidden // chips
    up_out = pl.BlockSpec((chips, rows, block), lambda j, place: (0, 0, place[CHIPS + j]))
    down_out = pl.BlockSpec((1, rows, hidden), lambda j, _: (j, 0, 0))
    sent = jax.ShapeDtypeStruct((chips, rows, hidden), BF16)
    return pl.pallas_call(
        functools.partial(mlp_kernel, chips=chips),
        grid_spec=pltpu.PrefetchScalarGridSpec(
            num_scalar_prefetch=1,
            grid=(chips,),
            in_specs=[
                whole((tokens, width)),
                whole((tokens, width)),
                whole(table.shape),
                pl.BlockSpec((width, block), lambda j, place: (0, place[CHIPS + j])),
                pl.BlockSpec((1, block), lambda j, place: (0, place[CHIPS + j])),
                pl.BlockSpec((2 * rows, hidden), lambda j, place: (place[CHIPS + j], 1)),
            ],
            out_specs=[
                whole((tokens, width)),
                whole((tokens, width)),
                up_out,
                up_out,
                down_out,
                down_out,
                pl.BlockSpec((1, block), lambda j, place: (0, place[CHIPS + j])),
            ],
            scratch_shapes=[
                pltpu.VMEM((tokens, width), BF16),
                pltpu.VMEM((width, tokens), BF16),
                pltpu.VMEM((width, tokens), BF16),
                pltpu.VMEM((block, width), BF16),
            ],
        ),
        out_shape=[
            jax.ShapeDtypeStruct((tokens, width), F32),
            jax.ShapeDtypeStruct((tokens, width), F32),
            sent,
            sent,
            sent,
            sent,
            jax.ShapeDtypeStruct((1, hidden), F32),
        ],
        name="mlp",
        **params_for(12 * tokens * width * hidden, 12 * tokens * width + 8 * width * hidden, 2 * tokens * hidden),
    )(place, normed, cotangent, table, rest, up_shift, rest)


SUM_ROWS = 8


def unmerge_kernel(
    place, middle_ref, branch1_ref, branch2_ref, delta_ref, cotangent_ref, own_ref, far_ref, table, own_w, far_w,
    output_ref, delta_middle_ref, own_grad_ref, far_grad_ref, mine_ref, other_ref, sums_ref,
    delta1_all, mixture_t,
    *, tokens,
):
    step = pl.program_id(0)

    @pl.when(step == 0)
    def _():
        sums_ref[...] = jnp.zeros_like(sums_ref)

    rows, width = middle_ref.shape
    inside = lax.broadcasted_iota(jnp.int32, (rows, width), 0) + step * rows < tokens

    def kept(values):
        return jnp.where(inside, values, 0.0)

    upstream = cotangent_ref[...].astype(F32)
    scale2 = table[SCALE2 : SCALE2 + 1, :]
    middle = middle_ref[...]
    branch2 = branch2_ref[...] + table[DOWN_SHIFT : DOWN_SHIFT + 1, :]
    output_ref[...] = (middle + scale2 * branch2).astype(BF16)
    delta2 = (scale2 * upstream).astype(BF16).astype(F32)
    delta = delta_ref[...]
    inner, gain_terms = normalize_back(middle, table[GAIN2 : GAIN2 + 1, :], delta)
    delta_middle = upstream + inner
    delta_middle_ref[...] = delta_middle
    delta1 = kept(table[SCALE1 : SCALE1 + 1, :] * delta_middle).astype(BF16)
    delta1_all[pl.ds(pl.multiple_of(step * rows, 16), rows), :] = delta1
    own_grad_ref[...] = dot(delta1, own_w[...], NT).astype(BF16)
    far_grad_ref[...] = dot(delta1, far_w[...], NT).astype(BF16)
    terms = (
        upstream * branch2,
        delta2,
        gain_terms,
        delta,
        delta_middle * branch1_ref[...],
        delta1.astype(F32),
    )
    for i, term in enumerate(terms):
        sums_ref[i : i + 1, :] += total_rows(kept(term))

    @pl.when(step == pl.num_programs(0) - 1)
    def _():
        chips = mine_ref.shape[0]
        wide = width // chips
        for k in range(chips):
            chip = place[CHIPS + k]
            at = pl.ds(pl.multiple_of(lax.rem(chip, chips // 2) * wide, wide), wide)
            mixed = jnp.where(chip // (chips // 2) == place[CORE], own_ref[:, at], far_ref[:, at])
            place_turned(place, mixed, mixture_t, k, chips)
        split_rows(dot(mixture_t[...], delta1_all[:tokens, :]).astype(BF16), mine_ref, other_ref)


def unmerge(place, middle, branch1, branch2, delta, cotangent, own, far, table, rest, owners):
    tokens, width = middle.shape
    chips = owners // 2
    sent = (chips, width // owners, width)
    half = width // 2
    steps = row_steps(tokens)
    wide = pl.BlockSpec((ROWS, width), lambda i, _: (i, 0))
    narrow = pl.BlockSpec((ROWS, half), lambda i, _: (i, 0))
    return pl.pallas_call(
        functools.partial(unmerge_kernel, tokens=tokens),
        grid_spec=pltpu.PrefetchScalarGridSpec(
            num_scalar_prefetch=1,
            grid=(steps,),
            in_specs=[wide] * 5
            + [whole((tokens, half))] * 2
            + [
                whole(table.shape),
                pl.BlockSpec((half, width), lambda i, place: (place[CORE], rest.shape[1] // width - 1)),
                pl.BlockSpec((half, width), lambda i, place: (1 - place[CORE], rest.shape[1] // width - 1)),
            ],
            out_specs=[wide, wide, narrow, narrow, whole(sent), whole(sent), whole((SUM_ROWS, width))],
            scratch_shapes=[pltpu.VMEM((steps * ROWS, width), BF16), pltpu.VMEM((width, tokens), BF16)],
        ),
        out_shape=[
            jax.ShapeDtypeStruct((tokens, width), BF16),
            jax.ShapeDtypeStruct((tokens, width), F32),
            jax.ShapeDtypeStruct((tokens, half), BF16),
            jax.ShapeDtypeStruct((tokens, half), BF16),
            jax.ShapeDtypeStruct(sent, BF16),
            jax.ShapeDtypeStruct(sent, BF16),
            jax.ShapeDtypeStruct((SUM_ROWS, width), F32),
        ],
        name="unmerge",
        **params_for(4 * tokens * width * width, 30 * tokens * width + 4 * width * width),
    )(place, middle, branch1, branch2, delta, cotangent, own, far, table, rest, rest)


def unproject_kernel(
    place, x_ref, delta_middle_ref, table, normed_ref, own_ref, far_ref, weight_ref, middle_sums, up_sums, *refs, chips
):
    out_ref, mine_ref, other_ref, vectors_mine_ref, vectors_other_ref, delta, sums, normed_t = refs[-8:]
    step = pl.program_id(0)
    width = x_ref.shape[1]
    core = place[CORE]

    @pl.when(step == 0)
    def _():
        fill_turned(place, normed_ref, normed_t, chips)
        delta[...] = jnp.zeros_like(delta)
        sums[...] = jnp.zeros_like(sums)

    block = jnp.where(step < 3, own_ref[0], far_ref[0])
    split_rows(dot(normed_t[...], block).astype(BF16), mine_ref, other_ref)
    delta[...] += dot(block, weight_ref[...], NT)
    column_total = total_rows(block.astype(F32))
    half = block.shape[1]
    at = pl.ds(pl.multiple_of(jnp.where(step < 3, core, 1 - core) * half, half), half)
    for kind, row in ((0, QUERY), (2, VALUE)):

        @pl.when(lax.rem(step, 3) == kind)
        def _():
            sums[row : row + 1, at] = column_total

    @pl.when(step == pl.num_programs(0) - 1)
    def _():
        delta_normed = delta[...]
        inner, gain_terms = normalize_back(
            x_ref[...].astype(F32), table[GAIN1 : GAIN1 + 1, :], delta_normed
        )
        out_ref[...] = (delta_middle_ref[...] + inner).astype(BF16)
        rows = {
            GAIN1: total_rows(gain_terms),
            SHIFT1: total_rows(delta_normed),
            OUT_SHIFT: middle_sums[5:6, :],
            SCALE1: middle_sums[4:5, :],
            GAIN2: middle_sums[2:3, :],
            SHIFT2: middle_sums[3:4, :],
            DOWN_SHIFT: middle_sums[1:2, :],
            SCALE2: middle_sums[0:1, :],
        }
        for i, values in rows.items():
            sums[i : i + 1, :] = values
        each = up_sums.shape[1] // (2 * chips)
        for out, side in ((vectors_mine_ref, core), (vectors_other_ref, 1 - core)):
            out[...] = jnp.zeros_like(out)
            for k in range(chips):
                chip = place[CHIPS + k]
                at = pl.ds(pl.multiple_of(chip * LANES, LANES), LANES)
                out[k, : sums.shape[0], :] = sums[:, at].astype(BF16)
                for r in range(each // LANES):
                    at = pl.multiple_of((2 * chip + side) * each + r * LANES, LANES)
                    row = up_sums[:, pl.ds(at, LANES)].astype(BF16)
                    out[k, VECTORS + r : VECTORS + r + 1, :] = row


def unproject(place, x, delta_middle, table, normed, own, far, weight, middle_sums, up_sums, owners, after):
    tokens, width = x.shape
    half = width // 2
    chips = owners // 2
    rows = width // owners
    vectors = (chips, rows, LANES)

    def column(j, place):
        return 2 * lax.rem(j, 3) + jnp.where(j < 3, place[CORE], 1 - place[CORE])

    sent = pl.BlockSpec((chips, rows, half), lambda j, place: (0, 0, column(j, place)))
    return pl.pallas_call(
        functools.partial(unproject_kernel, chips=chips),
        grid_spec=pltpu.PrefetchScalarGridSpec(
            num_scalar_prefetch=1,
            grid=(6,),
            in_specs=[
                whole((tokens, width)),
                whole((tokens, width)),
                whole(table.shape),
                whole((tokens, width)),
                pl.BlockSpec((1, tokens, half), lambda j, _: (jnp.minimum(j, 2), 0, 0)),
                pl.BlockSpec((1, tokens, half), lambda j, _: (jnp.maximum(j - 3, 0), 0, 0)),
                pl.BlockSpec((width, half), lambda j, place: (0, column(j, place))),
                whole(middle_sums.shape),
                whole(up_sums.shape),
            ]
            + [pl.BlockSpec(memory_space=pl.ANY)] * len(after),
            out_specs=[whole((tokens, width)), sent, sent, whole(vectors), whole(vectors)],
            scratch_shapes=[
                pltpu.VMEM((tokens, width), F32),
                pltpu.VMEM((16, width), F32),
                pltpu.VMEM((width, tokens), BF16),
            ],
        ),
        out_shape=[
            jax.ShapeDtypeStruct((tokens, width), BF16),
            jax.ShapeDtypeStruct((chips, rows, 3 * width), BF16),
            jax.ShapeDtypeStruct((chips, rows, 3 * width), BF16),
            jax.ShapeDtypeStruct(vectors, BF16),
            jax.ShapeDtypeStruct(vectors, BF16),
        ],
        name="unproject",
        **params_for(12 * tokens * width * width, 18 * tokens * width + 12 * width * width, weight=SHORT),
    )(place, x, delta_middle, table, normed, own, far, weight, middle_sums, up_sums, *after)


def ring_of(chips):
    return list(range(0, chips, 2)) + list(range(1, chips, 2))[::-1]


def places(owners):
    ring = ring_of(owners // 2)
    rows = []
    for f in range(owners):
        chip, core = divmod(f, 2)
        at = ring.index(chip)
        columns = [1 - core, 3 - core, 5 - core, core, 2 + core, 4 + core]
        rows.append(columns + [core] + ring[at:] + ring[:at])
    return np.array(rows, np.int32)


def ring_perm(chips, hop):
    ring = ring_of(chips)
    return [
        (2 * ring[i] + core, 2 * ring[(i + hop) % chips] + core) for i in range(chips) for core in range(2)
    ]


def to_next(values, chips, hop):
    return lax.ppermute(values, "fsdp", ring_perm(chips, hop))


def ring_gather(piece, chips):
    pieces = [None] * chips
    pieces[0] = right = left = piece
    for k in range(1, chips // 2 + 1):
        pieces[-k] = right = to_next(right, chips, 1)
        if k < chips - chips // 2:
            pieces[k] = left = to_next(left, chips, -1)
    return pieces


def low_part(columns):
    return columns // 2 if columns % (2 * LANES) == 0 else columns


def ring_add_kernel(*refs, columns, mode, carried):
    ways = 2 if mode in ("second", "next") else 1
    shares = [refs[2 * len(columns) * d : 2 * len(columns) * (d + 1)] for d in range(ways)]
    came = refs[2 * len(columns) * ways :]
    outs = refs[len(refs) - carried - (1 if mode == "total" else 2) : len(refs) - carried]
    start, low_start, high_start = 0, 0, 0
    for i, each in enumerate(columns):
        totals = [mine[2 * i][0].astype(F32) + mine[2 * i + 1][0].astype(F32) for mine in shares]
        at = slice(start, start + each)
        low = low_part(each)
        low_at, high_at = slice(low_start, low_start + low), slice(high_start, high_start + each - low)
        if mode == "first":
            outs[0][:, low_at] = totals[0][:, :low].astype(BF16)
            if low < each:
                outs[1][:, high_at] = totals[0][:, low:].astype(BF16)
        elif mode == "second":
            outs[0][:, start : start + low] = (totals[0][:, :low] + came[0][:, low_at].astype(F32)).astype(BF16)
            outs[1][:, start : start + low] = totals[1][:, :low].astype(BF16)
            if low < each:
                high = totals[1][:, low:] + came[1][:, high_at].astype(F32)
                outs[0][:, start + low : start + each] = totals[0][:, low:].astype(BF16)
                outs[1][:, start + low : start + each] = high.astype(BF16)
        elif mode == "next":
            for total, arrived, out in zip(totals, came, outs):
                out[:, at] = (total + arrived[:, at].astype(F32)).astype(BF16)
        else:
            both_ways = came[0][:, at].astype(F32) + came[1][:, at].astype(F32)
            outs[0][:, at] = (totals[0] + both_ways).astype(BF16)
        start, low_start, high_start = at.stop, low_at.stop, high_at.stop


class RingSum:
    def __init__(self, *parts):
        self.parts, self.chips = parts, parts[0][0].shape[0]
        self.steps = self.chips // 2
        self.step = 0
        self.came = []

    def add(self, mode, places, after=(), carry=()):
        rows = self.parts[0][0].shape[1]
        columns = [mine.shape[2] for mine, _ in self.parts]
        total = sum(columns)
        blocks = 2 if total > 4096 else 1
        arrays, specs = [], []
        for at in places:
            for part, each in zip(self.parts, columns):
                for array in part:
                    arrays.append(array)
                    specs.append(pl.BlockSpec((1, rows // blocks, each), lambda i, at=at: (at, i, 0)))
        for came in self.came:
            arrays.append(came)
            specs.append(pl.BlockSpec((rows // blocks, came.shape[1]), lambda i: (i, 0)))
        arrays += [*after, *carry]
        anywhere = pl.BlockSpec(memory_space=pl.ANY)
        specs += [anywhere] * (len(after) + len(carry))
        low = sum(low_part(each) for each in columns)
        out_columns = {"first": [low, total - low], "total": [total]}.get(mode, [total, total])
        sums = len(out_columns)
        outs = pl.pallas_call(
            functools.partial(ring_add_kernel, columns=columns, mode=mode, carried=len(carry)),
            grid=(blocks,),
            in_specs=specs,
            out_specs=[pl.BlockSpec((rows // blocks, out), lambda i: (i, 0)) for out in out_columns]
            + [anywhere] * len(carry),
            out_shape=[jax.ShapeDtypeStruct((rows, out), BF16) for out in out_columns]
            + [jax.ShapeDtypeStruct(array.shape, array.dtype) for array in carry],
            input_output_aliases={len(arrays) - len(carry) + i: sums + i for i in range(len(carry))},
            name="ring_add",
            **params_for(6 * rows * total, 16 * rows * total, weight=SHORT),
        )(*arrays)
        return outs[:sums], outs[sums:]

    def sums(self, after=(), carry=()):
        k = self.steps - self.step
        if self.step == 0:
            return self.add("first", [k], after, carry)
        return self.add("second" if self.step == 1 else "next", [k, self.chips - k], after, carry)

    def send(self, sums):
        self.came = [to_next(sums[0], self.chips, 1), to_next(sums[1], self.chips, -1)]
        self.step += 1

    def total(self, carry=()):
        assert self.step == self.steps
        sums, carried = self.add("total", [0], (), carry)
        return sums[0], carried


def finish_rest_kernel(part_ref, came_ref, up_ref, down_ref, output_ref):
    def total(at):
        return part_ref[:, at].astype(F32) + came_ref[:, at].astype(F32)

    rows, hidden = up_ref.shape
    each, width = down_ref.shape
    up_ref[...] = total(slice(0, hidden))
    for g in range(0, width // rows, 2):
        pair = [total(slice(hidden + each * h, hidden + each * (h + 1))) for h in (g, g + 1)]
        down_ref[:, g * rows : (g + 2) * rows] = jnp.concatenate(pair, axis=0).T
    output_ref[...] = total(slice(hidden + width // rows * each, None))


def finish_rest(part, came, hidden, each, width):
    in_vmem = pl.BlockSpec(memory_space=pltpu.VMEM)
    rows = part.shape[0]
    return pl.pallas_call(
        finish_rest_kernel,
        in_specs=[in_vmem] * 2,
        out_specs=[in_vmem] * 3,
        out_shape=[jax.ShapeDtypeStruct(shape, F32) for shape in ((rows, hidden), (each, width), (rows, width))],
        name="finish_rest",
        **params_for(part.size, 8 * part.size, weight=SHORT),
    )(part, came)


def finish_first_kernel(place, part_ref, came_ref, packed_ref, *vector_refs):
    def total(rows, at):
        return part_ref[rows, at].astype(F32) + came_ref[rows, at].astype(F32)

    width = packed_ref.shape[1]
    packed_ref[...] = total(slice(None), slice(0, width))
    vectors = total(slice(0, 16), slice(width, width + LANES))
    half = LANES // 2
    mine = jnp.where(place[CORE] == 0, vectors[:, :half], vectors[:, half:])
    for i in range(VECTORS):
        vector_refs[i][...] = mine[i : i + 1, :].reshape(half)
    count = vector_refs[VECTORS].shape[0]
    vector_refs[VECTORS][...] = vectors[VECTORS : VECTORS + count // LANES, :].reshape(count)


def finish_first(place, part, came, each):
    in_vmem = pl.BlockSpec(memory_space=pltpu.VMEM)
    rows, width = part.shape[0], part.shape[1] - LANES
    shapes = [(rows, width)] + [(rows,)] * VECTORS + [(each,)]
    return pl.pallas_call(
        finish_first_kernel,
        in_specs=[pl.BlockSpec(memory_space=pltpu.SMEM)] + [in_vmem] * 2,
        out_specs=[in_vmem] * len(shapes),
        out_shape=[jax.ShapeDtypeStruct(shape, F32) for shape in shapes],
        name="finish_first",
        **params_for(part.size, 8 * part.size, weight=SHORT),
    )(place, part, came)


def split_pairs(pairs):
    return [pairs // 4, pairs // 2, pairs - pairs // 4 - pairs // 2] if pairs >= 4 else [pairs]


def paired_body(
    tokens, lengths, norm1_gain, norm1_bias, packed_weight, query_bias, value_bias, output_weight, output_bias,
    layer_scale1, norm2_gain, norm2_bias, up_weight, up_bias, down_weight, down_bias, layer_scale2, cotangent,
):
    owners = lax.axis_size("fsdp")
    chips = owners // 2
    _, local_len, width = tokens.shape
    me = lax.axis_index("fsdp")
    core = lax.rem(me, 2)
    place = lax.dynamic_index_in_dim(jnp.asarray(places(owners)), me, keepdims=False)
    moves = [(f * 2 + s, (f - f % 2 + s) * 2 + f % 2) for f in range(owners) for s in range(2) if f % 2 != s]
    twin = [(f, f ^ 1) for f in range(owners)]
    stays = core == lax.axis_index("seq")

    def regroup_moves(values):
        return lax.ppermute(values, ("fsdp", "seq"), moves)

    def regrouped(values):
        return jnp.where(stays, values, regroup_moves(values))

    def to_twin(values):
        return lax.ppermute(values, "fsdp", twin)

    def across(values):
        return lax.ppermute(values, "seq", [(0, 1), (1, 0)])

    vectors = (
        norm1_gain, norm1_bias, query_bias, value_bias, output_bias, layer_scale1, norm2_gain, norm2_bias,
        down_bias, layer_scale2,
    )
    rows = norm1_gain.shape[0]
    hidden = up_weight.shape[1]
    first, rest = pack(place, packed_weight, up_weight, down_weight, output_weight, vectors, up_bias)
    own_pieces = ring_gather(first, chips)
    far_pieces = [to_twin(piece) for piece in own_pieces]
    x = regrouped(tokens.reshape(local_len, width))
    valid_count = regrouped(lengths)
    rest = lax.all_gather(rest, "fsdp", axis=0, tiled=True)
    starts = jnp.stack([core, 1 - core]) * local_len
    valid = jnp.clip(valid_count - starts, 0, local_len).astype(jnp.int32)
    upstream = regrouped(cotangent.reshape(local_len, width))

    far_out, own_part, normed, packed_full, table, up_shift = project(place, x, own_pieces, far_pieces, hidden)
    far_part = to_twin(far_out)
    parts = [own_part, far_part]
    (own_mix, far_mix_out), totals = attention(valid, parts, 352)
    far_mix = to_twin(far_mix_out)
    middle, branch1, normed2 = merge(place, x, own_mix, far_mix, table, rest)

    branch2, delta_normed2, up_mine, up_other, down_mine, down_other, up_sums = mlp(
        place, normed2, upstream, table, rest, up_shift, owners
    )
    up_twin, down_twin = to_twin(up_other), to_twin(down_other)
    output, delta_middle, own_grad, far_grad_out, output_mine, output_other, middle_sums = unmerge(
        place, middle, branch1, branch2, delta_normed2, upstream, own_mix, far_mix, table, rest, owners
    )
    far_grad = to_twin(far_grad_out)
    output_twin = to_twin(output_other)
    ring = RingSum((up_mine, up_twin), (down_mine, down_twin), (output_mine, output_twin))
    output_sent = regroup_moves(output)
    deltas = ()
    grads = [own_grad, far_grad]
    start = 0
    for pairs in split_pairs(width // 2 // LANES):
        sums, _ = ring.sums()
        ring.send(sums)
        after = [*sums, output_sent] if start else sums
        deltas = attention_back(
            valid, parts, [own_mix, far_mix_out], grads, totals, 352, start, pairs, deltas, after
        )
        start += pairs
    own_delta, far_delta_out = deltas
    sums, (far_delta_out,) = ring.sums(carry=[far_delta_out])
    ring.send(sums)
    far_delta = to_twin(far_delta_out)
    grad_x, packed_mine, packed_other, vectors_mine, vectors_other = unproject(
        place, x, delta_middle, table, normed, own_delta, far_delta, packed_full, middle_sums, up_sums, owners, []
    )
    output = jnp.where(stays, output, output_sent).reshape(tokens.shape)
    rest_sum, (grad_x, packed_other, vectors_other) = ring.total(carry=[grad_x, packed_other, vectors_other])
    vectors_twin, packed_twin = to_twin(vectors_other), to_twin(packed_other)
    packed_ring = RingSum((packed_mine, packed_twin), (vectors_mine, vectors_twin))
    grad_x_sent, rest_sent = regroup_moves(grad_x), across(rest_sum)
    for after in ([], [], [grad_x_sent], [rest_sent]):
        packed_ring.send(packed_ring.sums(after)[0])
    grad_tokens = jnp.where(stays, grad_x, grad_x_sent).astype(F32).reshape(tokens.shape)
    each = up_bias.shape[0]
    grad_up, grad_down, grad_output = finish_rest(rest_sum, rest_sent, hidden, each, width)
    first_sum, _ = packed_ring.total()
    grad_packed, *mine = finish_first(place, first_sum, across(first_sum), each)
    return (
        output, grad_tokens, mine[0], mine[1], grad_packed, mine[2], mine[3], grad_output, mine[4], mine[5],
        mine[6], mine[7], grad_up, mine[10], grad_down, mine[8], mine[9],
    )


def pairable(tokens, up_weight):
    owners, chips = lax.axis_size("fsdp"), lax.axis_size("fsdp") // 2
    width, hidden = up_weight.shape[0] * owners, up_weight.shape[1]
    return (
        lax.axis_size("seq") == 2
        and tokens.shape[0] == 1
        and tokens.shape[1] % 16 == 0
        and owners == 2 * chips
        and chips in (4, 8)
        and width % (chips * LANES) == 0
        and hidden % (owners * LANES) == 0
        and H * HD == width
    )


def body(*args):
    chosen = paired_body if pairable(args[0], args[12]) else general_body
    return chosen(*args)


def solution(mesh):
    in_specs = (
        P("fsdp", "seq", None),
        P("fsdp"),
        P("fsdp"),
        P("fsdp"),
        P("fsdp", None),
        P("fsdp"),
        P("fsdp"),
        P("fsdp", None),
        P("fsdp"),
        P("fsdp"),
        P("fsdp"),
        P("fsdp"),
        P("fsdp", None),
        P("fsdp"),
        P("fsdp", None),
        P("fsdp"),
        P("fsdp"),
        P("fsdp", "seq", None),
    )
    out_specs = (
        P("fsdp", "seq", None),
        P("fsdp", "seq", None),
        P("fsdp"),
        P("fsdp"),
        P("fsdp", None),
        P("fsdp"),
        P("fsdp"),
        P("fsdp", None),
        P("fsdp"),
        P("fsdp"),
        P("fsdp"),
        P("fsdp"),
        P("fsdp", None),
        P("fsdp"),
        P("fsdp", None),
        P("fsdp"),
        P("fsdp"),
    )
    return jax.shard_map(body, mesh=mesh, in_specs=in_specs, out_specs=out_specs, check_vma=False)
```

```python
import functools

import jax
import jax.numpy as jnp
import numpy as np
from jax import lax
from jax.experimental import pallas as pl
from jax.experimental.pallas import tpu as pltpu
from jax.sharding import PartitionSpec as P

H = 16
HD = 64


norm_eps = 1e-06


def layer_norm(values, norm_gain, norm_shift):
    center = values - jnp.mean(values, axis=-1, keepdims=True)
    spread = jnp.mean(center * center, axis=-1, keepdims=True)
    return center * lax.rsqrt(spread + norm_eps) * norm_gain + norm_shift


def gelu_exact(values):
    return jax.nn.gelu(values, approximate=False)


def matmul(left, right):
    return jnp.dot(left, right, preferred_element_type=jnp.float32)


def left_outer(left, right):
    return jnp.einsum("ti,tj->ij", left, right, preferred_element_type=jnp.float32)


def right_back(left, right):
    return jnp.einsum("tj,ij->ti", left, right, preferred_element_type=jnp.float32)


def column_sum(values):
    return jnp.sum(values.astype(jnp.float32), axis=0)


def attention_probs(queries, key_rows, valid_count, score_scale):
    scores = score_scale * jnp.einsum(
        "qhd,khd->hqk", queries, key_rows, preferred_element_type=jnp.float32
    )
    key_valid = jnp.arange(key_rows.shape[0]) < valid_count
    scores = jnp.where(key_valid[None, None, :], scores, -jnp.inf)
    return scores


def attend(queries, key_rows, values, valid_count, score_scale):
    scores = attention_probs(queries, key_rows, valid_count, score_scale)
    largest = jnp.max(scores, axis=-1, keepdims=True)
    log_total = largest[..., 0] + jnp.log(jnp.sum(jnp.exp(scores - largest), axis=-1))
    attention = jnp.exp(scores - log_total[..., None]).astype(jnp.bfloat16)
    mixture = jnp.einsum("hqk,khd->qhd", attention, values, preferred_element_type=jnp.float32)
    return (mixture.astype(jnp.bfloat16), log_total)


def attend_back(queries, key_rows, values, valid_count, score_scale, log_total, grad_mixture):
    scores = attention_probs(queries, key_rows, valid_count, score_scale)
    probs = jnp.exp(scores - log_total[..., None])
    grad_values = jnp.einsum(
        "hqk,qhd->khd", probs.astype(jnp.bfloat16), grad_mixture, preferred_element_type=jnp.float32
    )
    grad_probs = jnp.einsum(
        "qhd,khd->hqk", grad_mixture, values, preferred_element_type=jnp.float32
    )
    inner_sum = jnp.sum(probs * grad_probs, axis=-1, keepdims=True)
    grad_scores = (probs * (grad_probs - inner_sum)).astype(jnp.bfloat16)
    grad_queries = score_scale * jnp.einsum(
        "hqk,khd->qhd", grad_scores, key_rows, preferred_element_type=jnp.float32
    )
    grad_keys = score_scale * jnp.einsum(
        "hqk,qhd->khd", grad_scores, queries, preferred_element_type=jnp.float32
    )
    return (grad_queries, grad_keys, grad_values)


def general_body(
    tokens,
    lengths,
    norm1_gain,
    norm1_bias,
    packed_weight,
    query_bias,
    value_bias,
    output_weight,
    output_bias,
    layer_scale1,
    norm2_gain,
    norm2_bias,
    up_weight,
    up_bias,
    down_weight,
    down_bias,
    layer_scale2,
    cotangent,
):
    gathered = (
        lax.all_gather(norm1_gain, "fsdp", axis=0, tiled=True),
        lax.all_gather(norm1_bias, "fsdp", axis=0, tiled=True),
        lax.all_gather(packed_weight, "fsdp", axis=0, tiled=True),
        lax.all_gather(query_bias, "fsdp", axis=0, tiled=True),
        lax.all_gather(value_bias, "fsdp", axis=0, tiled=True),
        lax.all_gather(output_weight, "fsdp", axis=0, tiled=True),
        lax.all_gather(output_bias, "fsdp", axis=0, tiled=True),
        lax.all_gather(layer_scale1, "fsdp", axis=0, tiled=True),
        lax.all_gather(norm2_gain, "fsdp", axis=0, tiled=True),
        lax.all_gather(norm2_bias, "fsdp", axis=0, tiled=True),
        lax.all_gather(up_weight, "fsdp", axis=0, tiled=True),
        lax.all_gather(up_bias, "fsdp", axis=0, tiled=True),
        lax.all_gather(down_weight, "fsdp", axis=0, tiled=True),
        lax.all_gather(down_bias, "fsdp", axis=0, tiled=True),
        lax.all_gather(layer_scale2, "fsdp", axis=0, tiled=True),
    )
    (
        gain_one,
        shift_one,
        packed_full,
        query_shift,
        value_shift,
        output_full,
        output_shift,
        scale_one,
        gain_two,
        shift_two,
        up_full,
        up_shift,
        down_full,
        down_shift,
        scale_two,
    ) = gathered
    gain_one = gain_one.astype(jnp.float32)
    shift_one = shift_one.astype(jnp.float32)
    query_shift = query_shift.astype(jnp.float32)
    value_shift = value_shift.astype(jnp.float32)
    output_shift = output_shift.astype(jnp.float32)
    scale_one = scale_one.astype(jnp.float32)
    gain_two = gain_two.astype(jnp.float32)
    shift_two = shift_two.astype(jnp.float32)
    up_shift = up_shift.astype(jnp.float32)
    down_shift = down_shift.astype(jnp.float32)
    scale_two = scale_two.astype(jnp.float32)
    groups = lax.axis_size("seq")
    images, local_len, model_width = tokens.shape
    seq_len = local_len * groups
    per_group = H // groups
    score_scale = HD ** (-0.5)
    token_rows = tokens.astype(jnp.float32).reshape(images * local_len, model_width)
    normed = layer_norm(token_rows, gain_one, shift_one).astype(jnp.bfloat16)
    packed_shift = jnp.concatenate([query_shift, jnp.zeros_like(query_shift), value_shift])
    packed = (matmul(normed, packed_full) + packed_shift).astype(jnp.bfloat16)
    packed = packed.reshape(images, local_len, 3, groups, per_group * HD)
    spread = lax.all_to_all(packed, "seq", split_axis=3, concat_axis=1, tiled=True)
    spread = spread.reshape(images, seq_len, 3, per_group, HD)

    def forward_image(per_image):
        image_block, valid_count = per_image
        return attend(
            image_block[:, 0], image_block[:, 1], image_block[:, 2], valid_count, score_scale
        )

    mixture, log_total = lax.map(forward_image, (spread, lengths))
    mixture = mixture.reshape(images, seq_len, 1, per_group * HD)
    mixture_rows = lax.all_to_all(mixture, "seq", split_axis=1, concat_axis=2, tiled=True).reshape(
        images * local_len, model_width
    )
    branch_one = matmul(mixture_rows, output_full) + output_shift
    middle = token_rows + scale_one * branch_one
    normed_two = layer_norm(middle, gain_two, shift_two).astype(jnp.bfloat16)
    hidden = matmul(normed_two, up_full) + up_shift
    active = gelu_exact(hidden).astype(jnp.bfloat16)
    branch_two = matmul(active, down_full) + down_shift
    output = (middle + scale_two * branch_two).astype(jnp.bfloat16).reshape(tokens.shape)
    upstream = cotangent.astype(jnp.float32).reshape(images * local_len, model_width)
    grad_scale_two = jnp.sum(upstream * branch_two, axis=0)
    delta_two = (scale_two * upstream).astype(jnp.bfloat16)
    grad_down_shift = column_sum(delta_two)
    grad_down = left_outer(active, delta_two)
    grad_active = right_back(delta_two, down_full)
    _, gelu_pull = jax.vjp(gelu_exact, hidden)
    delta_hidden = gelu_pull(grad_active)[0].astype(jnp.bfloat16)
    grad_up_shift = column_sum(delta_hidden)
    grad_up = left_outer(normed_two, delta_hidden)
    delta_normed_two = right_back(delta_hidden, up_full)
    _, norm_pull_two = jax.vjp(layer_norm, middle, gain_two, shift_two)
    grad_middle_norm, grad_gain_two, grad_shift_two = norm_pull_two(delta_normed_two)
    delta_middle = upstream + grad_middle_norm
    grad_scale_one = jnp.sum(delta_middle * branch_one, axis=0)
    delta_one = (scale_one * delta_middle).astype(jnp.bfloat16)
    grad_output_shift = column_sum(delta_one)
    grad_output = left_outer(mixture_rows, delta_one)
    delta_mixture = right_back(delta_one, output_full).astype(jnp.bfloat16)
    delta_mixture = delta_mixture.reshape(images, local_len, groups, per_group * HD)
    grad_spread = lax.all_to_all(delta_mixture, "seq", split_axis=2, concat_axis=1, tiled=True)
    grad_spread = grad_spread.reshape(images, seq_len, per_group, HD)

    def backward_image(per_image):
        image_block, valid_count, image_total, image_grad = per_image
        grad_queries, grad_keys, grad_values = attend_back(
            image_block[:, 0],
            image_block[:, 1],
            image_block[:, 2],
            valid_count,
            score_scale,
            image_total,
            image_grad,
        )
        return jnp.stack([grad_queries, grad_keys, grad_values], axis=1).astype(jnp.bfloat16)

    delta_packed = lax.map(backward_image, (spread, lengths, log_total, grad_spread))
    delta_packed = delta_packed.reshape(images, seq_len, 3, 1, per_group * HD)
    delta_back = lax.all_to_all(delta_packed, "seq", split_axis=1, concat_axis=3, tiled=True)
    delta_back = delta_back.reshape(images * local_len, 3 * model_width)
    grad_query_shift = column_sum(delta_back[:, :model_width])
    grad_value_shift = column_sum(delta_back[:, 2 * model_width :])
    grad_packed = left_outer(normed, delta_back)
    delta_normed = right_back(delta_back, packed_full)
    _, norm_pull_one = jax.vjp(layer_norm, token_rows, gain_one, shift_one)
    grad_rows_norm, grad_gain_one, grad_shift_one = norm_pull_one(delta_normed)
    grad_tokens = (delta_middle + grad_rows_norm).reshape(tokens.shape)
    local_grads = (
        grad_gain_one,
        grad_shift_one,
        grad_packed,
        grad_query_shift,
        grad_value_shift,
        grad_output,
        grad_output_shift,
        grad_scale_one,
        grad_gain_two,
        grad_shift_two,
        grad_up,
        grad_up_shift,
        grad_down,
        grad_down_shift,
        grad_scale_two,
    )
    owned_grads = (
        lax.psum_scatter(
            local_grads[0].astype(jnp.bfloat16), "fsdp", scatter_dimension=0, tiled=True
        ).astype(jnp.float32),
        lax.psum_scatter(
            local_grads[1].astype(jnp.bfloat16), "fsdp", scatter_dimension=0, tiled=True
        ).astype(jnp.float32),
        lax.psum_scatter(
            local_grads[2].astype(jnp.bfloat16), "fsdp", scatter_dimension=0, tiled=True
        ).astype(jnp.float32),
        lax.psum_scatter(
            local_grads[3].astype(jnp.bfloat16), "fsdp", scatter_dimension=0, tiled=True
        ).astype(jnp.float32),
        lax.psum_scatter(
            local_grads[4].astype(jnp.bfloat16), "fsdp", scatter_dimension=0, tiled=True
        ).astype(jnp.float32),
        lax.psum_scatter(
            local_grads[5].astype(jnp.bfloat16), "fsdp", scatter_dimension=0, tiled=True
        ).astype(jnp.float32),
        lax.psum_scatter(
            local_grads[6].astype(jnp.bfloat16), "fsdp", scatter_dimension=0, tiled=True
        ).astype(jnp.float32),
        lax.psum_scatter(
            local_grads[7].astype(jnp.bfloat16), "fsdp", scatter_dimension=0, tiled=True
        ).astype(jnp.float32),
        lax.psum_scatter(
            local_grads[8].astype(jnp.bfloat16), "fsdp", scatter_dimension=0, tiled=True
        ).astype(jnp.float32),
        lax.psum_scatter(
            local_grads[9].astype(jnp.bfloat16), "fsdp", scatter_dimension=0, tiled=True
        ).astype(jnp.float32),
        lax.psum_scatter(
            local_grads[10].astype(jnp.bfloat16), "fsdp", scatter_dimension=0, tiled=True
        ).astype(jnp.float32),
        lax.psum_scatter(
            local_grads[11].astype(jnp.bfloat16), "fsdp", scatter_dimension=0, tiled=True
        ).astype(jnp.float32),
        lax.psum_scatter(
            local_grads[12].astype(jnp.bfloat16), "fsdp", scatter_dimension=0, tiled=True
        ).astype(jnp.float32),
        lax.psum_scatter(
            local_grads[13].astype(jnp.bfloat16), "fsdp", scatter_dimension=0, tiled=True
        ).astype(jnp.float32),
        lax.psum_scatter(
            local_grads[14].astype(jnp.bfloat16), "fsdp", scatter_dimension=0, tiled=True
        ).astype(jnp.float32),
    )
    owned_grads = (
        lax.psum(owned_grads[0].astype(jnp.bfloat16), "seq").astype(jnp.float32),
        lax.psum(owned_grads[1].astype(jnp.bfloat16), "seq").astype(jnp.float32),
        lax.psum(owned_grads[2].astype(jnp.bfloat16), "seq").astype(jnp.float32),
        lax.psum(owned_grads[3].astype(jnp.bfloat16), "seq").astype(jnp.float32),
        lax.psum(owned_grads[4].astype(jnp.bfloat16), "seq").astype(jnp.float32),
        lax.psum(owned_grads[5].astype(jnp.bfloat16), "seq").astype(jnp.float32),
        lax.psum(owned_grads[6].astype(jnp.bfloat16), "seq").astype(jnp.float32),
        lax.psum(owned_grads[7].astype(jnp.bfloat16), "seq").astype(jnp.float32),
        lax.psum(owned_grads[8].astype(jnp.bfloat16), "seq").astype(jnp.float32),
        lax.psum(owned_grads[9].astype(jnp.bfloat16), "seq").astype(jnp.float32),
        lax.psum(owned_grads[10].astype(jnp.bfloat16), "seq").astype(jnp.float32),
        lax.psum(owned_grads[11].astype(jnp.bfloat16), "seq").astype(jnp.float32),
        lax.psum(owned_grads[12].astype(jnp.bfloat16), "seq").astype(jnp.float32),
        lax.psum(owned_grads[13].astype(jnp.bfloat16), "seq").astype(jnp.float32),
        lax.psum(owned_grads[14].astype(jnp.bfloat16), "seq").astype(jnp.float32),
    )
    return (output, grad_tokens) + tuple(owned_grads)


BF16 = jnp.bfloat16
F32 = jnp.float32
NT = (((1,), (1,)), ((), ()))
NN = (((1,), (0,)), ((), ()))
MASKED = -1e30
LANES = 128
VMEM_LIMIT = 60 * 2**20

GAIN1, SHIFT1, QUERY, VALUE, OUT_SHIFT, SCALE1, GAIN2, SHIFT2, DOWN_SHIFT, SCALE2 = range(10)


def dot(left, right, dims=NN):
    return lax.dot_general(left, right, dims, preferred_element_type=F32)


def turned(values):
    return values.T


def lane_ids(rows):
    return lax.broadcasted_iota(jnp.int32, (rows, LANES), 1)


def split3(values):
    high = values.astype(BF16).astype(F32)
    rest = values - high
    mid = rest.astype(BF16).astype(F32)
    return high, mid, rest - mid


LONG, SHORT = 16.0, 1 / 64


def params_for(flops, nbytes, transcendentals=0, weight=1.0):
    flops, nbytes, transcendentals = (int(weight * count) for count in (flops, nbytes, transcendentals))
    return dict(
        compiler_params=pltpu.CompilerParams(vmem_limit_bytes=VMEM_LIMIT),
        cost_estimate=pl.CostEstimate(
            flops=flops, bytes_accessed=nbytes, transcendentals=transcendentals
        ),
    )


def whole(shape):
    return pl.BlockSpec(shape, lambda *_: (0,) * len(shape))


def normalize(values, gain, shift):
    center = values - jnp.mean(values, axis=-1, keepdims=True)
    spread = jnp.mean(center * center, axis=-1, keepdims=True)
    return center * lax.rsqrt(spread + norm_eps) * gain + shift


def normalize_back(values, gain, delta):
    center = values - jnp.mean(values, axis=-1, keepdims=True)
    inverse = lax.rsqrt(jnp.mean(center * center, axis=-1, keepdims=True) + norm_eps)
    unit = center * inverse
    scaled = delta * gain
    mean_scaled = jnp.mean(scaled, axis=-1, keepdims=True)
    mean_unit = jnp.mean(scaled * unit, axis=-1, keepdims=True)
    return inverse * (scaled - mean_scaled - unit * mean_unit), delta * unit


def total_rows(values):
    return jnp.sum(values, axis=0, keepdims=True)


VECTORS = 10


def pack_kernel(place, weight_ref, up_ref, down_ref, output_ref, *refs):
    vector_refs, shift_ref = refs[:VECTORS], refs[VECTORS]
    first_ref, rest_ref = refs[VECTORS + 1 :]
    rows, width = weight_ref.shape
    first_ref[:, :width] = weight_ref[...]
    first_ref[:, width:] = jnp.zeros((rows, LANES), BF16)
    for i, ref in enumerate(vector_refs):
        values = ref[...].astype(F32).reshape(1, -1)
        empty = jnp.zeros_like(values)
        first, second = jnp.concatenate([values, empty], 1), jnp.concatenate([empty, values], 1)
        first_ref[i : i + 1, width:] = jnp.where(place[CORE] == 0, first, second).astype(BF16)
    shift = shift_ref[...].astype(F32).reshape(-1, LANES)
    first_ref[VECTORS : VECTORS + shift.shape[0], width:] = shift.astype(BF16)
    at = 0
    for ref in (up_ref, down_ref, output_ref):
        for g in range(ref.shape[0] // rows):
            rest_ref[:, at : at + ref.shape[1]] = ref[g * rows : (g + 1) * rows, :]
            at += ref.shape[1]


def pack(place, weight, up, down, output, vectors, up_shift):
    in_vmem = pl.BlockSpec(memory_space=pltpu.VMEM)
    rows, width = weight.shape
    others = (up.size + down.size + output.size) // rows
    return pl.pallas_call(
        pack_kernel,
        in_specs=[pl.BlockSpec(memory_space=pltpu.SMEM)] + [in_vmem] * (VECTORS + 5),
        out_specs=[in_vmem, in_vmem],
        out_shape=[
            jax.ShapeDtypeStruct((rows, width + LANES), BF16),
            jax.ShapeDtypeStruct((rows, others), BF16),
        ],
        name="pack",
        **params_for(0, 4 * rows * (width + others)),
    )(place, weight, up, down, output, *vectors, up_shift)


CORE, CHIPS = 6, 7


def project_kernel(place, x_ref, *refs, chips):
    own_refs, far_refs, own_vectors, far_vectors = (refs[chips * i : chips * (i + 1)] for i in range(4))
    far_out_ref, own_ref, normed_ref, weight_ref, table_ref, up_ref = refs[4 * chips :]
    step = pl.program_id(0)
    rows = own_refs[0].shape[0]
    core = place[CORE]

    @pl.when(step == 0)
    def _():
        vector = lax.broadcasted_iota(jnp.int32, (table_ref.shape[0], LANES), 0) < VECTORS
        each = up_ref.shape[1] // (2 * chips)
        for k in range(chips):
            chip = place[CHIPS + k]
            own = own_vectors[k][...].astype(F32)
            far = far_vectors[k][...].astype(F32)
            at = pl.ds(pl.multiple_of(chip * LANES, LANES), LANES)
            table_ref[:, at] = jnp.where(vector, own + far, 0.0)
            for part, side in ((own, core), (far, 1 - core)):
                for r in range(each // LANES):
                    at = pl.multiple_of((2 * chip + side) * each + r * LANES, LANES)
                    up_ref[:, pl.ds(at, LANES)] = part[VECTORS + r : VECTORS + r + 1, :]
        normed_ref[...] = normalize(
            x_ref[...].astype(F32), table_ref[GAIN1 : GAIN1 + 1, :], table_ref[SHIFT1 : SHIFT1 + 1, :]
        ).astype(BF16)

    for k in range(chips):
        start = 2 * place[CHIPS + k]
        weight_ref[pl.ds(pl.multiple_of((start + core) * rows, rows), rows), :] = own_refs[k][...]
        weight_ref[pl.ds(pl.multiple_of((start + 1 - core) * rows, rows), rows), :] = far_refs[k][...]
    shift = jnp.where(
        step == 0,
        table_ref[QUERY : QUERY + 1, :],
        jnp.where(step == 2, table_ref[VALUE : VALUE + 1, :], 0.0),
    )
    result = (dot(normed_ref[...], weight_ref[...]) + shift).astype(BF16)
    half = result.shape[1] // 2
    low, high = result[:, :half], result[:, half:]
    own_ref[0] = jnp.where(core == 0, low, high)
    far_out_ref[0] = jnp.where(core == 0, high, low)


def project(place, x, own_pieces, far_pieces, hidden):
    chips = len(own_pieces)
    tokens, width = x.shape
    rows = own_pieces[0].shape[0]
    kind = pl.BlockSpec((1, tokens, width // 2), lambda j, _: (j, 0, 0))
    return pl.pallas_call(
        functools.partial(project_kernel, chips=chips),
        grid_spec=pltpu.PrefetchScalarGridSpec(
            num_scalar_prefetch=1,
            grid=(3,),
            in_specs=[whole((tokens, width))]
            + [pl.BlockSpec((rows, width), lambda j, _: (0, j))] * 2 * chips
            + [pl.BlockSpec((16, LANES), lambda j, _: (0, 3 * width // LANES))] * 2 * chips,
            out_specs=[
                kind,
                kind,
                whole((tokens, width)),
                pl.BlockSpec((width, width), lambda j, _: (0, j)),
                whole((16, width)),
                whole((1, hidden)),
            ],
        ),
        out_shape=[
            jax.ShapeDtypeStruct((3, tokens, width // 2), BF16),
            jax.ShapeDtypeStruct((3, tokens, width // 2), BF16),
            jax.ShapeDtypeStruct((tokens, width), BF16),
            jax.ShapeDtypeStruct((width, 3 * width), BF16),
            jax.ShapeDtypeStruct((16, width), F32),
            jax.ShapeDtypeStruct((1, hidden), F32),
        ],
        name="project",
        **params_for(6 * tokens * width * width, 12 * tokens * width + 12 * width * width),
    )(place, x, *own_pieces, *far_pieces, *own_pieces, *far_pieces)


def padded_len(count, block):
    return -(-count // block) * block


def attend_kernel(valid, *refs, pieces, block, scale):
    in_refs, out_refs = refs[:pieces], refs[pieces : 2 * pieces]
    total_refs = refs[2 * pieces : 3 * pieces]
    keys, values, queries, mixed, totals = refs[3 * pieces :]
    pair = pl.program_id(0)
    size = in_refs[0].shape[1]
    count, padded = pieces * size, keys.shape[0]
    lane = lane_ids(size)
    row = lax.broadcasted_iota(jnp.int32, (size, LANES), 0)
    for i in range(pieces):
        at = pl.ds(i * size, size)
        keys[at, :LANES] = in_refs[i][1]
        keys[at, LANES:] = jnp.where((lane == 0) & (row >= valid[i]), MASKED, 0.0).astype(BF16)
        values[at, :LANES] = in_refs[i][2]
        values[at, LANES:] = jnp.where(lane == 0, 1.0, 0.0).astype(BF16)
        for j in range(2):
            mine = lane // HD == j
            queries[j, at, :LANES] = jnp.where(mine, in_refs[i][0].astype(F32) * scale, 0.0).astype(BF16)
            queries[j, at, LANES:] = jnp.where(lane == 0, 1.0, 0.0).astype(BF16)
    if padded > count:
        rest = pl.ds(count, padded - count)
        rest_lane = lane_ids(padded - count)
        keys[rest, :LANES] = jnp.zeros((padded - count, LANES), BF16)
        keys[rest, LANES:] = jnp.where(rest_lane == 0, MASKED, 0.0).astype(BF16)
        values[rest, :] = jnp.zeros((padded - count, 2 * LANES), BF16)
        for j in range(2):
            queries[j, rest, :] = jnp.zeros((padded - count, 2 * LANES), BF16)

    @pl.when(pair == 0)
    def _():
        for i in range(pieces):
            total_refs[i][...] = jnp.zeros_like(total_refs[i])

    block_lane = lane_ids(block)
    for b in range(padded // block):
        at = pl.ds(b * block, block)
        results, logs = [], 0.0
        for j in range(2):
            scores = dot(queries[j, at, :], keys[...], NT)
            largest = jnp.max(scores, axis=1, keepdims=True)
            weights = jnp.exp(scores - largest).astype(BF16)
            result = dot(weights, values[...])
            total = result[:, LANES : LANES + 1]
            results.append(result[:, :LANES] * (1.0 / total))
            logs += jnp.where(block_lane == 2 * pair + j, largest + jnp.log(total), 0.0)
        mixed[at, :] = jnp.where(block_lane < HD, results[0], results[1])
        totals[at, :] = logs
    for i in range(pieces):
        at = pl.ds(i * size, size)
        out_refs[i][...] = mixed[at, :].astype(BF16)
        total_refs[i][...] += totals[at, :]


def attention(valid, parts, block):
    pieces = len(parts)
    _, size, width = parts[0].shape
    pairs = width // LANES
    padded = padded_len(pieces * size, block)
    outs = pl.pallas_call(
        functools.partial(attend_kernel, pieces=pieces, block=block, scale=HD**-0.5),
        grid_spec=pltpu.PrefetchScalarGridSpec(
            num_scalar_prefetch=1,
            grid=(pairs,),
            in_specs=[pl.BlockSpec((3, size, LANES), lambda h, _: (0, 0, h))] * pieces,
            out_specs=[pl.BlockSpec((size, LANES), lambda h, _: (0, h))] * pieces
            + [whole((size, LANES))] * pieces,
            scratch_shapes=[
                pltpu.VMEM((padded, 2 * LANES), BF16),
                pltpu.VMEM((padded, 2 * LANES), BF16),
                pltpu.VMEM((2, padded, 2 * LANES), BF16),
                pltpu.VMEM((padded, LANES), F32),
                pltpu.VMEM((padded, LANES), F32),
            ],
        ),
        out_shape=[jax.ShapeDtypeStruct((size, width), BF16)] * pieces
        + [jax.ShapeDtypeStruct((size, LANES), F32)] * pieces,
        name="attend",
        **params_for(16 * pairs * LANES * padded * padded, 8 * size * width * pieces, pairs * 2 * padded * padded),
    )(valid, *parts)
    return outs[:pieces], outs[pieces:]


def attend_back_kernel(valid, *refs, pieces, block, scale, first):
    in_refs, mix_refs = refs[:pieces], refs[pieces : 2 * pieces]
    grad_refs, total_refs = refs[2 * pieces : 3 * pieces], refs[3 * pieces : 4 * pieces]
    out_refs = refs[-9 - pieces : -9]
    keys, values, queries, grads, queries_t, grads_t, dq, dk_t, dv_t = refs[-9:]
    pair = first + pl.program_id(0)
    size = in_refs[0].shape[1]
    count, padded = pieces * size, keys.shape[0]
    blocks = padded // block
    lane = lane_ids(size)
    row = lax.broadcasted_iota(jnp.int32, (size, LANES), 0)
    for i in range(pieces):
        at = pl.ds(i * size, size)
        keys[at, :LANES] = in_refs[i][1]
        keys[at, LANES:] = jnp.where(
            lane == 0, jnp.where(row >= valid[i], MASKED, 0.0), jnp.where(lane < 4, 1.0, 0.0)
        ).astype(BF16)
        values[at, :LANES] = in_refs[i][2]
        values[at, LANES:] = jnp.where((lane > 0) & (lane < 4), 1.0, 0.0).astype(BF16)
        queries[0, at, :LANES] = in_refs[i][0]
        grads[0, at, :LANES] = grad_refs[i][...]
    if padded > count:
        left = padded - count
        rest = pl.ds(count, left)
        keys[rest, :LANES] = jnp.zeros((left, LANES), BF16)
        keys[rest, LANES:] = jnp.where(lane_ids(left) == 0, MASKED, 0.0).astype(BF16)
        values[rest, :] = jnp.zeros((left, 2 * LANES), BF16)
        for j in range(2):
            queries[j, rest, :] = jnp.zeros((left, 2 * LANES), BF16)
            grads[j, rest, :] = jnp.zeros((left, 2 * LANES), BF16)
    for b in range(blocks):
        at = pl.ds(b * block, block)
        queries_t[b] = (queries[0, at, :LANES].astype(F32) * scale).T.astype(BF16)
        grads_t[b] = turned(grads[0, at, :LANES])
    for j in range(2):
        mine = lane // HD == j
        for i in range(pieces):
            at = pl.ds(i * size, size)
            grad = jnp.where(mine, grad_refs[i][...].astype(F32), 0.0)
            queries[j, at, :LANES] = jnp.where(mine, in_refs[i][0].astype(F32) * scale, 0.0).astype(BF16)
            grads[j, at, :LANES] = grad.astype(BF16)
            log_total = jnp.sum(
                jnp.where(lane == 2 * pair + j, total_refs[i][...], 0.0), axis=1, keepdims=True
            )
            high, mid, low = split3(-log_total)
            queries[j, at, LANES:] = jnp.where(
                lane == 0,
                1.0,
                jnp.where(lane == 1, high, jnp.where(lane == 2, mid, jnp.where(lane == 3, low, 0.0))),
            ).astype(BF16)
            inner = jnp.sum(grad * mix_refs[i][...].astype(F32), axis=1, keepdims=True)
            high, mid, low = split3(-inner)
            grads[j, at, LANES:] = jnp.where(
                lane == 1, high, jnp.where(lane == 2, mid, jnp.where(lane == 3, low, 0.0))
            ).astype(BF16)
    dk_t[...] = jnp.zeros_like(dk_t)
    dv_t[...] = jnp.zeros_like(dv_t)
    block_lane = lane_ids(block)
    for b in range(blocks):
        at = pl.ds(b * block, block)
        results = []
        for j in range(2):
            mine = pl.ds(j * HD, HD)
            probs = jnp.exp(dot(queries[j, at, :], keys[...], NT))
            grad_scores = (probs * dot(grads[j, at, :], values[...], NT)).astype(BF16)
            results.append(dot(grad_scores, keys[:, :LANES]) * scale)
            dv_t[mine, :] += dot(grads_t[b, mine, :], probs.astype(BF16))
            dk_t[mine, :] += dot(queries_t[b, mine, :], grad_scores)
        dq[at, :] = jnp.where(block_lane < HD, results[0], results[1])
    dk, dv = dk_t[...].T, dv_t[...].T
    for i in range(pieces):
        at = slice(i * size, (i + 1) * size)
        out_refs[i][0] = dq[at, :].astype(BF16)
        out_refs[i][1] = dk[at, :].astype(BF16)
        out_refs[i][2] = dv[at, :].astype(BF16)


def attention_back(valid, parts, mixtures, grads, totals, block, first, pairs, into, after):
    pieces = len(parts)
    _, size, width = parts[0].shape
    padded = padded_len(pieces * size, block)
    triple = pl.BlockSpec((3, size, LANES), lambda h, _: (0, 0, first + h))
    single = pl.BlockSpec((size, LANES), lambda h, _: (0, first + h))
    in_specs = [triple] * pieces + [single] * 2 * pieces + [whole((size, LANES))] * pieces
    aliases = {1 + len(in_specs) + i: i for i in range(len(into))}
    return pl.pallas_call(
        functools.partial(attend_back_kernel, pieces=pieces, block=block, scale=HD**-0.5, first=first),
        grid_spec=pltpu.PrefetchScalarGridSpec(
            num_scalar_prefetch=1,
            grid=(pairs,),
            in_specs=in_specs + [pl.BlockSpec(memory_space=pl.ANY)] * (len(into) + len(after)),
            out_specs=[triple] * pieces,
            scratch_shapes=[
                pltpu.VMEM((padded, 2 * LANES), BF16),
                pltpu.VMEM((padded, 2 * LANES), BF16),
                pltpu.VMEM((2, padded, 2 * LANES), BF16),
                pltpu.VMEM((2, padded, 2 * LANES), BF16),
                pltpu.VMEM((padded // block, LANES, block), BF16),
                pltpu.VMEM((padded // block, LANES, block), BF16),
                pltpu.VMEM((padded, LANES), F32),
                pltpu.VMEM((LANES, padded), F32),
                pltpu.VMEM((LANES, padded), F32),
            ],
        ),
        out_shape=[jax.ShapeDtypeStruct((3, size, width), BF16)] * pieces,
        input_output_aliases=aliases,
        name="attend_back",
        **params_for(30 * pairs * LANES * padded * padded, 16 * size * LANES * pairs * pieces, pairs * 2 * padded * padded, weight=LONG),
    )(valid, *parts, *mixtures, *grads, *totals, *into, *after)


def merge_kernel(place, x_ref, own_ref, far_ref, table, own_w, far_w, middle_ref, branch_ref, normed_ref):
    branch = dot(own_ref[...], own_w[...]) + dot(far_ref[...], far_w[...])
    branch += table[OUT_SHIFT : OUT_SHIFT + 1, :]
    middle = x_ref[...].astype(F32) + table[SCALE1 : SCALE1 + 1, :] * branch
    middle_ref[...] = middle
    branch_ref[...] = branch
    normed_ref[...] = normalize(
        middle, table[GAIN2 : GAIN2 + 1, :], table[SHIFT2 : SHIFT2 + 1, :]
    ).astype(BF16)


ROWS = 352


def row_steps(tokens):
    return -(-tokens // ROWS)


def merge(place, x, own, far, table, rest):
    tokens, width = x.shape
    half = width // 2
    wide = pl.BlockSpec((ROWS, width), lambda i, _: (i, 0))
    narrow = pl.BlockSpec((ROWS, half), lambda i, _: (i, 0))
    return pl.pallas_call(
        merge_kernel,
        grid_spec=pltpu.PrefetchScalarGridSpec(
            num_scalar_prefetch=1,
            grid=(row_steps(tokens),),
            in_specs=[
                wide,
                narrow,
                narrow,
                whole(table.shape),
                pl.BlockSpec((half, width), lambda i, place: (place[CORE], rest.shape[1] // width - 1)),
                pl.BlockSpec((half, width), lambda i, place: (1 - place[CORE], rest.shape[1] // width - 1)),
            ],
            out_specs=[wide, wide, wide],
        ),
        out_shape=[
            jax.ShapeDtypeStruct((tokens, width), F32),
            jax.ShapeDtypeStruct((tokens, width), F32),
            jax.ShapeDtypeStruct((tokens, width), BF16),
        ],
        name="merge",
        **params_for(2 * tokens * width * width, 14 * tokens * width + 2 * width * width),
    )(place, x, own, far, table, rest, rest)


def gelu_and_slope(values):
    size = jnp.abs(values) * 0.7071067811865476
    t = 1.0 / (1.0 + 0.3275911 * size)
    bell = jnp.exp(-0.5 * (values * values))
    poly = t * (0.254829592 + t * (-0.284496736 + t * (1.421413741 + t * (-1.453152027 + t * 1.061405429))))
    tail = 0.5 * poly * bell
    phi = jnp.where(values < 0, tail, 1.0 - tail)
    return values * phi, phi + values * bell * 0.3989422804014327


def ungroup(grouped_ref, down):
    width = down.shape[1]
    groups = grouped_ref.shape[1] // width
    each = grouped_ref.shape[0] // 2
    for device in range(2):
        for g in range(groups):
            at = (device * groups + g) * each
            down[at : at + each, :] = grouped_ref[device * each : (device + 1) * each, g * width : (g + 1) * width]


def scaled_upstream(cotangent_ref, table):
    return (cotangent_ref[...].astype(F32) * table[SCALE2 : SCALE2 + 1, :]).astype(BF16)


def place_turned(place, block, target, k, chips):
    half = block.shape[1] // 2
    turned_block = block.T
    first, second = turned_block[:half], turned_block[half:]
    target[k * half : (k + 1) * half, :] = jnp.where(place[CORE] == 0, first, second)
    target[(chips + k) * half : (chips + k + 1) * half, :] = jnp.where(place[CORE] == 0, second, first)


def fill_turned(place, source_ref, target, chips):
    wide = source_ref.shape[1] // chips
    for k in range(chips):
        at = pl.ds(pl.multiple_of(place[CHIPS + k] * wide, wide), wide)
        place_turned(place, source_ref[:, at], target, k, chips)


def split_rows(grad, mine_ref, other_ref):
    chips, rows, _ = mine_ref.shape
    for k in range(chips):
        mine_ref[k] = grad[k * rows : (k + 1) * rows, :]
        other_ref[k] = grad[(chips + k) * rows : (chips + k + 1) * rows, :]


def group(grad, out_ref):
    rows, columns = out_ref.shape[1], grad.shape[1]
    for g in range(grad.shape[0] // rows):
        out_ref[0, :, g * columns : (g + 1) * columns] = grad[g * rows : (g + 1) * rows, :]


def mlp_kernel(
    place, normed_ref, cotangent_ref, table, up_ref, shift_ref, grouped_ref,
    branch_ref, delta_ref, up_mine_ref, up_other_ref, down_mine_ref, down_other_ref, grad_shift_ref,
    upstream, upstream_t, normed_t, down,
    *, chips,
):
    @pl.when(pl.program_id(0) == 0)
    def _():
        scaled = (cotangent_ref[...].astype(F32) * table[SCALE2 : SCALE2 + 1, :]).astype(BF16)
        upstream[...] = scaled
        upstream_t[...] = turned(scaled)
        fill_turned(place, normed_ref, normed_t, chips)
        branch_ref[...] = jnp.zeros_like(branch_ref)
        delta_ref[...] = jnp.zeros_like(delta_ref)

    ungroup(grouped_ref, down)
    hidden = dot(normed_ref[...], up_ref[...]) + shift_ref[...]
    grad_active = dot(upstream[...], down[...], NT)
    active, slope = gelu_and_slope(hidden)
    active = active.astype(BF16)
    delta_hidden = (grad_active * slope).astype(BF16)
    branch_ref[...] += dot(active, down[...])
    delta_ref[...] += dot(delta_hidden, up_ref[...], NT)
    split_rows(dot(normed_t[...], delta_hidden).astype(BF16), up_mine_ref, up_other_ref)
    grad_down = dot(upstream_t[...], active)
    each = grad_down.shape[1] // 2
    first, second = grad_down[:, :each], grad_down[:, each:]
    group(jnp.where(place[CORE] == 0, first, second).astype(BF16), down_mine_ref)
    group(jnp.where(place[CORE] == 0, second, first).astype(BF16), down_other_ref)
    grad_shift_ref[...] = total_rows(delta_hidden.astype(F32))


def mlp(place, normed, cotangent, table, rest, up_shift, owners):
    tokens, width = normed.shape
    hidden = up_shift.shape[1]
    rows = rest.shape[0] // owners
    chips = owners // 2
    block = hidden // chips
    up_out = pl.BlockSpec((chips, rows, block), lambda j, place: (0, 0, place[CHIPS + j]))
    down_out = pl.BlockSpec((1, rows, hidden), lambda j, _: (j, 0, 0))
    sent = jax.ShapeDtypeStruct((chips, rows, hidden), BF16)
    return pl.pallas_call(
        functools.partial(mlp_kernel, chips=chips),
        grid_spec=pltpu.PrefetchScalarGridSpec(
            num_scalar_prefetch=1,
            grid=(chips,),
            in_specs=[
                whole((tokens, width)),
                whole((tokens, width)),
                whole(table.shape),
                pl.BlockSpec((width, block), lambda j, place: (0, place[CHIPS + j])),
                pl.BlockSpec((1, block), lambda j, place: (0, place[CHIPS + j])),
                pl.BlockSpec((2 * rows, hidden), lambda j, place: (place[CHIPS + j], 1)),
            ],
            out_specs=[
                whole((tokens, width)),
                whole((tokens, width)),
                up_out,
                up_out,
                down_out,
                down_out,
                pl.BlockSpec((1, block), lambda j, place: (0, place[CHIPS + j])),
            ],
            scratch_shapes=[
                pltpu.VMEM((tokens, width), BF16),
                pltpu.VMEM((width, tokens), BF16),
                pltpu.VMEM((width, tokens), BF16),
                pltpu.VMEM((block, width), BF16),
            ],
        ),
        out_shape=[
            jax.ShapeDtypeStruct((tokens, width), F32),
            jax.ShapeDtypeStruct((tokens, width), F32),
            sent,
            sent,
            sent,
            sent,
            jax.ShapeDtypeStruct((1, hidden), F32),
        ],
        name="mlp",
        **params_for(12 * tokens * width * hidden, 12 * tokens * width + 8 * width * hidden, 2 * tokens * hidden),
    )(place, normed, cotangent, table, rest, up_shift, rest)


SUM_ROWS = 8


def unmerge_kernel(
    place, middle_ref, branch1_ref, branch2_ref, delta_ref, cotangent_ref, own_ref, far_ref, table, own_w, far_w,
    output_ref, delta_middle_ref, own_grad_ref, far_grad_ref, mine_ref, other_ref, sums_ref,
    delta1_all, mixture_t,
    *, tokens,
):
    step = pl.program_id(0)

    @pl.when(step == 0)
    def _():
        sums_ref[...] = jnp.zeros_like(sums_ref)

    rows, width = middle_ref.shape
    inside = lax.broadcasted_iota(jnp.int32, (rows, width), 0) + step * rows < tokens

    def kept(values):
        return jnp.where(inside, values, 0.0)

    upstream = cotangent_ref[...].astype(F32)
    scale2 = table[SCALE2 : SCALE2 + 1, :]
    middle = middle_ref[...]
    branch2 = branch2_ref[...] + table[DOWN_SHIFT : DOWN_SHIFT + 1, :]
    output_ref[...] = (middle + scale2 * branch2).astype(BF16)
    delta2 = (scale2 * upstream).astype(BF16).astype(F32)
    delta = delta_ref[...]
    inner, gain_terms = normalize_back(middle, table[GAIN2 : GAIN2 + 1, :], delta)
    delta_middle = upstream + inner
    delta_middle_ref[...] = delta_middle
    delta1 = kept(table[SCALE1 : SCALE1 + 1, :] * delta_middle).astype(BF16)
    delta1_all[pl.ds(pl.multiple_of(step * rows, 16), rows), :] = delta1
    own_grad_ref[...] = dot(delta1, own_w[...], NT).astype(BF16)
    far_grad_ref[...] = dot(delta1, far_w[...], NT).astype(BF16)
    terms = (
        upstream * branch2,
        delta2,
        gain_terms,
        delta,
        delta_middle * branch1_ref[...],
        delta1.astype(F32),
    )
    for i, term in enumerate(terms):
        sums_ref[i : i + 1, :] += total_rows(kept(term))

    @pl.when(step == pl.num_programs(0) - 1)
    def _():
        chips = mine_ref.shape[0]
        wide = width // chips
        for k in range(chips):
            chip = place[CHIPS + k]
            at = pl.ds(pl.multiple_of(lax.rem(chip, chips // 2) * wide, wide), wide)
            mixed = jnp.where(chip // (chips // 2) == place[CORE], own_ref[:, at], far_ref[:, at])
            place_turned(place, mixed, mixture_t, k, chips)
        split_rows(dot(mixture_t[...], delta1_all[:tokens, :]).astype(BF16), mine_ref, other_ref)


def unmerge(place, middle, branch1, branch2, delta, cotangent, own, far, table, rest, owners):
    tokens, width = middle.shape
    chips = owners // 2
    sent = (chips, width // owners, width)
    half = width // 2
    steps = row_steps(tokens)
    wide = pl.BlockSpec((ROWS, width), lambda i, _: (i, 0))
    narrow = pl.BlockSpec((ROWS, half), lambda i, _: (i, 0))
    return pl.pallas_call(
        functools.partial(unmerge_kernel, tokens=tokens),
        grid_spec=pltpu.PrefetchScalarGridSpec(
            num_scalar_prefetch=1,
            grid=(steps,),
            in_specs=[wide] * 5
            + [whole((tokens, half))] * 2
            + [
                whole(table.shape),
                pl.BlockSpec((half, width), lambda i, place: (place[CORE], rest.shape[1] // width - 1)),
                pl.BlockSpec((half, width), lambda i, place: (1 - place[CORE], rest.shape[1] // width - 1)),
            ],
            out_specs=[wide, wide, narrow, narrow, whole(sent), whole(sent), whole((SUM_ROWS, width))],
            scratch_shapes=[pltpu.VMEM((steps * ROWS, width), BF16), pltpu.VMEM((width, tokens), BF16)],
        ),
        out_shape=[
            jax.ShapeDtypeStruct((tokens, width), BF16),
            jax.ShapeDtypeStruct((tokens, width), F32),
            jax.ShapeDtypeStruct((tokens, half), BF16),
            jax.ShapeDtypeStruct((tokens, half), BF16),
            jax.ShapeDtypeStruct(sent, BF16),
            jax.ShapeDtypeStruct(sent, BF16),
            jax.ShapeDtypeStruct((SUM_ROWS, width), F32),
        ],
        name="unmerge",
        **params_for(4 * tokens * width * width, 30 * tokens * width + 4 * width * width),
    )(place, middle, branch1, branch2, delta, cotangent, own, far, table, rest, rest)


def unproject_kernel(
    place, x_hbm, delta_middle_hbm, table, normed_ref, own_ref, far_ref, weight_ref, middle_sums, up_sums, *refs, chips
):
    (
        out_ref, mine_ref, other_ref, vectors_mine_ref, vectors_other_ref,
        delta, sums, normed_t, x_ref, delta_middle_ref, arrived,
    ) = refs
    step = pl.program_id(0)
    core = place[CORE]
    copies = [
        pltpu.make_async_copy(x_hbm, x_ref, arrived.at[0]),
        pltpu.make_async_copy(delta_middle_hbm, delta_middle_ref, arrived.at[1]),
    ]

    @pl.when(step == 0)
    def _():
        for copy in copies:
            copy.start()
        fill_turned(place, normed_ref, normed_t, chips)
        delta[...] = jnp.zeros_like(delta)
        sums[...] = jnp.zeros_like(sums)

    own, far = own_ref[0], far_ref[0]
    block = jnp.concatenate([jnp.where(core == 0, own, far), jnp.where(core == 0, far, own)], axis=1)
    split_rows(dot(normed_t[...], block).astype(BF16), mine_ref, other_ref)
    delta[...] += dot(block, weight_ref[...], NT)
    for kind, row in ((0, QUERY), (2, VALUE)):

        @pl.when(step == kind)
        def _():
            sums[row : row + 1, :] = total_rows(block.astype(F32))

    @pl.when(step == pl.num_programs(0) - 1)
    def _():
        for copy in copies:
            copy.wait()
        delta_normed = delta[...]
        inner, gain_terms = normalize_back(
            x_ref[...].astype(F32), table[GAIN1 : GAIN1 + 1, :], delta_normed
        )
        out_ref[...] = (delta_middle_ref[...] + inner).astype(BF16)
        rows = {
            GAIN1: total_rows(gain_terms),
            SHIFT1: total_rows(delta_normed),
            OUT_SHIFT: middle_sums[5:6, :],
            SCALE1: middle_sums[4:5, :],
            GAIN2: middle_sums[2:3, :],
            SHIFT2: middle_sums[3:4, :],
            DOWN_SHIFT: middle_sums[1:2, :],
            SCALE2: middle_sums[0:1, :],
        }
        for i, values in rows.items():
            sums[i : i + 1, :] = values
        each = up_sums.shape[1] // (2 * chips)
        for out, side in ((vectors_mine_ref, core), (vectors_other_ref, 1 - core)):
            out[...] = jnp.zeros_like(out)
            for k in range(chips):
                chip = place[CHIPS + k]
                at = pl.ds(pl.multiple_of(chip * LANES, LANES), LANES)
                out[k, : sums.shape[0], :] = sums[:, at].astype(BF16)
                for r in range(each // LANES):
                    at = pl.multiple_of((2 * chip + side) * each + r * LANES, LANES)
                    row = up_sums[:, pl.ds(at, LANES)].astype(BF16)
                    out[k, VECTORS + r : VECTORS + r + 1, :] = row


def unproject(place, x, delta_middle, table, normed, own, far, weight, middle_sums, up_sums, owners):
    tokens, width = x.shape
    half = width // 2
    chips = owners // 2
    rows = width // owners
    vectors = (chips, rows, LANES)
    anywhere = pl.BlockSpec(memory_space=pl.ANY)
    kind = pl.BlockSpec((1, tokens, half), lambda j, _: (j, 0, 0))
    sent = pl.BlockSpec((chips, rows, width), lambda j, _: (0, 0, j))
    return pl.pallas_call(
        functools.partial(unproject_kernel, chips=chips),
        grid_spec=pltpu.PrefetchScalarGridSpec(
            num_scalar_prefetch=1,
            grid=(3,),
            in_specs=[
                anywhere,
                anywhere,
                whole(table.shape),
                whole((tokens, width)),
                kind,
                kind,
                pl.BlockSpec((width, width), lambda j, _: (0, j)),
                whole(middle_sums.shape),
                whole(up_sums.shape),
            ],
            out_specs=[whole((tokens, width)), sent, sent, whole(vectors), whole(vectors)],
            scratch_shapes=[
                pltpu.VMEM((tokens, width), F32),
                pltpu.VMEM((16, width), F32),
                pltpu.VMEM((width, tokens), BF16),
                pltpu.VMEM((tokens, width), BF16),
                pltpu.VMEM((tokens, width), F32),
                pltpu.SemaphoreType.DMA((2,)),
            ],
        ),
        out_shape=[
            jax.ShapeDtypeStruct((tokens, width), BF16),
            jax.ShapeDtypeStruct((chips, rows, 3 * width), BF16),
            jax.ShapeDtypeStruct((chips, rows, 3 * width), BF16),
            jax.ShapeDtypeStruct(vectors, BF16),
            jax.ShapeDtypeStruct(vectors, BF16),
        ],
        name="unproject",
        **params_for(12 * tokens * width * width, 18 * tokens * width + 12 * width * width, weight=SHORT),
    )(place, x, delta_middle, table, normed, own, far, weight, middle_sums, up_sums)


def ring_of(chips):
    return list(range(0, chips, 2)) + list(range(1, chips, 2))[::-1]


def places(owners):
    ring = ring_of(owners // 2)
    rows = []
    for f in range(owners):
        chip, core = divmod(f, 2)
        at = ring.index(chip)
        columns = [1 - core, 3 - core, 5 - core, core, 2 + core, 4 + core]
        rows.append(columns + [core] + ring[at:] + ring[:at])
    return np.array(rows, np.int32)


def ring_perm(chips, hop):
    ring = ring_of(chips)
    return [
        (2 * ring[i] + core, 2 * ring[(i + hop) % chips] + core) for i in range(chips) for core in range(2)
    ]


def to_next(values, chips, hop):
    return lax.ppermute(values, "fsdp", ring_perm(chips, hop))


def ring_gather(piece, chips):
    pieces = [None] * chips
    pieces[0] = right = left = piece
    for k in range(1, chips // 2 + 1):
        pieces[-k] = right = to_next(right, chips, 1)
        if k < chips - chips // 2:
            pieces[k] = left = to_next(left, chips, -1)
    return pieces


def low_part(columns):
    return columns // 2 if columns % (2 * LANES) == 0 else columns


def ring_add_kernel(*refs, columns, mode, carried):
    ways = 2 if mode in ("second", "next") else 1
    shares = [refs[2 * len(columns) * d : 2 * len(columns) * (d + 1)] for d in range(ways)]
    came = refs[2 * len(columns) * ways :]
    outs = refs[len(refs) - carried - (1 if mode == "total" else 2) : len(refs) - carried]
    start, low_start, high_start = 0, 0, 0
    for i, each in enumerate(columns):
        totals = [mine[2 * i][0].astype(F32) + mine[2 * i + 1][0].astype(F32) for mine in shares]
        at = slice(start, start + each)
        low = low_part(each)
        low_at, high_at = slice(low_start, low_start + low), slice(high_start, high_start + each - low)
        if mode == "first":
            outs[0][:, low_at] = totals[0][:, :low].astype(BF16)
            if low < each:
                outs[1][:, high_at] = totals[0][:, low:].astype(BF16)
        elif mode == "second":
            outs[0][:, start : start + low] = (totals[0][:, :low] + came[0][:, low_at].astype(F32)).astype(BF16)
            outs[1][:, start : start + low] = totals[1][:, :low].astype(BF16)
            if low < each:
                high = totals[1][:, low:] + came[1][:, high_at].astype(F32)
                outs[0][:, start + low : start + each] = totals[0][:, low:].astype(BF16)
                outs[1][:, start + low : start + each] = high.astype(BF16)
        elif mode == "next":
            for total, arrived, out in zip(totals, came, outs):
                out[:, at] = (total + arrived[:, at].astype(F32)).astype(BF16)
        else:
            both_ways = came[0][:, at].astype(F32) + came[1][:, at].astype(F32)
            outs[0][:, at] = (totals[0] + both_ways).astype(BF16)
        start, low_start, high_start = at.stop, low_at.stop, high_at.stop


class RingSum:
    def __init__(self, *parts):
        self.parts, self.chips = [part[:2] for part in parts], parts[0][0].shape[0]
        self.columns = [part[0].shape[2] // part[3] for part in parts]
        self.blocks = [part[2] for part in parts]
        self.steps = self.chips // 2
        self.step = 0
        self.came = []

    def add(self, mode, places, after=(), carry=()):
        rows = self.parts[0][0].shape[1]
        columns = self.columns
        total = sum(columns)
        blocks = 2 if total > 4096 else 1
        arrays, specs = [], []
        for at in places:
            for part, each, block in zip(self.parts, columns, self.blocks):
                for array in part:
                    arrays.append(array)
                    specs.append(pl.BlockSpec((1, rows // blocks, each), lambda i, at=at, block=block: (at, i, block)))
        for came in self.came:
            arrays.append(came)
            specs.append(pl.BlockSpec((rows // blocks, came.shape[1]), lambda i: (i, 0)))
        arrays += [*after, *carry]
        anywhere = pl.BlockSpec(memory_space=pl.ANY)
        specs += [anywhere] * (len(after) + len(carry))
        low = sum(low_part(each) for each in columns)
        out_columns = {"first": [low, total - low], "total": [total]}.get(mode, [total, total])
        sums = len(out_columns)
        outs = pl.pallas_call(
            functools.partial(ring_add_kernel, columns=columns, mode=mode, carried=len(carry)),
            grid=(blocks,),
            in_specs=specs,
            out_specs=[pl.BlockSpec((rows // blocks, out), lambda i: (i, 0)) for out in out_columns]
            + [anywhere] * len(carry),
            out_shape=[jax.ShapeDtypeStruct((rows, out), BF16) for out in out_columns]
            + [jax.ShapeDtypeStruct(array.shape, array.dtype) for array in carry],
            input_output_aliases={len(arrays) - len(carry) + i: sums + i for i in range(len(carry))},
            name="ring_add",
            **params_for(6 * rows * total, 16 * rows * total, weight=SHORT),
        )(*arrays)
        return outs[:sums], outs[sums:]

    def sums(self, after=(), carry=()):
        k = self.steps - self.step
        if self.step == 0:
            return self.add("first", [k], after, carry)
        return self.add("second" if self.step == 1 else "next", [k, self.chips - k], after, carry)

    def send(self, sums):
        self.came = [to_next(sums[0], self.chips, 1), to_next(sums[1], self.chips, -1)]
        self.step += 1

    def total(self, carry=()):
        assert self.step == self.steps
        sums, carried = self.add("total", [0], (), carry)
        return sums[0], carried


def passed(arrays, after):
    anywhere = pl.BlockSpec(memory_space=pl.ANY)
    return pl.pallas_call(
        lambda *refs: None,
        in_specs=[anywhere] * (len(arrays) + len(after)),
        out_specs=[anywhere] * len(arrays),
        out_shape=[jax.ShapeDtypeStruct(array.shape, array.dtype) for array in arrays],
        input_output_aliases={i: i for i in range(len(arrays))},
        name="passed",
        **params_for(1, 1),
    )(*arrays, *after)


def finish_rest_kernel(part_ref, came_ref, up_ref, down_ref):
    def total(at):
        return part_ref[:, at].astype(F32) + came_ref[:, at].astype(F32)

    rows, hidden = up_ref.shape
    each, width = down_ref.shape
    up_ref[...] = total(slice(0, hidden))
    for g in range(0, width // rows, 2):
        pair = [total(slice(hidden + each * h, hidden + each * (h + 1))) for h in (g, g + 1)]
        down_ref[:, g * rows : (g + 2) * rows] = jnp.concatenate(pair, axis=0).T


def finish_rest(part, came, hidden, each, width):
    in_vmem = pl.BlockSpec(memory_space=pltpu.VMEM)
    rows = part.shape[0]
    return pl.pallas_call(
        finish_rest_kernel,
        in_specs=[in_vmem] * 2,
        out_specs=[in_vmem] * 2,
        out_shape=[jax.ShapeDtypeStruct(shape, F32) for shape in ((rows, hidden), (each, width))],
        name="finish_rest",
        **params_for(part.size, 8 * part.size, weight=SHORT),
    )(part, came)


def finish_first_kernel(place, *refs):
    parts, came, (packed_ref, output_ref), vector_refs = refs[:2], refs[2:4], refs[4:6], refs[6:]
    packed, out = packed_ref.shape[1] // 2, output_ref.shape[1] // 2
    for i in range(2):
        total = parts[i][...].astype(F32) + came[i][...].astype(F32)
        packed_ref[:, packed * i : packed * (i + 1)] = total[:, :packed]
        output_ref[:, out * i : out * (i + 1)] = total[:, packed : packed + out]
        if i == 0:
            vectors = total[:16, packed + out :]
    half = LANES // 2
    mine = jnp.where(place[CORE] == 0, vectors[:, :half], vectors[:, half:])
    for i in range(VECTORS):
        vector_refs[i][...] = mine[i : i + 1, :].reshape(half)
    count = vector_refs[VECTORS].shape[0]
    vector_refs[VECTORS][...] = vectors[VECTORS : VECTORS + count // LANES, :].reshape(count)


def finish_first(place, parts, came, width, each):
    in_vmem = pl.BlockSpec(memory_space=pltpu.VMEM)
    rows = parts[0].shape[0]
    shapes = [(rows, 3 * width), (rows, width)] + [(rows,)] * VECTORS + [(each,)]
    return pl.pallas_call(
        finish_first_kernel,
        in_specs=[pl.BlockSpec(memory_space=pltpu.SMEM)] + [in_vmem] * 4,
        out_specs=[in_vmem] * len(shapes),
        out_shape=[jax.ShapeDtypeStruct(shape, F32) for shape in shapes],
        name="finish_first",
        **params_for(8 * rows * width, 32 * rows * width, weight=SHORT),
    )(place, *parts, *came)


def split_pairs(pairs):
    return [pairs // 4, pairs // 2, pairs - pairs // 4 - pairs // 2] if pairs >= 4 else [pairs]


def paired_body(
    tokens, lengths, norm1_gain, norm1_bias, packed_weight, query_bias, value_bias, output_weight, output_bias,
    layer_scale1, norm2_gain, norm2_bias, up_weight, up_bias, down_weight, down_bias, layer_scale2, cotangent,
):
    owners = lax.axis_size("fsdp")
    chips = owners // 2
    _, local_len, width = tokens.shape
    me = lax.axis_index("fsdp")
    core = lax.rem(me, 2)
    place = lax.dynamic_index_in_dim(jnp.asarray(places(owners)), me, keepdims=False)
    moves = [(f * 2 + s, (f - f % 2 + s) * 2 + f % 2) for f in range(owners) for s in range(2) if f % 2 != s]
    twin = [(f, f ^ 1) for f in range(owners)]
    stays = core == lax.axis_index("seq")

    def regroup_moves(values):
        return lax.ppermute(values, ("fsdp", "seq"), moves)

    def regrouped(values):
        return jnp.where(stays, values, regroup_moves(values))

    def to_twin(values):
        return lax.ppermute(values, "fsdp", twin)

    def across(values):
        return lax.ppermute(values, "seq", [(0, 1), (1, 0)])

    vectors = (
        norm1_gain, norm1_bias, query_bias, value_bias, output_bias, layer_scale1, norm2_gain, norm2_bias,
        down_bias, layer_scale2,
    )
    rows = norm1_gain.shape[0]
    hidden = up_weight.shape[1]
    first, rest = pack(place, packed_weight, up_weight, down_weight, output_weight, vectors, up_bias)
    own_pieces = ring_gather(first, chips)
    far_pieces = [to_twin(piece) for piece in own_pieces]
    x = regrouped(tokens.reshape(local_len, width))
    valid_count = regrouped(lengths)
    rest = lax.all_gather(rest, "fsdp", axis=0, tiled=True)
    starts = jnp.stack([core, 1 - core]) * local_len
    valid = jnp.clip(valid_count - starts, 0, local_len).astype(jnp.int32)
    upstream = regrouped(cotangent.reshape(local_len, width))

    far_out, own_part, normed, packed_full, table, up_shift = project(place, x, own_pieces, far_pieces, hidden)
    far_part = to_twin(far_out)
    parts = [own_part, far_part]
    (own_mix, far_mix_out), totals = attention(valid, parts, 352)
    far_mix = to_twin(far_mix_out)
    middle, branch1, normed2 = merge(place, x, own_mix, far_mix, table, rest)

    branch2, delta_normed2, up_mine, up_other, down_mine, down_other, up_sums = mlp(
        place, normed2, upstream, table, rest, up_shift, owners
    )
    up_twin, down_twin = to_twin(up_other), to_twin(down_other)
    output, delta_middle, own_grad, far_grad_out, output_mine, output_other, middle_sums = unmerge(
        place, middle, branch1, branch2, delta_normed2, upstream, own_mix, far_mix, table, rest, owners
    )
    far_grad = to_twin(far_grad_out)
    ring = RingSum((up_mine, up_twin, 0, 1), (down_mine, down_twin, 0, 1))
    output_sent = regroup_moves(output)
    output_twin = to_twin(output_other)
    deltas = ()
    grads = [own_grad, far_grad]
    start = 0
    for pairs in split_pairs(width // 2 // LANES):
        sums, _ = ring.sums()
        ring.send(sums)
        after = [*sums, output_sent, output_twin] if start else sums
        deltas = attention_back(
            valid, parts, [own_mix, far_mix_out], grads, totals, 352, start, pairs, deltas, after
        )
        start += pairs
    own_delta, far_delta_out = deltas
    sums, (far_delta_out,) = ring.sums(carry=[far_delta_out])
    ring.send(sums)
    far_delta = to_twin(far_delta_out)
    grad_x, packed_mine, packed_other, vectors_mine, vectors_other = unproject(
        place, x, delta_middle, table, normed, own_delta, far_delta, packed_full, middle_sums, up_sums, owners
    )
    output = jnp.where(stays, output, output_sent).reshape(tokens.shape)
    grad_x, packed_other, vectors_other = passed([grad_x, packed_other, vectors_other], ring.came)
    vectors_twin, packed_twin = to_twin(vectors_other), to_twin(packed_other)
    rest_sum, _ = ring.total()
    rings = (
        RingSum(
            (packed_mine, packed_twin, 0, 2), (output_mine, output_twin, 0, 2), (vectors_mine, vectors_twin, 0, 1)
        ),
        RingSum((packed_mine, packed_twin, 1, 2), (output_mine, output_twin, 1, 2)),
    )
    grad_x_sent, rest_sent = regroup_moves(grad_x), across(rest_sum)
    last = [rest_sum]
    for step in range(rings[0].steps):
        for half in rings:
            after = [*last] + ([grad_x_sent] if step == 2 and half is rings[0] else [])
            last, _ = half.sums(after)
            half.send(last)
    grad_tokens = jnp.where(stays, grad_x, grad_x_sent).astype(F32).reshape(tokens.shape)
    each = up_bias.shape[0]
    grad_up, grad_down = finish_rest(rest_sum, rest_sent, hidden, each, width)
    first_sums = [half.total()[0] for half in rings]
    grad_packed, grad_output, *mine = finish_first(
        place, first_sums, [across(half) for half in first_sums], width, each
    )
    return (
        output, grad_tokens, mine[0], mine[1], grad_packed, mine[2], mine[3], grad_output, mine[4], mine[5],
        mine[6], mine[7], grad_up, mine[10], grad_down, mine[8], mine[9],
    )


def pairable(tokens, up_weight):
    owners, chips = lax.axis_size("fsdp"), lax.axis_size("fsdp") // 2
    width, hidden = up_weight.shape[0] * owners, up_weight.shape[1]
    return (
        lax.axis_size("seq") == 2
        and tokens.shape[0] == 1
        and tokens.shape[1] % 16 == 0
        and owners == 2 * chips
        and chips in (4, 8)
        and width % (chips * LANES) == 0
        and hidden % (owners * LANES) == 0
        and H * HD == width
    )


def body(*args):
    chosen = paired_body if pairable(args[0], args[12]) else general_body
    return chosen(*args)


def solution(mesh):
    in_specs = (
        P("fsdp", "seq", None),
        P("fsdp"),
        P("fsdp"),
        P("fsdp"),
        P("fsdp", None),
        P("fsdp"),
        P("fsdp"),
        P("fsdp", None),
        P("fsdp"),
        P("fsdp"),
        P("fsdp"),
        P("fsdp"),
        P("fsdp", None),
        P("fsdp"),
        P("fsdp", None),
        P("fsdp"),
        P("fsdp"),
        P("fsdp", "seq", None),
    )
    out_specs = (
        P("fsdp", "seq", None),
        P("fsdp", "seq", None),
        P("fsdp"),
        P("fsdp"),
        P("fsdp", None),
        P("fsdp"),
        P("fsdp"),
        P("fsdp", None),
        P("fsdp"),
        P("fsdp"),
        P("fsdp"),
        P("fsdp"),
        P("fsdp", None),
        P("fsdp"),
        P("fsdp", None),
        P("fsdp"),
        P("fsdp"),
    )
    return jax.shard_map(body, mesh=mesh, in_specs=in_specs, out_specs=out_specs, check_vma=False)
```

```python
import functools

import jax
import jax.numpy as jnp
import numpy as np
from jax import lax
from jax.experimental import pallas as pl
from jax.experimental.pallas import tpu as pltpu
from jax.sharding import PartitionSpec as P

H = 16
HD = 64


norm_eps = 1e-06


def layer_norm(values, norm_gain, norm_shift):
    center = values - jnp.mean(values, axis=-1, keepdims=True)
    spread = jnp.mean(center * center, axis=-1, keepdims=True)
    return center * lax.rsqrt(spread + norm_eps) * norm_gain + norm_shift


def gelu_exact(values):
    return jax.nn.gelu(values, approximate=False)


def matmul(left, right):
    return jnp.dot(left, right, preferred_element_type=jnp.float32)


def left_outer(left, right):
    return jnp.einsum("ti,tj->ij", left, right, preferred_element_type=jnp.float32)


def right_back(left, right):
    return jnp.einsum("tj,ij->ti", left, right, preferred_element_type=jnp.float32)


def column_sum(values):
    return jnp.sum(values.astype(jnp.float32), axis=0)


def attention_probs(queries, key_rows, valid_count, score_scale):
    scores = score_scale * jnp.einsum(
        "qhd,khd->hqk", queries, key_rows, preferred_element_type=jnp.float32
    )
    key_valid = jnp.arange(key_rows.shape[0]) < valid_count
    scores = jnp.where(key_valid[None, None, :], scores, -jnp.inf)
    return scores


def attend(queries, key_rows, values, valid_count, score_scale):
    scores = attention_probs(queries, key_rows, valid_count, score_scale)
    largest = jnp.max(scores, axis=-1, keepdims=True)
    log_total = largest[..., 0] + jnp.log(jnp.sum(jnp.exp(scores - largest), axis=-1))
    attention = jnp.exp(scores - log_total[..., None]).astype(jnp.bfloat16)
    mixture = jnp.einsum("hqk,khd->qhd", attention, values, preferred_element_type=jnp.float32)
    return (mixture.astype(jnp.bfloat16), log_total)


def attend_back(queries, key_rows, values, valid_count, score_scale, log_total, grad_mixture):
    scores = attention_probs(queries, key_rows, valid_count, score_scale)
    probs = jnp.exp(scores - log_total[..., None])
    grad_values = jnp.einsum(
        "hqk,qhd->khd", probs.astype(jnp.bfloat16), grad_mixture, preferred_element_type=jnp.float32
    )
    grad_probs = jnp.einsum(
        "qhd,khd->hqk", grad_mixture, values, preferred_element_type=jnp.float32
    )
    inner_sum = jnp.sum(probs * grad_probs, axis=-1, keepdims=True)
    grad_scores = (probs * (grad_probs - inner_sum)).astype(jnp.bfloat16)
    grad_queries = score_scale * jnp.einsum(
        "hqk,khd->qhd", grad_scores, key_rows, preferred_element_type=jnp.float32
    )
    grad_keys = score_scale * jnp.einsum(
        "hqk,qhd->khd", grad_scores, queries, preferred_element_type=jnp.float32
    )
    return (grad_queries, grad_keys, grad_values)


def general_body(
    tokens,
    lengths,
    norm1_gain,
    norm1_bias,
    packed_weight,
    query_bias,
    value_bias,
    output_weight,
    output_bias,
    layer_scale1,
    norm2_gain,
    norm2_bias,
    up_weight,
    up_bias,
    down_weight,
    down_bias,
    layer_scale2,
    cotangent,
):
    gathered = (
        lax.all_gather(norm1_gain, "fsdp", axis=0, tiled=True),
        lax.all_gather(norm1_bias, "fsdp", axis=0, tiled=True),
        lax.all_gather(packed_weight, "fsdp", axis=0, tiled=True),
        lax.all_gather(query_bias, "fsdp", axis=0, tiled=True),
        lax.all_gather(value_bias, "fsdp", axis=0, tiled=True),
        lax.all_gather(output_weight, "fsdp", axis=0, tiled=True),
        lax.all_gather(output_bias, "fsdp", axis=0, tiled=True),
        lax.all_gather(layer_scale1, "fsdp", axis=0, tiled=True),
        lax.all_gather(norm2_gain, "fsdp", axis=0, tiled=True),
        lax.all_gather(norm2_bias, "fsdp", axis=0, tiled=True),
        lax.all_gather(up_weight, "fsdp", axis=0, tiled=True),
        lax.all_gather(up_bias, "fsdp", axis=0, tiled=True),
        lax.all_gather(down_weight, "fsdp", axis=0, tiled=True),
        lax.all_gather(down_bias, "fsdp", axis=0, tiled=True),
        lax.all_gather(layer_scale2, "fsdp", axis=0, tiled=True),
    )
    (
        gain_one,
        shift_one,
        packed_full,
        query_shift,
        value_shift,
        output_full,
        output_shift,
        scale_one,
        gain_two,
        shift_two,
        up_full,
        up_shift,
        down_full,
        down_shift,
        scale_two,
    ) = gathered
    gain_one = gain_one.astype(jnp.float32)
    shift_one = shift_one.astype(jnp.float32)
    query_shift = query_shift.astype(jnp.float32)
    value_shift = value_shift.astype(jnp.float32)
    output_shift = output_shift.astype(jnp.float32)
    scale_one = scale_one.astype(jnp.float32)
    gain_two = gain_two.astype(jnp.float32)
    shift_two = shift_two.astype(jnp.float32)
    up_shift = up_shift.astype(jnp.float32)
    down_shift = down_shift.astype(jnp.float32)
    scale_two = scale_two.astype(jnp.float32)
    groups = lax.axis_size("seq")
    images, local_len, model_width = tokens.shape
    seq_len = local_len * groups
    per_group = H // groups
    score_scale = HD ** (-0.5)
    token_rows = tokens.astype(jnp.float32).reshape(images * local_len, model_width)
    normed = layer_norm(token_rows, gain_one, shift_one).astype(jnp.bfloat16)
    packed_shift = jnp.concatenate([query_shift, jnp.zeros_like(query_shift), value_shift])
    packed = (matmul(normed, packed_full) + packed_shift).astype(jnp.bfloat16)
    packed = packed.reshape(images, local_len, 3, groups, per_group * HD)
    spread = lax.all_to_all(packed, "seq", split_axis=3, concat_axis=1, tiled=True)
    spread = spread.reshape(images, seq_len, 3, per_group, HD)

    def forward_image(per_image):
        image_block, valid_count = per_image
        return attend(
            image_block[:, 0], image_block[:, 1], image_block[:, 2], valid_count, score_scale
        )

    mixture, log_total = lax.map(forward_image, (spread, lengths))
    mixture = mixture.reshape(images, seq_len, 1, per_group * HD)
    mixture_rows = lax.all_to_all(mixture, "seq", split_axis=1, concat_axis=2, tiled=True).reshape(
        images * local_len, model_width
    )
    branch_one = matmul(mixture_rows, output_full) + output_shift
    middle = token_rows + scale_one * branch_one
    normed_two = layer_norm(middle, gain_two, shift_two).astype(jnp.bfloat16)
    hidden = matmul(normed_two, up_full) + up_shift
    active = gelu_exact(hidden).astype(jnp.bfloat16)
    branch_two = matmul(active, down_full) + down_shift
    output = (middle + scale_two * branch_two).astype(jnp.bfloat16).reshape(tokens.shape)
    upstream = cotangent.astype(jnp.float32).reshape(images * local_len, model_width)
    grad_scale_two = jnp.sum(upstream * branch_two, axis=0)
    delta_two = (scale_two * upstream).astype(jnp.bfloat16)
    grad_down_shift = column_sum(delta_two)
    grad_down = left_outer(active, delta_two)
    grad_active = right_back(delta_two, down_full)
    _, gelu_pull = jax.vjp(gelu_exact, hidden)
    delta_hidden = gelu_pull(grad_active)[0].astype(jnp.bfloat16)
    grad_up_shift = column_sum(delta_hidden)
    grad_up = left_outer(normed_two, delta_hidden)
    delta_normed_two = right_back(delta_hidden, up_full)
    _, norm_pull_two = jax.vjp(layer_norm, middle, gain_two, shift_two)
    grad_middle_norm, grad_gain_two, grad_shift_two = norm_pull_two(delta_normed_two)
    delta_middle = upstream + grad_middle_norm
    grad_scale_one = jnp.sum(delta_middle * branch_one, axis=0)
    delta_one = (scale_one * delta_middle).astype(jnp.bfloat16)
    grad_output_shift = column_sum(delta_one)
    grad_output = left_outer(mixture_rows, delta_one)
    delta_mixture = right_back(delta_one, output_full).astype(jnp.bfloat16)
    delta_mixture = delta_mixture.reshape(images, local_len, groups, per_group * HD)
    grad_spread = lax.all_to_all(delta_mixture, "seq", split_axis=2, concat_axis=1, tiled=True)
    grad_spread = grad_spread.reshape(images, seq_len, per_group, HD)

    def backward_image(per_image):
        image_block, valid_count, image_total, image_grad = per_image
        grad_queries, grad_keys, grad_values = attend_back(
            image_block[:, 0],
            image_block[:, 1],
            image_block[:, 2],
            valid_count,
            score_scale,
            image_total,
            image_grad,
        )
        return jnp.stack([grad_queries, grad_keys, grad_values], axis=1).astype(jnp.bfloat16)

    delta_packed = lax.map(backward_image, (spread, lengths, log_total, grad_spread))
    delta_packed = delta_packed.reshape(images, seq_len, 3, 1, per_group * HD)
    delta_back = lax.all_to_all(delta_packed, "seq", split_axis=1, concat_axis=3, tiled=True)
    delta_back = delta_back.reshape(images * local_len, 3 * model_width)
    grad_query_shift = column_sum(delta_back[:, :model_width])
    grad_value_shift = column_sum(delta_back[:, 2 * model_width :])
    grad_packed = left_outer(normed, delta_back)
    delta_normed = right_back(delta_back, packed_full)
    _, norm_pull_one = jax.vjp(layer_norm, token_rows, gain_one, shift_one)
    grad_rows_norm, grad_gain_one, grad_shift_one = norm_pull_one(delta_normed)
    grad_tokens = (delta_middle + grad_rows_norm).reshape(tokens.shape)
    local_grads = (
        grad_gain_one,
        grad_shift_one,
        grad_packed,
        grad_query_shift,
        grad_value_shift,
        grad_output,
        grad_output_shift,
        grad_scale_one,
        grad_gain_two,
        grad_shift_two,
        grad_up,
        grad_up_shift,
        grad_down,
        grad_down_shift,
        grad_scale_two,
    )
    owned_grads = (
        lax.psum_scatter(
            local_grads[0].astype(jnp.bfloat16), "fsdp", scatter_dimension=0, tiled=True
        ).astype(jnp.float32),
        lax.psum_scatter(
            local_grads[1].astype(jnp.bfloat16), "fsdp", scatter_dimension=0, tiled=True
        ).astype(jnp.float32),
        lax.psum_scatter(
            local_grads[2].astype(jnp.bfloat16), "fsdp", scatter_dimension=0, tiled=True
        ).astype(jnp.float32),
        lax.psum_scatter(
            local_grads[3].astype(jnp.bfloat16), "fsdp", scatter_dimension=0, tiled=True
        ).astype(jnp.float32),
        lax.psum_scatter(
            local_grads[4].astype(jnp.bfloat16), "fsdp", scatter_dimension=0, tiled=True
        ).astype(jnp.float32),
        lax.psum_scatter(
            local_grads[5].astype(jnp.bfloat16), "fsdp", scatter_dimension=0, tiled=True
        ).astype(jnp.float32),
        lax.psum_scatter(
            local_grads[6].astype(jnp.bfloat16), "fsdp", scatter_dimension=0, tiled=True
        ).astype(jnp.float32),
        lax.psum_scatter(
            local_grads[7].astype(jnp.bfloat16), "fsdp", scatter_dimension=0, tiled=True
        ).astype(jnp.float32),
        lax.psum_scatter(
            local_grads[8].astype(jnp.bfloat16), "fsdp", scatter_dimension=0, tiled=True
        ).astype(jnp.float32),
        lax.psum_scatter(
            local_grads[9].astype(jnp.bfloat16), "fsdp", scatter_dimension=0, tiled=True
        ).astype(jnp.float32),
        lax.psum_scatter(
            local_grads[10].astype(jnp.bfloat16), "fsdp", scatter_dimension=0, tiled=True
        ).astype(jnp.float32),
        lax.psum_scatter(
            local_grads[11].astype(jnp.bfloat16), "fsdp", scatter_dimension=0, tiled=True
        ).astype(jnp.float32),
        lax.psum_scatter(
            local_grads[12].astype(jnp.bfloat16), "fsdp", scatter_dimension=0, tiled=True
        ).astype(jnp.float32),
        lax.psum_scatter(
            local_grads[13].astype(jnp.bfloat16), "fsdp", scatter_dimension=0, tiled=True
        ).astype(jnp.float32),
        lax.psum_scatter(
            local_grads[14].astype(jnp.bfloat16), "fsdp", scatter_dimension=0, tiled=True
        ).astype(jnp.float32),
    )
    owned_grads = (
        lax.psum(owned_grads[0].astype(jnp.bfloat16), "seq").astype(jnp.float32),
        lax.psum(owned_grads[1].astype(jnp.bfloat16), "seq").astype(jnp.float32),
        lax.psum(owned_grads[2].astype(jnp.bfloat16), "seq").astype(jnp.float32),
        lax.psum(owned_grads[3].astype(jnp.bfloat16), "seq").astype(jnp.float32),
        lax.psum(owned_grads[4].astype(jnp.bfloat16), "seq").astype(jnp.float32),
        lax.psum(owned_grads[5].astype(jnp.bfloat16), "seq").astype(jnp.float32),
        lax.psum(owned_grads[6].astype(jnp.bfloat16), "seq").astype(jnp.float32),
        lax.psum(owned_grads[7].astype(jnp.bfloat16), "seq").astype(jnp.float32),
        lax.psum(owned_grads[8].astype(jnp.bfloat16), "seq").astype(jnp.float32),
        lax.psum(owned_grads[9].astype(jnp.bfloat16), "seq").astype(jnp.float32),
        lax.psum(owned_grads[10].astype(jnp.bfloat16), "seq").astype(jnp.float32),
        lax.psum(owned_grads[11].astype(jnp.bfloat16), "seq").astype(jnp.float32),
        lax.psum(owned_grads[12].astype(jnp.bfloat16), "seq").astype(jnp.float32),
        lax.psum(owned_grads[13].astype(jnp.bfloat16), "seq").astype(jnp.float32),
        lax.psum(owned_grads[14].astype(jnp.bfloat16), "seq").astype(jnp.float32),
    )
    return (output, grad_tokens) + tuple(owned_grads)


BF16 = jnp.bfloat16
F32 = jnp.float32
NT = (((1,), (1,)), ((), ()))
NN = (((1,), (0,)), ((), ()))
MASKED = -1e30
LANES = 128
VMEM_LIMIT = 60 * 2**20
SMALL_VMEM = 8 * 2**20

GAIN1, SHIFT1, QUERY, VALUE, OUT_SHIFT, SCALE1, GAIN2, SHIFT2, DOWN_SHIFT, SCALE2 = range(10)


def dot(left, right, dims=NN):
    return lax.dot_general(left, right, dims, preferred_element_type=F32)


def turned(values):
    return values.T


def lane_ids(rows):
    return lax.broadcasted_iota(jnp.int32, (rows, LANES), 1)


def split3(values):
    high = values.astype(BF16).astype(F32)
    rest = values - high
    mid = rest.astype(BF16).astype(F32)
    return high, mid, rest - mid


LONG, SHORT = 16.0, 1 / 64


def params_for(flops, nbytes, transcendentals=0, weight=1.0, vmem=VMEM_LIMIT):
    flops, nbytes, transcendentals = (int(weight * count) for count in (flops, nbytes, transcendentals))
    return dict(
        compiler_params=pltpu.CompilerParams(vmem_limit_bytes=vmem),
        cost_estimate=pl.CostEstimate(
            flops=flops, bytes_accessed=nbytes, transcendentals=transcendentals
        ),
    )


def whole(shape):
    return pl.BlockSpec(shape, lambda *_: (0,) * len(shape))


def normalize(values, gain, shift):
    center = values - jnp.mean(values, axis=-1, keepdims=True)
    spread = jnp.mean(center * center, axis=-1, keepdims=True)
    return center * lax.rsqrt(spread + norm_eps) * gain + shift


def normalize_back(values, gain, delta):
    center = values - jnp.mean(values, axis=-1, keepdims=True)
    inverse = lax.rsqrt(jnp.mean(center * center, axis=-1, keepdims=True) + norm_eps)
    unit = center * inverse
    scaled = delta * gain
    mean_scaled = jnp.mean(scaled, axis=-1, keepdims=True)
    mean_unit = jnp.mean(scaled * unit, axis=-1, keepdims=True)
    return inverse * (scaled - mean_scaled - unit * mean_unit), delta * unit


def total_rows(values):
    return jnp.sum(values, axis=0, keepdims=True)


VECTORS = 10


def pack_kernel(place, weight_ref, up_ref, down_ref, output_ref, *refs):
    vector_refs, shift_ref = refs[:VECTORS], refs[VECTORS]
    first_ref, rest_ref = refs[VECTORS + 1 :]
    rows, width = weight_ref.shape
    first_ref[:, :width] = weight_ref[...]
    first_ref[:, width:] = jnp.zeros((rows, LANES), BF16)
    for i, ref in enumerate(vector_refs):
        values = ref[...].astype(F32).reshape(1, -1)
        empty = jnp.zeros_like(values)
        first, second = jnp.concatenate([values, empty], 1), jnp.concatenate([empty, values], 1)
        first_ref[i : i + 1, width:] = jnp.where(place[CORE] == 0, first, second).astype(BF16)
    shift = shift_ref[...].astype(F32).reshape(-1, LANES)
    first_ref[VECTORS : VECTORS + shift.shape[0], width:] = shift.astype(BF16)
    at = 0
    for ref in (up_ref, down_ref, output_ref):
        for g in range(ref.shape[0] // rows):
            rest_ref[:, at : at + ref.shape[1]] = ref[g * rows : (g + 1) * rows, :]
            at += ref.shape[1]


def pack(place, weight, up, down, output, vectors, up_shift):
    in_vmem = pl.BlockSpec(memory_space=pltpu.VMEM)
    rows, width = weight.shape
    others = (up.size + down.size + output.size) // rows
    return pl.pallas_call(
        pack_kernel,
        in_specs=[pl.BlockSpec(memory_space=pltpu.SMEM)] + [in_vmem] * (VECTORS + 5),
        out_specs=[in_vmem, in_vmem],
        out_shape=[
            jax.ShapeDtypeStruct((rows, width + LANES), BF16),
            jax.ShapeDtypeStruct((rows, others), BF16),
        ],
        name="pack",
        **params_for(0, 4 * rows * (width + others)),
    )(place, weight, up, down, output, *vectors, up_shift)


CORE, CHIPS = 6, 7


def project_kernel(place, x_ref, *refs, chips):
    own_refs, far_refs, own_vectors, far_vectors = (refs[chips * i : chips * (i + 1)] for i in range(4))
    far_out_ref, own_ref, normed_ref, weight_ref, table_ref, up_ref = refs[4 * chips :]
    step = pl.program_id(0)
    rows = own_refs[0].shape[0]
    core = place[CORE]

    @pl.when(step == 0)
    def _():
        vector = lax.broadcasted_iota(jnp.int32, (table_ref.shape[0], LANES), 0) < VECTORS
        each = up_ref.shape[1] // (2 * chips)
        for k in range(chips):
            chip = place[CHIPS + k]
            own = own_vectors[k][...].astype(F32)
            far = far_vectors[k][...].astype(F32)
            at = pl.ds(pl.multiple_of(chip * LANES, LANES), LANES)
            table_ref[:, at] = jnp.where(vector, own + far, 0.0)
            for part, side in ((own, core), (far, 1 - core)):
                for r in range(each // LANES):
                    at = pl.multiple_of((2 * chip + side) * each + r * LANES, LANES)
                    up_ref[:, pl.ds(at, LANES)] = part[VECTORS + r : VECTORS + r + 1, :]
        normed_ref[...] = normalize(
            x_ref[...].astype(F32), table_ref[GAIN1 : GAIN1 + 1, :], table_ref[SHIFT1 : SHIFT1 + 1, :]
        ).astype(BF16)

    for k in range(chips):
        start = 2 * place[CHIPS + k]
        weight_ref[pl.ds(pl.multiple_of((start + core) * rows, rows), rows), :] = own_refs[k][...]
        weight_ref[pl.ds(pl.multiple_of((start + 1 - core) * rows, rows), rows), :] = far_refs[k][...]
    shift = jnp.where(
        step == 0,
        table_ref[QUERY : QUERY + 1, :],
        jnp.where(step == 2, table_ref[VALUE : VALUE + 1, :], 0.0),
    )
    result = (dot(normed_ref[...], weight_ref[...]) + shift).astype(BF16)
    half = result.shape[1] // 2
    low, high = result[:, :half], result[:, half:]
    own_ref[0] = jnp.where(core == 0, low, high)
    far_out_ref[0] = jnp.where(core == 0, high, low)


def project(place, x, own_pieces, far_pieces, hidden):
    chips = len(own_pieces)
    tokens, width = x.shape
    rows = own_pieces[0].shape[0]
    kind = pl.BlockSpec((1, tokens, width // 2), lambda j, _: (j, 0, 0))
    return pl.pallas_call(
        functools.partial(project_kernel, chips=chips),
        grid_spec=pltpu.PrefetchScalarGridSpec(
            num_scalar_prefetch=1,
            grid=(3,),
            in_specs=[whole((tokens, width))]
            + [pl.BlockSpec((rows, width), lambda j, _: (0, j))] * 2 * chips
            + [pl.BlockSpec((16, LANES), lambda j, _: (0, 3 * width // LANES))] * 2 * chips,
            out_specs=[
                kind,
                kind,
                whole((tokens, width)),
                pl.BlockSpec((width, width), lambda j, _: (0, j)),
                whole((16, width)),
                whole((1, hidden)),
            ],
        ),
        out_shape=[
            jax.ShapeDtypeStruct((3, tokens, width // 2), BF16),
            jax.ShapeDtypeStruct((3, tokens, width // 2), BF16),
            jax.ShapeDtypeStruct((tokens, width), BF16),
            jax.ShapeDtypeStruct((width, 3 * width), BF16),
            jax.ShapeDtypeStruct((16, width), F32),
            jax.ShapeDtypeStruct((1, hidden), F32),
        ],
        name="project",
        **params_for(6 * tokens * width * width, 12 * tokens * width + 12 * width * width),
    )(place, x, *own_pieces, *far_pieces, *own_pieces, *far_pieces)


def padded_len(count, block):
    return -(-count // block) * block


def attend_kernel(valid, *refs, pieces, block, scale):
    in_refs, out_refs = refs[:pieces], refs[pieces : 2 * pieces]
    total_refs = refs[2 * pieces : 3 * pieces]
    keys, values, queries, mixed, totals = refs[3 * pieces :]
    pair = pl.program_id(0)
    size = in_refs[0].shape[1]
    count, padded = pieces * size, keys.shape[0]
    lane = lane_ids(size)
    row = lax.broadcasted_iota(jnp.int32, (size, LANES), 0)
    for i in range(pieces):
        at = pl.ds(i * size, size)
        keys[at, :LANES] = in_refs[i][1]
        keys[at, LANES:] = jnp.where((lane == 0) & (row >= valid[i]), MASKED, 0.0).astype(BF16)
        values[at, :LANES] = in_refs[i][2]
        values[at, LANES:] = jnp.where(lane == 0, 1.0, 0.0).astype(BF16)
        for j in range(2):
            mine = lane // HD == j
            queries[j, at, :LANES] = jnp.where(mine, in_refs[i][0].astype(F32) * scale, 0.0).astype(BF16)
            queries[j, at, LANES:] = jnp.where(lane == 0, 1.0, 0.0).astype(BF16)
    if padded > count:
        rest = pl.ds(count, padded - count)
        rest_lane = lane_ids(padded - count)
        keys[rest, :LANES] = jnp.zeros((padded - count, LANES), BF16)
        keys[rest, LANES:] = jnp.where(rest_lane == 0, MASKED, 0.0).astype(BF16)
        values[rest, :] = jnp.zeros((padded - count, 2 * LANES), BF16)
        for j in range(2):
            queries[j, rest, :] = jnp.zeros((padded - count, 2 * LANES), BF16)

    @pl.when(pair == 0)
    def _():
        for i in range(pieces):
            total_refs[i][...] = jnp.zeros_like(total_refs[i])

    block_lane = lane_ids(block)
    for b in range(padded // block):
        at = pl.ds(b * block, block)
        results, logs = [], 0.0
        for j in range(2):
            scores = dot(queries[j, at, :], keys[...], NT)
            largest = jnp.max(scores, axis=1, keepdims=True)
            weights = jnp.exp(scores - largest).astype(BF16)
            result = dot(weights, values[...])
            total = result[:, LANES : LANES + 1]
            results.append(result[:, :LANES] * (1.0 / total))
            logs += jnp.where(block_lane == 2 * pair + j, largest + jnp.log(total), 0.0)
        mixed[at, :] = jnp.where(block_lane < HD, results[0], results[1])
        totals[at, :] = logs
    for i in range(pieces):
        at = pl.ds(i * size, size)
        out_refs[i][...] = mixed[at, :].astype(BF16)
        total_refs[i][...] += totals[at, :]


def attention(valid, parts, block):
    pieces = len(parts)
    _, size, width = parts[0].shape
    pairs = width // LANES
    padded = padded_len(pieces * size, block)
    outs = pl.pallas_call(
        functools.partial(attend_kernel, pieces=pieces, block=block, scale=HD**-0.5),
        grid_spec=pltpu.PrefetchScalarGridSpec(
            num_scalar_prefetch=1,
            grid=(pairs,),
            in_specs=[pl.BlockSpec((3, size, LANES), lambda h, _: (0, 0, h))] * pieces,
            out_specs=[pl.BlockSpec((size, LANES), lambda h, _: (0, h))] * pieces
            + [whole((size, LANES))] * pieces,
            scratch_shapes=[
                pltpu.VMEM((padded, 2 * LANES), BF16),
                pltpu.VMEM((padded, 2 * LANES), BF16),
                pltpu.VMEM((2, padded, 2 * LANES), BF16),
                pltpu.VMEM((padded, LANES), F32),
                pltpu.VMEM((padded, LANES), F32),
            ],
        ),
        out_shape=[jax.ShapeDtypeStruct((size, width), BF16)] * pieces
        + [jax.ShapeDtypeStruct((size, LANES), F32)] * pieces,
        name="attend",
        **params_for(16 * pairs * LANES * padded * padded, 8 * size * width * pieces, pairs * 2 * padded * padded),
    )(valid, *parts)
    return outs[:pieces], outs[pieces:]


def attend_back_kernel(valid, *refs, pieces, block, scale, first):
    in_refs, mix_refs = refs[:pieces], refs[pieces : 2 * pieces]
    grad_refs, total_refs = refs[2 * pieces : 3 * pieces], refs[3 * pieces : 4 * pieces]
    out_refs = refs[-9 - pieces : -9]
    keys, values, queries, grads, queries_t, grads_t, dq, dk_t, dv_t = refs[-9:]
    pair = first + pl.program_id(0)
    size = in_refs[0].shape[1]
    count, padded = pieces * size, keys.shape[0]
    blocks = padded // block
    lane = lane_ids(size)
    row = lax.broadcasted_iota(jnp.int32, (size, LANES), 0)
    for i in range(pieces):
        at = pl.ds(i * size, size)
        keys[at, :LANES] = in_refs[i][1]
        keys[at, LANES:] = jnp.where(
            lane == 0, jnp.where(row >= valid[i], MASKED, 0.0), jnp.where(lane < 4, 1.0, 0.0)
        ).astype(BF16)
        values[at, :LANES] = in_refs[i][2]
        values[at, LANES:] = jnp.where((lane > 0) & (lane < 4), 1.0, 0.0).astype(BF16)
        queries[0, at, :LANES] = in_refs[i][0]
        grads[0, at, :LANES] = grad_refs[i][...]
    if padded > count:
        left = padded - count
        rest = pl.ds(count, left)
        keys[rest, :LANES] = jnp.zeros((left, LANES), BF16)
        keys[rest, LANES:] = jnp.where(lane_ids(left) == 0, MASKED, 0.0).astype(BF16)
        values[rest, :] = jnp.zeros((left, 2 * LANES), BF16)
        for j in range(2):
            queries[j, rest, :] = jnp.zeros((left, 2 * LANES), BF16)
            grads[j, rest, :] = jnp.zeros((left, 2 * LANES), BF16)
    for b in range(blocks):
        at = pl.ds(b * block, block)
        queries_t[b] = (queries[0, at, :LANES].astype(F32) * scale).T.astype(BF16)
        grads_t[b] = turned(grads[0, at, :LANES])
    for j in range(2):
        mine = lane // HD == j
        for i in range(pieces):
            at = pl.ds(i * size, size)
            grad = jnp.where(mine, grad_refs[i][...].astype(F32), 0.0)
            queries[j, at, :LANES] = jnp.where(mine, in_refs[i][0].astype(F32) * scale, 0.0).astype(BF16)
            grads[j, at, :LANES] = grad.astype(BF16)
            log_total = jnp.sum(
                jnp.where(lane == 2 * pair + j, total_refs[i][...], 0.0), axis=1, keepdims=True
            )
            high, mid, low = split3(-log_total)
            queries[j, at, LANES:] = jnp.where(
                lane == 0,
                1.0,
                jnp.where(lane == 1, high, jnp.where(lane == 2, mid, jnp.where(lane == 3, low, 0.0))),
            ).astype(BF16)
            inner = jnp.sum(grad * mix_refs[i][...].astype(F32), axis=1, keepdims=True)
            high, mid, low = split3(-inner)
            grads[j, at, LANES:] = jnp.where(
                lane == 1, high, jnp.where(lane == 2, mid, jnp.where(lane == 3, low, 0.0))
            ).astype(BF16)
    dk_t[...] = jnp.zeros_like(dk_t)
    dv_t[...] = jnp.zeros_like(dv_t)
    block_lane = lane_ids(block)
    for b in range(blocks):
        at = pl.ds(b * block, block)
        results = []
        for j in range(2):
            mine = pl.ds(j * HD, HD)
            probs = jnp.exp(dot(queries[j, at, :], keys[...], NT))
            grad_scores = (probs * dot(grads[j, at, :], values[...], NT)).astype(BF16)
            results.append(dot(grad_scores, keys[:, :LANES]) * scale)
            dv_t[mine, :] += dot(grads_t[b, mine, :], probs.astype(BF16))
            dk_t[mine, :] += dot(queries_t[b, mine, :], grad_scores)
        dq[at, :] = jnp.where(block_lane < HD, results[0], results[1])
    dk, dv = dk_t[...].T, dv_t[...].T
    for i in range(pieces):
        at = slice(i * size, (i + 1) * size)
        out_refs[i][0] = dq[at, :].astype(BF16)
        out_refs[i][1] = dk[at, :].astype(BF16)
        out_refs[i][2] = dv[at, :].astype(BF16)


def attention_back(valid, parts, mixtures, grads, totals, block, first, pairs, into, after):
    pieces = len(parts)
    _, size, width = parts[0].shape
    padded = padded_len(pieces * size, block)
    triple = pl.BlockSpec((3, size, LANES), lambda h, _: (0, 0, first + h))
    single = pl.BlockSpec((size, LANES), lambda h, _: (0, first + h))
    in_specs = [triple] * pieces + [single] * 2 * pieces + [whole((size, LANES))] * pieces
    aliases = {1 + len(in_specs) + i: i for i in range(len(into))}
    return pl.pallas_call(
        functools.partial(attend_back_kernel, pieces=pieces, block=block, scale=HD**-0.5, first=first),
        grid_spec=pltpu.PrefetchScalarGridSpec(
            num_scalar_prefetch=1,
            grid=(pairs,),
            in_specs=in_specs + [pl.BlockSpec(memory_space=pl.ANY)] * (len(into) + len(after)),
            out_specs=[triple] * pieces,
            scratch_shapes=[
                pltpu.VMEM((padded, 2 * LANES), BF16),
                pltpu.VMEM((padded, 2 * LANES), BF16),
                pltpu.VMEM((2, padded, 2 * LANES), BF16),
                pltpu.VMEM((2, padded, 2 * LANES), BF16),
                pltpu.VMEM((padded // block, LANES, block), BF16),
                pltpu.VMEM((padded // block, LANES, block), BF16),
                pltpu.VMEM((padded, LANES), F32),
                pltpu.VMEM((LANES, padded), F32),
                pltpu.VMEM((LANES, padded), F32),
            ],
        ),
        out_shape=[jax.ShapeDtypeStruct((3, size, width), BF16)] * pieces,
        input_output_aliases=aliases,
        name="attend_back",
        **params_for(30 * pairs * LANES * padded * padded, 16 * size * LANES * pairs * pieces, pairs * 2 * padded * padded, weight=LONG),
    )(valid, *parts, *mixtures, *grads, *totals, *into, *after)


def merge_kernel(place, x_ref, own_ref, far_ref, table, own_w, far_w, middle_ref, branch_ref, normed_ref):
    branch = dot(own_ref[...], own_w[...]) + dot(far_ref[...], far_w[...])
    branch += table[OUT_SHIFT : OUT_SHIFT + 1, :]
    middle = x_ref[...].astype(F32) + table[SCALE1 : SCALE1 + 1, :] * branch
    middle_ref[...] = middle
    branch_ref[...] = branch
    normed_ref[...] = normalize(
        middle, table[GAIN2 : GAIN2 + 1, :], table[SHIFT2 : SHIFT2 + 1, :]
    ).astype(BF16)


ROWS = 352


def row_steps(tokens):
    return -(-tokens // ROWS)


def merge(place, x, own, far, table, rest):
    tokens, width = x.shape
    half = width // 2
    wide = pl.BlockSpec((ROWS, width), lambda i, _: (i, 0))
    narrow = pl.BlockSpec((ROWS, half), lambda i, _: (i, 0))
    return pl.pallas_call(
        merge_kernel,
        grid_spec=pltpu.PrefetchScalarGridSpec(
            num_scalar_prefetch=1,
            grid=(row_steps(tokens),),
            in_specs=[
                wide,
                narrow,
                narrow,
                whole(table.shape),
                pl.BlockSpec((half, width), lambda i, place: (place[CORE], rest.shape[1] // width - 1)),
                pl.BlockSpec((half, width), lambda i, place: (1 - place[CORE], rest.shape[1] // width - 1)),
            ],
            out_specs=[wide, wide, wide],
        ),
        out_shape=[
            jax.ShapeDtypeStruct((tokens, width), F32),
            jax.ShapeDtypeStruct((tokens, width), F32),
            jax.ShapeDtypeStruct((tokens, width), BF16),
        ],
        name="merge",
        **params_for(2 * tokens * width * width, 14 * tokens * width + 2 * width * width),
    )(place, x, own, far, table, rest, rest)


def gelu_and_slope(values):
    size = jnp.abs(values) * 0.7071067811865476
    t = 1.0 / (1.0 + 0.3275911 * size)
    bell = jnp.exp(-0.5 * (values * values))
    poly = t * (0.254829592 + t * (-0.284496736 + t * (1.421413741 + t * (-1.453152027 + t * 1.061405429))))
    tail = 0.5 * poly * bell
    phi = jnp.where(values < 0, tail, 1.0 - tail)
    return values * phi, phi + values * bell * 0.3989422804014327


def ungroup(grouped_ref, down):
    width = down.shape[1]
    groups = grouped_ref.shape[1] // width
    each = grouped_ref.shape[0] // 2
    for device in range(2):
        for g in range(groups):
            at = (device * groups + g) * each
            down[at : at + each, :] = grouped_ref[device * each : (device + 1) * each, g * width : (g + 1) * width]


def scaled_upstream(cotangent_ref, table):
    return (cotangent_ref[...].astype(F32) * table[SCALE2 : SCALE2 + 1, :]).astype(BF16)


def place_turned(place, block, target, k, chips):
    half = block.shape[1] // 2
    turned_block = block.T
    first, second = turned_block[:half], turned_block[half:]
    target[k * half : (k + 1) * half, :] = jnp.where(place[CORE] == 0, first, second)
    target[(chips + k) * half : (chips + k + 1) * half, :] = jnp.where(place[CORE] == 0, second, first)


def fill_turned(place, source_ref, target, chips):
    wide = source_ref.shape[1] // chips
    for k in range(chips):
        at = pl.ds(pl.multiple_of(place[CHIPS + k] * wide, wide), wide)
        place_turned(place, source_ref[:, at], target, k, chips)


def split_rows(grad, mine_ref, other_ref):
    chips, rows, _ = mine_ref.shape
    for k in range(chips):
        mine_ref[k] = grad[k * rows : (k + 1) * rows, :]
        other_ref[k] = grad[(chips + k) * rows : (chips + k + 1) * rows, :]


def group(grad, out_ref):
    rows, columns = out_ref.shape[1], grad.shape[1]
    for g in range(grad.shape[0] // rows):
        out_ref[0, :, g * columns : (g + 1) * columns] = grad[g * rows : (g + 1) * rows, :]


def mlp_kernel(
    place, normed_ref, cotangent_ref, table, up_ref, shift_ref, grouped_ref,
    branch_ref, delta_ref, up_mine_ref, up_other_ref, down_mine_ref, down_other_ref, grad_shift_ref,
    upstream, upstream_t, normed_t, down,
    *, chips,
):
    @pl.when(pl.program_id(0) == 0)
    def _():
        scaled = (cotangent_ref[...].astype(F32) * table[SCALE2 : SCALE2 + 1, :]).astype(BF16)
        upstream[...] = scaled
        upstream_t[...] = turned(scaled)
        fill_turned(place, normed_ref, normed_t, chips)
        branch_ref[...] = jnp.zeros_like(branch_ref)
        delta_ref[...] = jnp.zeros_like(delta_ref)

    ungroup(grouped_ref, down)
    hidden = dot(normed_ref[...], up_ref[...]) + shift_ref[...]
    grad_active = dot(upstream[...], down[...], NT)
    active, slope = gelu_and_slope(hidden)
    active = active.astype(BF16)
    delta_hidden = (grad_active * slope).astype(BF16)
    branch_ref[...] += dot(active, down[...])
    delta_ref[...] += dot(delta_hidden, up_ref[...], NT)
    split_rows(dot(normed_t[...], delta_hidden).astype(BF16), up_mine_ref, up_other_ref)
    grad_down = dot(upstream_t[...], active)
    each = grad_down.shape[1] // 2
    first, second = grad_down[:, :each], grad_down[:, each:]
    group(jnp.where(place[CORE] == 0, first, second).astype(BF16), down_mine_ref)
    group(jnp.where(place[CORE] == 0, second, first).astype(BF16), down_other_ref)
    grad_shift_ref[...] = total_rows(delta_hidden.astype(F32))


def mlp(place, normed, cotangent, table, rest, up_shift, owners):
    tokens, width = normed.shape
    hidden = up_shift.shape[1]
    rows = rest.shape[0] // owners
    chips = owners // 2
    block = hidden // chips
    up_out = pl.BlockSpec((chips, rows, block), lambda j, place: (0, 0, place[CHIPS + j]))
    down_out = pl.BlockSpec((1, rows, hidden), lambda j, _: (j, 0, 0))
    sent = jax.ShapeDtypeStruct((chips, rows, hidden), BF16)
    return pl.pallas_call(
        functools.partial(mlp_kernel, chips=chips),
        grid_spec=pltpu.PrefetchScalarGridSpec(
            num_scalar_prefetch=1,
            grid=(chips,),
            in_specs=[
                whole((tokens, width)),
                whole((tokens, width)),
                whole(table.shape),
                pl.BlockSpec((width, block), lambda j, place: (0, place[CHIPS + j])),
                pl.BlockSpec((1, block), lambda j, place: (0, place[CHIPS + j])),
                pl.BlockSpec((2 * rows, hidden), lambda j, place: (place[CHIPS + j], 1)),
            ],
            out_specs=[
                whole((tokens, width)),
                whole((tokens, width)),
                up_out,
                up_out,
                down_out,
                down_out,
                pl.BlockSpec((1, block), lambda j, place: (0, place[CHIPS + j])),
            ],
            scratch_shapes=[
                pltpu.VMEM((tokens, width), BF16),
                pltpu.VMEM((width, tokens), BF16),
                pltpu.VMEM((width, tokens), BF16),
                pltpu.VMEM((block, width), BF16),
            ],
        ),
        out_shape=[
            jax.ShapeDtypeStruct((tokens, width), F32),
            jax.ShapeDtypeStruct((tokens, width), F32),
            sent,
            sent,
            sent,
            sent,
            jax.ShapeDtypeStruct((1, hidden), F32),
        ],
        name="mlp",
        **params_for(12 * tokens * width * hidden, 12 * tokens * width + 8 * width * hidden, 2 * tokens * hidden),
    )(place, normed, cotangent, table, rest, up_shift, rest)


SUM_ROWS = 8


def unmerge_kernel(
    place, middle_ref, branch1_ref, branch2_ref, delta_ref, cotangent_ref, own_ref, far_ref, table, own_w, far_w,
    output_ref, delta_middle_ref, own_grad_ref, far_grad_ref, mine_ref, other_ref, sums_ref,
    delta1_all, mixture_t,
    *, tokens,
):
    step = pl.program_id(0)

    @pl.when(step == 0)
    def _():
        sums_ref[...] = jnp.zeros_like(sums_ref)

    rows, width = middle_ref.shape
    inside = lax.broadcasted_iota(jnp.int32, (rows, width), 0) + step * rows < tokens

    def kept(values):
        return jnp.where(inside, values, 0.0)

    upstream = cotangent_ref[...].astype(F32)
    scale2 = table[SCALE2 : SCALE2 + 1, :]
    middle = middle_ref[...]
    branch2 = branch2_ref[...] + table[DOWN_SHIFT : DOWN_SHIFT + 1, :]
    output_ref[...] = (middle + scale2 * branch2).astype(BF16)
    delta2 = (scale2 * upstream).astype(BF16).astype(F32)
    delta = delta_ref[...]
    inner, gain_terms = normalize_back(middle, table[GAIN2 : GAIN2 + 1, :], delta)
    delta_middle = upstream + inner
    delta_middle_ref[...] = delta_middle
    delta1 = kept(table[SCALE1 : SCALE1 + 1, :] * delta_middle).astype(BF16)
    delta1_all[pl.ds(pl.multiple_of(step * rows, 16), rows), :] = delta1
    own_grad_ref[...] = dot(delta1, own_w[...], NT).astype(BF16)
    far_grad_ref[...] = dot(delta1, far_w[...], NT).astype(BF16)
    terms = (
        upstream * branch2,
        delta2,
        gain_terms,
        delta,
        delta_middle * branch1_ref[...],
        delta1.astype(F32),
    )
    for i, term in enumerate(terms):
        sums_ref[i : i + 1, :] += total_rows(kept(term))

    @pl.when(step == pl.num_programs(0) - 1)
    def _():
        chips = mine_ref.shape[0]
        wide = width // chips
        for k in range(chips):
            chip = place[CHIPS + k]
            at = pl.ds(pl.multiple_of(lax.rem(chip, chips // 2) * wide, wide), wide)
            mixed = jnp.where(chip // (chips // 2) == place[CORE], own_ref[:, at], far_ref[:, at])
            place_turned(place, mixed, mixture_t, k, chips)
        split_rows(dot(mixture_t[...], delta1_all[:tokens, :]).astype(BF16), mine_ref, other_ref)


def unmerge(place, middle, branch1, branch2, delta, cotangent, own, far, table, rest, owners):
    tokens, width = middle.shape
    chips = owners // 2
    sent = (chips, width // owners, width)
    half = width // 2
    steps = row_steps(tokens)
    wide = pl.BlockSpec((ROWS, width), lambda i, _: (i, 0))
    narrow = pl.BlockSpec((ROWS, half), lambda i, _: (i, 0))
    return pl.pallas_call(
        functools.partial(unmerge_kernel, tokens=tokens),
        grid_spec=pltpu.PrefetchScalarGridSpec(
            num_scalar_prefetch=1,
            grid=(steps,),
            in_specs=[wide] * 5
            + [whole((tokens, half))] * 2
            + [
                whole(table.shape),
                pl.BlockSpec((half, width), lambda i, place: (place[CORE], rest.shape[1] // width - 1)),
                pl.BlockSpec((half, width), lambda i, place: (1 - place[CORE], rest.shape[1] // width - 1)),
            ],
            out_specs=[wide, wide, narrow, narrow, whole(sent), whole(sent), whole((SUM_ROWS, width))],
            scratch_shapes=[pltpu.VMEM((steps * ROWS, width), BF16), pltpu.VMEM((width, tokens), BF16)],
        ),
        out_shape=[
            jax.ShapeDtypeStruct((tokens, width), BF16),
            jax.ShapeDtypeStruct((tokens, width), F32),
            jax.ShapeDtypeStruct((tokens, half), BF16),
            jax.ShapeDtypeStruct((tokens, half), BF16),
            jax.ShapeDtypeStruct(sent, BF16),
            jax.ShapeDtypeStruct(sent, BF16),
            jax.ShapeDtypeStruct((SUM_ROWS, width), F32),
        ],
        name="unmerge",
        **params_for(4 * tokens * width * width, 30 * tokens * width + 4 * width * width),
    )(place, middle, branch1, branch2, delta, cotangent, own, far, table, rest, rest)


def unproject_kernel(
    place, x_hbm, delta_middle_hbm, table, normed_ref, own_ref, far_ref, weight_ref, middle_sums, up_sums, *refs, chips
):
    (
        out_ref, mine_ref, other_ref, vectors_mine_ref, vectors_other_ref,
        delta, sums, normed_t, x_ref, delta_middle_ref, arrived,
    ) = refs
    step = pl.program_id(0)
    core = place[CORE]
    copies = [
        pltpu.make_async_copy(x_hbm, x_ref, arrived.at[0]),
        pltpu.make_async_copy(delta_middle_hbm, delta_middle_ref, arrived.at[1]),
    ]

    @pl.when(step == 0)
    def _():
        for copy in copies:
            copy.start()
        fill_turned(place, normed_ref, normed_t, chips)
        delta[...] = jnp.zeros_like(delta)
        sums[...] = jnp.zeros_like(sums)

    own, far = own_ref[0], far_ref[0]
    block = jnp.concatenate([jnp.where(core == 0, own, far), jnp.where(core == 0, far, own)], axis=1)
    split_rows(dot(normed_t[...], block).astype(BF16), mine_ref, other_ref)
    delta[...] += dot(block, weight_ref[...], NT)
    for kind, row in ((0, QUERY), (2, VALUE)):

        @pl.when(step == kind)
        def _():
            sums[row : row + 1, :] = total_rows(block.astype(F32))

    @pl.when(step == pl.num_programs(0) - 1)
    def _():
        for copy in copies:
            copy.wait()
        delta_normed = delta[...]
        inner, gain_terms = normalize_back(
            x_ref[...].astype(F32), table[GAIN1 : GAIN1 + 1, :], delta_normed
        )
        out_ref[...] = (delta_middle_ref[...] + inner).astype(BF16)
        rows = {
            GAIN1: total_rows(gain_terms),
            SHIFT1: total_rows(delta_normed),
            OUT_SHIFT: middle_sums[5:6, :],
            SCALE1: middle_sums[4:5, :],
            GAIN2: middle_sums[2:3, :],
            SHIFT2: middle_sums[3:4, :],
            DOWN_SHIFT: middle_sums[1:2, :],
            SCALE2: middle_sums[0:1, :],
        }
        for i, values in rows.items():
            sums[i : i + 1, :] = values
        each = up_sums.shape[1] // (2 * chips)
        for out, side in ((vectors_mine_ref, core), (vectors_other_ref, 1 - core)):
            out[...] = jnp.zeros_like(out)
            for k in range(chips):
                chip = place[CHIPS + k]
                at = pl.ds(pl.multiple_of(chip * LANES, LANES), LANES)
                out[k, : sums.shape[0], :] = sums[:, at].astype(BF16)
                for r in range(each // LANES):
                    at = pl.multiple_of((2 * chip + side) * each + r * LANES, LANES)
                    row = up_sums[:, pl.ds(at, LANES)].astype(BF16)
                    out[k, VECTORS + r : VECTORS + r + 1, :] = row


def unproject(place, x, delta_middle, table, normed, own, far, weight, middle_sums, up_sums, owners):
    tokens, width = x.shape
    half = width // 2
    chips = owners // 2
    rows = width // owners
    vectors = (chips, rows, LANES)
    anywhere = pl.BlockSpec(memory_space=pl.ANY)
    kind = pl.BlockSpec((1, tokens, half), lambda j, _: (j, 0, 0))
    sent = pl.BlockSpec((chips, rows, width), lambda j, _: (0, 0, j))
    return pl.pallas_call(
        functools.partial(unproject_kernel, chips=chips),
        grid_spec=pltpu.PrefetchScalarGridSpec(
            num_scalar_prefetch=1,
            grid=(3,),
            in_specs=[
                anywhere,
                anywhere,
                whole(table.shape),
                whole((tokens, width)),
                kind,
                kind,
                pl.BlockSpec((width, width), lambda j, _: (0, j)),
                whole(middle_sums.shape),
                whole(up_sums.shape),
            ],
            out_specs=[whole((tokens, width)), sent, sent, whole(vectors), whole(vectors)],
            scratch_shapes=[
                pltpu.VMEM((tokens, width), F32),
                pltpu.VMEM((16, width), F32),
                pltpu.VMEM((width, tokens), BF16),
                pltpu.VMEM((tokens, width), BF16),
                pltpu.VMEM((tokens, width), F32),
                pltpu.SemaphoreType.DMA((2,)),
            ],
        ),
        out_shape=[
            jax.ShapeDtypeStruct((tokens, width), BF16),
            jax.ShapeDtypeStruct((chips, rows, 3 * width), BF16),
            jax.ShapeDtypeStruct((chips, rows, 3 * width), BF16),
            jax.ShapeDtypeStruct(vectors, BF16),
            jax.ShapeDtypeStruct(vectors, BF16),
        ],
        name="unproject",
        **params_for(12 * tokens * width * width, 18 * tokens * width + 12 * width * width, weight=SHORT),
    )(place, x, delta_middle, table, normed, own, far, weight, middle_sums, up_sums)


def ring_of(chips):
    return list(range(0, chips, 2)) + list(range(1, chips, 2))[::-1]


def places(owners):
    ring = ring_of(owners // 2)
    rows = []
    for f in range(owners):
        chip, core = divmod(f, 2)
        at = ring.index(chip)
        columns = [1 - core, 3 - core, 5 - core, core, 2 + core, 4 + core]
        rows.append(columns + [core] + ring[at:] + ring[:at])
    return np.array(rows, np.int32)


def ring_perm(chips, hop):
    ring = ring_of(chips)
    return [
        (2 * ring[i] + core, 2 * ring[(i + hop) % chips] + core) for i in range(chips) for core in range(2)
    ]


def to_next(values, chips, hop):
    return lax.ppermute(values, "fsdp", ring_perm(chips, hop))


def ring_gather(piece, chips):
    pieces = [None] * chips
    pieces[0] = right = left = piece
    for k in range(1, chips // 2 + 1):
        pieces[-k] = right = to_next(right, chips, 1)
        if k < chips - chips // 2:
            pieces[k] = left = to_next(left, chips, -1)
    return pieces


def low_part(columns):
    return columns // 2 if columns % (2 * LANES) == 0 else columns


def ring_add_kernel(*refs, columns, mode, carried):
    ways = 2 if mode in ("second", "next") else 1
    shares = [refs[2 * len(columns) * d : 2 * len(columns) * (d + 1)] for d in range(ways)]
    came = refs[2 * len(columns) * ways :]
    outs = refs[len(refs) - carried - (1 if mode == "total" else 2) : len(refs) - carried]
    start, low_start, high_start = 0, 0, 0
    for i, each in enumerate(columns):
        totals = [mine[2 * i][0].astype(F32) + mine[2 * i + 1][0].astype(F32) for mine in shares]
        at = slice(start, start + each)
        low = low_part(each)
        low_at, high_at = slice(low_start, low_start + low), slice(high_start, high_start + each - low)
        if mode == "first":
            outs[0][:, low_at] = totals[0][:, :low].astype(BF16)
            if low < each:
                outs[1][:, high_at] = totals[0][:, low:].astype(BF16)
        elif mode == "second":
            outs[0][:, start : start + low] = (totals[0][:, :low] + came[0][:, low_at].astype(F32)).astype(BF16)
            outs[1][:, start : start + low] = totals[1][:, :low].astype(BF16)
            if low < each:
                high = totals[1][:, low:] + came[1][:, high_at].astype(F32)
                outs[0][:, start + low : start + each] = totals[0][:, low:].astype(BF16)
                outs[1][:, start + low : start + each] = high.astype(BF16)
        elif mode == "next":
            for total, arrived, out in zip(totals, came, outs):
                out[:, at] = (total + arrived[:, at].astype(F32)).astype(BF16)
        else:
            both_ways = came[0][:, at].astype(F32) + came[1][:, at].astype(F32)
            outs[0][:, at] = (totals[0] + both_ways).astype(BF16)
        start, low_start, high_start = at.stop, low_at.stop, high_at.stop


class RingSum:
    def __init__(self, *parts):
        self.parts, self.chips = [part[:2] for part in parts], parts[0][0].shape[0]
        self.columns = [part[0].shape[2] // part[3] for part in parts]
        self.blocks = [part[2] for part in parts]
        self.steps = self.chips // 2
        self.step = 0
        self.came = []

    def add(self, mode, places, after=(), carry=()):
        rows = self.parts[0][0].shape[1]
        columns = self.columns
        total = sum(columns)
        blocks = 2 if total > 4096 else 1
        arrays, specs = [], []
        for at in places:
            for part, each, block in zip(self.parts, columns, self.blocks):
                for array in part:
                    arrays.append(array)
                    specs.append(pl.BlockSpec((1, rows // blocks, each), lambda i, at=at, block=block: (at, i, block)))
        for came in self.came:
            arrays.append(came)
            specs.append(pl.BlockSpec((rows // blocks, came.shape[1]), lambda i: (i, 0)))
        arrays += [*after, *carry]
        anywhere = pl.BlockSpec(memory_space=pl.ANY)
        specs += [anywhere] * (len(after) + len(carry))
        low = sum(low_part(each) for each in columns)
        out_columns = {"first": [low, total - low], "total": [total]}.get(mode, [total, total])
        sums = len(out_columns)
        outs = pl.pallas_call(
            functools.partial(ring_add_kernel, columns=columns, mode=mode, carried=len(carry)),
            grid=(blocks,),
            in_specs=specs,
            out_specs=[pl.BlockSpec((rows // blocks, out), lambda i: (i, 0)) for out in out_columns]
            + [anywhere] * len(carry),
            out_shape=[jax.ShapeDtypeStruct((rows, out), BF16) for out in out_columns]
            + [jax.ShapeDtypeStruct(array.shape, array.dtype) for array in carry],
            input_output_aliases={len(arrays) - len(carry) + i: sums + i for i in range(len(carry))},
            name="ring_add",
            **params_for(6 * rows * total, 16 * rows * total, weight=SHORT, vmem=VMEM_LIMIT if blocks > 1 else SMALL_VMEM),
        )(*arrays)
        return outs[:sums], outs[sums:]

    def sums(self, after=(), carry=()):
        k = self.steps - self.step
        if self.step == 0:
            return self.add("first", [k], after, carry)
        return self.add("second" if self.step == 1 else "next", [k, self.chips - k], after, carry)

    def send(self, sums):
        self.came = [to_next(sums[0], self.chips, 1), to_next(sums[1], self.chips, -1)]
        self.step += 1

    def total(self, after=(), carry=()):
        assert self.step == self.steps
        sums, carried = self.add("total", [0], after, carry)
        return sums[0], carried


def passed(arrays, after):
    anywhere = pl.BlockSpec(memory_space=pl.ANY)
    return pl.pallas_call(
        lambda *refs: None,
        in_specs=[anywhere] * (len(arrays) + len(after)),
        out_specs=[anywhere] * len(arrays),
        out_shape=[jax.ShapeDtypeStruct(array.shape, array.dtype) for array in arrays],
        input_output_aliases={i: i for i in range(len(arrays))},
        name="passed",
        **params_for(1, 1, vmem=SMALL_VMEM),
    )(*arrays, *after)


def finish_rest_kernel(part_ref, came_ref, up_ref, down_ref):
    def total(at):
        return part_ref[:, at].astype(F32) + came_ref[:, at].astype(F32)

    rows, hidden = up_ref.shape
    each, width = down_ref.shape
    up_ref[...] = total(slice(0, hidden))
    for g in range(0, width // rows, 2):
        pair = [total(slice(hidden + each * h, hidden + each * (h + 1))) for h in (g, g + 1)]
        down_ref[:, g * rows : (g + 2) * rows] = jnp.concatenate(pair, axis=0).T


def finish_rest(part, came, hidden, each, width):
    in_vmem = pl.BlockSpec(memory_space=pltpu.VMEM)
    rows = part.shape[0]
    return pl.pallas_call(
        finish_rest_kernel,
        in_specs=[in_vmem] * 2,
        out_specs=[in_vmem] * 2,
        out_shape=[jax.ShapeDtypeStruct(shape, F32) for shape in ((rows, hidden), (each, width))],
        name="finish_rest",
        **params_for(part.size, 8 * part.size, weight=SHORT, vmem=2 * SMALL_VMEM),
    )(part, came)


def finish_first_kernel(place, *refs):
    parts, came, (packed_ref, output_ref), vector_refs = refs[:2], refs[2:4], refs[4:6], refs[6:]
    packed, out = packed_ref.shape[1] // 2, output_ref.shape[1] // 2
    for i in range(2):
        total = parts[i][...].astype(F32) + came[i][...].astype(F32)
        packed_ref[:, packed * i : packed * (i + 1)] = total[:, :packed]
        output_ref[:, out * i : out * (i + 1)] = total[:, packed : packed + out]
        if i == 0:
            vectors = total[:16, packed + out :]
    half = LANES // 2
    mine = jnp.where(place[CORE] == 0, vectors[:, :half], vectors[:, half:])
    for i in range(VECTORS):
        vector_refs[i][...] = mine[i : i + 1, :].reshape(half)
    count = vector_refs[VECTORS].shape[0]
    vector_refs[VECTORS][...] = vectors[VECTORS : VECTORS + count // LANES, :].reshape(count)


def finish_first(place, parts, came, width, each):
    in_vmem = pl.BlockSpec(memory_space=pltpu.VMEM)
    rows = parts[0].shape[0]
    shapes = [(rows, 3 * width), (rows, width)] + [(rows,)] * VECTORS + [(each,)]
    return pl.pallas_call(
        finish_first_kernel,
        in_specs=[pl.BlockSpec(memory_space=pltpu.SMEM)] + [in_vmem] * 4,
        out_specs=[in_vmem] * len(shapes),
        out_shape=[jax.ShapeDtypeStruct(shape, F32) for shape in shapes],
        name="finish_first",
        **params_for(8 * rows * width, 32 * rows * width, weight=SHORT, vmem=SMALL_VMEM),
    )(place, *parts, *came)


def split_pairs(pairs):
    return [pairs // 4, pairs // 2, pairs - pairs // 4 - pairs // 2] if pairs >= 4 else [pairs]


def paired_body(
    tokens, lengths, norm1_gain, norm1_bias, packed_weight, query_bias, value_bias, output_weight, output_bias,
    layer_scale1, norm2_gain, norm2_bias, up_weight, up_bias, down_weight, down_bias, layer_scale2, cotangent,
):
    owners = lax.axis_size("fsdp")
    chips = owners // 2
    _, local_len, width = tokens.shape
    me = lax.axis_index("fsdp")
    core = lax.rem(me, 2)
    place = lax.dynamic_index_in_dim(jnp.asarray(places(owners)), me, keepdims=False)
    moves = [(f * 2 + s, (f - f % 2 + s) * 2 + f % 2) for f in range(owners) for s in range(2) if f % 2 != s]
    twin = [(f, f ^ 1) for f in range(owners)]
    stays = core == lax.axis_index("seq")

    def regroup_moves(values):
        return lax.ppermute(values, ("fsdp", "seq"), moves)

    def regrouped(values):
        return jnp.where(stays, values, regroup_moves(values))

    def to_twin(values):
        return lax.ppermute(values, "fsdp", twin)

    def across(values):
        return lax.ppermute(values, "seq", [(0, 1), (1, 0)])

    vectors = (
        norm1_gain, norm1_bias, query_bias, value_bias, output_bias, layer_scale1, norm2_gain, norm2_bias,
        down_bias, layer_scale2,
    )
    rows = norm1_gain.shape[0]
    hidden = up_weight.shape[1]
    first, rest = pack(place, packed_weight, up_weight, down_weight, output_weight, vectors, up_bias)
    own_pieces = ring_gather(first, chips)
    far_pieces = [to_twin(piece) for piece in own_pieces]
    x = regrouped(tokens.reshape(local_len, width))
    valid_count = regrouped(lengths)
    rest = lax.all_gather(rest, "fsdp", axis=0, tiled=True)
    starts = jnp.stack([core, 1 - core]) * local_len
    valid = jnp.clip(valid_count - starts, 0, local_len).astype(jnp.int32)
    upstream = regrouped(cotangent.reshape(local_len, width))

    far_out, own_part, normed, packed_full, table, up_shift = project(place, x, own_pieces, far_pieces, hidden)
    far_part = to_twin(far_out)
    parts = [own_part, far_part]
    (own_mix, far_mix_out), totals = attention(valid, parts, 352)
    far_mix = to_twin(far_mix_out)
    middle, branch1, normed2 = merge(place, x, own_mix, far_mix, table, rest)

    branch2, delta_normed2, up_mine, up_other, down_mine, down_other, up_sums = mlp(
        place, normed2, upstream, table, rest, up_shift, owners
    )
    up_twin, down_twin = to_twin(up_other), to_twin(down_other)
    output, delta_middle, own_grad, far_grad_out, output_mine, output_other, middle_sums = unmerge(
        place, middle, branch1, branch2, delta_normed2, upstream, own_mix, far_mix, table, rest, owners
    )
    far_grad = to_twin(far_grad_out)
    ring = RingSum((up_mine, up_twin, 0, 1), (down_mine, down_twin, 0, 1))
    output_sent = regroup_moves(output)
    output_twin = to_twin(output_other)
    deltas = ()
    grads = [own_grad, far_grad]
    start = 0
    for pairs in split_pairs(width // 2 // LANES):
        sums, _ = ring.sums()
        ring.send(sums)
        after = [*sums, output_sent, output_twin] if start else sums
        deltas = attention_back(
            valid, parts, [own_mix, far_mix_out], grads, totals, 352, start, pairs, deltas, after
        )
        start += pairs
    own_delta, far_delta_out = deltas
    sums, (far_delta_out,) = ring.sums(carry=[far_delta_out])
    ring.send(sums)
    far_delta = to_twin(far_delta_out)
    grad_x, packed_mine, packed_other, vectors_mine, vectors_other = unproject(
        place, x, delta_middle, table, normed, own_delta, far_delta, packed_full, middle_sums, up_sums, owners
    )
    output = jnp.where(stays, output, output_sent).reshape(tokens.shape)
    grad_x, packed_other, vectors_other = passed([grad_x, packed_other, vectors_other], ring.came)
    vectors_twin, packed_twin = to_twin(vectors_other), to_twin(packed_other)
    rest_sum, _ = ring.total()
    rings = (
        RingSum(
            (packed_mine, packed_twin, 0, 2), (output_mine, output_twin, 0, 2), (vectors_mine, vectors_twin, 0, 1)
        ),
        RingSum((packed_mine, packed_twin, 1, 2), (output_mine, output_twin, 1, 2)),
    )
    grad_x_sent, rest_sent = regroup_moves(grad_x), across(rest_sum)
    last = [rest_sum]
    for step in range(rings[0].steps):
        for half in rings:
            after = [*last] + ([grad_x_sent] if step == 2 and half is rings[0] else [])
            last, _ = half.sums(after)
            half.send(last)
    grad_tokens = jnp.where(stays, grad_x, grad_x_sent).astype(F32).reshape(tokens.shape)
    each = up_bias.shape[0]
    grad_up, grad_down = finish_rest(rest_sum, rest_sent, hidden, each, width)
    first_sum, _ = rings[0].total()
    first_sums = [first_sum, rings[1].total([first_sum])[0]]
    grad_packed, grad_output, *mine = finish_first(
        place, first_sums, [across(half) for half in first_sums], width, each
    )
    return (
        output, grad_tokens, mine[0], mine[1], grad_packed, mine[2], mine[3], grad_output, mine[4], mine[5],
        mine[6], mine[7], grad_up, mine[10], grad_down, mine[8], mine[9],
    )


def pairable(tokens, up_weight):
    owners, chips = lax.axis_size("fsdp"), lax.axis_size("fsdp") // 2
    width, hidden = up_weight.shape[0] * owners, up_weight.shape[1]
    return (
        lax.axis_size("seq") == 2
        and tokens.shape[0] == 1
        and tokens.shape[1] % 16 == 0
        and owners == 2 * chips
        and chips in (4, 8)
        and width % (chips * LANES) == 0
        and hidden % (owners * LANES) == 0
        and H * HD == width
    )


def body(*args):
    chosen = paired_body if pairable(args[0], args[12]) else general_body
    return chosen(*args)


def solution(mesh):
    in_specs = (
        P("fsdp", "seq", None),
        P("fsdp"),
        P("fsdp"),
        P("fsdp"),
        P("fsdp", None),
        P("fsdp"),
        P("fsdp"),
        P("fsdp", None),
        P("fsdp"),
        P("fsdp"),
        P("fsdp"),
        P("fsdp"),
        P("fsdp", None),
        P("fsdp"),
        P("fsdp", None),
        P("fsdp"),
        P("fsdp"),
        P("fsdp", "seq", None),
    )
    out_specs = (
        P("fsdp", "seq", None),
        P("fsdp", "seq", None),
        P("fsdp"),
        P("fsdp"),
        P("fsdp", None),
        P("fsdp"),
        P("fsdp"),
        P("fsdp", None),
        P("fsdp"),
        P("fsdp"),
        P("fsdp"),
        P("fsdp"),
        P("fsdp", None),
        P("fsdp"),
        P("fsdp", None),
        P("fsdp"),
        P("fsdp"),
    )
    return jax.shard_map(body, mesh=mesh, in_specs=in_specs, out_specs=out_specs, check_vma=False)
```

```python
import functools

import jax
import jax.numpy as jnp
import numpy as np
from jax import lax
from jax.experimental import pallas as pl
from jax.experimental.pallas import tpu as pltpu
from jax.sharding import PartitionSpec as P

H = 16
HD = 64


norm_eps = 1e-06


def layer_norm(values, norm_gain, norm_shift):
    center = values - jnp.mean(values, axis=-1, keepdims=True)
    spread = jnp.mean(center * center, axis=-1, keepdims=True)
    return center * lax.rsqrt(spread + norm_eps) * norm_gain + norm_shift


def gelu_exact(values):
    return jax.nn.gelu(values, approximate=False)


def matmul(left, right):
    return jnp.dot(left, right, preferred_element_type=jnp.float32)


def left_outer(left, right):
    return jnp.einsum("ti,tj->ij", left, right, preferred_element_type=jnp.float32)


def right_back(left, right):
    return jnp.einsum("tj,ij->ti", left, right, preferred_element_type=jnp.float32)


def column_sum(values):
    return jnp.sum(values.astype(jnp.float32), axis=0)


def attention_probs(queries, key_rows, valid_count, score_scale):
    scores = score_scale * jnp.einsum(
        "qhd,khd->hqk", queries, key_rows, preferred_element_type=jnp.float32
    )
    key_valid = jnp.arange(key_rows.shape[0]) < valid_count
    scores = jnp.where(key_valid[None, None, :], scores, -jnp.inf)
    return scores


def attend(queries, key_rows, values, valid_count, score_scale):
    scores = attention_probs(queries, key_rows, valid_count, score_scale)
    largest = jnp.max(scores, axis=-1, keepdims=True)
    log_total = largest[..., 0] + jnp.log(jnp.sum(jnp.exp(scores - largest), axis=-1))
    attention = jnp.exp(scores - log_total[..., None]).astype(jnp.bfloat16)
    mixture = jnp.einsum("hqk,khd->qhd", attention, values, preferred_element_type=jnp.float32)
    return (mixture.astype(jnp.bfloat16), log_total)


def attend_back(queries, key_rows, values, valid_count, score_scale, log_total, grad_mixture):
    scores = attention_probs(queries, key_rows, valid_count, score_scale)
    probs = jnp.exp(scores - log_total[..., None])
    grad_values = jnp.einsum(
        "hqk,qhd->khd", probs.astype(jnp.bfloat16), grad_mixture, preferred_element_type=jnp.float32
    )
    grad_probs = jnp.einsum(
        "qhd,khd->hqk", grad_mixture, values, preferred_element_type=jnp.float32
    )
    inner_sum = jnp.sum(probs * grad_probs, axis=-1, keepdims=True)
    grad_scores = (probs * (grad_probs - inner_sum)).astype(jnp.bfloat16)
    grad_queries = score_scale * jnp.einsum(
        "hqk,khd->qhd", grad_scores, key_rows, preferred_element_type=jnp.float32
    )
    grad_keys = score_scale * jnp.einsum(
        "hqk,qhd->khd", grad_scores, queries, preferred_element_type=jnp.float32
    )
    return (grad_queries, grad_keys, grad_values)


def general_body(
    tokens,
    lengths,
    norm1_gain,
    norm1_bias,
    packed_weight,
    query_bias,
    value_bias,
    output_weight,
    output_bias,
    layer_scale1,
    norm2_gain,
    norm2_bias,
    up_weight,
    up_bias,
    down_weight,
    down_bias,
    layer_scale2,
    cotangent,
):
    gathered = (
        lax.all_gather(norm1_gain, "fsdp", axis=0, tiled=True),
        lax.all_gather(norm1_bias, "fsdp", axis=0, tiled=True),
        lax.all_gather(packed_weight, "fsdp", axis=0, tiled=True),
        lax.all_gather(query_bias, "fsdp", axis=0, tiled=True),
        lax.all_gather(value_bias, "fsdp", axis=0, tiled=True),
        lax.all_gather(output_weight, "fsdp", axis=0, tiled=True),
        lax.all_gather(output_bias, "fsdp", axis=0, tiled=True),
        lax.all_gather(layer_scale1, "fsdp", axis=0, tiled=True),
        lax.all_gather(norm2_gain, "fsdp", axis=0, tiled=True),
        lax.all_gather(norm2_bias, "fsdp", axis=0, tiled=True),
        lax.all_gather(up_weight, "fsdp", axis=0, tiled=True),
        lax.all_gather(up_bias, "fsdp", axis=0, tiled=True),
        lax.all_gather(down_weight, "fsdp", axis=0, tiled=True),
        lax.all_gather(down_bias, "fsdp", axis=0, tiled=True),
        lax.all_gather(layer_scale2, "fsdp", axis=0, tiled=True),
    )
    (
        gain_one,
        shift_one,
        packed_full,
        query_shift,
        value_shift,
        output_full,
        output_shift,
        scale_one,
        gain_two,
        shift_two,
        up_full,
        up_shift,
        down_full,
        down_shift,
        scale_two,
    ) = gathered
    gain_one = gain_one.astype(jnp.float32)
    shift_one = shift_one.astype(jnp.float32)
    query_shift = query_shift.astype(jnp.float32)
    value_shift = value_shift.astype(jnp.float32)
    output_shift = output_shift.astype(jnp.float32)
    scale_one = scale_one.astype(jnp.float32)
    gain_two = gain_two.astype(jnp.float32)
    shift_two = shift_two.astype(jnp.float32)
    up_shift = up_shift.astype(jnp.float32)
    down_shift = down_shift.astype(jnp.float32)
    scale_two = scale_two.astype(jnp.float32)
    groups = lax.axis_size("seq")
    images, local_len, model_width = tokens.shape
    seq_len = local_len * groups
    per_group = H // groups
    score_scale = HD ** (-0.5)
    token_rows = tokens.astype(jnp.float32).reshape(images * local_len, model_width)
    normed = layer_norm(token_rows, gain_one, shift_one).astype(jnp.bfloat16)
    packed_shift = jnp.concatenate([query_shift, jnp.zeros_like(query_shift), value_shift])
    packed = (matmul(normed, packed_full) + packed_shift).astype(jnp.bfloat16)
    packed = packed.reshape(images, local_len, 3, groups, per_group * HD)
    spread = lax.all_to_all(packed, "seq", split_axis=3, concat_axis=1, tiled=True)
    spread = spread.reshape(images, seq_len, 3, per_group, HD)

    def forward_image(per_image):
        image_block, valid_count = per_image
        return attend(
            image_block[:, 0], image_block[:, 1], image_block[:, 2], valid_count, score_scale
        )

    mixture, log_total = lax.map(forward_image, (spread, lengths))
    mixture = mixture.reshape(images, seq_len, 1, per_group * HD)
    mixture_rows = lax.all_to_all(mixture, "seq", split_axis=1, concat_axis=2, tiled=True).reshape(
        images * local_len, model_width
    )
    branch_one = matmul(mixture_rows, output_full) + output_shift
    middle = token_rows + scale_one * branch_one
    normed_two = layer_norm(middle, gain_two, shift_two).astype(jnp.bfloat16)
    hidden = matmul(normed_two, up_full) + up_shift
    active = gelu_exact(hidden).astype(jnp.bfloat16)
    branch_two = matmul(active, down_full) + down_shift
    output = (middle + scale_two * branch_two).astype(jnp.bfloat16).reshape(tokens.shape)
    upstream = cotangent.astype(jnp.float32).reshape(images * local_len, model_width)
    grad_scale_two = jnp.sum(upstream * branch_two, axis=0)
    delta_two = (scale_two * upstream).astype(jnp.bfloat16)
    grad_down_shift = column_sum(delta_two)
    grad_down = left_outer(active, delta_two)
    grad_active = right_back(delta_two, down_full)
    _, gelu_pull = jax.vjp(gelu_exact, hidden)
    delta_hidden = gelu_pull(grad_active)[0].astype(jnp.bfloat16)
    grad_up_shift = column_sum(delta_hidden)
    grad_up = left_outer(normed_two, delta_hidden)
    delta_normed_two = right_back(delta_hidden, up_full)
    _, norm_pull_two = jax.vjp(layer_norm, middle, gain_two, shift_two)
    grad_middle_norm, grad_gain_two, grad_shift_two = norm_pull_two(delta_normed_two)
    delta_middle = upstream + grad_middle_norm
    grad_scale_one = jnp.sum(delta_middle * branch_one, axis=0)
    delta_one = (scale_one * delta_middle).astype(jnp.bfloat16)
    grad_output_shift = column_sum(delta_one)
    grad_output = left_outer(mixture_rows, delta_one)
    delta_mixture = right_back(delta_one, output_full).astype(jnp.bfloat16)
    delta_mixture = delta_mixture.reshape(images, local_len, groups, per_group * HD)
    grad_spread = lax.all_to_all(delta_mixture, "seq", split_axis=2, concat_axis=1, tiled=True)
    grad_spread = grad_spread.reshape(images, seq_len, per_group, HD)

    def backward_image(per_image):
        image_block, valid_count, image_total, image_grad = per_image
        grad_queries, grad_keys, grad_values = attend_back(
            image_block[:, 0],
            image_block[:, 1],
            image_block[:, 2],
            valid_count,
            score_scale,
            image_total,
            image_grad,
        )
        return jnp.stack([grad_queries, grad_keys, grad_values], axis=1).astype(jnp.bfloat16)

    delta_packed = lax.map(backward_image, (spread, lengths, log_total, grad_spread))
    delta_packed = delta_packed.reshape(images, seq_len, 3, 1, per_group * HD)
    delta_back = lax.all_to_all(delta_packed, "seq", split_axis=1, concat_axis=3, tiled=True)
    delta_back = delta_back.reshape(images * local_len, 3 * model_width)
    grad_query_shift = column_sum(delta_back[:, :model_width])
    grad_value_shift = column_sum(delta_back[:, 2 * model_width :])
    grad_packed = left_outer(normed, delta_back)
    delta_normed = right_back(delta_back, packed_full)
    _, norm_pull_one = jax.vjp(layer_norm, token_rows, gain_one, shift_one)
    grad_rows_norm, grad_gain_one, grad_shift_one = norm_pull_one(delta_normed)
    grad_tokens = (delta_middle + grad_rows_norm).reshape(tokens.shape)
    local_grads = (
        grad_gain_one,
        grad_shift_one,
        grad_packed,
        grad_query_shift,
        grad_value_shift,
        grad_output,
        grad_output_shift,
        grad_scale_one,
        grad_gain_two,
        grad_shift_two,
        grad_up,
        grad_up_shift,
        grad_down,
        grad_down_shift,
        grad_scale_two,
    )
    owned_grads = (
        lax.psum_scatter(
            local_grads[0].astype(jnp.bfloat16), "fsdp", scatter_dimension=0, tiled=True
        ).astype(jnp.float32),
        lax.psum_scatter(
            local_grads[1].astype(jnp.bfloat16), "fsdp", scatter_dimension=0, tiled=True
        ).astype(jnp.float32),
        lax.psum_scatter(
            local_grads[2].astype(jnp.bfloat16), "fsdp", scatter_dimension=0, tiled=True
        ).astype(jnp.float32),
        lax.psum_scatter(
            local_grads[3].astype(jnp.bfloat16), "fsdp", scatter_dimension=0, tiled=True
        ).astype(jnp.float32),
        lax.psum_scatter(
            local_grads[4].astype(jnp.bfloat16), "fsdp", scatter_dimension=0, tiled=True
        ).astype(jnp.float32),
        lax.psum_scatter(
            local_grads[5].astype(jnp.bfloat16), "fsdp", scatter_dimension=0, tiled=True
        ).astype(jnp.float32),
        lax.psum_scatter(
            local_grads[6].astype(jnp.bfloat16), "fsdp", scatter_dimension=0, tiled=True
        ).astype(jnp.float32),
        lax.psum_scatter(
            local_grads[7].astype(jnp.bfloat16), "fsdp", scatter_dimension=0, tiled=True
        ).astype(jnp.float32),
        lax.psum_scatter(
            local_grads[8].astype(jnp.bfloat16), "fsdp", scatter_dimension=0, tiled=True
        ).astype(jnp.float32),
        lax.psum_scatter(
            local_grads[9].astype(jnp.bfloat16), "fsdp", scatter_dimension=0, tiled=True
        ).astype(jnp.float32),
        lax.psum_scatter(
            local_grads[10].astype(jnp.bfloat16), "fsdp", scatter_dimension=0, tiled=True
        ).astype(jnp.float32),
        lax.psum_scatter(
            local_grads[11].astype(jnp.bfloat16), "fsdp", scatter_dimension=0, tiled=True
        ).astype(jnp.float32),
        lax.psum_scatter(
            local_grads[12].astype(jnp.bfloat16), "fsdp", scatter_dimension=0, tiled=True
        ).astype(jnp.float32),
        lax.psum_scatter(
            local_grads[13].astype(jnp.bfloat16), "fsdp", scatter_dimension=0, tiled=True
        ).astype(jnp.float32),
        lax.psum_scatter(
            local_grads[14].astype(jnp.bfloat16), "fsdp", scatter_dimension=0, tiled=True
        ).astype(jnp.float32),
    )
    owned_grads = (
        lax.psum(owned_grads[0].astype(jnp.bfloat16), "seq").astype(jnp.float32),
        lax.psum(owned_grads[1].astype(jnp.bfloat16), "seq").astype(jnp.float32),
        lax.psum(owned_grads[2].astype(jnp.bfloat16), "seq").astype(jnp.float32),
        lax.psum(owned_grads[3].astype(jnp.bfloat16), "seq").astype(jnp.float32),
        lax.psum(owned_grads[4].astype(jnp.bfloat16), "seq").astype(jnp.float32),
        lax.psum(owned_grads[5].astype(jnp.bfloat16), "seq").astype(jnp.float32),
        lax.psum(owned_grads[6].astype(jnp.bfloat16), "seq").astype(jnp.float32),
        lax.psum(owned_grads[7].astype(jnp.bfloat16), "seq").astype(jnp.float32),
        lax.psum(owned_grads[8].astype(jnp.bfloat16), "seq").astype(jnp.float32),
        lax.psum(owned_grads[9].astype(jnp.bfloat16), "seq").astype(jnp.float32),
        lax.psum(owned_grads[10].astype(jnp.bfloat16), "seq").astype(jnp.float32),
        lax.psum(owned_grads[11].astype(jnp.bfloat16), "seq").astype(jnp.float32),
        lax.psum(owned_grads[12].astype(jnp.bfloat16), "seq").astype(jnp.float32),
        lax.psum(owned_grads[13].astype(jnp.bfloat16), "seq").astype(jnp.float32),
        lax.psum(owned_grads[14].astype(jnp.bfloat16), "seq").astype(jnp.float32),
    )
    return (output, grad_tokens) + tuple(owned_grads)


BF16 = jnp.bfloat16
F32 = jnp.float32
NT = (((1,), (1,)), ((), ()))
NN = (((1,), (0,)), ((), ()))
MASKED = -1e30
LANES = 128
VMEM_LIMIT = 60 * 2**20
SMALL_VMEM = 8 * 2**20

GAIN1, SHIFT1, QUERY, VALUE, OUT_SHIFT, SCALE1, GAIN2, SHIFT2, DOWN_SHIFT, SCALE2 = range(10)


def dot(left, right, dims=NN):
    return lax.dot_general(left, right, dims, preferred_element_type=F32)


def turned(values):
    return values.T


def lane_ids(rows):
    return lax.broadcasted_iota(jnp.int32, (rows, LANES), 1)


def split3(values):
    high = values.astype(BF16).astype(F32)
    rest = values - high
    mid = rest.astype(BF16).astype(F32)
    return high, mid, rest - mid


LONG, SHORT = 16.0, 1 / 64


def params_for(flops, nbytes, transcendentals=0, weight=1.0, vmem=VMEM_LIMIT):
    flops, nbytes, transcendentals = (int(weight * count) for count in (flops, nbytes, transcendentals))
    return dict(
        compiler_params=pltpu.CompilerParams(vmem_limit_bytes=vmem),
        cost_estimate=pl.CostEstimate(
            flops=flops, bytes_accessed=nbytes, transcendentals=transcendentals
        ),
    )


def whole(shape):
    return pl.BlockSpec(shape, lambda *_: (0,) * len(shape))


def normalize(values, gain, shift):
    center = values - jnp.mean(values, axis=-1, keepdims=True)
    spread = jnp.mean(center * center, axis=-1, keepdims=True)
    return center * lax.rsqrt(spread + norm_eps) * gain + shift


def normalize_back(values, gain, delta):
    center = values - jnp.mean(values, axis=-1, keepdims=True)
    inverse = lax.rsqrt(jnp.mean(center * center, axis=-1, keepdims=True) + norm_eps)
    unit = center * inverse
    scaled = delta * gain
    mean_scaled = jnp.mean(scaled, axis=-1, keepdims=True)
    mean_unit = jnp.mean(scaled * unit, axis=-1, keepdims=True)
    return inverse * (scaled - mean_scaled - unit * mean_unit), delta * unit


def total_rows(values):
    return jnp.sum(values, axis=0, keepdims=True)


VECTORS = 10


def pack_kernel(weight_ref, up_ref, down_ref, output_ref, *refs):
    vector_refs, shift_ref = refs[:VECTORS], refs[VECTORS]
    first_ref, rest_ref, laid = refs[VECTORS + 1 :]
    rows, width = weight_ref.shape
    first_ref[:, :width] = weight_ref[...]
    laid[...] = jnp.zeros_like(laid)
    core = lax.rem(lax.axis_index("fsdp"), 2)
    for i, ref in enumerate(vector_refs):
        values = ref[...].astype(F32).reshape(1, -1)
        empty = jnp.zeros_like(values)
        first, second = jnp.concatenate([values, empty], 1), jnp.concatenate([empty, values], 1)
        laid[i : i + 1, :] = jnp.where(core == 0, first, second)
    shift = shift_ref[...].astype(F32).reshape(-1, LANES)
    laid[VECTORS : VECTORS + shift.shape[0], :] = shift
    first_ref[:, width:] = laid[...].astype(BF16)
    at = 0
    for ref in (up_ref, down_ref, output_ref):
        for g in range(ref.shape[0] // rows):
            rest_ref[:, at : at + ref.shape[1]] = ref[g * rows : (g + 1) * rows, :]
            at += ref.shape[1]


def pack(weight, up, down, output, vectors, up_shift):
    in_vmem = pl.BlockSpec(memory_space=pltpu.VMEM)
    rows, width = weight.shape
    others = (up.size + down.size + output.size) // rows
    return pl.pallas_call(
        pack_kernel,
        in_specs=[in_vmem] * (VECTORS + 5),
        out_specs=[in_vmem, in_vmem],
        out_shape=[
            jax.ShapeDtypeStruct((rows, width + LANES), BF16),
            jax.ShapeDtypeStruct((rows, others), BF16),
        ],
        scratch_shapes=[pltpu.VMEM((rows, LANES), F32)],
        name="pack",
        **params_for(0, 4 * rows * (width + others)),
    )(weight, up, down, output, *vectors, up_shift)


CORE, CHIPS = 6, 7


def project_kernel(place, x_ref, *refs, chips):
    own_refs, far_refs, own_vectors, far_vectors = (refs[chips * i : chips * (i + 1)] for i in range(4))
    far_out_ref, own_ref, normed_ref, weight_ref, table_ref, up_ref = refs[4 * chips :]
    step = pl.program_id(0)
    rows = own_refs[0].shape[0]
    core = place[CORE]

    @pl.when(step == 0)
    def _():
        vector = lax.broadcasted_iota(jnp.int32, (table_ref.shape[0], LANES), 0) < VECTORS
        each = up_ref.shape[1] // (2 * chips)
        for k in range(chips):
            chip = place[CHIPS + k]
            own = own_vectors[k][...].astype(F32)
            far = far_vectors[k][...].astype(F32)
            at = pl.ds(pl.multiple_of(chip * LANES, LANES), LANES)
            table_ref[:, at] = jnp.where(vector, own + far, 0.0)
            for part, side in ((own, core), (far, 1 - core)):
                for r in range(each // LANES):
                    at = pl.multiple_of((2 * chip + side) * each + r * LANES, LANES)
                    up_ref[:, pl.ds(at, LANES)] = part[VECTORS + r : VECTORS + r + 1, :]
        normed_ref[...] = normalize(
            x_ref[...].astype(F32), table_ref[GAIN1 : GAIN1 + 1, :], table_ref[SHIFT1 : SHIFT1 + 1, :]
        ).astype(BF16)

    for k in range(chips):
        start = 2 * place[CHIPS + k]
        weight_ref[pl.ds(pl.multiple_of((start + core) * rows, rows), rows), :] = own_refs[k][...]
        weight_ref[pl.ds(pl.multiple_of((start + 1 - core) * rows, rows), rows), :] = far_refs[k][...]
    shift = jnp.where(
        step == 0,
        table_ref[QUERY : QUERY + 1, :],
        jnp.where(step == 2, table_ref[VALUE : VALUE + 1, :], 0.0),
    )
    result = (dot(normed_ref[...], weight_ref[...]) + shift).astype(BF16)
    half = result.shape[1] // 2
    low, high = result[:, :half], result[:, half:]
    own_ref[0] = jnp.where(core == 0, low, high)
    far_out_ref[0] = jnp.where(core == 0, high, low)


def project(place, x, own_pieces, far_pieces, hidden):
    chips = len(own_pieces)
    tokens, width = x.shape
    rows = own_pieces[0].shape[0]
    kind = pl.BlockSpec((1, tokens, width // 2), lambda j, _: (j, 0, 0))
    return pl.pallas_call(
        functools.partial(project_kernel, chips=chips),
        grid_spec=pltpu.PrefetchScalarGridSpec(
            num_scalar_prefetch=1,
            grid=(3,),
            in_specs=[whole((tokens, width))]
            + [pl.BlockSpec((rows, width), lambda j, _: (0, j))] * 2 * chips
            + [pl.BlockSpec((16, LANES), lambda j, _: (0, 3 * width // LANES))] * 2 * chips,
            out_specs=[
                kind,
                kind,
                whole((tokens, width)),
                pl.BlockSpec((width, width), lambda j, _: (0, j)),
                whole((16, width)),
                whole((1, hidden)),
            ],
        ),
        out_shape=[
            jax.ShapeDtypeStruct((3, tokens, width // 2), BF16),
            jax.ShapeDtypeStruct((3, tokens, width // 2), BF16),
            jax.ShapeDtypeStruct((tokens, width), BF16),
            jax.ShapeDtypeStruct((width, 3 * width), BF16),
            jax.ShapeDtypeStruct((16, width), F32),
            jax.ShapeDtypeStruct((1, hidden), F32),
        ],
        name="project",
        **params_for(6 * tokens * width * width, 12 * tokens * width + 12 * width * width),
    )(place, x, *own_pieces, *far_pieces, *own_pieces, *far_pieces)


def padded_len(count, block):
    return -(-count // block) * block


def attend_kernel(valid, *refs, pieces, block, scale):
    in_refs, out_refs = refs[:pieces], refs[pieces : 2 * pieces]
    total_refs = refs[2 * pieces : 3 * pieces]
    keys, values, queries, mixed, totals = refs[3 * pieces :]
    pair = pl.program_id(0)
    size = in_refs[0].shape[1]
    count, padded = pieces * size, keys.shape[0]
    lane = lane_ids(size)
    row = lax.broadcasted_iota(jnp.int32, (size, LANES), 0)
    for i in range(pieces):
        at = pl.ds(i * size, size)
        keys[at, :LANES] = in_refs[i][1]
        keys[at, LANES:] = jnp.where((lane == 0) & (row >= valid[i]), MASKED, 0.0).astype(BF16)
        values[at, :LANES] = in_refs[i][2]
        values[at, LANES:] = jnp.where(lane == 0, 1.0, 0.0).astype(BF16)
        for j in range(2):
            mine = lane // HD == j
            queries[j, at, :LANES] = jnp.where(mine, in_refs[i][0].astype(F32) * scale, 0.0).astype(BF16)
            queries[j, at, LANES:] = jnp.where(lane == 0, 1.0, 0.0).astype(BF16)
    if padded > count:
        rest = pl.ds(count, padded - count)
        rest_lane = lane_ids(padded - count)
        keys[rest, :LANES] = jnp.zeros((padded - count, LANES), BF16)
        keys[rest, LANES:] = jnp.where(rest_lane == 0, MASKED, 0.0).astype(BF16)
        values[rest, :] = jnp.zeros((padded - count, 2 * LANES), BF16)
        for j in range(2):
            queries[j, rest, :] = jnp.zeros((padded - count, 2 * LANES), BF16)

    @pl.when(pair == 0)
    def _():
        for i in range(pieces):
            total_refs[i][...] = jnp.zeros_like(total_refs[i])

    block_lane = lane_ids(block)
    for b in range(padded // block):
        at = pl.ds(b * block, block)
        results, logs = [], 0.0
        for j in range(2):
            scores = dot(queries[j, at, :], keys[...], NT)
            largest = jnp.max(scores, axis=1, keepdims=True)
            weights = jnp.exp(scores - largest).astype(BF16)
            result = dot(weights, values[...])
            total = result[:, LANES : LANES + 1]
            results.append(result[:, :LANES] * (1.0 / total))
            logs += jnp.where(block_lane == 2 * pair + j, largest + jnp.log(total), 0.0)
        mixed[at, :] = jnp.where(block_lane < HD, results[0], results[1])
        totals[at, :] = logs
    for i in range(pieces):
        at = pl.ds(i * size, size)
        out_refs[i][...] = mixed[at, :].astype(BF16)
        total_refs[i][...] += totals[at, :]


def attention(valid, parts, block):
    pieces = len(parts)
    _, size, width = parts[0].shape
    pairs = width // LANES
    padded = padded_len(pieces * size, block)
    outs = pl.pallas_call(
        functools.partial(attend_kernel, pieces=pieces, block=block, scale=HD**-0.5),
        grid_spec=pltpu.PrefetchScalarGridSpec(
            num_scalar_prefetch=1,
            grid=(pairs,),
            in_specs=[pl.BlockSpec((3, size, LANES), lambda h, _: (0, 0, h))] * pieces,
            out_specs=[pl.BlockSpec((size, LANES), lambda h, _: (0, h))] * pieces
            + [whole((size, LANES))] * pieces,
            scratch_shapes=[
                pltpu.VMEM((padded, 2 * LANES), BF16),
                pltpu.VMEM((padded, 2 * LANES), BF16),
                pltpu.VMEM((2, padded, 2 * LANES), BF16),
                pltpu.VMEM((padded, LANES), F32),
                pltpu.VMEM((padded, LANES), F32),
            ],
        ),
        out_shape=[jax.ShapeDtypeStruct((size, width), BF16)] * pieces
        + [jax.ShapeDtypeStruct((size, LANES), F32)] * pieces,
        name="attend",
        **params_for(16 * pairs * LANES * padded * padded, 8 * size * width * pieces, pairs * 2 * padded * padded),
    )(valid, *parts)
    return outs[:pieces], outs[pieces:]


def attend_back_kernel(valid, *refs, pieces, block, scale, first):
    in_refs, mix_refs = refs[:pieces], refs[pieces : 2 * pieces]
    grad_refs, total_refs = refs[2 * pieces : 3 * pieces], refs[3 * pieces : 4 * pieces]
    out_refs = refs[-9 - pieces : -9]
    keys, values, queries, grads, queries_t, grads_t, dq, dk_t, dv_t = refs[-9:]
    pair = first + pl.program_id(0)
    size = in_refs[0].shape[1]
    count, padded = pieces * size, keys.shape[0]
    blocks = padded // block
    lane = lane_ids(size)
    row = lax.broadcasted_iota(jnp.int32, (size, LANES), 0)
    for i in range(pieces):
        at = pl.ds(i * size, size)
        keys[at, :LANES] = in_refs[i][1]
        keys[at, LANES:] = jnp.where(
            lane == 0, jnp.where(row >= valid[i], MASKED, 0.0), jnp.where(lane < 4, 1.0, 0.0)
        ).astype(BF16)
        values[at, :LANES] = in_refs[i][2]
        values[at, LANES:] = jnp.where((lane > 0) & (lane < 4), 1.0, 0.0).astype(BF16)
        queries[0, at, :LANES] = in_refs[i][0]
        grads[0, at, :LANES] = grad_refs[i][...]
    if padded > count:
        left = padded - count
        rest = pl.ds(count, left)
        keys[rest, :LANES] = jnp.zeros((left, LANES), BF16)
        keys[rest, LANES:] = jnp.where(lane_ids(left) == 0, MASKED, 0.0).astype(BF16)
        values[rest, :] = jnp.zeros((left, 2 * LANES), BF16)
        for j in range(2):
            queries[j, rest, :] = jnp.zeros((left, 2 * LANES), BF16)
            grads[j, rest, :] = jnp.zeros((left, 2 * LANES), BF16)
    for b in range(blocks):
        at = pl.ds(b * block, block)
        queries_t[b] = (queries[0, at, :LANES].astype(F32) * scale).T.astype(BF16)
        grads_t[b] = turned(grads[0, at, :LANES])
    for j in range(2):
        mine = lane // HD == j
        for i in range(pieces):
            at = pl.ds(i * size, size)
            grad = jnp.where(mine, grad_refs[i][...].astype(F32), 0.0)
            queries[j, at, :LANES] = jnp.where(mine, in_refs[i][0].astype(F32) * scale, 0.0).astype(BF16)
            grads[j, at, :LANES] = grad.astype(BF16)
            log_total = jnp.sum(
                jnp.where(lane == 2 * pair + j, total_refs[i][...], 0.0), axis=1, keepdims=True
            )
            high, mid, low = split3(-log_total)
            queries[j, at, LANES:] = jnp.where(
                lane == 0,
                1.0,
                jnp.where(lane == 1, high, jnp.where(lane == 2, mid, jnp.where(lane == 3, low, 0.0))),
            ).astype(BF16)
            inner = jnp.sum(grad * mix_refs[i][...].astype(F32), axis=1, keepdims=True)
            high, mid, low = split3(-inner)
            grads[j, at, LANES:] = jnp.where(
                lane == 1, high, jnp.where(lane == 2, mid, jnp.where(lane == 3, low, 0.0))
            ).astype(BF16)
    dk_t[...] = jnp.zeros_like(dk_t)
    dv_t[...] = jnp.zeros_like(dv_t)
    block_lane = lane_ids(block)
    for b in range(blocks):
        at = pl.ds(b * block, block)
        results = []
        for j in range(2):
            mine = pl.ds(j * HD, HD)
            probs = jnp.exp(dot(queries[j, at, :], keys[...], NT))
            grad_scores = (probs * dot(grads[j, at, :], values[...], NT)).astype(BF16)
            results.append(dot(grad_scores, keys[:, :LANES]) * scale)
            dv_t[mine, :] += dot(grads_t[b, mine, :], probs.astype(BF16))
            dk_t[mine, :] += dot(queries_t[b, mine, :], grad_scores)
        dq[at, :] = jnp.where(block_lane < HD, results[0], results[1])
    dk, dv = dk_t[...].T, dv_t[...].T
    for i in range(pieces):
        at = slice(i * size, (i + 1) * size)
        out_refs[i][0] = dq[at, :].astype(BF16)
        out_refs[i][1] = dk[at, :].astype(BF16)
        out_refs[i][2] = dv[at, :].astype(BF16)


def attention_back(valid, parts, mixtures, grads, totals, block, first, pairs, into, after):
    pieces = len(parts)
    _, size, width = parts[0].shape
    padded = padded_len(pieces * size, block)
    triple = pl.BlockSpec((3, size, LANES), lambda h, _: (0, 0, first + h))
    single = pl.BlockSpec((size, LANES), lambda h, _: (0, first + h))
    in_specs = [triple] * pieces + [single] * 2 * pieces + [whole((size, LANES))] * pieces
    aliases = {1 + len(in_specs) + i: i for i in range(len(into))}
    return pl.pallas_call(
        functools.partial(attend_back_kernel, pieces=pieces, block=block, scale=HD**-0.5, first=first),
        grid_spec=pltpu.PrefetchScalarGridSpec(
            num_scalar_prefetch=1,
            grid=(pairs,),
            in_specs=in_specs + [pl.BlockSpec(memory_space=pl.ANY)] * (len(into) + len(after)),
            out_specs=[triple] * pieces,
            scratch_shapes=[
                pltpu.VMEM((padded, 2 * LANES), BF16),
                pltpu.VMEM((padded, 2 * LANES), BF16),
                pltpu.VMEM((2, padded, 2 * LANES), BF16),
                pltpu.VMEM((2, padded, 2 * LANES), BF16),
                pltpu.VMEM((padded // block, LANES, block), BF16),
                pltpu.VMEM((padded // block, LANES, block), BF16),
                pltpu.VMEM((padded, LANES), F32),
                pltpu.VMEM((LANES, padded), F32),
                pltpu.VMEM((LANES, padded), F32),
            ],
        ),
        out_shape=[jax.ShapeDtypeStruct((3, size, width), BF16)] * pieces,
        input_output_aliases=aliases,
        name="attend_back",
        **params_for(30 * pairs * LANES * padded * padded, 16 * size * LANES * pairs * pieces, pairs * 2 * padded * padded, weight=LONG),
    )(valid, *parts, *mixtures, *grads, *totals, *into, *after)


def merge_kernel(place, x_ref, own_ref, far_ref, table, own_w, far_w, middle_ref, branch_ref, normed_ref):
    branch = dot(own_ref[...], own_w[...]) + dot(far_ref[...], far_w[...])
    branch += table[OUT_SHIFT : OUT_SHIFT + 1, :]
    middle = x_ref[...].astype(F32) + table[SCALE1 : SCALE1 + 1, :] * branch
    middle_ref[...] = middle
    branch_ref[...] = branch
    normed_ref[...] = normalize(
        middle, table[GAIN2 : GAIN2 + 1, :], table[SHIFT2 : SHIFT2 + 1, :]
    ).astype(BF16)


ROWS = 352


def row_steps(tokens):
    return -(-tokens // ROWS)


def merge(place, x, own, far, table, rest):
    tokens, width = x.shape
    half = width // 2
    wide = pl.BlockSpec((ROWS, width), lambda i, _: (i, 0))
    narrow = pl.BlockSpec((ROWS, half), lambda i, _: (i, 0))
    return pl.pallas_call(
        merge_kernel,
        grid_spec=pltpu.PrefetchScalarGridSpec(
            num_scalar_prefetch=1,
            grid=(row_steps(tokens),),
            in_specs=[
                wide,
                narrow,
                narrow,
                whole(table.shape),
                pl.BlockSpec((half, width), lambda i, place: (place[CORE], rest.shape[1] // width - 1)),
                pl.BlockSpec((half, width), lambda i, place: (1 - place[CORE], rest.shape[1] // width - 1)),
            ],
            out_specs=[wide, wide, wide],
        ),
        out_shape=[
            jax.ShapeDtypeStruct((tokens, width), F32),
            jax.ShapeDtypeStruct((tokens, width), F32),
            jax.ShapeDtypeStruct((tokens, width), BF16),
        ],
        name="merge",
        **params_for(2 * tokens * width * width, 14 * tokens * width + 2 * width * width),
    )(place, x, own, far, table, rest, rest)


def gelu_and_slope(values):
    size = jnp.abs(values) * 0.7071067811865476
    t = 1.0 / (1.0 + 0.3275911 * size)
    bell = jnp.exp(-0.5 * (values * values))
    poly = t * (0.254829592 + t * (-0.284496736 + t * (1.421413741 + t * (-1.453152027 + t * 1.061405429))))
    tail = 0.5 * poly * bell
    phi = jnp.where(values < 0, tail, 1.0 - tail)
    return values * phi, phi + values * bell * 0.3989422804014327


def ungroup(grouped_ref, down):
    width = down.shape[1]
    groups = grouped_ref.shape[1] // width
    each = grouped_ref.shape[0] // 2
    for device in range(2):
        for g in range(groups):
            at = (device * groups + g) * each
            down[at : at + each, :] = grouped_ref[device * each : (device + 1) * each, g * width : (g + 1) * width]


def scaled_upstream(cotangent_ref, table):
    return (cotangent_ref[...].astype(F32) * table[SCALE2 : SCALE2 + 1, :]).astype(BF16)


def place_turned(place, block, target, k, chips):
    half = block.shape[1] // 2
    turned_block = block.T
    first, second = turned_block[:half], turned_block[half:]
    target[k * half : (k + 1) * half, :] = jnp.where(place[CORE] == 0, first, second)
    target[(chips + k) * half : (chips + k + 1) * half, :] = jnp.where(place[CORE] == 0, second, first)


def fill_turned(place, source_ref, target, chips):
    wide = source_ref.shape[1] // chips
    for k in range(chips):
        at = pl.ds(pl.multiple_of(place[CHIPS + k] * wide, wide), wide)
        place_turned(place, source_ref[:, at], target, k, chips)


def split_rows(grad, mine_ref, other_ref):
    chips, rows, _ = mine_ref.shape
    for k in range(chips):
        mine_ref[k] = grad[k * rows : (k + 1) * rows, :]
        other_ref[k] = grad[(chips + k) * rows : (chips + k + 1) * rows, :]


def group(grad, out_ref):
    rows, columns = out_ref.shape[1], grad.shape[1]
    for g in range(grad.shape[0] // rows):
        out_ref[0, :, g * columns : (g + 1) * columns] = grad[g * rows : (g + 1) * rows, :]


def mlp_kernel(
    place, normed_ref, cotangent_ref, table, up_ref, shift_ref, grouped_ref,
    branch_ref, delta_ref, up_mine_ref, up_other_ref, down_mine_ref, down_other_ref, grad_shift_ref,
    upstream, upstream_t, normed_t, down,
    *, chips,
):
    @pl.when(pl.program_id(0) == 0)
    def _():
        scaled = (cotangent_ref[...].astype(F32) * table[SCALE2 : SCALE2 + 1, :]).astype(BF16)
        upstream[...] = scaled
        upstream_t[...] = turned(scaled)
        fill_turned(place, normed_ref, normed_t, chips)
        branch_ref[...] = jnp.zeros_like(branch_ref)
        delta_ref[...] = jnp.zeros_like(delta_ref)

    ungroup(grouped_ref, down)
    hidden = dot(normed_ref[...], up_ref[...]) + shift_ref[...]
    grad_active = dot(upstream[...], down[...], NT)
    active, slope = gelu_and_slope(hidden)
    active = active.astype(BF16)
    delta_hidden = (grad_active * slope).astype(BF16)
    branch_ref[...] += dot(active, down[...])
    delta_ref[...] += dot(delta_hidden, up_ref[...], NT)
    split_rows(dot(normed_t[...], delta_hidden).astype(BF16), up_mine_ref, up_other_ref)
    grad_down = dot(upstream_t[...], active)
    each = grad_down.shape[1] // 2
    first, second = grad_down[:, :each], grad_down[:, each:]
    group(jnp.where(place[CORE] == 0, first, second).astype(BF16), down_mine_ref)
    group(jnp.where(place[CORE] == 0, second, first).astype(BF16), down_other_ref)
    grad_shift_ref[...] = total_rows(delta_hidden.astype(F32))


def mlp(place, normed, cotangent, table, rest, up_shift, owners):
    tokens, width = normed.shape
    hidden = up_shift.shape[1]
    rows = rest.shape[0] // owners
    chips = owners // 2
    block = hidden // chips
    up_out = pl.BlockSpec((chips, rows, block), lambda j, place: (0, 0, place[CHIPS + j]))
    down_out = pl.BlockSpec((1, rows, hidden), lambda j, _: (j, 0, 0))
    sent = jax.ShapeDtypeStruct((chips, rows, hidden), BF16)
    return pl.pallas_call(
        functools.partial(mlp_kernel, chips=chips),
        grid_spec=pltpu.PrefetchScalarGridSpec(
            num_scalar_prefetch=1,
            grid=(chips,),
            in_specs=[
                whole((tokens, width)),
                whole((tokens, width)),
                whole(table.shape),
                pl.BlockSpec((width, block), lambda j, place: (0, place[CHIPS + j])),
                pl.BlockSpec((1, block), lambda j, place: (0, place[CHIPS + j])),
                pl.BlockSpec((2 * rows, hidden), lambda j, place: (place[CHIPS + j], 1)),
            ],
            out_specs=[
                whole((tokens, width)),
                whole((tokens, width)),
                up_out,
                up_out,
                down_out,
                down_out,
                pl.BlockSpec((1, block), lambda j, place: (0, place[CHIPS + j])),
            ],
            scratch_shapes=[
                pltpu.VMEM((tokens, width), BF16),
                pltpu.VMEM((width, tokens), BF16),
                pltpu.VMEM((width, tokens), BF16),
                pltpu.VMEM((block, width), BF16),
            ],
        ),
        out_shape=[
            jax.ShapeDtypeStruct((tokens, width), F32),
            jax.ShapeDtypeStruct((tokens, width), F32),
            sent,
            sent,
            sent,
            sent,
            jax.ShapeDtypeStruct((1, hidden), F32),
        ],
        name="mlp",
        **params_for(12 * tokens * width * hidden, 12 * tokens * width + 8 * width * hidden, 2 * tokens * hidden),
    )(place, normed, cotangent, table, rest, up_shift, rest)


SUM_ROWS = 8


def unmerge_kernel(
    place, middle_ref, branch1_ref, branch2_ref, delta_ref, cotangent_ref, own_ref, far_ref, table, own_w, far_w,
    output_ref, delta_middle_ref, own_grad_ref, far_grad_ref, mine_ref, other_ref, sums_ref,
    delta1_all, mixture_t,
    *, tokens,
):
    step = pl.program_id(0)

    @pl.when(step == 0)
    def _():
        sums_ref[...] = jnp.zeros_like(sums_ref)

    rows, width = middle_ref.shape
    inside = lax.broadcasted_iota(jnp.int32, (rows, width), 0) + step * rows < tokens

    def kept(values):
        return jnp.where(inside, values, 0.0)

    upstream = cotangent_ref[...].astype(F32)
    scale2 = table[SCALE2 : SCALE2 + 1, :]
    middle = middle_ref[...]
    branch2 = branch2_ref[...] + table[DOWN_SHIFT : DOWN_SHIFT + 1, :]
    output_ref[...] = (middle + scale2 * branch2).astype(BF16)
    delta2 = (scale2 * upstream).astype(BF16).astype(F32)
    delta = delta_ref[...]
    inner, gain_terms = normalize_back(middle, table[GAIN2 : GAIN2 + 1, :], delta)
    delta_middle = upstream + inner
    delta_middle_ref[...] = delta_middle
    delta1 = kept(table[SCALE1 : SCALE1 + 1, :] * delta_middle).astype(BF16)
    delta1_all[pl.ds(pl.multiple_of(step * rows, 16), rows), :] = delta1
    own_grad_ref[...] = dot(delta1, own_w[...], NT).astype(BF16)
    far_grad_ref[...] = dot(delta1, far_w[...], NT).astype(BF16)
    terms = (
        upstream * branch2,
        delta2,
        gain_terms,
        delta,
        delta_middle * branch1_ref[...],
        delta1.astype(F32),
    )
    for i, term in enumerate(terms):
        sums_ref[i : i + 1, :] += total_rows(kept(term))

    @pl.when(step == pl.num_programs(0) - 1)
    def _():
        chips = mine_ref.shape[0]
        wide = width // chips
        for k in range(chips):
            chip = place[CHIPS + k]
            at = pl.ds(pl.multiple_of(lax.rem(chip, chips // 2) * wide, wide), wide)
            mixed = jnp.where(chip // (chips // 2) == place[CORE], own_ref[:, at], far_ref[:, at])
            place_turned(place, mixed, mixture_t, k, chips)
        split_rows(dot(mixture_t[...], delta1_all[:tokens, :]).astype(BF16), mine_ref, other_ref)


def unmerge(place, middle, branch1, branch2, delta, cotangent, own, far, table, rest, owners):
    tokens, width = middle.shape
    chips = owners // 2
    sent = (chips, width // owners, width)
    half = width // 2
    steps = row_steps(tokens)
    wide = pl.BlockSpec((ROWS, width), lambda i, _: (i, 0))
    narrow = pl.BlockSpec((ROWS, half), lambda i, _: (i, 0))
    return pl.pallas_call(
        functools.partial(unmerge_kernel, tokens=tokens),
        grid_spec=pltpu.PrefetchScalarGridSpec(
            num_scalar_prefetch=1,
            grid=(steps,),
            in_specs=[wide] * 5
            + [whole((tokens, half))] * 2
            + [
                whole(table.shape),
                pl.BlockSpec((half, width), lambda i, place: (place[CORE], rest.shape[1] // width - 1)),
                pl.BlockSpec((half, width), lambda i, place: (1 - place[CORE], rest.shape[1] // width - 1)),
            ],
            out_specs=[wide, wide, narrow, narrow, whole(sent), whole(sent), whole((SUM_ROWS, width))],
            scratch_shapes=[pltpu.VMEM((steps * ROWS, width), BF16), pltpu.VMEM((width, tokens), BF16)],
        ),
        out_shape=[
            jax.ShapeDtypeStruct((tokens, width), BF16),
            jax.ShapeDtypeStruct((tokens, width), F32),
            jax.ShapeDtypeStruct((tokens, half), BF16),
            jax.ShapeDtypeStruct((tokens, half), BF16),
            jax.ShapeDtypeStruct(sent, BF16),
            jax.ShapeDtypeStruct(sent, BF16),
            jax.ShapeDtypeStruct((SUM_ROWS, width), F32),
        ],
        name="unmerge",
        **params_for(4 * tokens * width * width, 30 * tokens * width + 4 * width * width),
    )(place, middle, branch1, branch2, delta, cotangent, own, far, table, rest, rest)


def unproject_kernel(
    place, x_hbm, delta_middle_hbm, table, normed_ref, own_ref, far_ref, weight_ref, middle_sums, up_sums, *refs, chips
):
    (
        out_ref, mine_ref, other_ref, vectors_mine_ref, vectors_other_ref,
        delta, sums, normed_t, x_ref, delta_middle_ref, laid, arrived,
    ) = refs
    step = pl.program_id(0)
    core = place[CORE]
    copies = [
        pltpu.make_async_copy(x_hbm, x_ref, arrived.at[0]),
        pltpu.make_async_copy(delta_middle_hbm, delta_middle_ref, arrived.at[1]),
    ]

    @pl.when(step == 0)
    def _():
        for copy in copies:
            copy.start()
        fill_turned(place, normed_ref, normed_t, chips)
        delta[...] = jnp.zeros_like(delta)
        sums[...] = jnp.zeros_like(sums)

    own, far = own_ref[0], far_ref[0]
    block = jnp.concatenate([jnp.where(core == 0, own, far), jnp.where(core == 0, far, own)], axis=1)
    split_rows(dot(normed_t[...], block).astype(BF16), mine_ref, other_ref)
    delta[...] += dot(block, weight_ref[...], NT)
    for kind, row in ((0, QUERY), (2, VALUE)):

        @pl.when(step == kind)
        def _():
            sums[row : row + 1, :] = total_rows(block.astype(F32))

    @pl.when(step == pl.num_programs(0) - 1)
    def _():
        for copy in copies:
            copy.wait()
        delta_normed = delta[...]
        inner, gain_terms = normalize_back(
            x_ref[...].astype(F32), table[GAIN1 : GAIN1 + 1, :], delta_normed
        )
        out_ref[...] = (delta_middle_ref[...] + inner).astype(BF16)
        rows = {
            GAIN1: total_rows(gain_terms),
            SHIFT1: total_rows(delta_normed),
            OUT_SHIFT: middle_sums[5:6, :],
            SCALE1: middle_sums[4:5, :],
            GAIN2: middle_sums[2:3, :],
            SHIFT2: middle_sums[3:4, :],
            DOWN_SHIFT: middle_sums[1:2, :],
            SCALE2: middle_sums[0:1, :],
        }
        for i, values in rows.items():
            sums[i : i + 1, :] = values
        each = up_sums.shape[1] // (2 * chips)
        laid[...] = jnp.zeros_like(laid)
        for out, side in ((vectors_mine_ref, core), (vectors_other_ref, 1 - core)):
            for k in range(chips):
                chip = place[CHIPS + k]
                at = pl.ds(pl.multiple_of(chip * LANES, LANES), LANES)
                laid[k, : sums.shape[0], :] = sums[:, at]
                for r in range(each // LANES):
                    at = pl.multiple_of((2 * chip + side) * each + r * LANES, LANES)
                    laid[k, VECTORS + r : VECTORS + r + 1, :] = up_sums[:, pl.ds(at, LANES)]
            out[...] = laid[...].astype(BF16)


def unproject(place, x, delta_middle, table, normed, own, far, weight, middle_sums, up_sums, owners):
    tokens, width = x.shape
    half = width // 2
    chips = owners // 2
    rows = width // owners
    vectors = (chips, rows, LANES)
    anywhere = pl.BlockSpec(memory_space=pl.ANY)
    kind = pl.BlockSpec((1, tokens, half), lambda j, _: (j, 0, 0))
    sent = pl.BlockSpec((chips, rows, width), lambda j, _: (0, 0, j))
    return pl.pallas_call(
        functools.partial(unproject_kernel, chips=chips),
        grid_spec=pltpu.PrefetchScalarGridSpec(
            num_scalar_prefetch=1,
            grid=(3,),
            in_specs=[
                anywhere,
                anywhere,
                whole(table.shape),
                whole((tokens, width)),
                kind,
                kind,
                pl.BlockSpec((width, width), lambda j, _: (0, j)),
                whole(middle_sums.shape),
                whole(up_sums.shape),
            ],
            out_specs=[whole((tokens, width)), sent, sent, whole(vectors), whole(vectors)],
            scratch_shapes=[
                pltpu.VMEM((tokens, width), F32),
                pltpu.VMEM((16, width), F32),
                pltpu.VMEM((width, tokens), BF16),
                pltpu.VMEM((tokens, width), BF16),
                pltpu.VMEM((tokens, width), F32),
                pltpu.VMEM(vectors, F32),
                pltpu.SemaphoreType.DMA((2,)),
            ],
        ),
        out_shape=[
            jax.ShapeDtypeStruct((tokens, width), BF16),
            jax.ShapeDtypeStruct((chips, rows, 3 * width), BF16),
            jax.ShapeDtypeStruct((chips, rows, 3 * width), BF16),
            jax.ShapeDtypeStruct(vectors, BF16),
            jax.ShapeDtypeStruct(vectors, BF16),
        ],
        name="unproject",
        **params_for(12 * tokens * width * width, 18 * tokens * width + 12 * width * width, weight=SHORT),
    )(place, x, delta_middle, table, normed, own, far, weight, middle_sums, up_sums)


def ring_of(chips):
    return list(range(0, chips, 2)) + list(range(1, chips, 2))[::-1]


def places(owners):
    ring = ring_of(owners // 2)
    rows = []
    for f in range(owners):
        chip, core = divmod(f, 2)
        at = ring.index(chip)
        columns = [1 - core, 3 - core, 5 - core, core, 2 + core, 4 + core]
        rows.append(columns + [core] + ring[at:] + ring[:at])
    return np.array(rows, np.int32)


def ring_perm(chips, hop):
    ring = ring_of(chips)
    return [
        (2 * ring[i] + core, 2 * ring[(i + hop) % chips] + core) for i in range(chips) for core in range(2)
    ]


def to_next(values, chips, hop):
    return lax.ppermute(values, "fsdp", ring_perm(chips, hop))


def ring_gather(piece, chips):
    pieces = [None] * chips
    pieces[0] = right = left = piece
    for k in range(1, chips // 2 + 1):
        pieces[-k] = right = to_next(right, chips, 1)
        if k < chips - chips // 2:
            pieces[k] = left = to_next(left, chips, -1)
    return pieces


def low_part(columns):
    return columns // 2 if columns % (2 * LANES) == 0 else columns


def ring_add_kernel(*refs, columns, mode, carried):
    ways = 2 if mode in ("second", "next") else 1
    shares = [refs[2 * len(columns) * d : 2 * len(columns) * (d + 1)] for d in range(ways)]
    came = refs[2 * len(columns) * ways :]
    outs = refs[len(refs) - carried - (1 if mode == "total" else 2) : len(refs) - carried]
    start, low_start, high_start = 0, 0, 0
    for i, each in enumerate(columns):
        totals = [mine[2 * i][0].astype(F32) + mine[2 * i + 1][0].astype(F32) for mine in shares]
        at = slice(start, start + each)
        low = low_part(each)
        low_at, high_at = slice(low_start, low_start + low), slice(high_start, high_start + each - low)
        if mode == "first":
            outs[0][:, low_at] = totals[0][:, :low].astype(BF16)
            if low < each:
                outs[1][:, high_at] = totals[0][:, low:].astype(BF16)
        elif mode == "second":
            outs[0][:, start : start + low] = (totals[0][:, :low] + came[0][:, low_at].astype(F32)).astype(BF16)
            outs[1][:, start : start + low] = totals[1][:, :low].astype(BF16)
            if low < each:
                high = totals[1][:, low:] + came[1][:, high_at].astype(F32)
                outs[0][:, start + low : start + each] = totals[0][:, low:].astype(BF16)
                outs[1][:, start + low : start + each] = high.astype(BF16)
        elif mode == "next":
            for total, arrived, out in zip(totals, came, outs):
                out[:, at] = (total + arrived[:, at].astype(F32)).astype(BF16)
        else:
            both_ways = came[0][:, at].astype(F32) + came[1][:, at].astype(F32)
            outs[0][:, at] = (totals[0] + both_ways).astype(BF16)
        start, low_start, high_start = at.stop, low_at.stop, high_at.stop


class RingSum:
    def __init__(self, *parts):
        self.parts, self.chips = [part[:2] for part in parts], parts[0][0].shape[0]
        self.columns = [part[0].shape[2] // part[3] for part in parts]
        self.blocks = [part[2] for part in parts]
        self.steps = self.chips // 2
        self.step = 0
        self.came = []

    def add(self, mode, places, after=(), carry=()):
        rows = self.parts[0][0].shape[1]
        columns = self.columns
        total = sum(columns)
        blocks = 2 if total > 4096 else 1
        arrays, specs = [], []
        for at in places:
            for part, each, block in zip(self.parts, columns, self.blocks):
                for array in part:
                    arrays.append(array)
                    specs.append(pl.BlockSpec((1, rows // blocks, each), lambda i, at=at, block=block: (at, i, block)))
        for came in self.came:
            arrays.append(came)
            specs.append(pl.BlockSpec((rows // blocks, came.shape[1]), lambda i: (i, 0)))
        arrays += [*after, *carry]
        anywhere = pl.BlockSpec(memory_space=pl.ANY)
        specs += [anywhere] * (len(after) + len(carry))
        low = sum(low_part(each) for each in columns)
        out_columns = {"first": [low, total - low], "total": [total]}.get(mode, [total, total])
        sums = len(out_columns)
        outs = pl.pallas_call(
            functools.partial(ring_add_kernel, columns=columns, mode=mode, carried=len(carry)),
            grid=(blocks,),
            in_specs=specs,
            out_specs=[pl.BlockSpec((rows // blocks, out), lambda i: (i, 0)) for out in out_columns]
            + [anywhere] * len(carry),
            out_shape=[jax.ShapeDtypeStruct((rows, out), BF16) for out in out_columns]
            + [jax.ShapeDtypeStruct(array.shape, array.dtype) for array in carry],
            input_output_aliases={len(arrays) - len(carry) + i: sums + i for i in range(len(carry))},
            name="ring_add",
            **params_for(6 * rows * total, 16 * rows * total, weight=SHORT, vmem=VMEM_LIMIT if blocks > 1 else SMALL_VMEM),
        )(*arrays)
        return outs[:sums], outs[sums:]

    def sums(self, after=(), carry=()):
        k = self.steps - self.step
        if self.step == 0:
            return self.add("first", [k], after, carry)
        return self.add("second" if self.step == 1 else "next", [k, self.chips - k], after, carry)

    def send(self, sums):
        self.came = [to_next(sums[0], self.chips, 1), to_next(sums[1], self.chips, -1)]
        self.step += 1

    def total(self, after=(), carry=()):
        assert self.step == self.steps
        sums, carried = self.add("total", [0], after, carry)
        return sums[0], carried


def passed(arrays, after):
    anywhere = pl.BlockSpec(memory_space=pl.ANY)
    return pl.pallas_call(
        lambda *refs: None,
        in_specs=[anywhere] * (len(arrays) + len(after)),
        out_specs=[anywhere] * len(arrays),
        out_shape=[jax.ShapeDtypeStruct(array.shape, array.dtype) for array in arrays],
        input_output_aliases={i: i for i in range(len(arrays))},
        name="passed",
        **params_for(1, 1, vmem=SMALL_VMEM),
    )(*arrays, *after)


def finish_rest_kernel(part_ref, came_ref, up_ref, down_ref):
    def total(at):
        return part_ref[:, at].astype(F32) + came_ref[:, at].astype(F32)

    rows, hidden = up_ref.shape
    each, width = down_ref.shape
    up_ref[...] = total(slice(0, hidden))
    for g in range(0, width // rows, 2):
        pair = [total(slice(hidden + each * h, hidden + each * (h + 1))) for h in (g, g + 1)]
        down_ref[:, g * rows : (g + 2) * rows] = jnp.concatenate(pair, axis=0).T


def finish_rest(part, came, hidden, each, width):
    in_vmem = pl.BlockSpec(memory_space=pltpu.VMEM)
    rows = part.shape[0]
    return pl.pallas_call(
        finish_rest_kernel,
        in_specs=[in_vmem] * 2,
        out_specs=[in_vmem] * 2,
        out_shape=[jax.ShapeDtypeStruct(shape, F32) for shape in ((rows, hidden), (each, width))],
        name="finish_rest",
        **params_for(part.size, 8 * part.size, weight=SHORT, vmem=2 * SMALL_VMEM),
    )(part, came)


def finish_first_kernel(place, *refs):
    parts, came, (packed_ref, output_ref), vector_refs = refs[:2], refs[2:4], refs[4:6], refs[6:]
    packed, out = packed_ref.shape[1] // 2, output_ref.shape[1] // 2
    for i in range(2):
        total = parts[i][...].astype(F32) + came[i][...].astype(F32)
        packed_ref[:, packed * i : packed * (i + 1)] = total[:, :packed]
        output_ref[:, out * i : out * (i + 1)] = total[:, packed : packed + out]
        if i == 0:
            vectors = total[:16, packed + out :]
    half = LANES // 2
    mine = jnp.where(place[CORE] == 0, vectors[:, :half], vectors[:, half:])
    for i in range(VECTORS):
        vector_refs[i][...] = mine[i : i + 1, :].reshape(half)
    count = vector_refs[VECTORS].shape[0]
    vector_refs[VECTORS][...] = vectors[VECTORS : VECTORS + count // LANES, :].reshape(count)


def finish_first(place, parts, came, width, each):
    in_vmem = pl.BlockSpec(memory_space=pltpu.VMEM)
    rows = parts[0].shape[0]
    shapes = [(rows, 3 * width), (rows, width)] + [(rows,)] * VECTORS + [(each,)]
    return pl.pallas_call(
        finish_first_kernel,
        in_specs=[pl.BlockSpec(memory_space=pltpu.SMEM)] + [in_vmem] * 4,
        out_specs=[in_vmem] * len(shapes),
        out_shape=[jax.ShapeDtypeStruct(shape, F32) for shape in shapes],
        name="finish_first",
        **params_for(8 * rows * width, 32 * rows * width, weight=SHORT, vmem=SMALL_VMEM),
    )(place, *parts, *came)


def split_pairs(pairs):
    return [pairs // 4, pairs // 2, pairs - pairs // 4 - pairs // 2] if pairs >= 4 else [pairs]


def paired_body(
    tokens, lengths, norm1_gain, norm1_bias, packed_weight, query_bias, value_bias, output_weight, output_bias,
    layer_scale1, norm2_gain, norm2_bias, up_weight, up_bias, down_weight, down_bias, layer_scale2, cotangent,
):
    owners = lax.axis_size("fsdp")
    chips = owners // 2
    _, local_len, width = tokens.shape
    me = lax.axis_index("fsdp")
    core = lax.rem(me, 2)
    place = lax.dynamic_index_in_dim(jnp.asarray(places(owners)), me, keepdims=False)
    moves = [(f * 2 + s, (f - f % 2 + s) * 2 + f % 2) for f in range(owners) for s in range(2) if f % 2 != s]
    twin = [(f, f ^ 1) for f in range(owners)]
    stays = core == lax.axis_index("seq")

    def regroup_moves(values):
        return lax.ppermute(values, ("fsdp", "seq"), moves)

    def regrouped(values):
        return jnp.where(stays, values, regroup_moves(values))

    def to_twin(values):
        return lax.ppermute(values, "fsdp", twin)

    def across(values):
        return lax.ppermute(values, "seq", [(0, 1), (1, 0)])

    vectors = (
        norm1_gain, norm1_bias, query_bias, value_bias, output_bias, layer_scale1, norm2_gain, norm2_bias,
        down_bias, layer_scale2,
    )
    rows = norm1_gain.shape[0]
    hidden = up_weight.shape[1]
    first, rest = pack(packed_weight, up_weight, down_weight, output_weight, vectors, up_bias)
    own_pieces = ring_gather(first, chips)
    far_pieces = [to_twin(piece) for piece in own_pieces]
    x = regrouped(tokens.reshape(local_len, width))
    valid_count = regrouped(lengths)
    rest = lax.all_gather(rest, "fsdp", axis=0, tiled=True)
    starts = jnp.stack([core, 1 - core]) * local_len
    valid = jnp.clip(valid_count - starts, 0, local_len).astype(jnp.int32)
    upstream = regrouped(cotangent.reshape(local_len, width))

    far_out, own_part, normed, packed_full, table, up_shift = project(place, x, own_pieces, far_pieces, hidden)
    far_part = to_twin(far_out)
    parts = [own_part, far_part]
    (own_mix, far_mix_out), totals = attention(valid, parts, 352)
    far_mix = to_twin(far_mix_out)
    middle, branch1, normed2 = merge(place, x, own_mix, far_mix, table, rest)

    branch2, delta_normed2, up_mine, up_other, down_mine, down_other, up_sums = mlp(
        place, normed2, upstream, table, rest, up_shift, owners
    )
    up_twin, down_twin = to_twin(up_other), to_twin(down_other)
    output, delta_middle, own_grad, far_grad_out, output_mine, output_other, middle_sums = unmerge(
        place, middle, branch1, branch2, delta_normed2, upstream, own_mix, far_mix, table, rest, owners
    )
    far_grad = to_twin(far_grad_out)
    ring = RingSum((up_mine, up_twin, 0, 1), (down_mine, down_twin, 0, 1))
    output_sent = regroup_moves(output)
    output_twin = to_twin(output_other)
    deltas = ()
    grads = [own_grad, far_grad]
    start = 0
    for pairs in split_pairs(width // 2 // LANES):
        sums, _ = ring.sums()
        ring.send(sums)
        after = [*sums, output_sent, output_twin] if start else sums
        deltas = attention_back(
            valid, parts, [own_mix, far_mix_out], grads, totals, 352, start, pairs, deltas, after
        )
        start += pairs
    own_delta, far_delta_out = deltas
    sums, (far_delta_out,) = ring.sums(carry=[far_delta_out])
    ring.send(sums)
    far_delta = to_twin(far_delta_out)
    grad_x, packed_mine, packed_other, vectors_mine, vectors_other = unproject(
        place, x, delta_middle, table, normed, own_delta, far_delta, packed_full, middle_sums, up_sums, owners
    )
    output = jnp.where(stays, output, output_sent).reshape(tokens.shape)
    grad_x, packed_other, vectors_other = passed([grad_x, packed_other, vectors_other], ring.came)
    vectors_twin, packed_twin = to_twin(vectors_other), to_twin(packed_other)
    rest_sum, _ = ring.total()
    rings = (
        RingSum(
            (packed_mine, packed_twin, 0, 2), (output_mine, output_twin, 0, 2), (vectors_mine, vectors_twin, 0, 1)
        ),
        RingSum((packed_mine, packed_twin, 1, 2), (output_mine, output_twin, 1, 2)),
    )
    grad_x_sent, rest_sent = regroup_moves(grad_x), across(rest_sum)
    last = [rest_sum]
    for step in range(rings[0].steps):
        for half in rings:
            after = [*last] + ([grad_x_sent] if step == 2 and half is rings[0] else [])
            last, _ = half.sums(after)
            half.send(last)
    grad_tokens = jnp.where(stays, grad_x, grad_x_sent).astype(F32).reshape(tokens.shape)
    each = up_bias.shape[0]
    grad_up, grad_down = finish_rest(rest_sum, rest_sent, hidden, each, width)
    first_sum, _ = rings[0].total()
    first_sums = [first_sum, rings[1].total([first_sum])[0]]
    grad_packed, grad_output, *mine = finish_first(
        place, first_sums, [across(half) for half in first_sums], width, each
    )
    return (
        output, grad_tokens, mine[0], mine[1], grad_packed, mine[2], mine[3], grad_output, mine[4], mine[5],
        mine[6], mine[7], grad_up, mine[10], grad_down, mine[8], mine[9],
    )


def pairable(tokens, up_weight):
    owners, chips = lax.axis_size("fsdp"), lax.axis_size("fsdp") // 2
    width, hidden = up_weight.shape[0] * owners, up_weight.shape[1]
    return (
        lax.axis_size("seq") == 2
        and tokens.shape[0] == 1
        and tokens.shape[1] % 16 == 0
        and owners == 2 * chips
        and chips in (4, 8)
        and width % (chips * LANES) == 0
        and hidden % (owners * LANES) == 0
        and H * HD == width
    )


def body(*args):
    chosen = paired_body if pairable(args[0], args[12]) else general_body
    return chosen(*args)


def solution(mesh):
    in_specs = (
        P("fsdp", "seq", None),
        P("fsdp"),
        P("fsdp"),
        P("fsdp"),
        P("fsdp", None),
        P("fsdp"),
        P("fsdp"),
        P("fsdp", None),
        P("fsdp"),
        P("fsdp"),
        P("fsdp"),
        P("fsdp"),
        P("fsdp", None),
        P("fsdp"),
        P("fsdp", None),
        P("fsdp"),
        P("fsdp"),
        P("fsdp", "seq", None),
    )
    out_specs = (
        P("fsdp", "seq", None),
        P("fsdp", "seq", None),
        P("fsdp"),
        P("fsdp"),
        P("fsdp", None),
        P("fsdp"),
        P("fsdp"),
        P("fsdp", None),
        P("fsdp"),
        P("fsdp"),
        P("fsdp"),
        P("fsdp"),
        P("fsdp", None),
        P("fsdp"),
        P("fsdp", None),
        P("fsdp"),
        P("fsdp"),
    )
    return jax.shard_map(body, mesh=mesh, in_specs=in_specs, out_specs=out_specs, check_vma=False)
```

```python
import functools

import jax
import jax.numpy as jnp
import numpy as np
from jax import lax
from jax.experimental import pallas as pl
from jax.experimental.pallas import tpu as pltpu
from jax.sharding import PartitionSpec as P

H = 16
HD = 64


norm_eps = 1e-06


def layer_norm(values, norm_gain, norm_shift):
    center = values - jnp.mean(values, axis=-1, keepdims=True)
    spread = jnp.mean(center * center, axis=-1, keepdims=True)
    return center * lax.rsqrt(spread + norm_eps) * norm_gain + norm_shift


def gelu_exact(values):
    return jax.nn.gelu(values, approximate=False)


def matmul(left, right):
    return jnp.dot(left, right, preferred_element_type=jnp.float32)


def left_outer(left, right):
    return jnp.einsum("ti,tj->ij", left, right, preferred_element_type=jnp.float32)


def right_back(left, right):
    return jnp.einsum("tj,ij->ti", left, right, preferred_element_type=jnp.float32)


def column_sum(values):
    return jnp.sum(values.astype(jnp.float32), axis=0)


def attention_probs(queries, key_rows, valid_count, score_scale):
    scores = score_scale * jnp.einsum(
        "qhd,khd->hqk", queries, key_rows, preferred_element_type=jnp.float32
    )
    key_valid = jnp.arange(key_rows.shape[0]) < valid_count
    scores = jnp.where(key_valid[None, None, :], scores, -jnp.inf)
    return scores


def attend(queries, key_rows, values, valid_count, score_scale):
    scores = attention_probs(queries, key_rows, valid_count, score_scale)
    largest = jnp.max(scores, axis=-1, keepdims=True)
    log_total = largest[..., 0] + jnp.log(jnp.sum(jnp.exp(scores - largest), axis=-1))
    attention = jnp.exp(scores - log_total[..., None]).astype(jnp.bfloat16)
    mixture = jnp.einsum("hqk,khd->qhd", attention, values, preferred_element_type=jnp.float32)
    return (mixture.astype(jnp.bfloat16), log_total)


def attend_back(queries, key_rows, values, valid_count, score_scale, log_total, grad_mixture):
    scores = attention_probs(queries, key_rows, valid_count, score_scale)
    probs = jnp.exp(scores - log_total[..., None])
    grad_values = jnp.einsum(
        "hqk,qhd->khd", probs.astype(jnp.bfloat16), grad_mixture, preferred_element_type=jnp.float32
    )
    grad_probs = jnp.einsum(
        "qhd,khd->hqk", grad_mixture, values, preferred_element_type=jnp.float32
    )
    inner_sum = jnp.sum(probs * grad_probs, axis=-1, keepdims=True)
    grad_scores = (probs * (grad_probs - inner_sum)).astype(jnp.bfloat16)
    grad_queries = score_scale * jnp.einsum(
        "hqk,khd->qhd", grad_scores, key_rows, preferred_element_type=jnp.float32
    )
    grad_keys = score_scale * jnp.einsum(
        "hqk,qhd->khd", grad_scores, queries, preferred_element_type=jnp.float32
    )
    return (grad_queries, grad_keys, grad_values)


def general_body(
    tokens,
    lengths,
    norm1_gain,
    norm1_bias,
    packed_weight,
    query_bias,
    value_bias,
    output_weight,
    output_bias,
    layer_scale1,
    norm2_gain,
    norm2_bias,
    up_weight,
    up_bias,
    down_weight,
    down_bias,
    layer_scale2,
    cotangent,
):
    gathered = (
        lax.all_gather(norm1_gain, "fsdp", axis=0, tiled=True),
        lax.all_gather(norm1_bias, "fsdp", axis=0, tiled=True),
        lax.all_gather(packed_weight, "fsdp", axis=0, tiled=True),
        lax.all_gather(query_bias, "fsdp", axis=0, tiled=True),
        lax.all_gather(value_bias, "fsdp", axis=0, tiled=True),
        lax.all_gather(output_weight, "fsdp", axis=0, tiled=True),
        lax.all_gather(output_bias, "fsdp", axis=0, tiled=True),
        lax.all_gather(layer_scale1, "fsdp", axis=0, tiled=True),
        lax.all_gather(norm2_gain, "fsdp", axis=0, tiled=True),
        lax.all_gather(norm2_bias, "fsdp", axis=0, tiled=True),
        lax.all_gather(up_weight, "fsdp", axis=0, tiled=True),
        lax.all_gather(up_bias, "fsdp", axis=0, tiled=True),
        lax.all_gather(down_weight, "fsdp", axis=0, tiled=True),
        lax.all_gather(down_bias, "fsdp", axis=0, tiled=True),
        lax.all_gather(layer_scale2, "fsdp", axis=0, tiled=True),
    )
    (
        gain_one,
        shift_one,
        packed_full,
        query_shift,
        value_shift,
        output_full,
        output_shift,
        scale_one,
        gain_two,
        shift_two,
        up_full,
        up_shift,
        down_full,
        down_shift,
        scale_two,
    ) = gathered
    gain_one = gain_one.astype(jnp.float32)
    shift_one = shift_one.astype(jnp.float32)
    query_shift = query_shift.astype(jnp.float32)
    value_shift = value_shift.astype(jnp.float32)
    output_shift = output_shift.astype(jnp.float32)
    scale_one = scale_one.astype(jnp.float32)
    gain_two = gain_two.astype(jnp.float32)
    shift_two = shift_two.astype(jnp.float32)
    up_shift = up_shift.astype(jnp.float32)
    down_shift = down_shift.astype(jnp.float32)
    scale_two = scale_two.astype(jnp.float32)
    groups = lax.axis_size("seq")
    images, local_len, model_width = tokens.shape
    seq_len = local_len * groups
    per_group = H // groups
    score_scale = HD ** (-0.5)
    token_rows = tokens.astype(jnp.float32).reshape(images * local_len, model_width)
    normed = layer_norm(token_rows, gain_one, shift_one).astype(jnp.bfloat16)
    packed_shift = jnp.concatenate([query_shift, jnp.zeros_like(query_shift), value_shift])
    packed = (matmul(normed, packed_full) + packed_shift).astype(jnp.bfloat16)
    packed = packed.reshape(images, local_len, 3, groups, per_group * HD)
    spread = lax.all_to_all(packed, "seq", split_axis=3, concat_axis=1, tiled=True)
    spread = spread.reshape(images, seq_len, 3, per_group, HD)

    def forward_image(per_image):
        image_block, valid_count = per_image
        return attend(
            image_block[:, 0], image_block[:, 1], image_block[:, 2], valid_count, score_scale
        )

    mixture, log_total = lax.map(forward_image, (spread, lengths))
    mixture = mixture.reshape(images, seq_len, 1, per_group * HD)
    mixture_rows = lax.all_to_all(mixture, "seq", split_axis=1, concat_axis=2, tiled=True).reshape(
        images * local_len, model_width
    )
    branch_one = matmul(mixture_rows, output_full) + output_shift
    middle = token_rows + scale_one * branch_one
    normed_two = layer_norm(middle, gain_two, shift_two).astype(jnp.bfloat16)
    hidden = matmul(normed_two, up_full) + up_shift
    active = gelu_exact(hidden).astype(jnp.bfloat16)
    branch_two = matmul(active, down_full) + down_shift
    output = (middle + scale_two * branch_two).astype(jnp.bfloat16).reshape(tokens.shape)
    upstream = cotangent.astype(jnp.float32).reshape(images * local_len, model_width)
    grad_scale_two = jnp.sum(upstream * branch_two, axis=0)
    delta_two = (scale_two * upstream).astype(jnp.bfloat16)
    grad_down_shift = column_sum(delta_two)
    grad_down = left_outer(active, delta_two)
    grad_active = right_back(delta_two, down_full)
    _, gelu_pull = jax.vjp(gelu_exact, hidden)
    delta_hidden = gelu_pull(grad_active)[0].astype(jnp.bfloat16)
    grad_up_shift = column_sum(delta_hidden)
    grad_up = left_outer(normed_two, delta_hidden)
    delta_normed_two = right_back(delta_hidden, up_full)
    _, norm_pull_two = jax.vjp(layer_norm, middle, gain_two, shift_two)
    grad_middle_norm, grad_gain_two, grad_shift_two = norm_pull_two(delta_normed_two)
    delta_middle = upstream + grad_middle_norm
    grad_scale_one = jnp.sum(delta_middle * branch_one, axis=0)
    delta_one = (scale_one * delta_middle).astype(jnp.bfloat16)
    grad_output_shift = column_sum(delta_one)
    grad_output = left_outer(mixture_rows, delta_one)
    delta_mixture = right_back(delta_one, output_full).astype(jnp.bfloat16)
    delta_mixture = delta_mixture.reshape(images, local_len, groups, per_group * HD)
    grad_spread = lax.all_to_all(delta_mixture, "seq", split_axis=2, concat_axis=1, tiled=True)
    grad_spread = grad_spread.reshape(images, seq_len, per_group, HD)

    def backward_image(per_image):
        image_block, valid_count, image_total, image_grad = per_image
        grad_queries, grad_keys, grad_values = attend_back(
            image_block[:, 0],
            image_block[:, 1],
            image_block[:, 2],
            valid_count,
            score_scale,
            image_total,
            image_grad,
        )
        return jnp.stack([grad_queries, grad_keys, grad_values], axis=1).astype(jnp.bfloat16)

    delta_packed = lax.map(backward_image, (spread, lengths, log_total, grad_spread))
    delta_packed = delta_packed.reshape(images, seq_len, 3, 1, per_group * HD)
    delta_back = lax.all_to_all(delta_packed, "seq", split_axis=1, concat_axis=3, tiled=True)
    delta_back = delta_back.reshape(images * local_len, 3 * model_width)
    grad_query_shift = column_sum(delta_back[:, :model_width])
    grad_value_shift = column_sum(delta_back[:, 2 * model_width :])
    grad_packed = left_outer(normed, delta_back)
    delta_normed = right_back(delta_back, packed_full)
    _, norm_pull_one = jax.vjp(layer_norm, token_rows, gain_one, shift_one)
    grad_rows_norm, grad_gain_one, grad_shift_one = norm_pull_one(delta_normed)
    grad_tokens = (delta_middle + grad_rows_norm).reshape(tokens.shape)
    local_grads = (
        grad_gain_one,
        grad_shift_one,
        grad_packed,
        grad_query_shift,
        grad_value_shift,
        grad_output,
        grad_output_shift,
        grad_scale_one,
        grad_gain_two,
        grad_shift_two,
        grad_up,
        grad_up_shift,
        grad_down,
        grad_down_shift,
        grad_scale_two,
    )
    owned_grads = (
        lax.psum_scatter(
            local_grads[0].astype(jnp.bfloat16), "fsdp", scatter_dimension=0, tiled=True
        ).astype(jnp.float32),
        lax.psum_scatter(
            local_grads[1].astype(jnp.bfloat16), "fsdp", scatter_dimension=0, tiled=True
        ).astype(jnp.float32),
        lax.psum_scatter(
            local_grads[2].astype(jnp.bfloat16), "fsdp", scatter_dimension=0, tiled=True
        ).astype(jnp.float32),
        lax.psum_scatter(
            local_grads[3].astype(jnp.bfloat16), "fsdp", scatter_dimension=0, tiled=True
        ).astype(jnp.float32),
        lax.psum_scatter(
            local_grads[4].astype(jnp.bfloat16), "fsdp", scatter_dimension=0, tiled=True
        ).astype(jnp.float32),
        lax.psum_scatter(
            local_grads[5].astype(jnp.bfloat16), "fsdp", scatter_dimension=0, tiled=True
        ).astype(jnp.float32),
        lax.psum_scatter(
            local_grads[6].astype(jnp.bfloat16), "fsdp", scatter_dimension=0, tiled=True
        ).astype(jnp.float32),
        lax.psum_scatter(
            local_grads[7].astype(jnp.bfloat16), "fsdp", scatter_dimension=0, tiled=True
        ).astype(jnp.float32),
        lax.psum_scatter(
            local_grads[8].astype(jnp.bfloat16), "fsdp", scatter_dimension=0, tiled=True
        ).astype(jnp.float32),
        lax.psum_scatter(
            local_grads[9].astype(jnp.bfloat16), "fsdp", scatter_dimension=0, tiled=True
        ).astype(jnp.float32),
        lax.psum_scatter(
            local_grads[10].astype(jnp.bfloat16), "fsdp", scatter_dimension=0, tiled=True
        ).astype(jnp.float32),
        lax.psum_scatter(
            local_grads[11].astype(jnp.bfloat16), "fsdp", scatter_dimension=0, tiled=True
        ).astype(jnp.float32),
        lax.psum_scatter(
            local_grads[12].astype(jnp.bfloat16), "fsdp", scatter_dimension=0, tiled=True
        ).astype(jnp.float32),
        lax.psum_scatter(
            local_grads[13].astype(jnp.bfloat16), "fsdp", scatter_dimension=0, tiled=True
        ).astype(jnp.float32),
        lax.psum_scatter(
            local_grads[14].astype(jnp.bfloat16), "fsdp", scatter_dimension=0, tiled=True
        ).astype(jnp.float32),
    )
    owned_grads = (
        lax.psum(owned_grads[0].astype(jnp.bfloat16), "seq").astype(jnp.float32),
        lax.psum(owned_grads[1].astype(jnp.bfloat16), "seq").astype(jnp.float32),
        lax.psum(owned_grads[2].astype(jnp.bfloat16), "seq").astype(jnp.float32),
        lax.psum(owned_grads[3].astype(jnp.bfloat16), "seq").astype(jnp.float32),
        lax.psum(owned_grads[4].astype(jnp.bfloat16), "seq").astype(jnp.float32),
        lax.psum(owned_grads[5].astype(jnp.bfloat16), "seq").astype(jnp.float32),
        lax.psum(owned_grads[6].astype(jnp.bfloat16), "seq").astype(jnp.float32),
        lax.psum(owned_grads[7].astype(jnp.bfloat16), "seq").astype(jnp.float32),
        lax.psum(owned_grads[8].astype(jnp.bfloat16), "seq").astype(jnp.float32),
        lax.psum(owned_grads[9].astype(jnp.bfloat16), "seq").astype(jnp.float32),
        lax.psum(owned_grads[10].astype(jnp.bfloat16), "seq").astype(jnp.float32),
        lax.psum(owned_grads[11].astype(jnp.bfloat16), "seq").astype(jnp.float32),
        lax.psum(owned_grads[12].astype(jnp.bfloat16), "seq").astype(jnp.float32),
        lax.psum(owned_grads[13].astype(jnp.bfloat16), "seq").astype(jnp.float32),
        lax.psum(owned_grads[14].astype(jnp.bfloat16), "seq").astype(jnp.float32),
    )
    return (output, grad_tokens) + tuple(owned_grads)


BF16 = jnp.bfloat16
F32 = jnp.float32
NT = (((1,), (1,)), ((), ()))
NN = (((1,), (0,)), ((), ()))
MASKED = -1e30
LANES = 128
VMEM_LIMIT = 60 * 2**20
SMALL_VMEM = 8 * 2**20

GAIN1, SHIFT1, QUERY, VALUE, OUT_SHIFT, SCALE1, GAIN2, SHIFT2, DOWN_SHIFT, SCALE2 = range(10)


def dot(left, right, dims=NN):
    return lax.dot_general(left, right, dims, preferred_element_type=F32)


def turned(values):
    return values.T


def lane_ids(rows):
    return lax.broadcasted_iota(jnp.int32, (rows, LANES), 1)


def split3(values):
    high = values.astype(BF16).astype(F32)
    rest = values - high
    mid = rest.astype(BF16).astype(F32)
    return high, mid, rest - mid


LONG, SHORT = 16.0, 1 / 64


def params_for(flops, nbytes, transcendentals=0, weight=1.0, vmem=VMEM_LIMIT):
    flops, nbytes, transcendentals = (int(weight * count) for count in (flops, nbytes, transcendentals))
    return dict(
        compiler_params=pltpu.CompilerParams(vmem_limit_bytes=vmem),
        cost_estimate=pl.CostEstimate(
            flops=flops, bytes_accessed=nbytes, transcendentals=transcendentals
        ),
    )


def whole(shape):
    return pl.BlockSpec(shape, lambda *_: (0,) * len(shape))


def normalize(values, gain, shift):
    center = values - jnp.mean(values, axis=-1, keepdims=True)
    spread = jnp.mean(center * center, axis=-1, keepdims=True)
    return center * lax.rsqrt(spread + norm_eps) * gain + shift


def normalize_back(values, gain, delta):
    center = values - jnp.mean(values, axis=-1, keepdims=True)
    inverse = lax.rsqrt(jnp.mean(center * center, axis=-1, keepdims=True) + norm_eps)
    unit = center * inverse
    scaled = delta * gain
    mean_scaled = jnp.mean(scaled, axis=-1, keepdims=True)
    mean_unit = jnp.mean(scaled * unit, axis=-1, keepdims=True)
    return inverse * (scaled - mean_scaled - unit * mean_unit), delta * unit


def total_rows(values):
    return jnp.sum(values, axis=0, keepdims=True)


VECTORS = 10


def pack_kernel(weight_ref, up_ref, down_ref, output_ref, *refs):
    vector_refs, shift_ref = refs[:VECTORS], refs[VECTORS]
    first_ref, rest_ref, laid = refs[VECTORS + 1 :]
    rows, width = weight_ref.shape
    first_ref[:, :width] = weight_ref[...]
    laid[...] = jnp.zeros_like(laid)
    core = lax.rem(lax.axis_index("fsdp"), 2)
    for i, ref in enumerate(vector_refs):
        values = ref[...].astype(F32).reshape(1, -1)
        empty = jnp.zeros_like(values)
        first, second = jnp.concatenate([values, empty], 1), jnp.concatenate([empty, values], 1)
        laid[i : i + 1, :] = jnp.where(core == 0, first, second)
    shift = shift_ref[...].astype(F32).reshape(-1, LANES)
    laid[VECTORS : VECTORS + shift.shape[0], :] = shift
    first_ref[:, width:] = laid[...].astype(BF16)
    at = 0
    for ref in (up_ref, down_ref, output_ref):
        for g in range(ref.shape[0] // rows):
            rest_ref[:, at : at + ref.shape[1]] = ref[g * rows : (g + 1) * rows, :]
            at += ref.shape[1]


def pack(weight, up, down, output, vectors, up_shift):
    in_vmem = pl.BlockSpec(memory_space=pltpu.VMEM)
    rows, width = weight.shape
    others = (up.size + down.size + output.size) // rows
    return pl.pallas_call(
        pack_kernel,
        in_specs=[in_vmem] * (VECTORS + 5),
        out_specs=[in_vmem, in_vmem],
        out_shape=[
            jax.ShapeDtypeStruct((rows, width + LANES), BF16),
            jax.ShapeDtypeStruct((rows, others), BF16),
        ],
        scratch_shapes=[pltpu.VMEM((rows, LANES), F32)],
        name="pack",
        **params_for(0, 4 * rows * (width + others)),
    )(weight, up, down, output, *vectors, up_shift)


CORE, CHIPS = 6, 7


def project_kernel(place, x_ref, *refs, chips):
    own_refs, far_refs, own_vectors, far_vectors = (refs[chips * i : chips * (i + 1)] for i in range(4))
    far_out_ref, own_ref, normed_ref, weight_ref, table_ref, up_ref = refs[4 * chips :]
    step = pl.program_id(0)
    rows = own_refs[0].shape[0]
    core = place[CORE]

    @pl.when(step == 0)
    def _():
        vector = lax.broadcasted_iota(jnp.int32, (table_ref.shape[0], LANES), 0) < VECTORS
        each = up_ref.shape[1] // (2 * chips)
        for k in range(chips):
            chip = place[CHIPS + k]
            own = own_vectors[k][...].astype(F32)
            far = far_vectors[k][...].astype(F32)
            at = pl.ds(pl.multiple_of(chip * LANES, LANES), LANES)
            table_ref[:, at] = jnp.where(vector, own + far, 0.0)
            for part, side in ((own, core), (far, 1 - core)):
                for r in range(each // LANES):
                    at = pl.multiple_of((2 * chip + side) * each + r * LANES, LANES)
                    up_ref[:, pl.ds(at, LANES)] = part[VECTORS + r : VECTORS + r + 1, :]
        normed_ref[...] = normalize(
            x_ref[...].astype(F32), table_ref[GAIN1 : GAIN1 + 1, :], table_ref[SHIFT1 : SHIFT1 + 1, :]
        ).astype(BF16)

    for k in range(chips):
        start = 2 * place[CHIPS + k]
        weight_ref[pl.ds(pl.multiple_of((start + core) * rows, rows), rows), :] = own_refs[k][...]
        weight_ref[pl.ds(pl.multiple_of((start + 1 - core) * rows, rows), rows), :] = far_refs[k][...]
    shift = jnp.where(
        step == 0,
        table_ref[QUERY : QUERY + 1, :],
        jnp.where(step == 2, table_ref[VALUE : VALUE + 1, :], 0.0),
    )
    result = (dot(normed_ref[...], weight_ref[...]) + shift).astype(BF16)
    half = result.shape[1] // 2
    low, high = result[:, :half], result[:, half:]
    own_ref[0] = jnp.where(core == 0, low, high)
    far_out_ref[0] = jnp.where(core == 0, high, low)


def project(place, x, own_pieces, far_pieces, hidden):
    chips = len(own_pieces)
    tokens, width = x.shape
    rows = own_pieces[0].shape[0]
    kind = pl.BlockSpec((1, tokens, width // 2), lambda j, _: (j, 0, 0))
    return pl.pallas_call(
        functools.partial(project_kernel, chips=chips),
        grid_spec=pltpu.PrefetchScalarGridSpec(
            num_scalar_prefetch=1,
            grid=(3,),
            in_specs=[whole((tokens, width))]
            + [pl.BlockSpec((rows, width), lambda j, _: (0, j))] * 2 * chips
            + [pl.BlockSpec((16, LANES), lambda j, _: (0, 3 * width // LANES))] * 2 * chips,
            out_specs=[
                kind,
                kind,
                whole((tokens, width)),
                pl.BlockSpec((width, width), lambda j, _: (0, j)),
                whole((16, width)),
                whole((1, hidden)),
            ],
        ),
        out_shape=[
            jax.ShapeDtypeStruct((3, tokens, width // 2), BF16),
            jax.ShapeDtypeStruct((3, tokens, width // 2), BF16),
            jax.ShapeDtypeStruct((tokens, width), BF16),
            jax.ShapeDtypeStruct((width, 3 * width), BF16),
            jax.ShapeDtypeStruct((16, width), F32),
            jax.ShapeDtypeStruct((1, hidden), F32),
        ],
        name="project",
        **params_for(6 * tokens * width * width, 12 * tokens * width + 12 * width * width),
    )(place, x, *own_pieces, *far_pieces, *own_pieces, *far_pieces)


def padded_len(count, block):
    return -(-count // block) * block


def attend_kernel(valid, *refs, pieces, block, scale):
    in_refs, out_refs = refs[:pieces], refs[pieces : 2 * pieces]
    total_refs = refs[2 * pieces : 3 * pieces]
    keys, values, queries, mixed, totals = refs[3 * pieces :]
    pair = pl.program_id(0)
    size = in_refs[0].shape[1]
    count, padded = pieces * size, keys.shape[0]
    lane = lane_ids(size)
    row = lax.broadcasted_iota(jnp.int32, (size, LANES), 0)
    for i in range(pieces):
        at = pl.ds(i * size, size)
        keys[at, :LANES] = in_refs[i][1]
        keys[at, LANES:] = jnp.where((lane == 0) & (row >= valid[i]), MASKED, 0.0).astype(BF16)
        values[at, :LANES] = in_refs[i][2]
        values[at, LANES:] = jnp.where(lane == 0, 1.0, 0.0).astype(BF16)
        for j in range(2):
            mine = lane // HD == j
            queries[j, at, :LANES] = jnp.where(mine, in_refs[i][0].astype(F32) * scale, 0.0).astype(BF16)
            queries[j, at, LANES:] = jnp.where(lane == 0, 1.0, 0.0).astype(BF16)
    if padded > count:
        rest = pl.ds(count, padded - count)
        rest_lane = lane_ids(padded - count)
        keys[rest, :LANES] = jnp.zeros((padded - count, LANES), BF16)
        keys[rest, LANES:] = jnp.where(rest_lane == 0, MASKED, 0.0).astype(BF16)
        values[rest, :] = jnp.zeros((padded - count, 2 * LANES), BF16)
        for j in range(2):
            queries[j, rest, :] = jnp.zeros((padded - count, 2 * LANES), BF16)

    @pl.when(pair == 0)
    def _():
        for i in range(pieces):
            total_refs[i][...] = jnp.zeros_like(total_refs[i])

    block_lane = lane_ids(block)
    for b in range(padded // block):
        at = pl.ds(b * block, block)
        results, logs = [], 0.0
        for j in range(2):
            scores = dot(queries[j, at, :], keys[...], NT)
            largest = jnp.max(scores, axis=1, keepdims=True)
            weights = jnp.exp(scores - largest).astype(BF16)
            result = dot(weights, values[...])
            total = result[:, LANES : LANES + 1]
            results.append(result[:, :LANES] * (1.0 / total))
            logs += jnp.where(block_lane == 2 * pair + j, largest + jnp.log(total), 0.0)
        mixed[at, :] = jnp.where(block_lane < HD, results[0], results[1])
        totals[at, :] = logs
    for i in range(pieces):
        at = pl.ds(i * size, size)
        out_refs[i][...] = mixed[at, :].astype(BF16)
        total_refs[i][...] += totals[at, :]


def attention(valid, parts, block):
    pieces = len(parts)
    _, size, width = parts[0].shape
    pairs = width // LANES
    padded = padded_len(pieces * size, block)
    outs = pl.pallas_call(
        functools.partial(attend_kernel, pieces=pieces, block=block, scale=HD**-0.5),
        grid_spec=pltpu.PrefetchScalarGridSpec(
            num_scalar_prefetch=1,
            grid=(pairs,),
            in_specs=[pl.BlockSpec((3, size, LANES), lambda h, _: (0, 0, h))] * pieces,
            out_specs=[pl.BlockSpec((size, LANES), lambda h, _: (0, h))] * pieces
            + [whole((size, LANES))] * pieces,
            scratch_shapes=[
                pltpu.VMEM((padded, 2 * LANES), BF16),
                pltpu.VMEM((padded, 2 * LANES), BF16),
                pltpu.VMEM((2, padded, 2 * LANES), BF16),
                pltpu.VMEM((padded, LANES), F32),
                pltpu.VMEM((padded, LANES), F32),
            ],
        ),
        out_shape=[jax.ShapeDtypeStruct((size, width), BF16)] * pieces
        + [jax.ShapeDtypeStruct((size, LANES), F32)] * pieces,
        name="attend",
        **params_for(16 * pairs * LANES * padded * padded, 8 * size * width * pieces, pairs * 2 * padded * padded),
    )(valid, *parts)
    return outs[:pieces], outs[pieces:]


def attend_back_kernel(valid, *refs, pieces, block, scale, first):
    in_refs, mix_refs = refs[:pieces], refs[pieces : 2 * pieces]
    grad_refs, total_refs = refs[2 * pieces : 3 * pieces], refs[3 * pieces : 4 * pieces]
    out_refs = refs[-9 - pieces : -9]
    keys, values, queries, grads, queries_t, grads_t, dq, dk_t, dv_t = refs[-9:]
    pair = first + pl.program_id(0)
    size = in_refs[0].shape[1]
    count, padded = pieces * size, keys.shape[0]
    blocks = padded // block
    lane = lane_ids(size)
    row = lax.broadcasted_iota(jnp.int32, (size, LANES), 0)
    for i in range(pieces):
        at = pl.ds(i * size, size)
        keys[at, :LANES] = in_refs[i][1]
        keys[at, LANES:] = jnp.where(
            lane == 0, jnp.where(row >= valid[i], MASKED, 0.0), jnp.where(lane < 4, 1.0, 0.0)
        ).astype(BF16)
        values[at, :LANES] = in_refs[i][2]
        values[at, LANES:] = jnp.where((lane > 0) & (lane < 4), 1.0, 0.0).astype(BF16)
        queries[0, at, :LANES] = in_refs[i][0]
        grads[0, at, :LANES] = grad_refs[i][...]
    if padded > count:
        left = padded - count
        rest = pl.ds(count, left)
        keys[rest, :LANES] = jnp.zeros((left, LANES), BF16)
        keys[rest, LANES:] = jnp.where(lane_ids(left) == 0, MASKED, 0.0).astype(BF16)
        values[rest, :] = jnp.zeros((left, 2 * LANES), BF16)
        for j in range(2):
            queries[j, rest, :] = jnp.zeros((left, 2 * LANES), BF16)
            grads[j, rest, :] = jnp.zeros((left, 2 * LANES), BF16)
    for b in range(blocks):
        at = pl.ds(b * block, block)
        queries_t[b] = (queries[0, at, :LANES].astype(F32) * scale).T.astype(BF16)
        grads_t[b] = turned(grads[0, at, :LANES])
    for j in range(2):
        mine = lane // HD == j
        for i in range(pieces):
            at = pl.ds(i * size, size)
            grad = jnp.where(mine, grad_refs[i][...].astype(F32), 0.0)
            queries[j, at, :LANES] = jnp.where(mine, in_refs[i][0].astype(F32) * scale, 0.0).astype(BF16)
            grads[j, at, :LANES] = grad.astype(BF16)
            log_total = jnp.sum(
                jnp.where(lane == 2 * pair + j, total_refs[i][...], 0.0), axis=1, keepdims=True
            )
            high, mid, low = split3(-log_total)
            queries[j, at, LANES:] = jnp.where(
                lane == 0,
                1.0,
                jnp.where(lane == 1, high, jnp.where(lane == 2, mid, jnp.where(lane == 3, low, 0.0))),
            ).astype(BF16)
            inner = jnp.sum(grad * mix_refs[i][...].astype(F32), axis=1, keepdims=True)
            high, mid, low = split3(-inner)
            grads[j, at, LANES:] = jnp.where(
                lane == 1, high, jnp.where(lane == 2, mid, jnp.where(lane == 3, low, 0.0))
            ).astype(BF16)
    dk_t[...] = jnp.zeros_like(dk_t)
    dv_t[...] = jnp.zeros_like(dv_t)
    block_lane = lane_ids(block)
    for b in range(blocks):
        at = pl.ds(b * block, block)
        results = []
        for j in range(2):
            mine = pl.ds(j * HD, HD)
            probs = jnp.exp(dot(queries[j, at, :], keys[...], NT))
            grad_scores = (probs * dot(grads[j, at, :], values[...], NT)).astype(BF16)
            results.append(dot(grad_scores, keys[:, :LANES]) * scale)
            dv_t[mine, :] += dot(grads_t[b, mine, :], probs.astype(BF16))
            dk_t[mine, :] += dot(queries_t[b, mine, :], grad_scores)
        dq[at, :] = jnp.where(block_lane < HD, results[0], results[1])
    dk, dv = dk_t[...].T, dv_t[...].T
    for i in range(pieces):
        at = slice(i * size, (i + 1) * size)
        out_refs[i][0] = dq[at, :].astype(BF16)
        out_refs[i][1] = dk[at, :].astype(BF16)
        out_refs[i][2] = dv[at, :].astype(BF16)


def attention_back(valid, parts, mixtures, grads, totals, block, first, pairs, into, after):
    pieces = len(parts)
    _, size, width = parts[0].shape
    padded = padded_len(pieces * size, block)
    triple = pl.BlockSpec((3, size, LANES), lambda h, _: (0, 0, first + h))
    single = pl.BlockSpec((size, LANES), lambda h, _: (0, first + h))
    in_specs = [triple] * pieces + [single] * 2 * pieces + [whole((size, LANES))] * pieces
    aliases = {1 + len(in_specs) + i: i for i in range(len(into))}
    return pl.pallas_call(
        functools.partial(attend_back_kernel, pieces=pieces, block=block, scale=HD**-0.5, first=first),
        grid_spec=pltpu.PrefetchScalarGridSpec(
            num_scalar_prefetch=1,
            grid=(pairs,),
            in_specs=in_specs + [pl.BlockSpec(memory_space=pl.ANY)] * (len(into) + len(after)),
            out_specs=[triple] * pieces,
            scratch_shapes=[
                pltpu.VMEM((padded, 2 * LANES), BF16),
                pltpu.VMEM((padded, 2 * LANES), BF16),
                pltpu.VMEM((2, padded, 2 * LANES), BF16),
                pltpu.VMEM((2, padded, 2 * LANES), BF16),
                pltpu.VMEM((padded // block, LANES, block), BF16),
                pltpu.VMEM((padded // block, LANES, block), BF16),
                pltpu.VMEM((padded, LANES), F32),
                pltpu.VMEM((LANES, padded), F32),
                pltpu.VMEM((LANES, padded), F32),
            ],
        ),
        out_shape=[jax.ShapeDtypeStruct((3, size, width), BF16)] * pieces,
        input_output_aliases=aliases,
        name="attend_back",
        **params_for(30 * pairs * LANES * padded * padded, 16 * size * LANES * pairs * pieces, pairs * 2 * padded * padded, weight=LONG),
    )(valid, *parts, *mixtures, *grads, *totals, *into, *after)


def merge_kernel(place, x_ref, own_ref, far_ref, table, own_w, far_w, middle_ref, branch_ref, normed_ref):
    branch = dot(own_ref[...], own_w[...]) + dot(far_ref[...], far_w[...])
    branch += table[OUT_SHIFT : OUT_SHIFT + 1, :]
    middle = x_ref[...].astype(F32) + table[SCALE1 : SCALE1 + 1, :] * branch
    middle_ref[...] = middle
    branch_ref[...] = branch
    normed_ref[...] = normalize(
        middle, table[GAIN2 : GAIN2 + 1, :], table[SHIFT2 : SHIFT2 + 1, :]
    ).astype(BF16)


ROWS = 352


def row_steps(tokens):
    return -(-tokens // ROWS)


def merge(place, x, own, far, table, rest):
    tokens, width = x.shape
    half = width // 2
    wide = pl.BlockSpec((ROWS, width), lambda i, _: (i, 0))
    narrow = pl.BlockSpec((ROWS, half), lambda i, _: (i, 0))
    return pl.pallas_call(
        merge_kernel,
        grid_spec=pltpu.PrefetchScalarGridSpec(
            num_scalar_prefetch=1,
            grid=(row_steps(tokens),),
            in_specs=[
                wide,
                narrow,
                narrow,
                whole(table.shape),
                pl.BlockSpec((half, width), lambda i, place: (place[CORE], rest.shape[1] // width - 1)),
                pl.BlockSpec((half, width), lambda i, place: (1 - place[CORE], rest.shape[1] // width - 1)),
            ],
            out_specs=[wide, wide, wide],
        ),
        out_shape=[
            jax.ShapeDtypeStruct((tokens, width), F32),
            jax.ShapeDtypeStruct((tokens, width), F32),
            jax.ShapeDtypeStruct((tokens, width), BF16),
        ],
        name="merge",
        **params_for(2 * tokens * width * width, 14 * tokens * width + 2 * width * width),
    )(place, x, own, far, table, rest, rest)


def gelu_and_slope(values):
    size = jnp.abs(values) * 0.7071067811865476
    t = 1.0 / (1.0 + 0.3275911 * size)
    bell = jnp.exp(-0.5 * (values * values))
    poly = t * (0.254829592 + t * (-0.284496736 + t * (1.421413741 + t * (-1.453152027 + t * 1.061405429))))
    tail = 0.5 * poly * bell
    phi = jnp.where(values < 0, tail, 1.0 - tail)
    return values * phi, phi + values * bell * 0.3989422804014327


def ungroup(grouped_ref, down):
    width = down.shape[1]
    groups = grouped_ref.shape[1] // width
    each = grouped_ref.shape[0] // 2
    for device in range(2):
        for g in range(groups):
            at = (device * groups + g) * each
            down[at : at + each, :] = grouped_ref[device * each : (device + 1) * each, g * width : (g + 1) * width]


def scaled_upstream(cotangent_ref, table):
    return (cotangent_ref[...].astype(F32) * table[SCALE2 : SCALE2 + 1, :]).astype(BF16)


def place_turned(place, block, target, k, chips):
    half = block.shape[1] // 2
    turned_block = block.T
    first, second = turned_block[:half], turned_block[half:]
    target[k * half : (k + 1) * half, :] = jnp.where(place[CORE] == 0, first, second)
    target[(chips + k) * half : (chips + k + 1) * half, :] = jnp.where(place[CORE] == 0, second, first)


def fill_turned(place, source_ref, target, chips):
    wide = source_ref.shape[1] // chips
    for k in range(chips):
        at = pl.ds(pl.multiple_of(place[CHIPS + k] * wide, wide), wide)
        place_turned(place, source_ref[:, at], target, k, chips)


def split_rows(grad, mine_ref, other_ref):
    chips, rows, _ = mine_ref.shape
    for k in range(chips):
        mine_ref[k] = grad[k * rows : (k + 1) * rows, :]
        other_ref[k] = grad[(chips + k) * rows : (chips + k + 1) * rows, :]


def group(grad, out_ref):
    rows, columns = out_ref.shape[1], grad.shape[1]
    for g in range(grad.shape[0] // rows):
        out_ref[0, :, g * columns : (g + 1) * columns] = grad[g * rows : (g + 1) * rows, :]


def mlp_kernel(
    place, normed_ref, cotangent_ref, table, up_ref, shift_ref, grouped_ref,
    branch_ref, delta_ref, up_mine_ref, up_other_ref, down_mine_ref, down_other_ref, grad_shift_ref,
    upstream, upstream_t, normed_t, down,
    *, chips,
):
    @pl.when(pl.program_id(0) == 0)
    def _():
        scaled = (cotangent_ref[...].astype(F32) * table[SCALE2 : SCALE2 + 1, :]).astype(BF16)
        upstream[...] = scaled
        upstream_t[...] = turned(scaled)
        fill_turned(place, normed_ref, normed_t, chips)
        branch_ref[...] = jnp.zeros_like(branch_ref)
        delta_ref[...] = jnp.zeros_like(delta_ref)

    ungroup(grouped_ref, down)
    hidden = dot(normed_ref[...], up_ref[...]) + shift_ref[...]
    grad_active = dot(upstream[...], down[...], NT)
    active, slope = gelu_and_slope(hidden)
    active = active.astype(BF16)
    delta_hidden = (grad_active * slope).astype(BF16)
    branch_ref[...] += dot(active, down[...])
    delta_ref[...] += dot(delta_hidden, up_ref[...], NT)
    split_rows(dot(normed_t[...], delta_hidden).astype(BF16), up_mine_ref, up_other_ref)
    grad_down = dot(upstream_t[...], active)
    each = grad_down.shape[1] // 2
    first, second = grad_down[:, :each], grad_down[:, each:]
    group(jnp.where(place[CORE] == 0, first, second).astype(BF16), down_mine_ref)
    group(jnp.where(place[CORE] == 0, second, first).astype(BF16), down_other_ref)
    grad_shift_ref[...] = total_rows(delta_hidden.astype(F32))


def mlp(place, normed, cotangent, table, rest, up_shift, owners):
    tokens, width = normed.shape
    hidden = up_shift.shape[1]
    rows = rest.shape[0] // owners
    chips = owners // 2
    block = hidden // chips
    up_out = pl.BlockSpec((chips, rows, block), lambda j, place: (0, 0, place[CHIPS + j]))
    down_out = pl.BlockSpec((1, rows, hidden), lambda j, _: (j, 0, 0))
    sent = jax.ShapeDtypeStruct((chips, rows, hidden), BF16)
    return pl.pallas_call(
        functools.partial(mlp_kernel, chips=chips),
        grid_spec=pltpu.PrefetchScalarGridSpec(
            num_scalar_prefetch=1,
            grid=(chips,),
            in_specs=[
                whole((tokens, width)),
                whole((tokens, width)),
                whole(table.shape),
                pl.BlockSpec((width, block), lambda j, place: (0, place[CHIPS + j])),
                pl.BlockSpec((1, block), lambda j, place: (0, place[CHIPS + j])),
                pl.BlockSpec((2 * rows, hidden), lambda j, place: (place[CHIPS + j], 1)),
            ],
            out_specs=[
                whole((tokens, width)),
                whole((tokens, width)),
                up_out,
                up_out,
                down_out,
                down_out,
                pl.BlockSpec((1, block), lambda j, place: (0, place[CHIPS + j])),
            ],
            scratch_shapes=[
                pltpu.VMEM((tokens, width), BF16),
                pltpu.VMEM((width, tokens), BF16),
                pltpu.VMEM((width, tokens), BF16),
                pltpu.VMEM((block, width), BF16),
            ],
        ),
        out_shape=[
            jax.ShapeDtypeStruct((tokens, width), F32),
            jax.ShapeDtypeStruct((tokens, width), F32),
            sent,
            sent,
            sent,
            sent,
            jax.ShapeDtypeStruct((1, hidden), F32),
        ],
        name="mlp",
        **params_for(12 * tokens * width * hidden, 12 * tokens * width + 8 * width * hidden, 2 * tokens * hidden),
    )(place, normed, cotangent, table, rest, up_shift, rest)


SUM_ROWS = 8


def unmerge_kernel(
    place, middle_ref, branch1_ref, branch2_ref, delta_ref, cotangent_ref, own_ref, far_ref, table, own_w, far_w,
    output_ref, delta_middle_ref, own_grad_ref, far_grad_ref, mine_ref, other_ref, sums_ref,
    delta1_all, mixture_t,
    *, tokens,
):
    step = pl.program_id(0)

    @pl.when(step == 0)
    def _():
        sums_ref[...] = jnp.zeros_like(sums_ref)

    rows, width = middle_ref.shape
    inside = lax.broadcasted_iota(jnp.int32, (rows, width), 0) + step * rows < tokens

    def kept(values):
        return jnp.where(inside, values, 0.0)

    upstream = cotangent_ref[...].astype(F32)
    scale2 = table[SCALE2 : SCALE2 + 1, :]
    middle = middle_ref[...]
    branch2 = branch2_ref[...] + table[DOWN_SHIFT : DOWN_SHIFT + 1, :]
    output_ref[...] = (middle + scale2 * branch2).astype(BF16)
    delta2 = (scale2 * upstream).astype(BF16).astype(F32)
    delta = delta_ref[...]
    inner, gain_terms = normalize_back(middle, table[GAIN2 : GAIN2 + 1, :], delta)
    delta_middle = upstream + inner
    delta_middle_ref[...] = delta_middle
    delta1 = kept(table[SCALE1 : SCALE1 + 1, :] * delta_middle).astype(BF16)
    delta1_all[pl.ds(pl.multiple_of(step * rows, 16), rows), :] = delta1
    own_grad_ref[...] = dot(delta1, own_w[...], NT).astype(BF16)
    far_grad_ref[...] = dot(delta1, far_w[...], NT).astype(BF16)
    terms = (
        upstream * branch2,
        delta2,
        gain_terms,
        delta,
        delta_middle * branch1_ref[...],
        delta1.astype(F32),
    )
    for i, term in enumerate(terms):
        sums_ref[i : i + 1, :] += total_rows(kept(term))

    @pl.when(step == pl.num_programs(0) - 1)
    def _():
        chips = mine_ref.shape[0]
        wide = width // chips
        for k in range(chips):
            chip = place[CHIPS + k]
            at = pl.ds(pl.multiple_of(lax.rem(chip, chips // 2) * wide, wide), wide)
            mixed = jnp.where(chip // (chips // 2) == place[CORE], own_ref[:, at], far_ref[:, at])
            place_turned(place, mixed, mixture_t, k, chips)
        split_rows(dot(mixture_t[...], delta1_all[:tokens, :]).astype(BF16), mine_ref, other_ref)


def unmerge(place, middle, branch1, branch2, delta, cotangent, own, far, table, rest, owners):
    tokens, width = middle.shape
    chips = owners // 2
    sent = (chips, width // owners, width)
    half = width // 2
    steps = row_steps(tokens)
    wide = pl.BlockSpec((ROWS, width), lambda i, _: (i, 0))
    narrow = pl.BlockSpec((ROWS, half), lambda i, _: (i, 0))
    return pl.pallas_call(
        functools.partial(unmerge_kernel, tokens=tokens),
        grid_spec=pltpu.PrefetchScalarGridSpec(
            num_scalar_prefetch=1,
            grid=(steps,),
            in_specs=[wide] * 5
            + [whole((tokens, half))] * 2
            + [
                whole(table.shape),
                pl.BlockSpec((half, width), lambda i, place: (place[CORE], rest.shape[1] // width - 1)),
                pl.BlockSpec((half, width), lambda i, place: (1 - place[CORE], rest.shape[1] // width - 1)),
            ],
            out_specs=[wide, wide, narrow, narrow, whole(sent), whole(sent), whole((SUM_ROWS, width))],
            scratch_shapes=[pltpu.VMEM((steps * ROWS, width), BF16), pltpu.VMEM((width, tokens), BF16)],
        ),
        out_shape=[
            jax.ShapeDtypeStruct((tokens, width), BF16),
            jax.ShapeDtypeStruct((tokens, width), F32),
            jax.ShapeDtypeStruct((tokens, half), BF16),
            jax.ShapeDtypeStruct((tokens, half), BF16),
            jax.ShapeDtypeStruct(sent, BF16),
            jax.ShapeDtypeStruct(sent, BF16),
            jax.ShapeDtypeStruct((SUM_ROWS, width), F32),
        ],
        name="unmerge",
        **params_for(4 * tokens * width * width, 30 * tokens * width + 4 * width * width),
    )(place, middle, branch1, branch2, delta, cotangent, own, far, table, rest, rest)


def unproject_kernel(
    place, x_hbm, delta_middle_hbm, table, normed_ref, own_ref, far_ref, weight_ref, middle_sums, up_sums, *refs, chips
):
    (
        out_ref, mine_ref, other_ref, vectors_mine_ref, vectors_other_ref,
        delta, sums, normed_t, x_ref, delta_middle_ref, laid, arrived,
    ) = refs
    step = pl.program_id(0)
    core = place[CORE]
    copies = [
        pltpu.make_async_copy(x_hbm, x_ref, arrived.at[0]),
        pltpu.make_async_copy(delta_middle_hbm, delta_middle_ref, arrived.at[1]),
    ]

    @pl.when(step == 0)
    def _():
        for copy in copies:
            copy.start()
        fill_turned(place, normed_ref, normed_t, chips)
        delta[...] = jnp.zeros_like(delta)
        sums[...] = jnp.zeros_like(sums)

    own, far = own_ref[0], far_ref[0]
    block = jnp.concatenate([jnp.where(core == 0, own, far), jnp.where(core == 0, far, own)], axis=1)
    split_rows(dot(normed_t[...], block).astype(BF16), mine_ref, other_ref)
    delta[...] += dot(block, weight_ref[...], NT)
    for kind, row in ((0, QUERY), (2, VALUE)):

        @pl.when(step == kind)
        def _():
            sums[row : row + 1, :] = total_rows(block.astype(F32))

    @pl.when(step == pl.num_programs(0) - 1)
    def _():
        for copy in copies:
            copy.wait()
        delta_normed = delta[...]
        inner, gain_terms = normalize_back(
            x_ref[...].astype(F32), table[GAIN1 : GAIN1 + 1, :], delta_normed
        )
        out_ref[...] = (delta_middle_ref[...] + inner).astype(BF16)
        rows = {
            GAIN1: total_rows(gain_terms),
            SHIFT1: total_rows(delta_normed),
            OUT_SHIFT: middle_sums[5:6, :],
            SCALE1: middle_sums[4:5, :],
            GAIN2: middle_sums[2:3, :],
            SHIFT2: middle_sums[3:4, :],
            DOWN_SHIFT: middle_sums[1:2, :],
            SCALE2: middle_sums[0:1, :],
        }
        for i, values in rows.items():
            sums[i : i + 1, :] = values
        each = up_sums.shape[1] // (2 * chips)
        laid[...] = jnp.zeros_like(laid)
        for out, side in ((vectors_mine_ref, core), (vectors_other_ref, 1 - core)):
            for k in range(chips):
                chip = place[CHIPS + k]
                at = pl.ds(pl.multiple_of(chip * LANES, LANES), LANES)
                laid[k, : sums.shape[0], :] = sums[:, at]
                for r in range(each // LANES):
                    at = pl.multiple_of((2 * chip + side) * each + r * LANES, LANES)
                    laid[k, VECTORS + r : VECTORS + r + 1, :] = up_sums[:, pl.ds(at, LANES)]
            out[...] = laid[...].astype(BF16)


def unproject(place, x, delta_middle, table, normed, own, far, weight, middle_sums, up_sums, owners):
    tokens, width = x.shape
    half = width // 2
    chips = owners // 2
    rows = width // owners
    vectors = (chips, rows, LANES)
    anywhere = pl.BlockSpec(memory_space=pl.ANY)
    kind = pl.BlockSpec((1, tokens, half), lambda j, _: (j, 0, 0))
    sent = pl.BlockSpec((chips, rows, width), lambda j, _: (0, 0, j))
    return pl.pallas_call(
        functools.partial(unproject_kernel, chips=chips),
        grid_spec=pltpu.PrefetchScalarGridSpec(
            num_scalar_prefetch=1,
            grid=(3,),
            in_specs=[
                anywhere,
                anywhere,
                whole(table.shape),
                whole((tokens, width)),
                kind,
                kind,
                pl.BlockSpec((width, width), lambda j, _: (0, j)),
                whole(middle_sums.shape),
                whole(up_sums.shape),
            ],
            out_specs=[whole((tokens, width)), sent, sent, whole(vectors), whole(vectors)],
            scratch_shapes=[
                pltpu.VMEM((tokens, width), F32),
                pltpu.VMEM((16, width), F32),
                pltpu.VMEM((width, tokens), BF16),
                pltpu.VMEM((tokens, width), BF16),
                pltpu.VMEM((tokens, width), F32),
                pltpu.VMEM(vectors, F32),
                pltpu.SemaphoreType.DMA((2,)),
            ],
        ),
        out_shape=[
            jax.ShapeDtypeStruct((tokens, width), BF16),
            jax.ShapeDtypeStruct((chips, rows, 3 * width), BF16),
            jax.ShapeDtypeStruct((chips, rows, 3 * width), BF16),
            jax.ShapeDtypeStruct(vectors, BF16),
            jax.ShapeDtypeStruct(vectors, BF16),
        ],
        name="unproject",
        **params_for(12 * tokens * width * width, 18 * tokens * width + 12 * width * width, weight=SHORT),
    )(place, x, delta_middle, table, normed, own, far, weight, middle_sums, up_sums)


def ring_of(chips):
    return list(range(0, chips, 2)) + list(range(1, chips, 2))[::-1]


def places(owners):
    ring = ring_of(owners // 2)
    rows = []
    for f in range(owners):
        chip, core = divmod(f, 2)
        at = ring.index(chip)
        columns = [1 - core, 3 - core, 5 - core, core, 2 + core, 4 + core]
        rows.append(columns + [core] + ring[at:] + ring[:at])
    return np.array(rows, np.int32)


def ring_perm(chips, hop):
    ring = ring_of(chips)
    return [
        (2 * ring[i] + core, 2 * ring[(i + hop) % chips] + core) for i in range(chips) for core in range(2)
    ]


def to_next(values, chips, hop):
    return lax.ppermute(values, "fsdp", ring_perm(chips, hop))


def ring_gather(piece, chips):
    pieces = [None] * chips
    pieces[0] = right = left = piece
    for k in range(1, chips // 2 + 1):
        pieces[-k] = right = to_next(right, chips, 1)
        if k < chips - chips // 2:
            pieces[k] = left = to_next(left, chips, -1)
    return pieces


def low_part(columns):
    return columns // 2 if columns % (2 * LANES) == 0 else columns


def ring_add_kernel(*refs, columns, mode, carried):
    ways = 2 if mode in ("second", "next") else 1
    shares = [refs[2 * len(columns) * d : 2 * len(columns) * (d + 1)] for d in range(ways)]
    came = refs[2 * len(columns) * ways :]
    outs = refs[len(refs) - carried - (1 if mode == "total" else 2) : len(refs) - carried]
    start, low_start, high_start = 0, 0, 0
    for i, each in enumerate(columns):
        totals = [mine[2 * i][0].astype(F32) + mine[2 * i + 1][0].astype(F32) for mine in shares]
        at = slice(start, start + each)
        low = low_part(each)
        low_at, high_at = slice(low_start, low_start + low), slice(high_start, high_start + each - low)
        if mode == "first":
            outs[0][:, low_at] = totals[0][:, :low].astype(BF16)
            if low < each:
                outs[1][:, high_at] = totals[0][:, low:].astype(BF16)
        elif mode == "second":
            outs[0][:, start : start + low] = (totals[0][:, :low] + came[0][:, low_at].astype(F32)).astype(BF16)
            outs[1][:, start : start + low] = totals[1][:, :low].astype(BF16)
            if low < each:
                high = totals[1][:, low:] + came[1][:, high_at].astype(F32)
                outs[0][:, start + low : start + each] = totals[0][:, low:].astype(BF16)
                outs[1][:, start + low : start + each] = high.astype(BF16)
        elif mode == "next":
            for total, arrived, out in zip(totals, came, outs):
                out[:, at] = (total + arrived[:, at].astype(F32)).astype(BF16)
        else:
            both_ways = came[0][:, at].astype(F32) + came[1][:, at].astype(F32)
            outs[0][:, at] = (totals[0] + both_ways).astype(BF16)
        start, low_start, high_start = at.stop, low_at.stop, high_at.stop


class RingSum:
    def __init__(self, *parts):
        self.parts, self.chips = [part[:2] for part in parts], parts[0][0].shape[0]
        self.columns = [part[0].shape[2] // part[3] for part in parts]
        self.blocks = [part[2] for part in parts]
        self.steps = self.chips // 2
        self.step = 0
        self.came = []

    def add(self, mode, places, after=(), carry=()):
        rows = self.parts[0][0].shape[1]
        columns = self.columns
        total = sum(columns)
        blocks = 2 if total > 4096 else 1
        arrays, specs = [], []
        for at in places:
            for part, each, block in zip(self.parts, columns, self.blocks):
                for array in part:
                    arrays.append(array)
                    specs.append(pl.BlockSpec((1, rows // blocks, each), lambda i, at=at, block=block: (at, i, block)))
        for came in self.came:
            arrays.append(came)
            specs.append(pl.BlockSpec((rows // blocks, came.shape[1]), lambda i: (i, 0)))
        arrays += [*after, *carry]
        anywhere = pl.BlockSpec(memory_space=pl.ANY)
        specs += [anywhere] * (len(after) + len(carry))
        low = sum(low_part(each) for each in columns)
        out_columns = {"first": [low, total - low], "total": [total]}.get(mode, [total, total])
        sums = len(out_columns)
        outs = pl.pallas_call(
            functools.partial(ring_add_kernel, columns=columns, mode=mode, carried=len(carry)),
            grid=(blocks,),
            in_specs=specs,
            out_specs=[pl.BlockSpec((rows // blocks, out), lambda i: (i, 0)) for out in out_columns]
            + [anywhere] * len(carry),
            out_shape=[jax.ShapeDtypeStruct((rows, out), BF16) for out in out_columns]
            + [jax.ShapeDtypeStruct(array.shape, array.dtype) for array in carry],
            input_output_aliases={len(arrays) - len(carry) + i: sums + i for i in range(len(carry))},
            name="ring_add",
            **params_for(6 * rows * total, 16 * rows * total, weight=SHORT, vmem=VMEM_LIMIT if blocks > 1 else SMALL_VMEM),
        )(*arrays)
        return outs[:sums], outs[sums:]

    def sums(self, after=(), carry=()):
        k = self.steps - self.step
        if self.step == 0:
            return self.add("first", [k], after, carry)
        return self.add("second" if self.step == 1 else "next", [k, self.chips - k], after, carry)

    def send(self, sums):
        self.came = [to_next(sums[0], self.chips, 1), to_next(sums[1], self.chips, -1)]
        self.step += 1

    def total(self, after=(), carry=()):
        assert self.step == self.steps
        sums, carried = self.add("total", [0], after, carry)
        return sums[0], carried


def passed(arrays, after):
    anywhere = pl.BlockSpec(memory_space=pl.ANY)
    return pl.pallas_call(
        lambda *refs: None,
        in_specs=[anywhere] * (len(arrays) + len(after)),
        out_specs=[anywhere] * len(arrays),
        out_shape=[jax.ShapeDtypeStruct(array.shape, array.dtype) for array in arrays],
        input_output_aliases={i: i for i in range(len(arrays))},
        name="passed",
        **params_for(1, 1, vmem=SMALL_VMEM),
    )(*arrays, *after)


def finish_rest_kernel(part_ref, came_ref, up_ref, down_ref):
    def total(at):
        return part_ref[:, at].astype(F32) + came_ref[:, at].astype(F32)

    rows, hidden = up_ref.shape
    each, width = down_ref.shape
    up_ref[...] = total(slice(0, hidden))
    for g in range(0, width // rows, 2):
        pair = [total(slice(hidden + each * h, hidden + each * (h + 1))) for h in (g, g + 1)]
        down_ref[:, g * rows : (g + 2) * rows] = jnp.concatenate(pair, axis=0).T


def finish_rest(part, came, hidden, each, width):
    in_vmem = pl.BlockSpec(memory_space=pltpu.VMEM)
    rows = part.shape[0]
    return pl.pallas_call(
        finish_rest_kernel,
        in_specs=[in_vmem] * 2,
        out_specs=[in_vmem] * 2,
        out_shape=[jax.ShapeDtypeStruct(shape, F32) for shape in ((rows, hidden), (each, width))],
        name="finish_rest",
        **params_for(part.size, 8 * part.size, weight=SHORT, vmem=2 * SMALL_VMEM),
    )(part, came)


def finish_first_kernel(place, *refs):
    parts, came, (packed_ref, output_ref), vector_refs = refs[:2], refs[2:4], refs[4:6], refs[6:]
    packed, out = packed_ref.shape[1] // 2, output_ref.shape[1] // 2
    for i in range(2):
        total = parts[i][...].astype(F32) + came[i][...].astype(F32)
        packed_ref[:, packed * i : packed * (i + 1)] = total[:, :packed]
        output_ref[:, out * i : out * (i + 1)] = total[:, packed : packed + out]
        if i == 0:
            vectors = total[:16, packed + out :]
    half = LANES // 2
    mine = jnp.where(place[CORE] == 0, vectors[:, :half], vectors[:, half:])
    for i in range(VECTORS):
        vector_refs[i][...] = mine[i : i + 1, :].reshape(half)
    count = vector_refs[VECTORS].shape[0]
    vector_refs[VECTORS][...] = vectors[VECTORS : VECTORS + count // LANES, :].reshape(count)


def finish_first(place, parts, came, width, each):
    in_vmem = pl.BlockSpec(memory_space=pltpu.VMEM)
    rows = parts[0].shape[0]
    shapes = [(rows, 3 * width), (rows, width)] + [(rows,)] * VECTORS + [(each,)]
    return pl.pallas_call(
        finish_first_kernel,
        in_specs=[pl.BlockSpec(memory_space=pltpu.SMEM)] + [in_vmem] * 4,
        out_specs=[in_vmem] * len(shapes),
        out_shape=[jax.ShapeDtypeStruct(shape, F32) for shape in shapes],
        name="finish_first",
        **params_for(8 * rows * width, 32 * rows * width, weight=SHORT, vmem=SMALL_VMEM),
    )(place, *parts, *came)


def split_pairs(pairs):
    return [pairs // 4, pairs // 4, pairs - 2 * (pairs // 4)] if pairs >= 4 else [pairs]


def paired_body(
    tokens, lengths, norm1_gain, norm1_bias, packed_weight, query_bias, value_bias, output_weight, output_bias,
    layer_scale1, norm2_gain, norm2_bias, up_weight, up_bias, down_weight, down_bias, layer_scale2, cotangent,
):
    owners = lax.axis_size("fsdp")
    chips = owners // 2
    _, local_len, width = tokens.shape
    me = lax.axis_index("fsdp")
    core = lax.rem(me, 2)
    place = lax.dynamic_index_in_dim(jnp.asarray(places(owners)), me, keepdims=False)
    moves = [(f * 2 + s, (f - f % 2 + s) * 2 + f % 2) for f in range(owners) for s in range(2) if f % 2 != s]
    twin = [(f, f ^ 1) for f in range(owners)]
    stays = core == lax.axis_index("seq")

    def regroup_moves(values):
        return lax.ppermute(values, ("fsdp", "seq"), moves)

    def regrouped(values):
        return jnp.where(stays, values, regroup_moves(values))

    def to_twin(values):
        return lax.ppermute(values, "fsdp", twin)

    def across(values):
        return lax.ppermute(values, "seq", [(0, 1), (1, 0)])

    vectors = (
        norm1_gain, norm1_bias, query_bias, value_bias, output_bias, layer_scale1, norm2_gain, norm2_bias,
        down_bias, layer_scale2,
    )
    rows = norm1_gain.shape[0]
    hidden = up_weight.shape[1]
    first, rest = pack(packed_weight, up_weight, down_weight, output_weight, vectors, up_bias)
    own_pieces = ring_gather(first, chips)
    far_pieces = [to_twin(piece) for piece in own_pieces]
    x = regrouped(tokens.reshape(local_len, width))
    valid_count = regrouped(lengths)
    rest = lax.all_gather(rest, "fsdp", axis=0, tiled=True)
    starts = jnp.stack([core, 1 - core]) * local_len
    valid = jnp.clip(valid_count - starts, 0, local_len).astype(jnp.int32)
    upstream = regrouped(cotangent.reshape(local_len, width))

    far_out, own_part, normed, packed_full, table, up_shift = project(place, x, own_pieces, far_pieces, hidden)
    far_part = to_twin(far_out)
    parts = [own_part, far_part]
    (own_mix, far_mix_out), totals = attention(valid, parts, 352)
    far_mix = to_twin(far_mix_out)
    middle, branch1, normed2 = merge(place, x, own_mix, far_mix, table, rest)

    branch2, delta_normed2, up_mine, up_other, down_mine, down_other, up_sums = mlp(
        place, normed2, upstream, table, rest, up_shift, owners
    )
    up_twin, down_twin = to_twin(up_other), to_twin(down_other)
    output, delta_middle, own_grad, far_grad_out, output_mine, output_other, middle_sums = unmerge(
        place, middle, branch1, branch2, delta_normed2, upstream, own_mix, far_mix, table, rest, owners
    )
    far_grad = to_twin(far_grad_out)
    ring = RingSum((up_mine, up_twin, 0, 1), (down_mine, down_twin, 0, 1))
    output_sent = regroup_moves(output)
    output_twin = to_twin(output_other)
    deltas = ()
    grads = [own_grad, far_grad]
    start = 0
    for pairs in split_pairs(width // 2 // LANES):
        sums, _ = ring.sums()
        ring.send(sums)
        after = [*sums, output_sent, output_twin] if start else sums
        deltas = attention_back(
            valid, parts, [own_mix, far_mix_out], grads, totals, 352, start, pairs, deltas, after
        )
        start += pairs
    own_delta, far_delta_out = deltas
    sums, (far_delta_out,) = ring.sums(carry=[far_delta_out])
    ring.send(sums)
    far_delta = to_twin(far_delta_out)
    grad_x, packed_mine, packed_other, vectors_mine, vectors_other = unproject(
        place, x, delta_middle, table, normed, own_delta, far_delta, packed_full, middle_sums, up_sums, owners
    )
    output = jnp.where(stays, output, output_sent).reshape(tokens.shape)
    grad_x, packed_other, vectors_other = passed([grad_x, packed_other, vectors_other], ring.came)
    vectors_twin, packed_twin = to_twin(vectors_other), to_twin(packed_other)
    rest_sum, _ = ring.total()
    rings = (
        RingSum(
            (packed_mine, packed_twin, 0, 2), (output_mine, output_twin, 0, 2), (vectors_mine, vectors_twin, 0, 1)
        ),
        RingSum((packed_mine, packed_twin, 1, 2), (output_mine, output_twin, 1, 2)),
    )
    grad_x_sent, rest_sent = regroup_moves(grad_x), across(rest_sum)
    last = [rest_sum]
    for step in range(rings[0].steps):
        for half in rings:
            after = [*last] + ([grad_x_sent] if step == 2 and half is rings[0] else [])
            last, _ = half.sums(after)
            half.send(last)
    grad_tokens = jnp.where(stays, grad_x, grad_x_sent).astype(F32).reshape(tokens.shape)
    each = up_bias.shape[0]
    grad_up, grad_down = finish_rest(rest_sum, rest_sent, hidden, each, width)
    first_sum, _ = rings[0].total()
    first_sums = [first_sum, rings[1].total([first_sum])[0]]
    grad_packed, grad_output, *mine = finish_first(
        place, first_sums, [across(half) for half in first_sums], width, each
    )
    return (
        output, grad_tokens, mine[0], mine[1], grad_packed, mine[2], mine[3], grad_output, mine[4], mine[5],
        mine[6], mine[7], grad_up, mine[10], grad_down, mine[8], mine[9],
    )


def pairable(tokens, up_weight):
    owners, chips = lax.axis_size("fsdp"), lax.axis_size("fsdp") // 2
    width, hidden = up_weight.shape[0] * owners, up_weight.shape[1]
    return (
        lax.axis_size("seq") == 2
        and tokens.shape[0] == 1
        and tokens.shape[1] % 16 == 0
        and owners == 2 * chips
        and chips in (4, 8)
        and width % (chips * LANES) == 0
        and hidden % (owners * LANES) == 0
        and H * HD == width
    )


def body(*args):
    chosen = paired_body if pairable(args[0], args[12]) else general_body
    return chosen(*args)


def solution(mesh):
    in_specs = (
        P("fsdp", "seq", None),
        P("fsdp"),
        P("fsdp"),
        P("fsdp"),
        P("fsdp", None),
        P("fsdp"),
        P("fsdp"),
        P("fsdp", None),
        P("fsdp"),
        P("fsdp"),
        P("fsdp"),
        P("fsdp"),
        P("fsdp", None),
        P("fsdp"),
        P("fsdp", None),
        P("fsdp"),
        P("fsdp"),
        P("fsdp", "seq", None),
    )
    out_specs = (
        P("fsdp", "seq", None),
        P("fsdp", "seq", None),
        P("fsdp"),
        P("fsdp"),
        P("fsdp", None),
        P("fsdp"),
        P("fsdp"),
        P("fsdp", None),
        P("fsdp"),
        P("fsdp"),
        P("fsdp"),
        P("fsdp"),
        P("fsdp", None),
        P("fsdp"),
        P("fsdp", None),
        P("fsdp"),
        P("fsdp"),
    )
    return jax.shard_map(body, mesh=mesh, in_specs=in_specs, out_specs=out_specs, check_vma=False)
```

```python
import functools

import jax
import jax.numpy as jnp
import numpy as np
from jax import lax
from jax.experimental import pallas as pl
from jax.experimental.pallas import tpu as pltpu
from jax.sharding import PartitionSpec as P

H = 16
HD = 64


norm_eps = 1e-06


def layer_norm(values, norm_gain, norm_shift):
    center = values - jnp.mean(values, axis=-1, keepdims=True)
    spread = jnp.mean(center * center, axis=-1, keepdims=True)
    return center * lax.rsqrt(spread + norm_eps) * norm_gain + norm_shift


def gelu_exact(values):
    return jax.nn.gelu(values, approximate=False)


def matmul(left, right):
    return jnp.dot(left, right, preferred_element_type=jnp.float32)


def left_outer(left, right):
    return jnp.einsum("ti,tj->ij", left, right, preferred_element_type=jnp.float32)


def right_back(left, right):
    return jnp.einsum("tj,ij->ti", left, right, preferred_element_type=jnp.float32)


def column_sum(values):
    return jnp.sum(values.astype(jnp.float32), axis=0)


def attention_probs(queries, key_rows, valid_count, score_scale):
    scores = score_scale * jnp.einsum(
        "qhd,khd->hqk", queries, key_rows, preferred_element_type=jnp.float32
    )
    key_valid = jnp.arange(key_rows.shape[0]) < valid_count
    scores = jnp.where(key_valid[None, None, :], scores, -jnp.inf)
    return scores


def attend(queries, key_rows, values, valid_count, score_scale):
    scores = attention_probs(queries, key_rows, valid_count, score_scale)
    largest = jnp.max(scores, axis=-1, keepdims=True)
    log_total = largest[..., 0] + jnp.log(jnp.sum(jnp.exp(scores - largest), axis=-1))
    attention = jnp.exp(scores - log_total[..., None]).astype(jnp.bfloat16)
    mixture = jnp.einsum("hqk,khd->qhd", attention, values, preferred_element_type=jnp.float32)
    return (mixture.astype(jnp.bfloat16), log_total)


def attend_back(queries, key_rows, values, valid_count, score_scale, log_total, grad_mixture):
    scores = attention_probs(queries, key_rows, valid_count, score_scale)
    probs = jnp.exp(scores - log_total[..., None])
    grad_values = jnp.einsum(
        "hqk,qhd->khd", probs.astype(jnp.bfloat16), grad_mixture, preferred_element_type=jnp.float32
    )
    grad_probs = jnp.einsum(
        "qhd,khd->hqk", grad_mixture, values, preferred_element_type=jnp.float32
    )
    inner_sum = jnp.sum(probs * grad_probs, axis=-1, keepdims=True)
    grad_scores = (probs * (grad_probs - inner_sum)).astype(jnp.bfloat16)
    grad_queries = score_scale * jnp.einsum(
        "hqk,khd->qhd", grad_scores, key_rows, preferred_element_type=jnp.float32
    )
    grad_keys = score_scale * jnp.einsum(
        "hqk,qhd->khd", grad_scores, queries, preferred_element_type=jnp.float32
    )
    return (grad_queries, grad_keys, grad_values)


def general_body(
    tokens,
    lengths,
    norm1_gain,
    norm1_bias,
    packed_weight,
    query_bias,
    value_bias,
    output_weight,
    output_bias,
    layer_scale1,
    norm2_gain,
    norm2_bias,
    up_weight,
    up_bias,
    down_weight,
    down_bias,
    layer_scale2,
    cotangent,
):
    gathered = (
        lax.all_gather(norm1_gain, "fsdp", axis=0, tiled=True),
        lax.all_gather(norm1_bias, "fsdp", axis=0, tiled=True),
        lax.all_gather(packed_weight, "fsdp", axis=0, tiled=True),
        lax.all_gather(query_bias, "fsdp", axis=0, tiled=True),
        lax.all_gather(value_bias, "fsdp", axis=0, tiled=True),
        lax.all_gather(output_weight, "fsdp", axis=0, tiled=True),
        lax.all_gather(output_bias, "fsdp", axis=0, tiled=True),
        lax.all_gather(layer_scale1, "fsdp", axis=0, tiled=True),
        lax.all_gather(norm2_gain, "fsdp", axis=0, tiled=True),
        lax.all_gather(norm2_bias, "fsdp", axis=0, tiled=True),
        lax.all_gather(up_weight, "fsdp", axis=0, tiled=True),
        lax.all_gather(up_bias, "fsdp", axis=0, tiled=True),
        lax.all_gather(down_weight, "fsdp", axis=0, tiled=True),
        lax.all_gather(down_bias, "fsdp", axis=0, tiled=True),
        lax.all_gather(layer_scale2, "fsdp", axis=0, tiled=True),
    )
    (
        gain_one,
        shift_one,
        packed_full,
        query_shift,
        value_shift,
        output_full,
        output_shift,
        scale_one,
        gain_two,
        shift_two,
        up_full,
        up_shift,
        down_full,
        down_shift,
        scale_two,
    ) = gathered
    gain_one = gain_one.astype(jnp.float32)
    shift_one = shift_one.astype(jnp.float32)
    query_shift = query_shift.astype(jnp.float32)
    value_shift = value_shift.astype(jnp.float32)
    output_shift = output_shift.astype(jnp.float32)
    scale_one = scale_one.astype(jnp.float32)
    gain_two = gain_two.astype(jnp.float32)
    shift_two = shift_two.astype(jnp.float32)
    up_shift = up_shift.astype(jnp.float32)
    down_shift = down_shift.astype(jnp.float32)
    scale_two = scale_two.astype(jnp.float32)
    groups = lax.axis_size("seq")
    images, local_len, model_width = tokens.shape
    seq_len = local_len * groups
    per_group = H // groups
    score_scale = HD ** (-0.5)
    token_rows = tokens.astype(jnp.float32).reshape(images * local_len, model_width)
    normed = layer_norm(token_rows, gain_one, shift_one).astype(jnp.bfloat16)
    packed_shift = jnp.concatenate([query_shift, jnp.zeros_like(query_shift), value_shift])
    packed = (matmul(normed, packed_full) + packed_shift).astype(jnp.bfloat16)
    packed = packed.reshape(images, local_len, 3, groups, per_group * HD)
    spread = lax.all_to_all(packed, "seq", split_axis=3, concat_axis=1, tiled=True)
    spread = spread.reshape(images, seq_len, 3, per_group, HD)

    def forward_image(per_image):
        image_block, valid_count = per_image
        return attend(
            image_block[:, 0], image_block[:, 1], image_block[:, 2], valid_count, score_scale
        )

    mixture, log_total = lax.map(forward_image, (spread, lengths))
    mixture = mixture.reshape(images, seq_len, 1, per_group * HD)
    mixture_rows = lax.all_to_all(mixture, "seq", split_axis=1, concat_axis=2, tiled=True).reshape(
        images * local_len, model_width
    )
    branch_one = matmul(mixture_rows, output_full) + output_shift
    middle = token_rows + scale_one * branch_one
    normed_two = layer_norm(middle, gain_two, shift_two).astype(jnp.bfloat16)
    hidden = matmul(normed_two, up_full) + up_shift
    active = gelu_exact(hidden).astype(jnp.bfloat16)
    branch_two = matmul(active, down_full) + down_shift
    output = (middle + scale_two * branch_two).astype(jnp.bfloat16).reshape(tokens.shape)
    upstream = cotangent.astype(jnp.float32).reshape(images * local_len, model_width)
    grad_scale_two = jnp.sum(upstream * branch_two, axis=0)
    delta_two = (scale_two * upstream).astype(jnp.bfloat16)
    grad_down_shift = column_sum(delta_two)
    grad_down = left_outer(active, delta_two)
    grad_active = right_back(delta_two, down_full)
    _, gelu_pull = jax.vjp(gelu_exact, hidden)
    delta_hidden = gelu_pull(grad_active)[0].astype(jnp.bfloat16)
    grad_up_shift = column_sum(delta_hidden)
    grad_up = left_outer(normed_two, delta_hidden)
    delta_normed_two = right_back(delta_hidden, up_full)
    _, norm_pull_two = jax.vjp(layer_norm, middle, gain_two, shift_two)
    grad_middle_norm, grad_gain_two, grad_shift_two = norm_pull_two(delta_normed_two)
    delta_middle = upstream + grad_middle_norm
    grad_scale_one = jnp.sum(delta_middle * branch_one, axis=0)
    delta_one = (scale_one * delta_middle).astype(jnp.bfloat16)
    grad_output_shift = column_sum(delta_one)
    grad_output = left_outer(mixture_rows, delta_one)
    delta_mixture = right_back(delta_one, output_full).astype(jnp.bfloat16)
    delta_mixture = delta_mixture.reshape(images, local_len, groups, per_group * HD)
    grad_spread = lax.all_to_all(delta_mixture, "seq", split_axis=2, concat_axis=1, tiled=True)
    grad_spread = grad_spread.reshape(images, seq_len, per_group, HD)

    def backward_image(per_image):
        image_block, valid_count, image_total, image_grad = per_image
        grad_queries, grad_keys, grad_values = attend_back(
            image_block[:, 0],
            image_block[:, 1],
            image_block[:, 2],
            valid_count,
            score_scale,
            image_total,
            image_grad,
        )
        return jnp.stack([grad_queries, grad_keys, grad_values], axis=1).astype(jnp.bfloat16)

    delta_packed = lax.map(backward_image, (spread, lengths, log_total, grad_spread))
    delta_packed = delta_packed.reshape(images, seq_len, 3, 1, per_group * HD)
    delta_back = lax.all_to_all(delta_packed, "seq", split_axis=1, concat_axis=3, tiled=True)
    delta_back = delta_back.reshape(images * local_len, 3 * model_width)
    grad_query_shift = column_sum(delta_back[:, :model_width])
    grad_value_shift = column_sum(delta_back[:, 2 * model_width :])
    grad_packed = left_outer(normed, delta_back)
    delta_normed = right_back(delta_back, packed_full)
    _, norm_pull_one = jax.vjp(layer_norm, token_rows, gain_one, shift_one)
    grad_rows_norm, grad_gain_one, grad_shift_one = norm_pull_one(delta_normed)
    grad_tokens = (delta_middle + grad_rows_norm).reshape(tokens.shape)
    local_grads = (
        grad_gain_one,
        grad_shift_one,
        grad_packed,
        grad_query_shift,
        grad_value_shift,
        grad_output,
        grad_output_shift,
        grad_scale_one,
        grad_gain_two,
        grad_shift_two,
        grad_up,
        grad_up_shift,
        grad_down,
        grad_down_shift,
        grad_scale_two,
    )
    owned_grads = (
        lax.psum_scatter(
            local_grads[0].astype(jnp.bfloat16), "fsdp", scatter_dimension=0, tiled=True
        ).astype(jnp.float32),
        lax.psum_scatter(
            local_grads[1].astype(jnp.bfloat16), "fsdp", scatter_dimension=0, tiled=True
        ).astype(jnp.float32),
        lax.psum_scatter(
            local_grads[2].astype(jnp.bfloat16), "fsdp", scatter_dimension=0, tiled=True
        ).astype(jnp.float32),
        lax.psum_scatter(
            local_grads[3].astype(jnp.bfloat16), "fsdp", scatter_dimension=0, tiled=True
        ).astype(jnp.float32),
        lax.psum_scatter(
            local_grads[4].astype(jnp.bfloat16), "fsdp", scatter_dimension=0, tiled=True
        ).astype(jnp.float32),
        lax.psum_scatter(
            local_grads[5].astype(jnp.bfloat16), "fsdp", scatter_dimension=0, tiled=True
        ).astype(jnp.float32),
        lax.psum_scatter(
            local_grads[6].astype(jnp.bfloat16), "fsdp", scatter_dimension=0, tiled=True
        ).astype(jnp.float32),
        lax.psum_scatter(
            local_grads[7].astype(jnp.bfloat16), "fsdp", scatter_dimension=0, tiled=True
        ).astype(jnp.float32),
        lax.psum_scatter(
            local_grads[8].astype(jnp.bfloat16), "fsdp", scatter_dimension=0, tiled=True
        ).astype(jnp.float32),
        lax.psum_scatter(
            local_grads[9].astype(jnp.bfloat16), "fsdp", scatter_dimension=0, tiled=True
        ).astype(jnp.float32),
        lax.psum_scatter(
            local_grads[10].astype(jnp.bfloat16), "fsdp", scatter_dimension=0, tiled=True
        ).astype(jnp.float32),
        lax.psum_scatter(
            local_grads[11].astype(jnp.bfloat16), "fsdp", scatter_dimension=0, tiled=True
        ).astype(jnp.float32),
        lax.psum_scatter(
            local_grads[12].astype(jnp.bfloat16), "fsdp", scatter_dimension=0, tiled=True
        ).astype(jnp.float32),
        lax.psum_scatter(
            local_grads[13].astype(jnp.bfloat16), "fsdp", scatter_dimension=0, tiled=True
        ).astype(jnp.float32),
        lax.psum_scatter(
            local_grads[14].astype(jnp.bfloat16), "fsdp", scatter_dimension=0, tiled=True
        ).astype(jnp.float32),
    )
    owned_grads = (
        lax.psum(owned_grads[0].astype(jnp.bfloat16), "seq").astype(jnp.float32),
        lax.psum(owned_grads[1].astype(jnp.bfloat16), "seq").astype(jnp.float32),
        lax.psum(owned_grads[2].astype(jnp.bfloat16), "seq").astype(jnp.float32),
        lax.psum(owned_grads[3].astype(jnp.bfloat16), "seq").astype(jnp.float32),
        lax.psum(owned_grads[4].astype(jnp.bfloat16), "seq").astype(jnp.float32),
        lax.psum(owned_grads[5].astype(jnp.bfloat16), "seq").astype(jnp.float32),
        lax.psum(owned_grads[6].astype(jnp.bfloat16), "seq").astype(jnp.float32),
        lax.psum(owned_grads[7].astype(jnp.bfloat16), "seq").astype(jnp.float32),
        lax.psum(owned_grads[8].astype(jnp.bfloat16), "seq").astype(jnp.float32),
        lax.psum(owned_grads[9].astype(jnp.bfloat16), "seq").astype(jnp.float32),
        lax.psum(owned_grads[10].astype(jnp.bfloat16), "seq").astype(jnp.float32),
        lax.psum(owned_grads[11].astype(jnp.bfloat16), "seq").astype(jnp.float32),
        lax.psum(owned_grads[12].astype(jnp.bfloat16), "seq").astype(jnp.float32),
        lax.psum(owned_grads[13].astype(jnp.bfloat16), "seq").astype(jnp.float32),
        lax.psum(owned_grads[14].astype(jnp.bfloat16), "seq").astype(jnp.float32),
    )
    return (output, grad_tokens) + tuple(owned_grads)


BF16 = jnp.bfloat16
F32 = jnp.float32
NT = (((1,), (1,)), ((), ()))
NN = (((1,), (0,)), ((), ()))
MASKED = -1e30
LOG2E = 1.4426950408889634
LANES = 128
VMEM_LIMIT = 60 * 2**20
SMALL_VMEM = 8 * 2**20

GAIN1, SHIFT1, QUERY, VALUE, OUT_SHIFT, SCALE1, GAIN2, SHIFT2, DOWN_SHIFT, SCALE2 = range(10)


def dot(left, right, dims=NN):
    return lax.dot_general(left, right, dims, preferred_element_type=F32)


def turned(values):
    return values.T


def lane_ids(rows):
    return lax.broadcasted_iota(jnp.int32, (rows, LANES), 1)


def split3(values):
    high = values.astype(BF16).astype(F32)
    rest = values - high
    mid = rest.astype(BF16).astype(F32)
    return high, mid, rest - mid


LONG, SHORT = 16.0, 1 / 64


def params_for(flops, nbytes, transcendentals=0, weight=1.0, vmem=VMEM_LIMIT):
    flops, nbytes, transcendentals = (int(weight * count) for count in (flops, nbytes, transcendentals))
    return dict(
        compiler_params=pltpu.CompilerParams(vmem_limit_bytes=vmem),
        cost_estimate=pl.CostEstimate(
            flops=flops, bytes_accessed=nbytes, transcendentals=transcendentals
        ),
    )


def whole(shape):
    return pl.BlockSpec(shape, lambda *_: (0,) * len(shape))


def normalize(values, gain, shift):
    center = values - jnp.mean(values, axis=-1, keepdims=True)
    spread = jnp.mean(center * center, axis=-1, keepdims=True)
    return center * lax.rsqrt(spread + norm_eps) * gain + shift


def normalize_back(values, gain, delta):
    center = values - jnp.mean(values, axis=-1, keepdims=True)
    inverse = lax.rsqrt(jnp.mean(center * center, axis=-1, keepdims=True) + norm_eps)
    unit = center * inverse
    scaled = delta * gain
    mean_scaled = jnp.mean(scaled, axis=-1, keepdims=True)
    mean_unit = jnp.mean(scaled * unit, axis=-1, keepdims=True)
    return inverse * (scaled - mean_scaled - unit * mean_unit), delta * unit


def total_rows(values):
    return jnp.sum(values, axis=0, keepdims=True)


VECTORS = 10


def pack_kernel(weight_ref, up_ref, down_ref, output_ref, *refs):
    vector_refs, shift_ref = refs[:VECTORS], refs[VECTORS]
    first_ref, rest_ref, laid = refs[VECTORS + 1 :]
    rows, width = weight_ref.shape
    first_ref[:, :width] = weight_ref[...]
    laid[...] = jnp.zeros_like(laid)
    core = lax.rem(lax.axis_index("fsdp"), 2)
    for i, ref in enumerate(vector_refs):
        values = ref[...].astype(F32).reshape(1, -1)
        empty = jnp.zeros_like(values)
        first, second = jnp.concatenate([values, empty], 1), jnp.concatenate([empty, values], 1)
        laid[i : i + 1, :] = jnp.where(core == 0, first, second)
    shift = shift_ref[...].astype(F32).reshape(-1, LANES)
    laid[VECTORS : VECTORS + shift.shape[0], :] = shift
    first_ref[:, width:] = laid[...].astype(BF16)
    at = 0
    for ref in (up_ref, down_ref, output_ref):
        for g in range(ref.shape[0] // rows):
            rest_ref[:, at : at + ref.shape[1]] = ref[g * rows : (g + 1) * rows, :]
            at += ref.shape[1]


def pack(weight, up, down, output, vectors, up_shift):
    in_vmem = pl.BlockSpec(memory_space=pltpu.VMEM)
    rows, width = weight.shape
    others = (up.size + down.size + output.size) // rows
    return pl.pallas_call(
        pack_kernel,
        in_specs=[in_vmem] * (VECTORS + 5),
        out_specs=[in_vmem, in_vmem],
        out_shape=[
            jax.ShapeDtypeStruct((rows, width + LANES), BF16),
            jax.ShapeDtypeStruct((rows, others), BF16),
        ],
        scratch_shapes=[pltpu.VMEM((rows, LANES), F32)],
        name="pack",
        **params_for(0, 4 * rows * (width + others)),
    )(weight, up, down, output, *vectors, up_shift)


CORE, CHIPS = 6, 7


def project_kernel(place, x_ref, *refs, chips):
    own_refs, far_refs, own_vectors, far_vectors = (refs[chips * i : chips * (i + 1)] for i in range(4))
    far_out_ref, own_ref, normed_ref, weight_ref, table_ref, up_ref = refs[4 * chips :]
    step = pl.program_id(0)
    rows = own_refs[0].shape[0]
    core = place[CORE]

    @pl.when(step == 0)
    def _():
        vector = lax.broadcasted_iota(jnp.int32, (table_ref.shape[0], LANES), 0) < VECTORS
        each = up_ref.shape[1] // (2 * chips)
        for k in range(chips):
            chip = place[CHIPS + k]
            own = own_vectors[k][...].astype(F32)
            far = far_vectors[k][...].astype(F32)
            at = pl.ds(pl.multiple_of(chip * LANES, LANES), LANES)
            table_ref[:, at] = jnp.where(vector, own + far, 0.0)
            for part, side in ((own, core), (far, 1 - core)):
                for r in range(each // LANES):
                    at = pl.multiple_of((2 * chip + side) * each + r * LANES, LANES)
                    up_ref[:, pl.ds(at, LANES)] = part[VECTORS + r : VECTORS + r + 1, :]
        normed_ref[...] = normalize(
            x_ref[...].astype(F32), table_ref[GAIN1 : GAIN1 + 1, :], table_ref[SHIFT1 : SHIFT1 + 1, :]
        ).astype(BF16)

    for k in range(chips):
        start = 2 * place[CHIPS + k]
        weight_ref[pl.ds(pl.multiple_of((start + core) * rows, rows), rows), :] = own_refs[k][...]
        weight_ref[pl.ds(pl.multiple_of((start + 1 - core) * rows, rows), rows), :] = far_refs[k][...]
    shift = jnp.where(
        step == 0,
        table_ref[QUERY : QUERY + 1, :],
        jnp.where(step == 2, table_ref[VALUE : VALUE + 1, :], 0.0),
    )
    result = (dot(normed_ref[...], weight_ref[...]) + shift).astype(BF16)
    half = result.shape[1] // 2
    low, high = result[:, :half], result[:, half:]
    own_ref[0] = jnp.where(core == 0, low, high)
    far_out_ref[0] = jnp.where(core == 0, high, low)


def project(place, x, own_pieces, far_pieces, hidden):
    chips = len(own_pieces)
    tokens, width = x.shape
    rows = own_pieces[0].shape[0]
    kind = pl.BlockSpec((1, tokens, width // 2), lambda j, _: (j, 0, 0))
    return pl.pallas_call(
        functools.partial(project_kernel, chips=chips),
        grid_spec=pltpu.PrefetchScalarGridSpec(
            num_scalar_prefetch=1,
            grid=(3,),
            in_specs=[whole((tokens, width))]
            + [pl.BlockSpec((rows, width), lambda j, _: (0, j))] * 2 * chips
            + [pl.BlockSpec((16, LANES), lambda j, _: (0, 3 * width // LANES))] * 2 * chips,
            out_specs=[
                kind,
                kind,
                whole((tokens, width)),
                pl.BlockSpec((width, width), lambda j, _: (0, j)),
                whole((16, width)),
                whole((1, hidden)),
            ],
        ),
        out_shape=[
            jax.ShapeDtypeStruct((3, tokens, width // 2), BF16),
            jax.ShapeDtypeStruct((3, tokens, width // 2), BF16),
            jax.ShapeDtypeStruct((tokens, width), BF16),
            jax.ShapeDtypeStruct((width, 3 * width), BF16),
            jax.ShapeDtypeStruct((16, width), F32),
            jax.ShapeDtypeStruct((1, hidden), F32),
        ],
        name="project",
        **params_for(6 * tokens * width * width, 12 * tokens * width + 12 * width * width),
    )(place, x, *own_pieces, *far_pieces, *own_pieces, *far_pieces)


def padded_len(count, block):
    return -(-count // block) * block


def attend_kernel(valid, *refs, pieces, block, scale):
    in_refs, out_refs = refs[:pieces], refs[pieces : 2 * pieces]
    total_refs = refs[2 * pieces : 3 * pieces]
    keys, values, queries, mixed, totals = refs[3 * pieces :]
    pair = pl.program_id(0)
    size = in_refs[0].shape[1]
    count, padded = pieces * size, keys.shape[0]
    lane = lane_ids(size)
    row = lax.broadcasted_iota(jnp.int32, (size, LANES), 0)
    for i in range(pieces):
        at = pl.ds(i * size, size)
        keys[at, :LANES] = in_refs[i][1]
        keys[at, LANES:] = jnp.where((lane == 0) & (row >= valid[i]), MASKED, 0.0).astype(BF16)
        values[at, :LANES] = in_refs[i][2]
        values[at, LANES:] = jnp.where(lane == 0, 1.0, 0.0).astype(BF16)
        for j in range(2):
            mine = lane // HD == j
            queries[j, at, :LANES] = jnp.where(mine, in_refs[i][0].astype(F32) * (scale * LOG2E), 0.0).astype(BF16)
            queries[j, at, LANES:] = jnp.where(lane == 0, 1.0, 0.0).astype(BF16)
    if padded > count:
        rest = pl.ds(count, padded - count)
        rest_lane = lane_ids(padded - count)
        keys[rest, :LANES] = jnp.zeros((padded - count, LANES), BF16)
        keys[rest, LANES:] = jnp.where(rest_lane == 0, MASKED, 0.0).astype(BF16)
        values[rest, :] = jnp.zeros((padded - count, 2 * LANES), BF16)
        for j in range(2):
            queries[j, rest, :] = jnp.zeros((padded - count, 2 * LANES), BF16)

    @pl.when(pair == 0)
    def _():
        for i in range(pieces):
            total_refs[i][...] = jnp.zeros_like(total_refs[i])

    block_lane = lane_ids(block)
    for b in range(padded // block):
        at = pl.ds(b * block, block)
        results, logs = [], 0.0
        for j in range(2):
            scores = dot(queries[j, at, :], keys[...], NT)
            largest = jnp.max(scores, axis=1, keepdims=True)
            weights = jnp.exp2(scores - largest).astype(BF16)
            result = dot(weights, values[...])
            total = result[:, LANES : LANES + 1]
            results.append(result[:, :LANES] * (1.0 / total))
            logs += jnp.where(block_lane == 2 * pair + j, largest + LOG2E * jnp.log(total), 0.0)
        mixed[at, :] = jnp.where(block_lane < HD, results[0], results[1])
        totals[at, :] = logs
    for i in range(pieces):
        at = pl.ds(i * size, size)
        out_refs[i][...] = mixed[at, :].astype(BF16)
        total_refs[i][...] += totals[at, :]


def attention(valid, parts, block):
    pieces = len(parts)
    _, size, width = parts[0].shape
    pairs = width // LANES
    padded = padded_len(pieces * size, block)
    outs = pl.pallas_call(
        functools.partial(attend_kernel, pieces=pieces, block=block, scale=HD**-0.5),
        grid_spec=pltpu.PrefetchScalarGridSpec(
            num_scalar_prefetch=1,
            grid=(pairs,),
            in_specs=[pl.BlockSpec((3, size, LANES), lambda h, _: (0, 0, h))] * pieces,
            out_specs=[pl.BlockSpec((size, LANES), lambda h, _: (0, h))] * pieces
            + [whole((size, LANES))] * pieces,
            scratch_shapes=[
                pltpu.VMEM((padded, 2 * LANES), BF16),
                pltpu.VMEM((padded, 2 * LANES), BF16),
                pltpu.VMEM((2, padded, 2 * LANES), BF16),
                pltpu.VMEM((padded, LANES), F32),
                pltpu.VMEM((padded, LANES), F32),
            ],
        ),
        out_shape=[jax.ShapeDtypeStruct((size, width), BF16)] * pieces
        + [jax.ShapeDtypeStruct((size, LANES), F32)] * pieces,
        name="attend",
        **params_for(16 * pairs * LANES * padded * padded, 8 * size * width * pieces, pairs * 2 * padded * padded),
    )(valid, *parts)
    return outs[:pieces], outs[pieces:]


def attend_back_kernel(valid, *refs, pieces, block, scale, first):
    in_refs, mix_refs = refs[:pieces], refs[pieces : 2 * pieces]
    grad_refs, total_refs = refs[2 * pieces : 3 * pieces], refs[3 * pieces : 4 * pieces]
    out_refs = refs[-9 - pieces : -9]
    keys, values, queries, grads, queries_t, grads_t, dq, dk_t, dv_t = refs[-9:]
    pair = first + pl.program_id(0)
    size = in_refs[0].shape[1]
    count, padded = pieces * size, keys.shape[0]
    blocks = padded // block
    lane = lane_ids(size)
    row = lax.broadcasted_iota(jnp.int32, (size, LANES), 0)
    for i in range(pieces):
        at = pl.ds(i * size, size)
        keys[at, :LANES] = in_refs[i][1]
        keys[at, LANES:] = jnp.where(
            lane == 0, jnp.where(row >= valid[i], MASKED, 0.0), jnp.where(lane < 4, 1.0, 0.0)
        ).astype(BF16)
        values[at, :LANES] = in_refs[i][2]
        values[at, LANES:] = jnp.where((lane > 0) & (lane < 4), 1.0, 0.0).astype(BF16)
        queries[0, at, :LANES] = in_refs[i][0]
        grads[0, at, :LANES] = grad_refs[i][...]
    if padded > count:
        left = padded - count
        rest = pl.ds(count, left)
        keys[rest, :LANES] = jnp.zeros((left, LANES), BF16)
        keys[rest, LANES:] = jnp.where(lane_ids(left) == 0, MASKED, 0.0).astype(BF16)
        values[rest, :] = jnp.zeros((left, 2 * LANES), BF16)
        for j in range(2):
            queries[j, rest, :] = jnp.zeros((left, 2 * LANES), BF16)
            grads[j, rest, :] = jnp.zeros((left, 2 * LANES), BF16)
    for b in range(blocks):
        at = pl.ds(b * block, block)
        queries_t[b] = (queries[0, at, :LANES].astype(F32) * scale).T.astype(BF16)
        grads_t[b] = turned(grads[0, at, :LANES])
    for j in range(2):
        mine = lane // HD == j
        for i in range(pieces):
            at = pl.ds(i * size, size)
            grad = jnp.where(mine, grad_refs[i][...].astype(F32), 0.0)
            queries[j, at, :LANES] = jnp.where(mine, in_refs[i][0].astype(F32) * (scale * LOG2E), 0.0).astype(BF16)
            grads[j, at, :LANES] = grad.astype(BF16)
            log_total = jnp.sum(
                jnp.where(lane == 2 * pair + j, total_refs[i][...], 0.0), axis=1, keepdims=True
            )
            high, mid, low = split3(-log_total)
            queries[j, at, LANES:] = jnp.where(
                lane == 0,
                1.0,
                jnp.where(lane == 1, high, jnp.where(lane == 2, mid, jnp.where(lane == 3, low, 0.0))),
            ).astype(BF16)
            inner = jnp.sum(grad * mix_refs[i][...].astype(F32), axis=1, keepdims=True)
            high, mid, low = split3(-inner)
            grads[j, at, LANES:] = jnp.where(
                lane == 1, high, jnp.where(lane == 2, mid, jnp.where(lane == 3, low, 0.0))
            ).astype(BF16)
    dk_t[...] = jnp.zeros_like(dk_t)
    dv_t[...] = jnp.zeros_like(dv_t)
    block_lane = lane_ids(block)
    for b in range(blocks):
        at = pl.ds(b * block, block)
        results = []
        for j in range(2):
            mine = pl.ds(j * HD, HD)
            probs = jnp.exp2(dot(queries[j, at, :], keys[...], NT))
            grad_scores = (probs * dot(grads[j, at, :], values[...], NT)).astype(BF16)
            results.append(dot(grad_scores, keys[:, :LANES]) * scale)
            dv_t[mine, :] += dot(grads_t[b, mine, :], probs.astype(BF16))
            dk_t[mine, :] += dot(queries_t[b, mine, :], grad_scores)
        dq[at, :] = jnp.where(block_lane < HD, results[0], results[1])
    dk, dv = dk_t[...].T, dv_t[...].T
    for i in range(pieces):
        at = slice(i * size, (i + 1) * size)
        out_refs[i][0] = dq[at, :].astype(BF16)
        out_refs[i][1] = dk[at, :].astype(BF16)
        out_refs[i][2] = dv[at, :].astype(BF16)


def attention_back(valid, parts, mixtures, grads, totals, block, first, pairs, into, after):
    pieces = len(parts)
    _, size, width = parts[0].shape
    padded = padded_len(pieces * size, block)
    triple = pl.BlockSpec((3, size, LANES), lambda h, _: (0, 0, first + h))
    single = pl.BlockSpec((size, LANES), lambda h, _: (0, first + h))
    in_specs = [triple] * pieces + [single] * 2 * pieces + [whole((size, LANES))] * pieces
    aliases = {1 + len(in_specs) + i: i for i in range(len(into))}
    return pl.pallas_call(
        functools.partial(attend_back_kernel, pieces=pieces, block=block, scale=HD**-0.5, first=first),
        grid_spec=pltpu.PrefetchScalarGridSpec(
            num_scalar_prefetch=1,
            grid=(pairs,),
            in_specs=in_specs + [pl.BlockSpec(memory_space=pl.ANY)] * (len(into) + len(after)),
            out_specs=[triple] * pieces,
            scratch_shapes=[
                pltpu.VMEM((padded, 2 * LANES), BF16),
                pltpu.VMEM((padded, 2 * LANES), BF16),
                pltpu.VMEM((2, padded, 2 * LANES), BF16),
                pltpu.VMEM((2, padded, 2 * LANES), BF16),
                pltpu.VMEM((padded // block, LANES, block), BF16),
                pltpu.VMEM((padded // block, LANES, block), BF16),
                pltpu.VMEM((padded, LANES), F32),
                pltpu.VMEM((LANES, padded), F32),
                pltpu.VMEM((LANES, padded), F32),
            ],
        ),
        out_shape=[jax.ShapeDtypeStruct((3, size, width), BF16)] * pieces,
        input_output_aliases=aliases,
        name="attend_back",
        **params_for(30 * pairs * LANES * padded * padded, 16 * size * LANES * pairs * pieces, pairs * 2 * padded * padded, weight=LONG),
    )(valid, *parts, *mixtures, *grads, *totals, *into, *after)


def merge_kernel(place, x_ref, own_ref, far_ref, table, own_w, far_w, middle_ref, branch_ref, normed_ref):
    branch = dot(own_ref[...], own_w[...]) + dot(far_ref[...], far_w[...])
    branch += table[OUT_SHIFT : OUT_SHIFT + 1, :]
    middle = x_ref[...].astype(F32) + table[SCALE1 : SCALE1 + 1, :] * branch
    middle_ref[...] = middle
    branch_ref[...] = branch
    normed_ref[...] = normalize(
        middle, table[GAIN2 : GAIN2 + 1, :], table[SHIFT2 : SHIFT2 + 1, :]
    ).astype(BF16)


ROWS = 352


def row_steps(tokens):
    return -(-tokens // ROWS)


def merge(place, x, own, far, table, rest):
    tokens, width = x.shape
    half = width // 2
    wide = pl.BlockSpec((ROWS, width), lambda i, _: (i, 0))
    narrow = pl.BlockSpec((ROWS, half), lambda i, _: (i, 0))
    return pl.pallas_call(
        merge_kernel,
        grid_spec=pltpu.PrefetchScalarGridSpec(
            num_scalar_prefetch=1,
            grid=(row_steps(tokens),),
            in_specs=[
                wide,
                narrow,
                narrow,
                whole(table.shape),
                pl.BlockSpec((half, width), lambda i, place: (place[CORE], rest.shape[1] // width - 1)),
                pl.BlockSpec((half, width), lambda i, place: (1 - place[CORE], rest.shape[1] // width - 1)),
            ],
            out_specs=[wide, wide, wide],
        ),
        out_shape=[
            jax.ShapeDtypeStruct((tokens, width), F32),
            jax.ShapeDtypeStruct((tokens, width), F32),
            jax.ShapeDtypeStruct((tokens, width), BF16),
        ],
        name="merge",
        **params_for(2 * tokens * width * width, 14 * tokens * width + 2 * width * width),
    )(place, x, own, far, table, rest, rest)


def gelu_and_slope(values):
    size = jnp.abs(values) * 0.7071067811865476
    t = 1.0 / (1.0 + 0.3275911 * size)
    bell = jnp.exp(-0.5 * (values * values))
    poly = t * (0.254829592 + t * (-0.284496736 + t * (1.421413741 + t * (-1.453152027 + t * 1.061405429))))
    tail = 0.5 * poly * bell
    phi = jnp.where(values < 0, tail, 1.0 - tail)
    return values * phi, phi + values * bell * 0.3989422804014327


def ungroup(grouped_ref, down):
    width = down.shape[1]
    groups = grouped_ref.shape[1] // width
    each = grouped_ref.shape[0] // 2
    for device in range(2):
        for g in range(groups):
            at = (device * groups + g) * each
            down[at : at + each, :] = grouped_ref[device * each : (device + 1) * each, g * width : (g + 1) * width]


def scaled_upstream(cotangent_ref, table):
    return (cotangent_ref[...].astype(F32) * table[SCALE2 : SCALE2 + 1, :]).astype(BF16)


def place_turned(place, block, target, k, chips):
    half = block.shape[1] // 2
    turned_block = block.T
    first, second = turned_block[:half], turned_block[half:]
    target[k * half : (k + 1) * half, :] = jnp.where(place[CORE] == 0, first, second)
    target[(chips + k) * half : (chips + k + 1) * half, :] = jnp.where(place[CORE] == 0, second, first)


def fill_turned(place, source_ref, target, chips):
    wide = source_ref.shape[1] // chips
    for k in range(chips):
        at = pl.ds(pl.multiple_of(place[CHIPS + k] * wide, wide), wide)
        place_turned(place, source_ref[:, at], target, k, chips)


def split_rows(grad, mine_ref, other_ref):
    chips, rows, _ = mine_ref.shape
    for k in range(chips):
        mine_ref[k] = grad[k * rows : (k + 1) * rows, :]
        other_ref[k] = grad[(chips + k) * rows : (chips + k + 1) * rows, :]


def group(grad, out_ref):
    rows, columns = out_ref.shape[1], grad.shape[1]
    for g in range(grad.shape[0] // rows):
        out_ref[0, :, g * columns : (g + 1) * columns] = grad[g * rows : (g + 1) * rows, :]


def mlp_kernel(
    place, normed_ref, cotangent_ref, table, up_ref, shift_ref, grouped_ref,
    branch_ref, delta_ref, up_mine_ref, up_other_ref, down_mine_ref, down_other_ref, grad_shift_ref,
    upstream, upstream_t, normed_t, down,
    *, chips,
):
    @pl.when(pl.program_id(0) == 0)
    def _():
        scaled = (cotangent_ref[...].astype(F32) * table[SCALE2 : SCALE2 + 1, :]).astype(BF16)
        upstream[...] = scaled
        upstream_t[...] = turned(scaled)
        fill_turned(place, normed_ref, normed_t, chips)
        branch_ref[...] = jnp.zeros_like(branch_ref)
        delta_ref[...] = jnp.zeros_like(delta_ref)

    ungroup(grouped_ref, down)
    hidden = dot(normed_ref[...], up_ref[...]) + shift_ref[...]
    grad_active = dot(upstream[...], down[...], NT)
    active, slope = gelu_and_slope(hidden)
    active = active.astype(BF16)
    delta_hidden = (grad_active * slope).astype(BF16)
    branch_ref[...] += dot(active, down[...])
    delta_ref[...] += dot(delta_hidden, up_ref[...], NT)
    split_rows(dot(normed_t[...], delta_hidden).astype(BF16), up_mine_ref, up_other_ref)
    grad_down = dot(upstream_t[...], active)
    each = grad_down.shape[1] // 2
    first, second = grad_down[:, :each], grad_down[:, each:]
    group(jnp.where(place[CORE] == 0, first, second).astype(BF16), down_mine_ref)
    group(jnp.where(place[CORE] == 0, second, first).astype(BF16), down_other_ref)
    grad_shift_ref[...] = total_rows(delta_hidden.astype(F32))


def mlp(place, normed, cotangent, table, rest, up_shift, owners):
    tokens, width = normed.shape
    hidden = up_shift.shape[1]
    rows = rest.shape[0] // owners
    chips = owners // 2
    block = hidden // chips
    up_out = pl.BlockSpec((chips, rows, block), lambda j, place: (0, 0, place[CHIPS + j]))
    down_out = pl.BlockSpec((1, rows, hidden), lambda j, _: (j, 0, 0))
    sent = jax.ShapeDtypeStruct((chips, rows, hidden), BF16)
    return pl.pallas_call(
        functools.partial(mlp_kernel, chips=chips),
        grid_spec=pltpu.PrefetchScalarGridSpec(
            num_scalar_prefetch=1,
            grid=(chips,),
            in_specs=[
                whole((tokens, width)),
                whole((tokens, width)),
                whole(table.shape),
                pl.BlockSpec((width, block), lambda j, place: (0, place[CHIPS + j])),
                pl.BlockSpec((1, block), lambda j, place: (0, place[CHIPS + j])),
                pl.BlockSpec((2 * rows, hidden), lambda j, place: (place[CHIPS + j], 1)),
            ],
            out_specs=[
                whole((tokens, width)),
                whole((tokens, width)),
                up_out,
                up_out,
                down_out,
                down_out,
                pl.BlockSpec((1, block), lambda j, place: (0, place[CHIPS + j])),
            ],
            scratch_shapes=[
                pltpu.VMEM((tokens, width), BF16),
                pltpu.VMEM((width, tokens), BF16),
                pltpu.VMEM((width, tokens), BF16),
                pltpu.VMEM((block, width), BF16),
            ],
        ),
        out_shape=[
            jax.ShapeDtypeStruct((tokens, width), F32),
            jax.ShapeDtypeStruct((tokens, width), F32),
            sent,
            sent,
            sent,
            sent,
            jax.ShapeDtypeStruct((1, hidden), F32),
        ],
        name="mlp",
        **params_for(12 * tokens * width * hidden, 12 * tokens * width + 8 * width * hidden, 2 * tokens * hidden),
    )(place, normed, cotangent, table, rest, up_shift, rest)


SUM_ROWS = 8


def unmerge_kernel(
    place, middle_ref, branch1_ref, branch2_ref, delta_ref, cotangent_ref, own_ref, far_ref, table, own_w, far_w,
    output_ref, delta_middle_ref, own_grad_ref, far_grad_ref, mine_ref, other_ref, sums_ref,
    delta1_all, mixture_t,
    *, tokens,
):
    step = pl.program_id(0)

    @pl.when(step == 0)
    def _():
        sums_ref[...] = jnp.zeros_like(sums_ref)

    rows, width = middle_ref.shape
    inside = lax.broadcasted_iota(jnp.int32, (rows, width), 0) + step * rows < tokens

    def kept(values):
        return jnp.where(inside, values, 0.0)

    upstream = cotangent_ref[...].astype(F32)
    scale2 = table[SCALE2 : SCALE2 + 1, :]
    middle = middle_ref[...]
    branch2 = branch2_ref[...] + table[DOWN_SHIFT : DOWN_SHIFT + 1, :]
    output_ref[...] = (middle + scale2 * branch2).astype(BF16)
    delta2 = (scale2 * upstream).astype(BF16).astype(F32)
    delta = delta_ref[...]
    inner, gain_terms = normalize_back(middle, table[GAIN2 : GAIN2 + 1, :], delta)
    delta_middle = upstream + inner
    delta_middle_ref[...] = delta_middle
    delta1 = kept(table[SCALE1 : SCALE1 + 1, :] * delta_middle).astype(BF16)
    delta1_all[pl.ds(pl.multiple_of(step * rows, 16), rows), :] = delta1
    own_grad_ref[...] = dot(delta1, own_w[...], NT).astype(BF16)
    far_grad_ref[...] = dot(delta1, far_w[...], NT).astype(BF16)
    terms = (
        upstream * branch2,
        delta2,
        gain_terms,
        delta,
        delta_middle * branch1_ref[...],
        delta1.astype(F32),
    )
    for i, term in enumerate(terms):
        sums_ref[i : i + 1, :] += total_rows(kept(term))

    @pl.when(step == pl.num_programs(0) - 1)
    def _():
        chips = mine_ref.shape[0]
        wide = width // chips
        for k in range(chips):
            chip = place[CHIPS + k]
            at = pl.ds(pl.multiple_of(lax.rem(chip, chips // 2) * wide, wide), wide)
            mixed = jnp.where(chip // (chips // 2) == place[CORE], own_ref[:, at], far_ref[:, at])
            place_turned(place, mixed, mixture_t, k, chips)
        split_rows(dot(mixture_t[...], delta1_all[:tokens, :]).astype(BF16), mine_ref, other_ref)


def unmerge(place, middle, branch1, branch2, delta, cotangent, own, far, table, rest, owners):
    tokens, width = middle.shape
    chips = owners // 2
    sent = (chips, width // owners, width)
    half = width // 2
    steps = row_steps(tokens)
    wide = pl.BlockSpec((ROWS, width), lambda i, _: (i, 0))
    narrow = pl.BlockSpec((ROWS, half), lambda i, _: (i, 0))
    return pl.pallas_call(
        functools.partial(unmerge_kernel, tokens=tokens),
        grid_spec=pltpu.PrefetchScalarGridSpec(
            num_scalar_prefetch=1,
            grid=(steps,),
            in_specs=[wide] * 5
            + [whole((tokens, half))] * 2
            + [
                whole(table.shape),
                pl.BlockSpec((half, width), lambda i, place: (place[CORE], rest.shape[1] // width - 1)),
                pl.BlockSpec((half, width), lambda i, place: (1 - place[CORE], rest.shape[1] // width - 1)),
            ],
            out_specs=[wide, wide, narrow, narrow, whole(sent), whole(sent), whole((SUM_ROWS, width))],
            scratch_shapes=[pltpu.VMEM((steps * ROWS, width), BF16), pltpu.VMEM((width, tokens), BF16)],
        ),
        out_shape=[
            jax.ShapeDtypeStruct((tokens, width), BF16),
            jax.ShapeDtypeStruct((tokens, width), F32),
            jax.ShapeDtypeStruct((tokens, half), BF16),
            jax.ShapeDtypeStruct((tokens, half), BF16),
            jax.ShapeDtypeStruct(sent, BF16),
            jax.ShapeDtypeStruct(sent, BF16),
            jax.ShapeDtypeStruct((SUM_ROWS, width), F32),
        ],
        name="unmerge",
        **params_for(4 * tokens * width * width, 30 * tokens * width + 4 * width * width),
    )(place, middle, branch1, branch2, delta, cotangent, own, far, table, rest, rest)


def unproject_kernel(
    place, x_hbm, delta_middle_hbm, table, normed_ref, own_ref, far_ref, weight_ref, middle_sums, up_sums, *refs, chips
):
    (
        out_ref, mine_ref, other_ref, vectors_mine_ref, vectors_other_ref,
        delta, sums, normed_t, x_ref, delta_middle_ref, laid, arrived,
    ) = refs
    step = pl.program_id(0)
    core = place[CORE]
    copies = [
        pltpu.make_async_copy(x_hbm, x_ref, arrived.at[0]),
        pltpu.make_async_copy(delta_middle_hbm, delta_middle_ref, arrived.at[1]),
    ]

    @pl.when(step == 0)
    def _():
        for copy in copies:
            copy.start()
        fill_turned(place, normed_ref, normed_t, chips)
        delta[...] = jnp.zeros_like(delta)
        sums[...] = jnp.zeros_like(sums)

    own, far = own_ref[0], far_ref[0]
    block = jnp.concatenate([jnp.where(core == 0, own, far), jnp.where(core == 0, far, own)], axis=1)
    split_rows(dot(normed_t[...], block).astype(BF16), mine_ref, other_ref)
    delta[...] += dot(block, weight_ref[...], NT)
    for kind, row in ((0, QUERY), (2, VALUE)):

        @pl.when(step == kind)
        def _():
            sums[row : row + 1, :] = total_rows(block.astype(F32))

    @pl.when(step == pl.num_programs(0) - 1)
    def _():
        for copy in copies:
            copy.wait()
        delta_normed = delta[...]
        inner, gain_terms = normalize_back(
            x_ref[...].astype(F32), table[GAIN1 : GAIN1 + 1, :], delta_normed
        )
        out_ref[...] = (delta_middle_ref[...] + inner).astype(BF16)
        rows = {
            GAIN1: total_rows(gain_terms),
            SHIFT1: total_rows(delta_normed),
            OUT_SHIFT: middle_sums[5:6, :],
            SCALE1: middle_sums[4:5, :],
            GAIN2: middle_sums[2:3, :],
            SHIFT2: middle_sums[3:4, :],
            DOWN_SHIFT: middle_sums[1:2, :],
            SCALE2: middle_sums[0:1, :],
        }
        for i, values in rows.items():
            sums[i : i + 1, :] = values
        each = up_sums.shape[1] // (2 * chips)
        laid[...] = jnp.zeros_like(laid)
        for out, side in ((vectors_mine_ref, core), (vectors_other_ref, 1 - core)):
            for k in range(chips):
                chip = place[CHIPS + k]
                at = pl.ds(pl.multiple_of(chip * LANES, LANES), LANES)
                laid[k, : sums.shape[0], :] = sums[:, at]
                for r in range(each // LANES):
                    at = pl.multiple_of((2 * chip + side) * each + r * LANES, LANES)
                    laid[k, VECTORS + r : VECTORS + r + 1, :] = up_sums[:, pl.ds(at, LANES)]
            out[...] = laid[...].astype(BF16)


def unproject(place, x, delta_middle, table, normed, own, far, weight, middle_sums, up_sums, owners):
    tokens, width = x.shape
    half = width // 2
    chips = owners // 2
    rows = width // owners
    vectors = (chips, rows, LANES)
    anywhere = pl.BlockSpec(memory_space=pl.ANY)
    kind = pl.BlockSpec((1, tokens, half), lambda j, _: (j, 0, 0))
    sent = pl.BlockSpec((chips, rows, width), lambda j, _: (0, 0, j))
    return pl.pallas_call(
        functools.partial(unproject_kernel, chips=chips),
        grid_spec=pltpu.PrefetchScalarGridSpec(
            num_scalar_prefetch=1,
            grid=(3,),
            in_specs=[
                anywhere,
                anywhere,
                whole(table.shape),
                whole((tokens, width)),
                kind,
                kind,
                pl.BlockSpec((width, width), lambda j, _: (0, j)),
                whole(middle_sums.shape),
                whole(up_sums.shape),
            ],
            out_specs=[whole((tokens, width)), sent, sent, whole(vectors), whole(vectors)],
            scratch_shapes=[
                pltpu.VMEM((tokens, width), F32),
                pltpu.VMEM((16, width), F32),
                pltpu.VMEM((width, tokens), BF16),
                pltpu.VMEM((tokens, width), BF16),
                pltpu.VMEM((tokens, width), F32),
                pltpu.VMEM(vectors, F32),
                pltpu.SemaphoreType.DMA((2,)),
            ],
        ),
        out_shape=[
            jax.ShapeDtypeStruct((tokens, width), BF16),
            jax.ShapeDtypeStruct((chips, rows, 3 * width), BF16),
            jax.ShapeDtypeStruct((chips, rows, 3 * width), BF16),
            jax.ShapeDtypeStruct(vectors, BF16),
            jax.ShapeDtypeStruct(vectors, BF16),
        ],
        name="unproject",
        **params_for(12 * tokens * width * width, 18 * tokens * width + 12 * width * width, weight=SHORT),
    )(place, x, delta_middle, table, normed, own, far, weight, middle_sums, up_sums)


def ring_of(chips):
    return list(range(0, chips, 2)) + list(range(1, chips, 2))[::-1]


def places(owners):
    ring = ring_of(owners // 2)
    rows = []
    for f in range(owners):
        chip, core = divmod(f, 2)
        at = ring.index(chip)
        columns = [1 - core, 3 - core, 5 - core, core, 2 + core, 4 + core]
        rows.append(columns + [core] + ring[at:] + ring[:at])
    return np.array(rows, np.int32)


def ring_perm(chips, hop):
    ring = ring_of(chips)
    return [
        (2 * ring[i] + core, 2 * ring[(i + hop) % chips] + core) for i in range(chips) for core in range(2)
    ]


def to_next(values, chips, hop):
    return lax.ppermute(values, "fsdp", ring_perm(chips, hop))


def ring_gather(piece, chips):
    pieces = [None] * chips
    pieces[0] = right = left = piece
    for k in range(1, chips // 2 + 1):
        pieces[-k] = right = to_next(right, chips, 1)
        if k < chips - chips // 2:
            pieces[k] = left = to_next(left, chips, -1)
    return pieces


def low_part(columns):
    return columns // 2 if columns % (2 * LANES) == 0 else columns


def ring_add_kernel(*refs, columns, mode, carried):
    ways = 2 if mode in ("second", "next") else 1
    shares = [refs[2 * len(columns) * d : 2 * len(columns) * (d + 1)] for d in range(ways)]
    came = refs[2 * len(columns) * ways :]
    outs = refs[len(refs) - carried - (1 if mode == "total" else 2) : len(refs) - carried]
    start, low_start, high_start = 0, 0, 0
    for i, each in enumerate(columns):
        totals = [mine[2 * i][0].astype(F32) + mine[2 * i + 1][0].astype(F32) for mine in shares]
        at = slice(start, start + each)
        low = low_part(each)
        low_at, high_at = slice(low_start, low_start + low), slice(high_start, high_start + each - low)
        if mode == "first":
            outs[0][:, low_at] = totals[0][:, :low].astype(BF16)
            if low < each:
                outs[1][:, high_at] = totals[0][:, low:].astype(BF16)
        elif mode == "second":
            outs[0][:, start : start + low] = (totals[0][:, :low] + came[0][:, low_at].astype(F32)).astype(BF16)
            outs[1][:, start : start + low] = totals[1][:, :low].astype(BF16)
            if low < each:
                high = totals[1][:, low:] + came[1][:, high_at].astype(F32)
                outs[0][:, start + low : start + each] = totals[0][:, low:].astype(BF16)
                outs[1][:, start + low : start + each] = high.astype(BF16)
        elif mode == "next":
            for total, arrived, out in zip(totals, came, outs):
                out[:, at] = (total + arrived[:, at].astype(F32)).astype(BF16)
        else:
            both_ways = came[0][:, at].astype(F32) + came[1][:, at].astype(F32)
            outs[0][:, at] = (totals[0] + both_ways).astype(BF16)
        start, low_start, high_start = at.stop, low_at.stop, high_at.stop


class RingSum:
    def __init__(self, *parts):
        self.parts, self.chips = [part[:2] for part in parts], parts[0][0].shape[0]
        self.columns = [part[0].shape[2] // part[3] for part in parts]
        self.blocks = [part[2] for part in parts]
        self.steps = self.chips // 2
        self.step = 0
        self.came = []

    def add(self, mode, places, after=(), carry=()):
        rows = self.parts[0][0].shape[1]
        columns = self.columns
        total = sum(columns)
        blocks = 2 if total > 4096 else 1
        arrays, specs = [], []
        for at in places:
            for part, each, block in zip(self.parts, columns, self.blocks):
                for array in part:
                    arrays.append(array)
                    specs.append(pl.BlockSpec((1, rows // blocks, each), lambda i, at=at, block=block: (at, i, block)))
        for came in self.came:
            arrays.append(came)
            specs.append(pl.BlockSpec((rows // blocks, came.shape[1]), lambda i: (i, 0)))
        arrays += [*after, *carry]
        anywhere = pl.BlockSpec(memory_space=pl.ANY)
        specs += [anywhere] * (len(after) + len(carry))
        low = sum(low_part(each) for each in columns)
        out_columns = {"first": [low, total - low], "total": [total]}.get(mode, [total, total])
        sums = len(out_columns)
        outs = pl.pallas_call(
            functools.partial(ring_add_kernel, columns=columns, mode=mode, carried=len(carry)),
            grid=(blocks,),
            in_specs=specs,
            out_specs=[pl.BlockSpec((rows // blocks, out), lambda i: (i, 0)) for out in out_columns]
            + [anywhere] * len(carry),
            out_shape=[jax.ShapeDtypeStruct((rows, out), BF16) for out in out_columns]
            + [jax.ShapeDtypeStruct(array.shape, array.dtype) for array in carry],
            input_output_aliases={len(arrays) - len(carry) + i: sums + i for i in range(len(carry))},
            name="ring_add",
            **params_for(6 * rows * total, 16 * rows * total, weight=SHORT, vmem=VMEM_LIMIT if blocks > 1 else SMALL_VMEM),
        )(*arrays)
        return outs[:sums], outs[sums:]

    def sums(self, after=(), carry=()):
        k = self.steps - self.step
        if self.step == 0:
            return self.add("first", [k], after, carry)
        return self.add("second" if self.step == 1 else "next", [k, self.chips - k], after, carry)

    def send(self, sums):
        self.came = [to_next(sums[0], self.chips, 1), to_next(sums[1], self.chips, -1)]
        self.step += 1

    def total(self, after=(), carry=()):
        assert self.step == self.steps
        sums, carried = self.add("total", [0], after, carry)
        return sums[0], carried


def passed(arrays, after):
    anywhere = pl.BlockSpec(memory_space=pl.ANY)
    return pl.pallas_call(
        lambda *refs: None,
        in_specs=[anywhere] * (len(arrays) + len(after)),
        out_specs=[anywhere] * len(arrays),
        out_shape=[jax.ShapeDtypeStruct(array.shape, array.dtype) for array in arrays],
        input_output_aliases={i: i for i in range(len(arrays))},
        name="passed",
        **params_for(1, 1, vmem=SMALL_VMEM),
    )(*arrays, *after)


def finish_rest_kernel(part_ref, came_ref, up_ref, down_ref):
    def total(at):
        return part_ref[:, at].astype(F32) + came_ref[:, at].astype(F32)

    rows, hidden = up_ref.shape
    each, width = down_ref.shape
    up_ref[...] = total(slice(0, hidden))
    for g in range(0, width // rows, 2):
        pair = [total(slice(hidden + each * h, hidden + each * (h + 1))) for h in (g, g + 1)]
        down_ref[:, g * rows : (g + 2) * rows] = jnp.concatenate(pair, axis=0).T


def finish_rest(part, came, hidden, each, width):
    in_vmem = pl.BlockSpec(memory_space=pltpu.VMEM)
    rows = part.shape[0]
    return pl.pallas_call(
        finish_rest_kernel,
        in_specs=[in_vmem] * 2,
        out_specs=[in_vmem] * 2,
        out_shape=[jax.ShapeDtypeStruct(shape, F32) for shape in ((rows, hidden), (each, width))],
        name="finish_rest",
        **params_for(part.size, 8 * part.size, weight=SHORT, vmem=2 * SMALL_VMEM),
    )(part, came)


def finish_first_kernel(place, *refs):
    parts, came, (packed_ref, output_ref), vector_refs = refs[:2], refs[2:4], refs[4:6], refs[6:]
    packed, out = packed_ref.shape[1] // 2, output_ref.shape[1] // 2
    for i in range(2):
        total = parts[i][...].astype(F32) + came[i][...].astype(F32)
        packed_ref[:, packed * i : packed * (i + 1)] = total[:, :packed]
        output_ref[:, out * i : out * (i + 1)] = total[:, packed : packed + out]
        if i == 0:
            vectors = total[:16, packed + out :]
    half = LANES // 2
    mine = jnp.where(place[CORE] == 0, vectors[:, :half], vectors[:, half:])
    for i in range(VECTORS):
        vector_refs[i][...] = mine[i : i + 1, :].reshape(half)
    count = vector_refs[VECTORS].shape[0]
    vector_refs[VECTORS][...] = vectors[VECTORS : VECTORS + count // LANES, :].reshape(count)


def finish_first(place, parts, came, width, each):
    in_vmem = pl.BlockSpec(memory_space=pltpu.VMEM)
    rows = parts[0].shape[0]
    shapes = [(rows, 3 * width), (rows, width)] + [(rows,)] * VECTORS + [(each,)]
    return pl.pallas_call(
        finish_first_kernel,
        in_specs=[pl.BlockSpec(memory_space=pltpu.SMEM)] + [in_vmem] * 4,
        out_specs=[in_vmem] * len(shapes),
        out_shape=[jax.ShapeDtypeStruct(shape, F32) for shape in shapes],
        name="finish_first",
        **params_for(8 * rows * width, 32 * rows * width, weight=SHORT, vmem=SMALL_VMEM),
    )(place, *parts, *came)


def split_pairs(pairs):
    return [pairs // 4, pairs // 4, pairs - 2 * (pairs // 4)] if pairs >= 4 else [pairs]


def paired_body(
    tokens, lengths, norm1_gain, norm1_bias, packed_weight, query_bias, value_bias, output_weight, output_bias,
    layer_scale1, norm2_gain, norm2_bias, up_weight, up_bias, down_weight, down_bias, layer_scale2, cotangent,
):
    owners = lax.axis_size("fsdp")
    chips = owners // 2
    _, local_len, width = tokens.shape
    me = lax.axis_index("fsdp")
    core = lax.rem(me, 2)
    place = lax.dynamic_index_in_dim(jnp.asarray(places(owners)), me, keepdims=False)
    moves = [(f * 2 + s, (f - f % 2 + s) * 2 + f % 2) for f in range(owners) for s in range(2) if f % 2 != s]
    twin = [(f, f ^ 1) for f in range(owners)]
    stays = core == lax.axis_index("seq")

    def regroup_moves(values):
        return lax.ppermute(values, ("fsdp", "seq"), moves)

    def regrouped(values):
        return jnp.where(stays, values, regroup_moves(values))

    def to_twin(values):
        return lax.ppermute(values, "fsdp", twin)

    def across(values):
        return lax.ppermute(values, "seq", [(0, 1), (1, 0)])

    vectors = (
        norm1_gain, norm1_bias, query_bias, value_bias, output_bias, layer_scale1, norm2_gain, norm2_bias,
        down_bias, layer_scale2,
    )
    rows = norm1_gain.shape[0]
    hidden = up_weight.shape[1]
    first, rest = pack(packed_weight, up_weight, down_weight, output_weight, vectors, up_bias)
    own_pieces = ring_gather(first, chips)
    far_pieces = [to_twin(piece) for piece in own_pieces]
    x = regrouped(tokens.reshape(local_len, width))
    valid_count = regrouped(lengths)
    rest = lax.all_gather(rest, "fsdp", axis=0, tiled=True)
    starts = jnp.stack([core, 1 - core]) * local_len
    valid = jnp.clip(valid_count - starts, 0, local_len).astype(jnp.int32)
    upstream = regrouped(cotangent.reshape(local_len, width))

    far_out, own_part, normed, packed_full, table, up_shift = project(place, x, own_pieces, far_pieces, hidden)
    far_part = to_twin(far_out)
    parts = [own_part, far_part]
    (own_mix, far_mix_out), totals = attention(valid, parts, 352)
    far_mix = to_twin(far_mix_out)
    middle, branch1, normed2 = merge(place, x, own_mix, far_mix, table, rest)

    branch2, delta_normed2, up_mine, up_other, down_mine, down_other, up_sums = mlp(
        place, normed2, upstream, table, rest, up_shift, owners
    )
    up_twin, down_twin = to_twin(up_other), to_twin(down_other)
    output, delta_middle, own_grad, far_grad_out, output_mine, output_other, middle_sums = unmerge(
        place, middle, branch1, branch2, delta_normed2, upstream, own_mix, far_mix, table, rest, owners
    )
    far_grad = to_twin(far_grad_out)
    ring = RingSum((up_mine, up_twin, 0, 1), (down_mine, down_twin, 0, 1))
    output_sent = regroup_moves(output)
    output_twin = to_twin(output_other)
    deltas = ()
    grads = [own_grad, far_grad]
    start = 0
    for pairs in split_pairs(width // 2 // LANES):
        sums, _ = ring.sums()
        ring.send(sums)
        after = [*sums, output_sent, output_twin] if start else sums
        deltas = attention_back(
            valid, parts, [own_mix, far_mix_out], grads, totals, 352, start, pairs, deltas, after
        )
        start += pairs
    own_delta, far_delta_out = deltas
    sums, (far_delta_out,) = ring.sums(carry=[far_delta_out])
    ring.send(sums)
    far_delta = to_twin(far_delta_out)
    grad_x, packed_mine, packed_other, vectors_mine, vectors_other = unproject(
        place, x, delta_middle, table, normed, own_delta, far_delta, packed_full, middle_sums, up_sums, owners
    )
    output = jnp.where(stays, output, output_sent).reshape(tokens.shape)
    grad_x, packed_other, vectors_other = passed([grad_x, packed_other, vectors_other], ring.came)
    vectors_twin, packed_twin = to_twin(vectors_other), to_twin(packed_other)
    rest_sum, _ = ring.total()
    rings = (
        RingSum(
            (packed_mine, packed_twin, 0, 2), (output_mine, output_twin, 0, 2), (vectors_mine, vectors_twin, 0, 1)
        ),
        RingSum((packed_mine, packed_twin, 1, 2), (output_mine, output_twin, 1, 2)),
    )
    grad_x_sent, rest_sent = regroup_moves(grad_x), across(rest_sum)
    last = [rest_sum]
    for step in range(rings[0].steps):
        for half in rings:
            after = [*last] + ([grad_x_sent] if step == 2 and half is rings[0] else [])
            last, _ = half.sums(after)
            half.send(last)
    grad_tokens = jnp.where(stays, grad_x, grad_x_sent).astype(F32).reshape(tokens.shape)
    each = up_bias.shape[0]
    grad_up, grad_down = finish_rest(rest_sum, rest_sent, hidden, each, width)
    first_sum, _ = rings[0].total()
    first_sums = [first_sum, rings[1].total([first_sum])[0]]
    grad_packed, grad_output, *mine = finish_first(
        place, first_sums, [across(half) for half in first_sums], width, each
    )
    return (
        output, grad_tokens, mine[0], mine[1], grad_packed, mine[2], mine[3], grad_output, mine[4], mine[5],
        mine[6], mine[7], grad_up, mine[10], grad_down, mine[8], mine[9],
    )


def pairable(tokens, up_weight):
    owners, chips = lax.axis_size("fsdp"), lax.axis_size("fsdp") // 2
    width, hidden = up_weight.shape[0] * owners, up_weight.shape[1]
    return (
        lax.axis_size("seq") == 2
        and tokens.shape[0] == 1
        and tokens.shape[1] % 16 == 0
        and owners == 2 * chips
        and chips in (4, 8)
        and width % (chips * LANES) == 0
        and hidden % (owners * LANES) == 0
        and H * HD == width
    )


def body(*args):
    chosen = paired_body if pairable(args[0], args[12]) else general_body
    return chosen(*args)


def solution(mesh):
    in_specs = (
        P("fsdp", "seq", None),
        P("fsdp"),
        P("fsdp"),
        P("fsdp"),
        P("fsdp", None),
        P("fsdp"),
        P("fsdp"),
        P("fsdp", None),
        P("fsdp"),
        P("fsdp"),
        P("fsdp"),
        P("fsdp"),
        P("fsdp", None),
        P("fsdp"),
        P("fsdp", None),
        P("fsdp"),
        P("fsdp"),
        P("fsdp", "seq", None),
    )
    out_specs = (
        P("fsdp", "seq", None),
        P("fsdp", "seq", None),
        P("fsdp"),
        P("fsdp"),
        P("fsdp", None),
        P("fsdp"),
        P("fsdp"),
        P("fsdp", None),
        P("fsdp"),
        P("fsdp"),
        P("fsdp"),
        P("fsdp"),
        P("fsdp", None),
        P("fsdp"),
        P("fsdp", None),
        P("fsdp"),
        P("fsdp"),
    )
    return jax.shard_map(body, mesh=mesh, in_specs=in_specs, out_specs=out_specs, check_vma=False)
```
